32 devices in a mesh: dp: 4 (over y, x), fsdp: 8 (over z, core).
Axes of the slice: x: 2, y: 2, z: 4, core: 2. Of those that a mesh axis runs over, the one named last changes fastest.
Arguments:
- images: bfloat16 [2048, 16, 256], P(('dp', 'fsdp')), as said below
- partner: int32 [2048], P(('dp', 'fsdp')), may hold values from 0 to 63
- mix_weight: float32 [2048], P(('dp', 'fsdp')), may hold values from 0.2 to 0.8
- labels: int32 [2048], P(('dp', 'fsdp')), may hold values from 0 to 999
- block_master: float32 [3, 1005120], P(None, 'fsdp')
- block_first: float32 [3, 1005120], P(None, 'fsdp')
- block_second: float32 [3, 1005120], P(None, 'fsdp'), as said below
- block_average: float32 [3, 1005120], P(None, 'fsdp')
- head_master: float32 [1610240], P('fsdp')
- head_first: float32 [1610240], P('fsdp')
- head_second: float32 [1610240], P('fsdp'), as said below
- head_average: float32 [1610240], P('fsdp')
- bias_master: float32 [1000], replicated, may hold values from -0.75 to 0.75
- bias_first: float32 [1000], replicated, may hold values from -0.015625 to 0.015625
- bias_second: float32 [1000], replicated, may hold values from 1e-06 to 4e-06
- bias_average: float32 [1000], replicated, may hold values from -0.75 to 0.75
Outputs:
- loss_sum: float32 [], replicated
- block_master_new: float32 [3, 1005120], P(None, 'fsdp')
- block_first_new: float32 [3, 1005120], P(None, 'fsdp')
- block_second_new: float32 [3, 1005120], P(None, 'fsdp')
- block_average_new: float32 [3, 1005120], P(None, 'fsdp')
- head_master_new: float32 [1610240], P('fsdp')
- head_first_new: float32 [1610240], P('fsdp')
- head_second_new: float32 [1610240], P('fsdp')
- head_average_new: float32 [1610240], P('fsdp')
- bias_master_new: float32 [1000], replicated
- bias_first_new: float32 [1000], replicated
- bias_second_new: float32 [1000], replicated
- bias_average_new: float32 [1000], replicated
The draws below stay inside these ranges and needn't reach their ends.
Inputs may be any that keep to these rules, and one draw needn't show every extreme that they name: The partner of image i is image 64 * floor(i / 64) + partner[i]. `images`: feature maps of order one. `block_second`: positive. `head_second`: positive.
All inputs are finite; a program needn't handle non-finite values.
Results may differ from the reference program's by a relative error of at most 0.028.
Values may be sent and summed in bfloat16 or wider, within the bound.
A program may use at most 320 MiB of HBM per device.

```python
import math
from functools import partial
import jax
import jax.numpy as jnp
import numpy as np
from jax import lax

C = 256
E = 1536
SQ = 64
HD = 1280
K = 1000
SIDE = 4
PIX = 16
LAYERS = 3
STEP = 5
IMG_DEV = 64
IMAGES = 2048
PB = 1005120
PH = 1610240
N_FSDP = 8


def block_tables():
    grad_unit = IMAGES ** (-0.5)
    table = [(C * E, C ** (-0.5), 0.0, 0.005), (E * C, E ** (-0.5), 0.0, 0.005), (E * SQ, 2.0 * E ** (-0.5), 0.0, 0.0005), (SQ * E, 2.0 * SQ ** (-0.5), 0.0, 0.0005), (9 * E, 1.0 / 3.0, 0.0, 0.005), (E, 0.1, 1.0, 0.005), (E, 0.1, 0.0, 0.005), (E, 0.1, 1.0, 0.005), (E, 0.1, 0.0, 0.005), (E, 0.3, 0.0, 0.0005), (SQ, 0.3, 0.0, 0.0005), (C, 0.1, 1.0, 0.005), (C, 0.1, 0.0, 0.005)]
    scales = np.concatenate([np.full(segment[0], segment[1], np.float32) for segment in table])
    offsets = np.concatenate([np.full(segment[0], segment[2], np.float32) for segment in table])
    grads = np.concatenate([np.full(segment[0], segment[3] * grad_unit, np.float32) for segment in table])
    return (jnp.asarray(scales), jnp.asarray(offsets), jnp.asarray(grads))


def head_tables():
    grad_unit = IMAGES ** (-0.5)
    table = [(C, C ** (-0.5), 0.0, 0.005), (1, 0.1, 1.0, 0.005), (1, 0.1, 0.0, 0.005), (K, 3.0 * HD ** (-0.5), 0.0, 0.01)]
    scales = np.tile(np.concatenate([np.full(segment[0], segment[1], np.float32) for segment in table]), HD)
    offsets = np.tile(np.concatenate([np.full(segment[0], segment[2], np.float32) for segment in table]), HD)
    grads = np.tile(np.concatenate([np.full(segment[0], segment[3] * grad_unit, np.float32) for segment in table]), HD)
    return (jnp.asarray(scales), jnp.asarray(offsets), jnp.asarray(grads))


def draw_images(key, part):
    key = jax.random.fold_in(key, 11)
    ranked = jnp.arange(IMAGES, dtype=jnp.float32) / max(IMAGES - 1, 1)
    noise = jax.random.normal(key, (IMAGES, PIX, C), jnp.float32)
    scales = jnp.exp(ranked * math.log(3.0))
    return (noise * scales[:, None, None]).astype(jnp.bfloat16)


def draw_block_master(key, part):
    key = jax.random.fold_in(key, 1)
    scales, offsets, grads = block_tables()
    return offsets + scales * jax.random.normal(key, (LAYERS, PB), jnp.float32)


def draw_block_first(key, part):
    key = jax.random.fold_in(key, 2)
    scales, offsets, grads = block_tables()
    return grads * jax.random.normal(key, (LAYERS, PB), jnp.float32)


def draw_block_second(key, part):
    key = jax.random.fold_in(key, 3)
    scales, offsets, grads = block_tables()
    factor = jnp.exp(jax.random.uniform(key, (LAYERS, PB), jnp.float32, 0.0, math.log(4.0)))
    return grads * grads * factor


def draw_block_average(key, part):
    key = jax.random.fold_in(key, 4)
    scales, offsets, grads = block_tables()
    return offsets + scales * jax.random.normal(key, (LAYERS, PB), jnp.float32)


def draw_head_master(key, part):
    key = jax.random.fold_in(key, 5)
    scales, offsets, grads = head_tables()
    return offsets + scales * jax.random.normal(key, (PH,), jnp.float32)


def draw_head_first(key, part):
    key = jax.random.fold_in(key, 6)
    scales, offsets, grads = head_tables()
    return grads * jax.random.normal(key, (PH,), jnp.float32)


def draw_head_second(key, part):
    key = jax.random.fold_in(key, 7)
    scales, offsets, grads = head_tables()
    factor = jnp.exp(jax.random.uniform(key, (PH,), jnp.float32, 0.0, math.log(4.0)))
    return grads * grads * factor


def draw_head_average(key, part):
    key = jax.random.fold_in(key, 8)
    scales, offsets, grads = head_tables()
    return offsets + scales * jax.random.normal(key, (PH,), jnp.float32)


def with_ends(drawn, rng, smallest, largest):
    shape = drawn.shape
    index_at = [jax.random.randint(jax.random.fold_in(rng, axis), (), 0, shape[axis]) for axis in range(len(shape))]
    drawn = drawn.at[tuple(index_at)].set(smallest)
    longest = shape.index(max(shape))
    index_at[longest] = (index_at[longest] + 1) % shape[longest]
    return drawn.at[tuple(index_at)].set(largest)


def shard_levels(own_key, dims, cuts, least, top_value):
    def one(position, shards_of):
        steps = jax.random.uniform(jax.random.fold_in(jax.random.fold_in(own_key, 6), position), (shards_of,), jnp.float32, least / len(cuts), top_value / len(cuts))
        return jnp.repeat(jnp.exp(steps), dims[position] // shards_of).reshape((-1,) + (1,) * (len(dims) - position - 1))

    level = one(*cuts[0])
    for cut in cuts[1:]:
        level = level * one(*cut)
    return level


def bell_draw(key, shape, scale, limit, kind=jnp.bfloat16):
    entries = jax.random.normal(key, shape, jnp.float32) * scale
    return jnp.minimum(jnp.maximum(entries, -limit), limit).astype(kind)


def setup_inputs(seed: int = 0) -> dict:
    key_of = jax.random.split(jax.random.key(seed), 17)
    images = draw_images(jax.random.fold_in(key_of[16], 71), 0)
    partner = with_ends(jax.random.randint(key_of[1], (IMAGES,), 0, IMG_DEV), jax.random.fold_in(key_of[1], 1), 0, IMG_DEV - 1).astype(jnp.int32)
    mix_weight = jnp.clip(0.2 + 0.6 * jax.random.uniform(key_of[2], (IMAGES,), jnp.float32) ** shard_levels(key_of[2], (IMAGES,), ((0, 32),), -0.2, 0.2), 0.2, 0.8)
    labels = with_ends(jax.random.randint(key_of[3], (IMAGES,), 0, K), jax.random.fold_in(key_of[3], 1), 0, K - 1).astype(jnp.int32)
    block_master = draw_block_master(jax.random.fold_in(key_of[16], 71), 0)
    block_first = draw_block_first(jax.random.fold_in(key_of[16], 71), 0)
    block_second = draw_block_second(jax.random.fold_in(key_of[16], 71), 0)
    block_average = draw_block_average(jax.random.fold_in(key_of[16], 71), 0)
    head_master = draw_head_master(jax.random.fold_in(key_of[16], 71), 0)
    head_first = draw_head_first(jax.random.fold_in(key_of[16], 71), 0)
    head_second = draw_head_second(jax.random.fold_in(key_of[16], 71), 0)
    head_average = draw_head_average(jax.random.fold_in(key_of[16], 71), 0)
    bias_master = bell_draw(key_of[12], (K,), 0.05, 0.75, jnp.float32)
    bias_first = bell_draw(key_of[13], (K,), (1.0 / K), 0.015625, jnp.float32)
    bias_second = jnp.clip(jnp.exp(jax.random.uniform(key_of[14], (K,), jnp.float32, math.log(9.999999974752427e-07), math.log(3.999999989900971e-06))), 9.999999974752427e-07, 3.999999989900971e-06)
    bias_average = bell_draw(key_of[15], (K,), 0.05, 0.75, jnp.float32)
    return dict(images=images, partner=partner, mix_weight=mix_weight, labels=labels, block_master=block_master, block_first=block_first, block_second=block_second, block_average=block_average, head_master=head_master, head_first=head_first, head_second=head_second, head_average=head_average, bias_master=bias_master, bias_first=bias_first, bias_second=bias_second, bias_average=bias_average)


EPS_NORM = 0.001
RATE = 0.05
DECAY_WEIGHT = 0.05
BETA_ONE = 0.5
BETA_TWO = 0.5
EPS_ADAM = 1e-08
EMA_RATE = 0.5
SMOOTHING = 0.1
PRECISE = lax.Precision.HIGHEST

@jax.custom_vjp
def low(v):
    return lax.optimization_barrier(v.astype(jnp.bfloat16)).astype(jnp.float32)

@jax.custom_vjp
def low_back(v):
    return v

def low_keep(v):
    return (low(v), None)

def low_pass(kept, grad):
    return (grad,)

def back_keep(v):
    return (v, None)

def back_low(kept, grad):
    return (low(grad),)
low.defvjp(low_keep, low_pass)
low_back.defvjp(back_keep, back_low)

def unpack_block(flat):
    lengths = [C * E, E * C, E * SQ, SQ * E, 9 * E, 5 * E, SQ, C, C]
    pieces = []
    offset = 0
    for length_part in lengths:
        pieces.append(lax.slice_in_dim(flat, offset, offset + length_part))
        offset += length_part
    return (pieces[0].reshape(C, E), pieces[1].reshape(E, C), pieces[2].reshape(E, SQ), pieces[3].reshape(SQ, E), pieces[4].reshape(9, E), pieces[5].reshape(5, E), pieces[6], pieces[7], pieces[8])

def moments(values_in):
    return (lax.optimization_barrier(jnp.sum(values_in, axis=(0, 1))), lax.optimization_barrier(jnp.sum(values_in * values_in, axis=(0, 1))))

def norm_stats(sums, squares, total):
    mean_val = sums / total
    return (mean_val, lax.rsqrt(squares / total - mean_val * mean_val + EPS_NORM))

def apply_norm(values_in, stat_pair, gain, shift):
    return (values_in - stat_pair[0]) * stat_pair[1] * gain + shift

def depthwise(field, w_depth):
    images_n = field.shape[0]
    width = field.shape[-1]
    grid = field.reshape(images_n, SIDE, SIDE, width)
    padded = jnp.pad(grid, ((0, 0), (1, 1), (1, 1), (0, 0)))
    result = jnp.zeros_like(grid)
    for tap_row in range(3):
        for tap_col in range(3):
            result = result + padded[:, tap_row:tap_row + SIDE, tap_col:tap_col + SIDE, :] * w_depth[3 * tap_row + tap_col]
    return result.reshape(images_n, SIDE * SIDE, width)

def spread(pre_one, w_depth):
    return depthwise(jax.nn.silu(pre_one), w_depth)

def excite(pre_two, w_reduce, b_reduce, w_excite, b_excite):
    act_two = jax.nn.silu(pre_two)
    pooled = lax.optimization_barrier(jnp.mean(act_two, axis=1))
    squeezed = jax.nn.silu(jnp.dot(pooled, w_reduce, precision=PRECISE) + b_reduce)
    gate = jax.nn.sigmoid(jnp.dot(squeezed, w_excite, precision=PRECISE) + b_excite)
    return act_two * gate[:, None, :]

def block_local(stream, weights, stat_list, section_idx):
    w_expand, w_project, w_reduce, w_excite, w_depth, vec_wide, b_reduce, g_proj, b_proj = weights
    expanded = low_back(jnp.einsum('npc,ce->npe', low(stream), w_expand, precision=PRECISE))
    if section_idx == 0:
        return moments(expanded)
    spread_out = spread(apply_norm(expanded, stat_list[0], vec_wide[0], vec_wide[1]), w_depth)
    if section_idx == 1:
        return moments(spread_out)
    gated = excite(apply_norm(spread_out, stat_list[1], vec_wide[2], vec_wide[3]), w_reduce, b_reduce, w_excite, vec_wide[4])
    projected = low_back(jnp.einsum('npe,ec->npc', low(gated), w_project, precision=PRECISE))
    if section_idx == 2:
        return moments(projected)
    return stream + apply_norm(projected, stat_list[2], g_proj, b_proj)

def run_layer(stream, weights):
    stat_list = []
    for section_idx in range(3):
        stat_part = jax.checkpoint(partial(block_local, section_idx=section_idx))
        totals = lax.map(lambda block_rows: stat_part(block_rows, weights, tuple(stat_list)), stream)
        stat_list.append(norm_stats(lax.optimization_barrier(jnp.sum(totals[0], axis=0)), lax.optimization_barrier(jnp.sum(totals[1], axis=0)), PIX * IMAGES))
    out_part = jax.checkpoint(partial(block_local, section_idx=3))
    return lax.map(lambda block_rows: out_part(block_rows, weights, tuple(stat_list)), stream)

def mix_targets(labels, partner_labels, weight):
    classes = jnp.arange(K, dtype=jnp.int32)
    first_hot = (labels[:, None] == classes[None, :]).astype(jnp.float32)
    second_hot = (partner_labels[:, None] == classes[None, :]).astype(jnp.float32)
    smooth_one = (1.0 - SMOOTHING) * first_hot + SMOOTHING / K
    smooth_two = (1.0 - SMOOTHING) * second_hot + SMOOTHING / K
    return weight[:, None] * smooth_one + (1.0 - weight[:, None]) * smooth_two

def head_local(stream, weights, stat_list, extra, section_idx):
    w_conv, gain, bias_norm, w_class = weights
    hidden = low_back(jnp.einsum('npc,hc->nph', low(stream), w_conv, precision=PRECISE))
    if section_idx == 0:
        return moments(hidden)
    pooled = lax.optimization_barrier(jnp.mean(jax.nn.silu(apply_norm(hidden, stat_list[0], gain, bias_norm)), axis=1))
    labels_part, partner_part, weight_part, class_bias = extra
    logits = low_back(jnp.dot(low(pooled), w_class, precision=PRECISE)) + class_bias
    targets = mix_targets(labels_part, partner_part, weight_part)
    return -jnp.sum(targets * jax.nn.log_softmax(logits, axis=-1))

def adam_update(master, first, second, average, grad):
    first_new = BETA_ONE * first + (1.0 - BETA_ONE) * grad
    second_new = BETA_TWO * second + (1.0 - BETA_TWO) * grad * grad
    fix_one = 1.0 - BETA_ONE ** STEP
    fix_two = 1.0 - BETA_TWO ** STEP
    master_new = master * (1.0 - RATE * DECAY_WEIGHT) - RATE * (first_new / fix_one) / (jnp.sqrt(second_new / fix_two) + EPS_ADAM)
    average_new = EMA_RATE * average + (1.0 - EMA_RATE) * master_new
    return (master_new, first_new, second_new, average_new)

def reference(images, partner, mix_weight, labels, block_master, block_first, block_second, block_average, head_master, head_first, head_second, head_average, bias_master, bias_first, bias_second, bias_average):
    index_all = jnp.arange(IMAGES, dtype=jnp.int32)
    partner_global = index_all // IMG_DEV * IMG_DEV + partner.astype(jnp.int32)
    pictures = images.astype(jnp.float32)
    mix_share = mix_weight[:, None, None]
    mixed = mix_share * pictures + (1.0 - mix_share) * pictures[partner_global]
    partner_labels = labels[partner_global]
    blocks_n = N_FSDP

    def shape_blocks(array_in):
        return array_in.reshape((blocks_n, IMAGES // blocks_n) + array_in.shape[1:])

    def objective(block_weights, head_weights, class_bias):
        stream = shape_blocks(mixed)
        rounded = low(block_weights)
        for layer_idx in range(LAYERS):
            stream = run_layer(stream, unpack_block(rounded[layer_idx]))
        head_grid = low(head_weights).reshape(HD, C + 2 + K)
        head_parts = (head_grid[:, :C], head_grid[:, C], head_grid[:, C + 1], head_grid[:, C + 2:])
        stat_part = jax.checkpoint(partial(head_local, section_idx=0))
        totals = lax.map(lambda block_rows: stat_part(block_rows, head_parts, (), ()), stream)
        head_stat = norm_stats(lax.optimization_barrier(jnp.sum(totals[0], axis=0)), lax.optimization_barrier(jnp.sum(totals[1], axis=0)), PIX * IMAGES)
        loss_part = jax.checkpoint(partial(head_local, section_idx=1))
        losses = lax.map(lambda packed: loss_part(packed[0], head_parts, (head_stat,), (packed[1], packed[2], packed[3], class_bias)), (stream, shape_blocks(labels), shape_blocks(partner_labels), shape_blocks(mix_weight)))
        total_loss = jnp.sum(losses)
        return (total_loss / IMAGES, total_loss)
    mean_loss, pull_back, loss_sum = jax.vjp(objective, block_master, head_master, bias_master, has_aux=True)
    grad_block, grad_head, grad_bias = pull_back(jnp.ones((), dtype=mean_loss.dtype))
    block_new = adam_update(block_master, block_first, block_second, block_average, grad_block)
    head_new = adam_update(head_master, head_first, head_second, head_average, grad_head)
    bias_new = adam_update(bias_master, bias_first, bias_second, bias_average, grad_bias)
    return (loss_sum, block_new[0], block_new[1], block_new[2], block_new[3], head_new[0], head_new[1], head_new[2], head_new[3], bias_new[0], bias_new[1], bias_new[2], bias_new[3])
```

```python
import functools

import jax
import jax.numpy as jnp
from jax import lax
from jax.experimental import pallas as pl
from jax.experimental.pallas import tpu as pltpu
from jax.sharding import PartitionSpec as P

C = 256
E = 1536
SQ = 64
K = 1000
SIDE = 4
PIX = 16
LAYERS = 3
STEP = 5
EPS_NORM = 0.001
RATE = 0.05
DECAY_WEIGHT = 0.05
BETA_ONE = 0.5
BETA_TWO = 0.5
EPS_ADAM = 1e-08
EMA_RATE = 0.5
SMOOTHING = 0.1

LANE = 128
KP = 1024
HEAD_W = C + LANE + KP
PB = 2 * C * E + 2 * E * SQ + 14 * E + SQ + 2 * C
ROW_P = C * E // LANE
ROW_R = ROW_P + E * C // LANE
ROW_X = ROW_R + E * SQ // LANE
ROW_D = ROW_X + SQ * E // LANE
ROW_S = ROW_D + 14 * E // LANE
NJ = E // LANE
GROUPS = 2
GW = E // GROUPS
MBLK = 4

MESH = pl.DeviceIdType.MESH
F32 = jnp.float32
BF16 = jnp.bfloat16
HIGH = lax.Precision.HIGHEST
VMEM_LIMIT = 60 * 1024 * 1024
VM = pl.BlockSpec(memory_space=pltpu.VMEM)


def ceil_to(value, unit):
    return -(-value // unit) * unit


class Plan:
    def __init__(self, mesh, images, head_rows):
        self.nd = mesh.shape["dp"]
        self.nf = mesh.shape["fsdp"]
        self.devices = self.nd * self.nf
        self.images = images
        self.rows = images * PIX
        self.count = float(self.rows * self.devices)
        self.shard = PB // self.nf
        self.base = [(self.shard * f // LANE) // 16 * 16 for f in range(self.nf)]
        self.chunk = ceil_to(-(-self.shard // LANE) + 17, 16)
        self.flat = self.base[-1] + self.chunk
        self.head_pad = ceil_to(head_rows, 16)
        self.hd = self.head_pad * self.nf
        self.head_rows = head_rows


def dot(a, b, dims=((1,), (0,)), precision=None):
    return lax.dot_general(a, b, (dims, ((), ())), precision=precision, preferred_element_type=F32)


def row_sum(value):
    return jnp.sum(value, axis=0, keepdims=True)


def my_index(plan):
    return lax.axis_index("dp") * plan.nf + lax.axis_index("fsdp")


def peer_id(plan, step):
    k = lax.rem(my_index(plan) + step, plan.devices)
    return (k // plan.nf, lax.rem(k, plan.nf))


def enter(plan):
    barrier = pltpu.get_barrier_semaphore()

    def greet(step, carry):
        pl.semaphore_signal(barrier, inc=1, device_id=peer_id(plan, step), device_id_type=MESH)
        return carry

    lax.fori_loop(1, plan.devices, greet, 0)


def entered(plan):
    pl.semaphore_wait(pltpu.get_barrier_semaphore(), plan.devices - 1)


def share(plan, buf, send, recv, first, second):
    buf[0, 0:1, :] = first
    buf[0, 1:2, :] = second

    def push(step, carry):
        pltpu.make_async_remote_copy(
            src_ref=buf.at[0],
            dst_ref=buf.at[step],
            send_sem=send,
            recv_sem=recv,
            device_id=peer_id(plan, step),
            device_id_type=MESH,
        ).start()
        return carry

    lax.fori_loop(1, plan.devices, push, 0)


def collect(plan, buf, send, recv):
    others = buf.at[pl.ds(1, plan.devices - 1)]
    pltpu.make_async_copy(others, others, recv).wait()
    total = jnp.sum(buf[...], axis=0)
    return total[0:1, :], total[1:2, :]


def finish(plan, buf, send, recv):
    others = buf.at[pl.ds(1, plan.devices - 1)]
    pltpu.make_async_copy(others, others, send).wait()


def exchange_scratch(plan, widths):
    shapes = [pltpu.VMEM((plan.devices, 2, w), F32) for w in widths]
    sems = [pltpu.SemaphoreType.DMA(()) for w in widths]
    return shapes + sems + sems


def exchange_refs(refs, n):
    return [(refs[i], refs[n + i], refs[2 * n + i]) for i in range(n)]


def moments(plan, pair):
    mean = pair[0] / plan.count
    return mean, lax.rsqrt(pair[1] / plan.count - mean * mean + EPS_NORM)


def taps():
    found = []
    for y in range(SIDE):
        for x in range(SIDE):
            for a in range(3):
                for b in range(3):
                    iy, ix = y + a - 1, x + b - 1
                    if 0 <= iy < SIDE and 0 <= ix < SIDE:
                        found.append((y * SIDE + x, 3 * a + b, iy * SIDE + ix))
    return found


TAPS = taps()


def half_tanh(half):
    return jnp.tanh(half)


def silu(z):
    half = 0.5 * z
    return half * half_tanh(half) + half


def sigmoid(z):
    return 0.5 * half_tanh(0.5 * z) + 0.5


def silu_slope(z):
    half = 0.5 * z
    t = half_tanh(half)
    return 0.5 * (1.0 + t + half * (1.0 - t * t))


def lanes(j):
    return pl.ds(pl.multiple_of(j * LANE, LANE), LANE)


def images_at(b):
    return pl.ds(pl.multiple_of(b * 8, 8), 8)


def over_tiles(plan, first_chunk, chunks, per_chunk, body, n_sums, store_sums):
    def chunk_step(jj, carry):
        j = first_chunk + jj
        hoisted = per_chunk(j)
        zero = tuple(jnp.zeros((8, LANE), F32) for _ in range(n_sums))
        sums = lax.fori_loop(
            0, plan.images // 8, lambda b, s: body(j, b, hoisted, s), zero
        )
        store_sums(j, sums)
        return carry

    lax.fori_loop(0, chunks, chunk_step, 0)


def unpack_kernel(plan, got, we, wp, wr, wx, small, tail, flat):
    lane = lax.broadcasted_iota(jnp.int32, (1, LANE), 1)
    low = lane < SQ
    for f in range(plan.nf):
        base, at = plan.base[f], f * plan.chunk
        head = got[at : at + 16, :].astype(F32)
        if f:
            head = head + flat[base : base + 16, :]
        flat[base : base + 16, :] = head
        flat[base + 16 : base + plan.chunk, :] = got[at + 16 : at + plan.chunk, :].astype(F32)
    for j in range(NJ):
        cols = slice(j * LANE, (j + 1) * LANE)
        we[:, cols] = flat[pl.ds(j, C, stride=NJ), :].astype(BF16)
        wx[0:SQ, cols] = flat[pl.ds(ROW_X + j, SQ, stride=NJ), :]
        wx[SQ:LANE, cols] = jnp.zeros((LANE - SQ, LANE), F32)
        small[0:14, cols] = flat[pl.ds(ROW_D + j, 14, stride=NJ), :]
        small[14:16, cols] = jnp.zeros((2, LANE), F32)
    for h in range(C // LANE):
        wp[:, h * LANE : (h + 1) * LANE] = flat[pl.ds(ROW_P + h, E, stride=2), :].astype(BF16)
    pairs = flat[ROW_R:ROW_X, :]
    wr[pl.ds(0, E // 2, stride=2), :] = jnp.where(low, pairs, 0.0)
    wr[pl.ds(1, E // 2, stride=2), :] = jnp.where(low, pltpu.roll(pairs, SQ, 1), 0.0)
    rows = [flat[ROW_S + i : ROW_S + i + 1, :] for i in range(5)]
    turned = [pltpu.roll(jnp.broadcast_to(r, (8, LANE)), SQ, 1)[0:1, :] for r in rows]
    tail[...] = jnp.zeros((8, C), F32)
    tail[0:1, 0:LANE] = jnp.where(low, rows[0], 0.0)
    for i, at in ((1, 0), (2, 2)):
        tail[i : i + 1, 0:LANE] = jnp.where(low, turned[at], turned[at + 1])
        tail[i : i + 1, LANE:C] = jnp.where(low, turned[at + 1], turned[at + 2])


def unpack(plan, gathered):
    return pl.pallas_call(
        functools.partial(unpack_kernel, plan),
        out_shape=(
            jax.ShapeDtypeStruct((C, E), BF16),
            jax.ShapeDtypeStruct((E, C), BF16),
            jax.ShapeDtypeStruct((E, LANE), F32),
            jax.ShapeDtypeStruct((LANE, E), F32),
            jax.ShapeDtypeStruct((16, E), F32),
            jax.ShapeDtypeStruct((8, C), F32),
        ),
        in_specs=[VM],
        out_specs=(VM,) * 6,
        scratch_shapes=[pltpu.VMEM((plan.flat, LANE), F32)],
        compiler_params=pltpu.CompilerParams(vmem_limit_bytes=VMEM_LIMIT),
        name="unpack",
    )(gathered)


def mix_kernel(plan, images, partner, weight, stream):
    n, rows = plan.images, plan.rows
    place = lax.broadcasted_iota(jnp.int32, (n, rows), 1)
    own = lax.broadcasted_iota(jnp.int32, (n, rows), 0)
    share_one = weight[...]
    for p in range(PIX):
        pick_own = jnp.where(place == own * PIX + p, 1.0, 0.0).astype(BF16)
        pick_partner = jnp.where(place == partner[...] * PIX + p, 1.0, 0.0).astype(BF16)
        mine = dot(pick_own, images[...])
        theirs = dot(pick_partner, images[...])
        stream[p * n : (p + 1) * n, :] = share_one * mine + (1.0 - share_one) * theirs


def mix(plan, images, partner, mix_weight):
    return pl.pallas_call(
        functools.partial(mix_kernel, plan),
        out_shape=jax.ShapeDtypeStruct((plan.rows, C), F32),
        in_specs=[VM] * 3,
        out_specs=VM,
        compiler_params=pltpu.CompilerParams(vmem_limit_bytes=VMEM_LIMIT),
        name="mix",
    )(
        images.reshape(plan.rows, C),
        partner.reshape(plan.images, 1),
        mix_weight.reshape(plan.images, 1),
    )


def forward_kernel(plan, x, we, wp, wr, wx, small, tail, *refs):
    out, expanded, depth, projected, stat_e, stat_c, pooled, presq, gate = refs[:9]
    x_low, act, sums = refs[9:12]
    ex = exchange_refs(refs[12:], 2 * GROUPS + 1)
    ex_one, ex_two, ex_three = ex[:GROUPS], ex[GROUPS : 2 * GROUPS], ex[2 * GROUPS]
    n = plan.images
    enter(plan)
    x_low[...] = x[...].astype(BF16)
    for g in range(GROUPS):
        cols = slice(g * GW, (g + 1) * GW)

        def expand(m, carry, cols=cols):
            rows = pl.ds(pl.multiple_of(m * MBLK * n, MBLK * n), MBLK * n)
            value = dot(x_low[rows, :], we[:, cols])
            expanded[pl.ds(m * MBLK, MBLK), :, cols] = value.reshape(MBLK, n, GW)
            return (
                carry[0] + jnp.sum(value.reshape(-1, 8, GW), axis=0),
                carry[1] + jnp.sum((value * value).reshape(-1, 8, GW), axis=0),
            )

        zero = jnp.zeros((8, GW), F32)
        s, q = lax.fori_loop(0, PIX // MBLK, expand, (zero, zero))
        if g == 0:
            entered(plan)
        share(plan, *ex_one[g], row_sum(s), row_sum(q))

    def put_sums(j, totals):
        for i, t in enumerate(totals):
            sums[i : i + 1, lanes(j)] = row_sum(t)

    for g in range(GROUPS):
        cols = slice(g * GW, (g + 1) * GW)
        mean, rstd = moments(plan, collect(plan, *ex_one[g]))
        stat_e[0:1, cols] = mean
        stat_e[1:2, cols] = rstd
        scale = rstd * small[9:10, cols]
        stat_e[4:5, cols] = 0.5 * scale
        stat_e[5:6, cols] = 0.5 * (small[10:11, cols] - mean * scale)

        def chunk(j):
            return (
                stat_e[4:5, lanes(j)],
                stat_e[5:6, lanes(j)],
                [small[t : t + 1, lanes(j)] for t in range(9)],
            )

        def spread(j, b, hoisted, totals):
            scale, shift, w = hoisted
            act_one = []
            for p in range(PIX):
                half = expanded[p, images_at(b), lanes(j)] * scale + shift
                act_one.append(half * half_tanh(half) + half)
            made = [None] * PIX
            for o, t, i in TAPS:
                term = act_one[i] * w[t]
                made[o] = term if made[o] is None else made[o] + term
            s, q = totals
            for p in range(PIX):
                depth[p, images_at(b), lanes(j)] = made[p]
                s = s + made[p]
                q = q + made[p] * made[p]
            return s, q

        over_tiles(plan, g * (GW // LANE), GW // LANE, chunk, spread, 2, put_sums)
        share(plan, *ex_two[g], sums[0:1, cols], sums[1:2, cols])

    for g in range(GROUPS):
        cols = slice(g * GW, (g + 1) * GW)
        mean, rstd = moments(plan, collect(plan, *ex_two[g]))
        stat_e[2:3, cols] = mean
        stat_e[3:4, cols] = rstd
        scale = rstd * small[11:12, cols]
        stat_e[6:7, cols] = 0.5 * scale
        stat_e[7:8, cols] = 0.5 * (small[12:13, cols] - mean * scale)

        def chunk_two(j):
            return stat_e[6:7, lanes(j)], stat_e[7:8, lanes(j)]

        def activate(j, b, hoisted, totals):
            scale, shift = hoisted
            total = None
            for p in range(PIX):
                half = depth[p, images_at(b), lanes(j)] * scale + shift
                made = half * half_tanh(half) + half
                act[p, images_at(b), lanes(j)] = made
                total = made if total is None else total + made
            pooled[images_at(b), lanes(j)] = total * (1.0 / PIX)
            return totals

        over_tiles(
            plan, g * (GW // LANE), GW // LANE, chunk_two, activate, 0, lambda j, s: None
        )
    reduced = dot(pooled[...], wr[...], precision=HIGH) + tail[0:1, 0:LANE]
    presq[...] = reduced
    gate[...] = sigmoid(dot(silu(reduced), wx[...], precision=HIGH) + small[13:14, :])

    def project(m, carry):
        rows = pl.ds(pl.multiple_of(m * MBLK * n, MBLK * n), MBLK * n)
        gated = (act[pl.ds(m * MBLK, MBLK), :, :] * gate[...][None]).astype(BF16)
        value = dot(gated.reshape(MBLK * n, E), wp[...])
        projected[rows, :] = value
        return (
            carry[0] + jnp.sum(value.reshape(-1, 8, C), axis=0),
            carry[1] + jnp.sum((value * value).reshape(-1, 8, C), axis=0),
        )

    zero = jnp.zeros((8, C), F32)
    s, q = lax.fori_loop(0, PIX // MBLK, project, (zero, zero))
    share(plan, *ex_three, row_sum(s), row_sum(q))
    mean, rstd = moments(plan, collect(plan, *ex_three))
    stat_c[...] = jnp.zeros((8, C), F32)
    stat_c[0:1, :] = mean
    stat_c[1:2, :] = rstd
    scale = rstd * tail[1:2, :]
    out[...] = x[...] + (projected[...] - mean) * scale + tail[2:3, :]
    for e in ex:
        finish(plan, *e)


def forward(plan, x, weights):
    n = plan.images
    big = (PIX, n, E)
    return pl.pallas_call(
        functools.partial(forward_kernel, plan),
        out_shape=(
            jax.ShapeDtypeStruct((plan.rows, C), F32),
            jax.ShapeDtypeStruct(big, F32),
            jax.ShapeDtypeStruct(big, F32),
            jax.ShapeDtypeStruct((plan.rows, C), F32),
            jax.ShapeDtypeStruct((8, E), F32),
            jax.ShapeDtypeStruct((8, C), F32),
            jax.ShapeDtypeStruct((n, E), F32),
            jax.ShapeDtypeStruct((n, LANE), F32),
            jax.ShapeDtypeStruct((n, E), F32),
        ),
        in_specs=[VM] * 7,
        out_specs=(VM,) * 9,
        scratch_shapes=[
            pltpu.VMEM((plan.rows, C), BF16),
            pltpu.VMEM(big, F32),
            pltpu.VMEM((8, E), F32),
        ]
        + exchange_scratch(plan, [GW] * (2 * GROUPS) + [C]),
        compiler_params=pltpu.CompilerParams(
            collective_id=1, has_side_effects=True, vmem_limit_bytes=VMEM_LIMIT
        ),
        name="layer_forward",
    )(x, *weights)


def head_kernel(plan, x, w_head, bias, label, label_row, partner, weight, *refs):
    grad_x, grad_head, totals_out = refs[:3]
    x_low, turned, hidden, slope, low_grad, pool, stat, sums, gain = refs[3:12]
    hd, n = plan.hd, plan.images
    halves = plan.head_groups
    ng = len(halves)
    ex = exchange_refs(refs[12:], 2 * ng + 1)
    ex_stat, ex_grad, ex_bias = ex[:ng], ex[ng : 2 * ng], ex[2 * ng]
    enter(plan)
    x_low[...] = x[...].astype(BF16)
    turned[...] = x[...].T.astype(BF16)
    gain[...] = w_head[:, C : C + LANE].astype(F32).T[0:8, :]
    for g, (start, width) in enumerate(halves):
        cols = slice(start, start + width)

        def convolve(m, carry, cols=cols, width=width):
            rows = pl.ds(pl.multiple_of(m * MBLK * n, MBLK * n), MBLK * n)
            value = dot(x_low[rows, :], w_head[cols, 0:C], ((1,), (1,)))
            hidden[pl.ds(m * MBLK, MBLK), :, cols] = value.reshape(MBLK, n, width)
            return (
                carry[0] + jnp.sum(value.reshape(-1, 8, width), axis=0),
                carry[1] + jnp.sum((value * value).reshape(-1, 8, width), axis=0),
            )

        zero = jnp.zeros((8, width), F32)
        s, q = lax.fori_loop(0, PIX // MBLK, convolve, (zero, zero))
        if g == 0:
            entered(plan)
        share(plan, *ex_stat[g], row_sum(s), row_sum(q))
    for g, (start, width) in enumerate(halves):
        cols = slice(start, start + width)
        mean, rstd = moments(plan, collect(plan, *ex_stat[g]))
        scale = rstd * gain[0:1, cols]
        stat[0:1, cols] = rstd
        stat[1:2, cols] = -mean * rstd
        stat[2:3, cols] = 0.5 * scale
        stat[3:4, cols] = 0.5 * (gain[1:2, cols] - mean * scale)

        def chunk(j):
            return stat[2:3, lanes(j)], stat[3:4, lanes(j)]

        def activate(j, b, hoisted, totals):
            scale, shift = hoisted
            total = None
            for p in range(PIX):
                half = hidden[p, images_at(b), lanes(j)] * scale + shift
                t = half_tanh(half)
                made = half * t + half
                slope[p, images_at(b), lanes(j)] = (1.0 + t) + half * (1.0 - t * t)
                total = made if total is None else total + made
            pool[images_at(b), lanes(j)] = total * (1.0 / PIX)
            return totals

        over_tiles(plan, start // LANE, width // LANE, chunk, activate, 0, lambda j, s: None)
    pool_low = pool[...].astype(BF16)
    classes = lax.broadcasted_iota(jnp.int32, (n, KP), 1)
    valid = classes < K
    logits = dot(pool_low, w_head[:, C + LANE :]) + bias[...]
    logits = jnp.where(valid, logits, -1e30)
    top = jnp.max(logits, axis=1, keepdims=True)
    lifted = logits - top
    powers = jnp.where(valid, jnp.exp(lifted), 0.0)
    norm = jnp.sum(powers, axis=1, keepdims=True)
    log_probs = lifted - jnp.log(norm)
    picked = lax.broadcasted_iota(jnp.int32, (n, n), 1) == partner[...]
    label_two = jnp.sum(jnp.where(picked, label_row[...], 0), axis=1, keepdims=True)
    w = weight[...]
    targets = w * jnp.where(classes == label[...], 1.0 - SMOOTHING, 0.0) + (1.0 - w) * jnp.where(
        classes == label_two, 1.0 - SMOOTHING, 0.0
    )
    targets = jnp.where(valid, targets + SMOOTHING / K, 0.0)
    loss = -jnp.sum(jnp.where(valid, targets * log_probs, 0.0))
    grad_logits = (powers / norm - targets) * (float(PIX) / plan.count)
    share(plan, *ex_bias, row_sum(grad_logits), jnp.full((1, KP), loss, F32))
    grad_low = grad_logits.astype(BF16)
    pool_grad = dot(grad_low, w_head[:, C + LANE :], ((1,), (1,)))
    pool[...] = pool_grad * (0.5 / PIX)

    def put_sums(j, totals):
        for i, t in enumerate(totals):
            sums[i : i + 1, lanes(j)] = row_sum(t)

    for g, (start, width) in enumerate(halves):
        cols = slice(start, start + width)

        def chunk_back(j):
            return stat[0:1, lanes(j)], stat[1:2, lanes(j)]

        def back(j, b, hoisted, totals):
            rstd, shift = hoisted
            s, q = totals
            flow = pool[images_at(b), lanes(j)]
            for p in range(PIX):
                made = slope[p, images_at(b), lanes(j)] * flow
                slope[p, images_at(b), lanes(j)] = made
                normed = hidden[p, images_at(b), lanes(j)] * rstd + shift
                s = s + made
                q = q + made * normed
            return s, q

        over_tiles(plan, start // LANE, width // LANE, chunk_back, back, 2, put_sums)
        share(plan, *ex_grad[g], sums[0:1, cols], sums[1:2, cols])
    grad_head[:, C + LANE :] = dot(pool_low.T, grad_low).astype(BF16)
    norm_grads = jnp.concatenate(
        [sums[1:2, :], sums[0:1, :], jnp.zeros((LANE - 2, hd), F32)], axis=0
    )
    grad_head[:, C : C + LANE] = norm_grads.T.astype(BF16)
    for g, (start, width) in enumerate(halves):
        cols = slice(start, start + width)
        shift_total, gain_total = collect(plan, *ex_grad[g])
        scale = stat[0:1, cols] * gain[0:1, cols]
        mean_one = shift_total / plan.count
        mean_two = gain_total / plan.count
        stat[4:5, cols] = scale
        stat[5:6, cols] = -scale * stat[0:1, cols] * mean_two
        stat[6:7, cols] = -scale * (mean_one + stat[1:2, cols] * mean_two)
    def into(m, carry):
        rows = pl.ds(pl.multiple_of(m * MBLK * n, MBLK * n), MBLK * n)
        spot = pl.ds(m * MBLK, MBLK)
        value = (
            slope[spot, :, :] * stat[4:5, :] + hidden[spot, :, :] * stat[5:6, :] + stat[6:7, :]
        )
        low = value.reshape(MBLK * n, hd).astype(BF16)
        low_grad[rows, :] = low
        grad_x[rows, :] = dot(low, w_head[:, 0:C])
        return carry

    lax.fori_loop(0, PIX // MBLK, into, 0)
    for at in range(0, hd, LANE):
        part = dot(turned[...], low_grad[:, at : at + LANE])
        grad_head[at : at + LANE, 0:C] = part.T.astype(BF16)
    bias_total, loss_total = collect(plan, *ex_bias)
    totals_out[0:1, :] = bias_total
    totals_out[1:2, :] = loss_total
    for e in ex:
        finish(plan, *e)


def head(plan, x, w_head, bias, labels, partner, mix_weight):
    n, hd = plan.images, plan.hd
    big = (PIX, n, hd)
    widths = [w for _, w in plan.head_groups]
    return pl.pallas_call(
        functools.partial(head_kernel, plan),
        out_shape=(
            jax.ShapeDtypeStruct((plan.rows, C), F32),
            jax.ShapeDtypeStruct((hd, HEAD_W), BF16),
            jax.ShapeDtypeStruct((2, KP), F32),
        ),
        in_specs=[VM] * 7,
        out_specs=(VM,) * 3,
        scratch_shapes=[
            pltpu.VMEM((plan.rows, C), BF16),
            pltpu.VMEM((C, plan.rows), BF16),
            pltpu.VMEM(big, F32),
            pltpu.VMEM(big, F32),
            pltpu.VMEM((plan.rows, hd), BF16),
            pltpu.VMEM((n, hd), F32),
            pltpu.VMEM((8, hd), F32),
            pltpu.VMEM((8, hd), F32),
            pltpu.VMEM((8, hd), F32),
        ]
        + exchange_scratch(plan, widths + widths + [KP]),
        compiler_params=pltpu.CompilerParams(
            collective_id=2, has_side_effects=True, vmem_limit_bytes=VMEM_LIMIT
        ),
        name="head",
    )(
        x,
        w_head,
        bias,
        labels.reshape(n, 1),
        labels.reshape(1, n),
        partner.reshape(n, 1),
        mix_weight.reshape(n, 1),
    )


def backward_kernel(plan, x, grad, expanded, depth, projected, stat_e, stat_c, pooled, presq, gate, we, wp, wr, wx, small, tail, *refs):
    grad_x, packed = refs[:2]
    turned, act, flow, low_proj, gated, sums, coef, squeeze_grad, flat = refs[2:11]
    ex = exchange_refs(refs[11:], 2 * GROUPS + 1)
    ex_two, ex_one, ex_three = ex[:GROUPS], ex[GROUPS : 2 * GROUPS], ex[2 * GROUPS]
    n = plan.images
    lane = lax.broadcasted_iota(jnp.int32, (1, LANE), 1)
    is_low = lane < SQ
    enter(plan)
    mean_c, rstd_c = stat_c[0:1, :], stat_c[1:2, :]
    s = row_sum(jnp.sum(grad[...].reshape(-1, 8, C), axis=0))
    q = row_sum(
        jnp.sum((grad[...] * ((projected[...] - mean_c) * rstd_c)).reshape(-1, 8, C), axis=0)
    )
    entered(plan)
    share(plan, *ex_three, s, q)
    bias_three, gain_three = s, q

    def chunk_two(j):
        return stat_e[6:7, lanes(j)], stat_e[7:8, lanes(j)]

    def activate(j, b, hoisted, totals):
        scale, shift = hoisted
        for p in range(PIX):
            half = depth[p, images_at(b), lanes(j)] * scale + shift
            act[p, images_at(b), lanes(j)] = half * half_tanh(half) + half
        return totals

    over_tiles(plan, 0, NJ, chunk_two, activate, 0, lambda j, s: None)

    def regate(m, carry):
        rows = pl.ds(pl.multiple_of(m * MBLK * n, MBLK * n), MBLK * n)
        value = (act[pl.ds(m * MBLK, MBLK), :, :] * gate[...][None]).astype(BF16)
        gated[rows, :] = value.reshape(MBLK * n, E)
        return carry

    lax.fori_loop(0, PIX // MBLK, regate, 0)
    turned[...] = x[...].T.astype(BF16)

    bias_total, gain_total = collect(plan, *ex_three)
    scale = rstd_c * tail[1:2, :]
    mean_one, mean_two = bias_total / plan.count, gain_total / plan.count
    low_proj[...] = (
        scale
        * (grad[...] - mean_one - (projected[...] - mean_c) * (rstd_c * mean_two))
    ).astype(BF16)

    def into_gated(m, carry):
        rows = pl.ds(pl.multiple_of(m * MBLK * n, MBLK * n), MBLK * n)
        value = dot(low_proj[rows, :], wp[...], ((1,), (1,)))
        flow[pl.ds(m * MBLK, MBLK), :, :] = value.reshape(MBLK, n, E)
        return carry

    lax.fori_loop(0, PIX // MBLK, into_gated, 0)

    def gate_back(j, b, hoisted, totals):
        total = None
        for p in range(PIX):
            term = flow[p, images_at(b), lanes(j)] * act[p, images_at(b), lanes(j)]
            total = term if total is None else total + term
        opened = gate[images_at(b), lanes(j)]
        squeeze_grad[images_at(b), lanes(j)] = total * opened * (1.0 - opened)
        return totals

    over_tiles(plan, 0, NJ, lambda j: None, gate_back, 0, lambda j, s: None)
    excite_grad = squeeze_grad[...]
    sums[13:14, :] = row_sum(excite_grad)
    squeezed = silu(presq[...])
    presq_grad = dot(excite_grad, wx[...], ((1,), (1,)), HIGH) * silu_slope(presq[...])
    grad_wx = dot(squeezed.T, excite_grad, precision=HIGH)
    for j in range(NJ):
        flat[pl.ds(ROW_X + j, SQ, stride=NJ), :] = grad_wx[0:SQ, j * LANE : (j + 1) * LANE]
    grad_reduce_b = row_sum(presq_grad)
    grad_wr = dot(pooled[...].T, presq_grad, precision=HIGH)
    squeeze_grad[...] = dot(presq_grad, wr[...], ((1,), (1,)), HIGH) * (1.0 / PIX)

    def put_sums(first_row):
        def put(j, totals):
            for i, t in enumerate(totals):
                sums[first_row + i : first_row + i + 1, lanes(j)] = row_sum(t)

        return put

    def chunk_norm(j):
        return (
            stat_e[6:7, lanes(j)],
            stat_e[7:8, lanes(j)],
            stat_e[2:3, lanes(j)],
            stat_e[3:4, lanes(j)],
        )

    def back_two(j, b, hoisted, totals):
        scale, shift, mean, rstd = hoisted
        gain_sum, bias_sum = totals
        opened = gate[images_at(b), lanes(j)] * 0.5
        pool_flow = squeeze_grad[images_at(b), lanes(j)] * 0.5
        for p in range(PIX):
            value = depth[p, images_at(b), lanes(j)]
            half = value * scale + shift
            t = half_tanh(half)
            made = (flow[p, images_at(b), lanes(j)] * opened + pool_flow) * (
                (1.0 + t) + half * (1.0 - t * t)
            )
            flow[p, images_at(b), lanes(j)] = made
            bias_sum = bias_sum + made
            gain_sum = gain_sum + made * ((value - mean) * rstd)
        return gain_sum, bias_sum

    for g in range(GROUPS):
        cols = slice(g * GW, (g + 1) * GW)
        over_tiles(plan, g * (GW // LANE), GW // LANE, chunk_norm, back_two, 2, put_sums(11))
        share(plan, *ex_two[g], sums[12:13, cols], sums[11:12, cols])

    proj_turned = low_proj[...].astype(F32).T.astype(BF16)
    for j in range(NJ):
        part = dot(proj_turned, gated[:, j * LANE : (j + 1) * LANE])
        for h in range(C // LANE):
            flat[pl.ds(ROW_P + 2 * j * LANE + h, LANE, stride=2), :] = part[
                h * LANE : (h + 1) * LANE, :
            ].T

    def norm_coefs(g, pair, row, stat_row, gain_row):
        cols = slice(g * GW, (g + 1) * GW)
        mean, rstd = stat_e[stat_row : stat_row + 1, cols], stat_e[stat_row + 1 : stat_row + 2, cols]
        scale = rstd * small[gain_row : gain_row + 1, cols]
        mean_one, mean_two = pair[0] / plan.count, pair[1] / plan.count
        coef[row : row + 1, cols] = scale
        coef[row + 1 : row + 2, cols] = -scale * rstd * mean_two
        coef[row + 2 : row + 3, cols] = -scale * (mean_one - mean * rstd * mean_two)

    def chunk_one(j):
        return (
            [coef[i : i + 1, lanes(j)] for i in range(3)],
            [small[t : t + 1, lanes(j)] for t in range(9)],
            [stat_e[i : i + 1, lanes(j)] for i in (4, 5, 0, 1)],
        )

    def back_one(j, b, hoisted, totals):
        (c_flow, c_value, c_const), w, (scale, shift, mean, rstd) = hoisted
        w_sums, gain_sum, bias_sum = list(totals[:9]), totals[9], totals[10]
        spread_grad = []
        for p in range(PIX):
            spread_grad.append(
                flow[p, images_at(b), lanes(j)] * c_flow
                + (depth[p, images_at(b), lanes(j)] * c_value + c_const)
            )
        act_one = []
        for p in range(PIX):
            half = expanded[p, images_at(b), lanes(j)] * scale + shift
            t = half_tanh(half)
            act_one.append(half * t + half)
        made = [None] * PIX
        for o, t, i in TAPS:
            w_sums[t] = w_sums[t] + spread_grad[o] * act_one[i]
            term = spread_grad[o] * w[t]
            made[i] = term if made[i] is None else made[i] + term
        for p in range(PIX):
            value = expanded[p, images_at(b), lanes(j)]
            half = value * scale + shift
            t = half_tanh(half)
            result = made[p] * (0.5 * ((1.0 + t) + half * (1.0 - t * t)))
            flow[p, images_at(b), lanes(j)] = result
            bias_sum = bias_sum + result
            gain_sum = gain_sum + result * ((value - mean) * rstd)
        return tuple(w_sums) + (gain_sum, bias_sum)

    for g in range(GROUPS):
        cols = slice(g * GW, (g + 1) * GW)
        norm_coefs(g, collect(plan, *ex_two[g]), 0, 2, 11)
        over_tiles(plan, g * (GW // LANE), GW // LANE, chunk_one, back_one, 11, put_sums(0))
        share(plan, *ex_one[g], sums[10:11, cols], sums[9:10, cols])

    for j in range(NJ):
        flat[pl.ds(ROW_D + j, 14, stride=NJ), :] = sums[0:14, j * LANE : (j + 1) * LANE]
    pair_buf = refs[11 + 3 * (2 * GROUPS + 1)]
    pair_buf[...] = grad_wr
    evens = pair_buf[pl.ds(0, E // 2, stride=2), :]
    odds = pair_buf[pl.ds(1, E // 2, stride=2), :]
    flat[ROW_R:ROW_X, :] = jnp.where(is_low, evens, pltpu.roll(odds, SQ, 1))

    def turn(row):
        return pltpu.roll(jnp.broadcast_to(row, (8, LANE)), SQ, 1)[0:1, :]

    pieces = [turn(v[:, h * LANE : (h + 1) * LANE]) for v in (gain_three, bias_three) for h in (0, 1)]
    flat[ROW_S : ROW_S + 1, :] = jnp.where(is_low, grad_reduce_b, pieces[0])
    for i in range(3):
        flat[ROW_S + 1 + i : ROW_S + 2 + i, :] = jnp.where(is_low, pieces[i], pieces[i + 1])
    flat[ROW_S + 4 : ROW_S + 5, :] = pieces[3]

    grad_x[...] = grad[...]
    for g in range(GROUPS):
        cols = slice(g * GW, (g + 1) * GW)
        norm_coefs(g, collect(plan, *ex_one[g]), 0, 0, 9)

        def into(m, carry, cols=cols):
            rows = pl.ds(pl.multiple_of(m * MBLK * n, MBLK * n), MBLK * n)
            spot = pl.ds(m * MBLK, MBLK)
            value = (
                flow[spot, :, cols] * coef[0:1, cols]
                + expanded[spot, :, cols] * coef[1:2, cols]
                + coef[2:3, cols]
            )
            low = value.reshape(MBLK * n, GW).astype(BF16)
            gated[rows, cols] = low
            grad_x[rows, :] += dot(low, we[:, cols], ((1,), (1,)))
            return carry

        lax.fori_loop(0, PIX // MBLK, into, 0)
        for j in range(g * (GW // LANE), (g + 1) * (GW // LANE)):
            flat[pl.ds(j, C, stride=NJ), :] = dot(
                turned[...], gated[:, j * LANE : (j + 1) * LANE]
            )
    for f in range(plan.nf):
        packed[f * plan.chunk : (f + 1) * plan.chunk, :] = flat[
            plan.base[f] : plan.base[f] + plan.chunk, :
        ].astype(BF16)
    for e in ex:
        finish(plan, *e)


def backward(plan, x, grad, kept, weights):
    n = plan.images
    big = (PIX, n, E)
    return pl.pallas_call(
        functools.partial(backward_kernel, plan),
        out_shape=(
            jax.ShapeDtypeStruct((plan.rows, C), F32),
            jax.ShapeDtypeStruct((plan.nf * plan.chunk, LANE), BF16),
        ),
        in_specs=[VM] * 16,
        out_specs=(VM,) * 2,
        scratch_shapes=[
            pltpu.VMEM((C, plan.rows), BF16),
            pltpu.VMEM(big, F32),
            pltpu.VMEM(big, F32),
            pltpu.VMEM((plan.rows, C), BF16),
            pltpu.VMEM((plan.rows, E), BF16),
            pltpu.VMEM((16, E), F32),
            pltpu.VMEM((8, E), F32),
            pltpu.VMEM((n, E), F32),
            pltpu.VMEM((plan.flat, LANE), F32),
        ]
        + exchange_scratch(plan, [GW] * (2 * GROUPS) + [C])
        + [pltpu.VMEM((E, LANE), F32)],
        compiler_params=pltpu.CompilerParams(
            collective_id=3, has_side_effects=True, vmem_limit_bytes=VMEM_LIMIT
        ),
        name="layer_backward",
    )(x, grad, *kept, *weights)


def adam_update(master, first, second, average, grad):
    first_new = BETA_ONE * first + (1.0 - BETA_ONE) * grad
    second_new = BETA_TWO * second + (1.0 - BETA_TWO) * grad * grad
    fix_one = 1.0 - BETA_ONE**STEP
    fix_two = 1.0 - BETA_TWO**STEP
    master_new = master * (1.0 - RATE * DECAY_WEIGHT) - RATE * (first_new / fix_one) / (
        jnp.sqrt(second_new / fix_two) + EPS_ADAM
    )
    average_new = EMA_RATE * average + (1.0 - EMA_RATE) * master_new
    return (master_new, first_new, second_new, average_new)


def on_device(mesh, images, partner, mix_weight, labels, *states):
    block, head_state, bias_state = states[0:4], states[4:8], states[8:12]
    row = C + 2 + K
    plan = Plan(mesh, images.shape[0], head_state[0].shape[0] // row)
    half = (plan.hd // LANE + 1) // 2 * LANE
    plan.head_groups = [(0, half), (half, plan.hd - half)]
    start = lax.axis_index("fsdp") * plan.shard
    offset = start - start // (16 * LANE) * (16 * LANE)
    weights = []
    for layer in range(LAYERS):
        flat = lax.dynamic_update_slice(
            jnp.zeros((plan.chunk * LANE,), BF16), block[0][layer].astype(BF16), (offset,)
        )
        gathered = lax.all_gather(flat.reshape(plan.chunk, LANE), "fsdp", axis=0, tiled=True)
        weights.append(unpack(plan, gathered))
    grid = head_state[0].astype(BF16).reshape(plan.head_rows, row)
    grid = jnp.concatenate(
        [
            grid[:, : C + 2],
            jnp.zeros((plan.head_rows, LANE - 2), BF16),
            grid[:, C + 2 :],
            jnp.zeros((plan.head_rows, KP - K), BF16),
        ],
        axis=1,
    )
    grid = jnp.pad(grid, ((0, plan.head_pad - plan.head_rows), (0, 0)))
    w_head = lax.all_gather(grid, "fsdp", axis=0, tiled=True)
    bias = jnp.pad(bias_state[0], (0, KP - K)).reshape(1, KP)

    stream = mix(plan, images, partner, mix_weight)
    inputs, kept = [], []
    for layer in range(LAYERS):
        inputs.append(stream)
        made = forward(plan, stream, weights[layer])
        stream = made[0]
        kept.append(made[1:])
    grad, head_grad, totals = head(plan, stream, w_head, bias, labels, partner, mix_weight)
    loss_sum = totals[1, 0]
    grad_bias = totals[0, :K]
    head_grad = lax.psum_scatter(head_grad, "fsdp", scatter_dimension=0, tiled=True)
    block_grads = [None] * LAYERS
    for layer in reversed(range(LAYERS)):
        grad, packed = backward(plan, inputs[layer], grad, kept[layer], weights[layer])
        block_grads[layer] = lax.psum_scatter(packed, "fsdp", scatter_dimension=0, tiled=True)
    block_grad, head_grad = lax.psum((jnp.stack(block_grads), head_grad), "dp")
    block_grad = lax.dynamic_slice(
        block_grad.reshape(LAYERS, plan.chunk * LANE), (0, offset), (LAYERS, plan.shard)
    ).astype(F32)
    head_grad = head_grad[: plan.head_rows].astype(F32)
    head_grad = jnp.concatenate(
        [head_grad[:, : C + 2], head_grad[:, C + LANE : C + LANE + K]], axis=1
    ).reshape(-1)
    return (
        (loss_sum,)
        + adam_update(*block, block_grad)
        + adam_update(*head_state, head_grad)
        + adam_update(*bias_state, grad_bias)
    )


def solution(mesh):
    data = P(("dp", "fsdp"))
    states = (P(None, "fsdp"),) * 4 + (P("fsdp"),) * 4 + (P(),) * 4
    return jax.shard_map(
        functools.partial(on_device, mesh),
        mesh=mesh,
        in_specs=(P(("dp", "fsdp"), None, None), data, data, data) + states,
        out_specs=(P(),) + states,
        check_vma=False,
    )
```

```python
import functools

import jax
import jax.numpy as jnp
from jax import lax
from jax.experimental import pallas as pl
from jax.experimental.pallas import tpu as pltpu
from jax.sharding import PartitionSpec as P

C = 256
E = 1536
SQ = 64
K = 1000
SIDE = 4
PIX = 16
LAYERS = 3
STEP = 5
EPS_NORM = 0.001
RATE = 0.05
DECAY_WEIGHT = 0.05
BETA_ONE = 0.5
BETA_TWO = 0.5
EPS_ADAM = 1e-08
EMA_RATE = 0.5
SMOOTHING = 0.1

LANE = 128
KP = 1024
HEAD_W = C + LANE + KP
PB = 2 * C * E + 2 * E * SQ + 14 * E + SQ + 2 * C
ROW_P = C * E // LANE
ROW_R = ROW_P + E * C // LANE
ROW_X = ROW_R + E * SQ // LANE
ROW_D = ROW_X + SQ * E // LANE
ROW_S = ROW_D + 14 * E // LANE
NJ = E // LANE
GROUPS = 2
GW = E // GROUPS
MBLK = 4

MESH = pl.DeviceIdType.MESH
F32 = jnp.float32
BF16 = jnp.bfloat16
HIGH = lax.Precision.HIGHEST
VMEM_LIMIT = 63 * 1024 * 1024
VM = pl.BlockSpec(memory_space=pltpu.VMEM)


def ceil_to(value, unit):
    return -(-value // unit) * unit


class Plan:
    def __init__(self, mesh, images, head_rows):
        self.nd = mesh.shape["dp"]
        self.nf = mesh.shape["fsdp"]
        self.devices = self.nd * self.nf
        self.images = images
        self.rows = images * PIX
        self.count = float(self.rows * self.devices)
        self.shard = PB // self.nf
        self.base = [(self.shard * f // LANE) // 16 * 16 for f in range(self.nf)]
        self.chunk = ceil_to(-(-self.shard // LANE) + 17, 16 * self.nd)
        self.flat = self.base[-1] + self.chunk
        self.head_pad = ceil_to(head_rows, 16)
        self.hd = self.head_pad * self.nf
        self.head_rows = head_rows
        self.head_part = ceil_to(-(-head_rows // self.nd), 16)
        self.head_flat = self.head_pad * (self.nf - 1) + self.head_part * self.nd
        self.depth = self.nf // 2

    def layer_unit(self):
        return Unit(self, LANE, self.chunk // self.nd, self.flat, lambda f: self.shard * f // (16 * LANE) * 16)

    def head_unit(self):
        return Unit(self, HEAD_W, self.head_part, self.head_flat, lambda f: self.head_pad * f)


class Unit:
    def __init__(self, plan, width, part, rows, base):
        self.plan, self.width, self.part, self.rows, self.base = plan, width, part, rows, base
        self.owned = part * plan.nd


def dot(a, b, dims=((1,), (0,)), precision=None):
    return lax.dot_general(a, b, (dims, ((), ())), precision=precision, preferred_element_type=F32)


def row_sum(value):
    return jnp.sum(value, axis=0, keepdims=True)


def my_index(plan):
    return lax.axis_index("dp") * plan.nf + lax.axis_index("fsdp")


def peer_id(plan, step):
    k = lax.rem(my_index(plan) + step, plan.devices)
    return (k // plan.nf, lax.rem(k, plan.nf))


def enter(plan):
    barrier = pltpu.get_barrier_semaphore()

    def greet(step, carry):
        pl.semaphore_signal(barrier, inc=1, device_id=peer_id(plan, step), device_id_type=MESH)
        return carry

    lax.fori_loop(1, plan.devices, greet, 0)


def entered(plan):
    pl.semaphore_wait(pltpu.get_barrier_semaphore(), plan.devices - 1)


def share(plan, buf, send, recv, first, second):
    half = buf.shape[1] // 2
    for r in range(half):
        cols = slice(r * LANE, (r + 1) * LANE)
        buf[0, r : r + 1, :] = first[:, cols]
        buf[0, half + r : half + r + 1, :] = second[:, cols]

    def push(step, carry):
        pltpu.make_async_remote_copy(
            src_ref=buf.at[0],
            dst_ref=buf.at[step],
            send_sem=send,
            recv_sem=recv,
            device_id=peer_id(plan, step),
            device_id_type=MESH,
        ).start()
        return carry

    lax.fori_loop(1, plan.devices, push, 0)


def collect(plan, buf, send, recv):
    others = buf.at[pl.ds(1, plan.devices - 1)]
    pltpu.make_async_copy(others, others, recv).wait()
    total = jnp.sum(buf[...], axis=0)
    rows = [total[r : r + 1, :] for r in range(buf.shape[1])]
    half = len(rows) // 2
    return jnp.concatenate(rows[:half], axis=1), jnp.concatenate(rows[half:], axis=1)


def finish(plan, buf, send, recv):
    others = buf.at[pl.ds(1, plan.devices - 1)]
    pltpu.make_async_copy(others, others, send).wait()


def exchange_scratch(plan, widths):
    shapes = [pltpu.VMEM((plan.devices, 2 * w // LANE, LANE), F32) for w in widths]
    sems = [pltpu.SemaphoreType.DMA(()) for w in widths]
    return shapes + sems + sems


def exchange_refs(refs, n):
    return [(refs[i], refs[n + i], refs[2 * n + i]) for i in range(n)]


def moments(plan, pair):
    mean = pair[0] / plan.count
    return mean, lax.rsqrt(pair[1] / plan.count - mean * mean + EPS_NORM)


class Reduction:
    def __init__(self, unit, source, result, refs):
        self.unit, self.source, self.result = unit, source, result
        self.got_core, self.sum_core, self.got_dp, self.sum_dp, self.got_rest = refs[:5]
        self.send, self.recv = refs[5:9], refs[9:13]
        plan = unit.plan
        self.dp, self.fs = lax.axis_index("dp"), lax.axis_index("fsdp")
        self.core, self.deep = lax.rem(self.fs, 2), self.fs // 2
        self.nd, self.nz = plan.nd, plan.depth

    @staticmethod
    def scratch(unit):
        plan = unit.plan
        nd, nz, w, part = plan.nd, plan.depth, unit.width, unit.part
        return [
            pltpu.VMEM((nz, nd, part, w), BF16),
            pltpu.VMEM((nd, nz, part, w), BF16),
            pltpu.VMEM((nd - 1, nz, part, w), BF16),
            pltpu.VMEM((nz, part, w), BF16),
            pltpu.VMEM((nz - 1, part, w), BF16),
        ] + [pltpu.SemaphoreType.DMA(())] * 8

    def push(self, stage, source, target, device):
        pltpu.make_async_remote_copy(
            src_ref=source,
            dst_ref=target,
            send_sem=self.send[stage],
            recv_sem=self.recv[stage],
            device_id=device,
            device_id_type=MESH,
        ).start()

    def rows_of(self, f, d=0):
        return pl.multiple_of(self.unit.base(f) + d * self.unit.part, 16)

    def start_core(self):
        def go(z, carry):
            for d in range(self.nd):
                self.push(
                    0,
                    self.source.at[pl.ds(self.rows_of(2 * z + 1 - self.core, d), self.unit.part)],
                    self.got_core.at[z, d],
                    (self.dp, 2 * self.deep + 1 - self.core),
                )
            return carry

        lax.fori_loop(0, self.nz, go, 0)

    def wait(self, sem, ref):
        pltpu.make_async_copy(ref, ref, sem).wait()

    def start_dp(self):
        self.wait(self.recv[0], self.got_core)

        def add(z, carry):
            for d in range(self.nd):
                own = self.source[pl.ds(self.rows_of(2 * z + self.core, d), self.unit.part), :]
                self.sum_core[d, z] = (own.astype(F32) + self.got_core[z, d].astype(F32)).astype(BF16)
            return carry

        lax.fori_loop(0, self.nz, add, 0)
        for i in range(1, self.nd):
            other = lax.rem(self.dp + i, self.nd)
            self.push(1, self.sum_core.at[other], self.got_dp.at[i - 1], (other, self.fs))

    def start_rest(self):
        self.wait(self.recv[1], self.got_dp)

        def add(z, carry):
            total = self.sum_core[self.dp, z].astype(F32)
            for i in range(self.nd - 1):
                total = total + self.got_dp[i, z].astype(F32)
            self.sum_dp[z] = total.astype(BF16)
            return carry

        lax.fori_loop(0, self.nz, add, 0)
        for i in range(1, self.nz):
            other = lax.rem(self.deep + i, self.nz)
            self.push(2, self.sum_dp.at[other], self.got_rest.at[i - 1], (self.dp, 2 * other + self.core))

    def start_copies(self):
        self.wait(self.recv[2], self.got_rest)
        total = self.sum_dp[self.deep].astype(F32)
        for i in range(self.nz - 1):
            total = total + self.got_rest[i].astype(F32)
        rows = pl.ds(pl.multiple_of(self.dp * self.unit.part, 16), self.unit.part)
        self.result[rows, :] = total.astype(BF16)
        for i in range(1, self.nd):
            other = lax.rem(self.dp + i, self.nd)
            self.push(3, self.result.at[rows], self.result.at[rows], (other, self.fs))

    def complete(self):
        others = self.result.at[pl.ds(0, (self.nd - 1) * self.unit.part)]
        self.wait(self.recv[3], others)
        self.wait(self.send[0], self.got_core)
        self.wait(self.send[1], self.got_dp)
        self.wait(self.send[2], self.got_rest)
        self.wait(self.send[3], others)


def reduce_kernel(unit, source, result, *refs):
    enter(unit.plan)
    work = Reduction(unit, source, result, refs)
    entered(unit.plan)
    work.start_core()
    work.start_dp()
    work.start_rest()
    work.start_copies()
    work.complete()


def reduce_last(plan, packed):
    unit = plan.layer_unit()
    return pl.pallas_call(
        functools.partial(reduce_kernel, unit),
        out_shape=jax.ShapeDtypeStruct((unit.owned, unit.width), BF16),
        in_specs=[VM],
        out_specs=VM,
        scratch_shapes=Reduction.scratch(unit),
        compiler_params=pltpu.CompilerParams(
            collective_id=5, has_side_effects=True, vmem_limit_bytes=VMEM_LIMIT
        ),
        name="reduce_last",
    )(packed)


def taps():
    found = []
    for y in range(SIDE):
        for x in range(SIDE):
            for a in range(3):
                for b in range(3):
                    iy, ix = y + a - 1, x + b - 1
                    if 0 <= iy < SIDE and 0 <= ix < SIDE:
                        found.append((y * SIDE + x, 3 * a + b, iy * SIDE + ix))
    return found


TAPS = taps()


def half_tanh(half):
    return jnp.tanh(half)


def silu(z):
    half = 0.5 * z
    return half * half_tanh(half) + half


def sigmoid(z):
    return 0.5 * half_tanh(0.5 * z) + 0.5


def silu_slope(z):
    half = 0.5 * z
    t = half_tanh(half)
    return 0.5 * (1.0 + t + half * (1.0 - t * t))


def lanes(j):
    return pl.ds(pl.multiple_of(j * LANE, LANE), LANE)


def images_at(b):
    return pl.ds(pl.multiple_of(b * 8, 8), 8)


def over_tiles(plan, first_chunk, chunks, per_chunk, body, n_sums, store_sums):
    def chunk_step(jj, carry):
        j = first_chunk + jj
        hoisted = per_chunk(j)
        zero = tuple(jnp.zeros((8, LANE), F32) for _ in range(n_sums))
        sums = lax.fori_loop(
            0, plan.images // 8, lambda b, s: body(j, b, hoisted, s), zero
        )
        store_sums(j, sums)
        return carry

    lax.fori_loop(0, chunks, chunk_step, 0)


def unpack_kernel(plan, got, we, wp, wr, wx, small, tail, flat):
    lane = lax.broadcasted_iota(jnp.int32, (1, LANE), 1)
    low = lane < SQ
    for f in range(plan.nf):
        base, at = plan.base[f], f * plan.chunk
        head = got[at : at + 16, :].astype(F32)
        if f:
            head = head + flat[base : base + 16, :]
        flat[base : base + 16, :] = head
        flat[base + 16 : base + plan.chunk, :] = got[at + 16 : at + plan.chunk, :].astype(F32)
    for j in range(NJ):
        cols = slice(j * LANE, (j + 1) * LANE)
        we[:, cols] = flat[pl.ds(j, C, stride=NJ), :].astype(BF16)
        wx[0:SQ, cols] = flat[pl.ds(ROW_X + j, SQ, stride=NJ), :]
        wx[SQ:LANE, cols] = jnp.zeros((LANE - SQ, LANE), F32)
        small[0:14, cols] = flat[pl.ds(ROW_D + j, 14, stride=NJ), :]
        small[14:16, cols] = jnp.zeros((2, LANE), F32)
    for h in range(C // LANE):
        wp[:, h * LANE : (h + 1) * LANE] = flat[pl.ds(ROW_P + h, E, stride=2), :].astype(BF16)
    pairs = flat[ROW_R:ROW_X, :]
    wr[pl.ds(0, E // 2, stride=2), :] = jnp.where(low, pairs, 0.0)
    wr[pl.ds(1, E // 2, stride=2), :] = jnp.where(low, pltpu.roll(pairs, SQ, 1), 0.0)
    rows = [flat[ROW_S + i : ROW_S + i + 1, :] for i in range(5)]
    turned = [pltpu.roll(jnp.broadcast_to(r, (8, LANE)), SQ, 1)[0:1, :] for r in rows]
    tail[...] = jnp.zeros((8, C), F32)
    tail[0:1, 0:LANE] = jnp.where(low, rows[0], 0.0)
    for i, at in ((1, 0), (2, 2)):
        tail[i : i + 1, 0:LANE] = jnp.where(low, turned[at], turned[at + 1])
        tail[i : i + 1, LANE:C] = jnp.where(low, turned[at + 1], turned[at + 2])


def unpack(plan, gathered):
    return pl.pallas_call(
        functools.partial(unpack_kernel, plan),
        out_shape=(
            jax.ShapeDtypeStruct((C, E), BF16),
            jax.ShapeDtypeStruct((E, C), BF16),
            jax.ShapeDtypeStruct((E, LANE), F32),
            jax.ShapeDtypeStruct((LANE, E), F32),
            jax.ShapeDtypeStruct((16, E), F32),
            jax.ShapeDtypeStruct((8, C), F32),
        ),
        in_specs=[VM],
        out_specs=(VM,) * 6,
        scratch_shapes=[pltpu.VMEM((plan.flat, LANE), F32)],
        compiler_params=pltpu.CompilerParams(vmem_limit_bytes=VMEM_LIMIT),
        name="unpack",
    )(gathered)


def mix_kernel(plan, images, partner, weight, stream):
    n, rows = plan.images, plan.rows
    place = lax.broadcasted_iota(jnp.int32, (n, rows), 1)
    own = lax.broadcasted_iota(jnp.int32, (n, rows), 0)
    share_one = weight[...]
    for p in range(PIX):
        pick_own = jnp.where(place == own * PIX + p, 1.0, 0.0).astype(BF16)
        pick_partner = jnp.where(place == partner[...] * PIX + p, 1.0, 0.0).astype(BF16)
        mine = dot(pick_own, images[...])
        theirs = dot(pick_partner, images[...])
        stream[p * n : (p + 1) * n, :] = share_one * mine + (1.0 - share_one) * theirs


def mix(plan, images, partner, mix_weight):
    return pl.pallas_call(
        functools.partial(mix_kernel, plan),
        out_shape=jax.ShapeDtypeStruct((plan.rows, C), F32),
        in_specs=[VM] * 3,
        out_specs=VM,
        compiler_params=pltpu.CompilerParams(vmem_limit_bytes=VMEM_LIMIT),
        name="mix",
    )(
        images.reshape(plan.rows, C),
        partner.reshape(plan.images, 1),
        mix_weight.reshape(plan.images, 1),
    )


def forward_kernel(plan, x, we, wp, wr, wx, small, tail, *refs):
    out, expanded, depth, projected, stat_e, stat_c, pooled, presq, gate = refs[:9]
    x_low, act, sums = refs[9:12]
    ex = exchange_refs(refs[12:], 2 * GROUPS + 1)
    ex_one, ex_two, ex_three = ex[:GROUPS], ex[GROUPS : 2 * GROUPS], ex[2 * GROUPS]
    n = plan.images
    enter(plan)
    x_low[...] = x[...].astype(BF16)
    for g in range(GROUPS):
        cols = slice(g * GW, (g + 1) * GW)

        def expand(m, carry, cols=cols):
            rows = pl.ds(pl.multiple_of(m * MBLK * n, MBLK * n), MBLK * n)
            value = dot(x_low[rows, :], we[:, cols])
            expanded[pl.ds(m * MBLK, MBLK), :, cols] = value.reshape(MBLK, n, GW)
            return (
                carry[0] + jnp.sum(value.reshape(-1, 8, GW), axis=0),
                carry[1] + jnp.sum((value * value).reshape(-1, 8, GW), axis=0),
            )

        zero = jnp.zeros((8, GW), F32)
        s, q = lax.fori_loop(0, PIX // MBLK, expand, (zero, zero))
        if g == 0:
            entered(plan)
        share(plan, *ex_one[g], row_sum(s), row_sum(q))

    def put_sums(j, totals):
        for i, t in enumerate(totals):
            sums[i : i + 1, lanes(j)] = row_sum(t)

    for g in range(GROUPS):
        cols = slice(g * GW, (g + 1) * GW)
        mean, rstd = moments(plan, collect(plan, *ex_one[g]))
        stat_e[0:1, cols] = mean
        stat_e[1:2, cols] = rstd
        scale = rstd * small[9:10, cols]
        stat_e[4:5, cols] = 0.5 * scale
        stat_e[5:6, cols] = 0.5 * (small[10:11, cols] - mean * scale)

        def chunk(j):
            return (
                stat_e[4:5, lanes(j)],
                stat_e[5:6, lanes(j)],
                [small[t : t + 1, lanes(j)] for t in range(9)],
            )

        def spread(j, b, hoisted, totals):
            scale, shift, w = hoisted
            act_one = []
            for p in range(PIX):
                half = expanded[p, images_at(b), lanes(j)] * scale + shift
                act_one.append(half * half_tanh(half) + half)
            made = [None] * PIX
            for o, t, i in TAPS:
                term = act_one[i] * w[t]
                made[o] = term if made[o] is None else made[o] + term
            s, q = totals
            for p in range(PIX):
                depth[p, images_at(b), lanes(j)] = made[p]
                s = s + made[p]
                q = q + made[p] * made[p]
            return s, q

        over_tiles(plan, g * (GW // LANE), GW // LANE, chunk, spread, 2, put_sums)
        share(plan, *ex_two[g], sums[0:1, cols], sums[1:2, cols])

    for g in range(GROUPS):
        cols = slice(g * GW, (g + 1) * GW)
        mean, rstd = moments(plan, collect(plan, *ex_two[g]))
        stat_e[2:3, cols] = mean
        stat_e[3:4, cols] = rstd
        scale = rstd * small[11:12, cols]
        stat_e[6:7, cols] = 0.5 * scale
        stat_e[7:8, cols] = 0.5 * (small[12:13, cols] - mean * scale)

        def chunk_two(j):
            return stat_e[6:7, lanes(j)], stat_e[7:8, lanes(j)]

        def activate(j, b, hoisted, totals):
            scale, shift = hoisted
            total = None
            for p in range(PIX):
                half = depth[p, images_at(b), lanes(j)] * scale + shift
                made = half * half_tanh(half) + half
                act[p, images_at(b), lanes(j)] = made
                total = made if total is None else total + made
            pooled[images_at(b), lanes(j)] = total * (1.0 / PIX)
            return totals

        over_tiles(
            plan, g * (GW // LANE), GW // LANE, chunk_two, activate, 0, lambda j, s: None
        )
    reduced = dot(pooled[...], wr[...], precision=HIGH) + tail[0:1, 0:LANE]
    presq[...] = reduced
    gate[...] = sigmoid(dot(silu(reduced), wx[...], precision=HIGH) + small[13:14, :])

    def project(m, carry):
        rows = pl.ds(pl.multiple_of(m * MBLK * n, MBLK * n), MBLK * n)
        gated = (act[pl.ds(m * MBLK, MBLK), :, :] * gate[...][None]).astype(BF16)
        value = dot(gated.reshape(MBLK * n, E), wp[...])
        projected[rows, :] = value
        return (
            carry[0] + jnp.sum(value.reshape(-1, 8, C), axis=0),
            carry[1] + jnp.sum((value * value).reshape(-1, 8, C), axis=0),
        )

    zero = jnp.zeros((8, C), F32)
    s, q = lax.fori_loop(0, PIX // MBLK, project, (zero, zero))
    share(plan, *ex_three, row_sum(s), row_sum(q))
    mean, rstd = moments(plan, collect(plan, *ex_three))
    stat_c[...] = jnp.zeros((8, C), F32)
    stat_c[0:1, :] = mean
    stat_c[1:2, :] = rstd
    scale = rstd * tail[1:2, :]
    out[...] = x[...] + (projected[...] - mean) * scale + tail[2:3, :]
    for e in ex:
        finish(plan, *e)


def forward(plan, x, weights):
    n = plan.images
    big = (PIX, n, E)
    return pl.pallas_call(
        functools.partial(forward_kernel, plan),
        out_shape=(
            jax.ShapeDtypeStruct((plan.rows, C), F32),
            jax.ShapeDtypeStruct(big, F32),
            jax.ShapeDtypeStruct(big, F32),
            jax.ShapeDtypeStruct((plan.rows, C), F32),
            jax.ShapeDtypeStruct((8, E), F32),
            jax.ShapeDtypeStruct((8, C), F32),
            jax.ShapeDtypeStruct((n, E), F32),
            jax.ShapeDtypeStruct((n, LANE), F32),
            jax.ShapeDtypeStruct((n, E), F32),
        ),
        in_specs=[VM] * 7,
        out_specs=(VM,) * 9,
        scratch_shapes=[
            pltpu.VMEM((plan.rows, C), BF16),
            pltpu.VMEM(big, F32),
            pltpu.VMEM((8, E), F32),
        ]
        + exchange_scratch(plan, [GW] * (2 * GROUPS) + [C]),
        compiler_params=pltpu.CompilerParams(
            collective_id=1, has_side_effects=True, vmem_limit_bytes=VMEM_LIMIT
        ),
        name="layer_forward",
    )(x, *weights)


def head_kernel(plan, x, w_head, bias, label, label_row, partner, weight, *refs):
    grad_x, grad_head, totals_out = refs[:3]
    x_low, turned, hidden, slope, low_grad, pool, stat, sums, gain = refs[3:12]
    hd, n = plan.hd, plan.images
    halves = plan.head_groups
    ng = len(halves)
    ex = exchange_refs(refs[12:], 2 * ng + 1)
    ex_stat, ex_grad, ex_bias = ex[:ng], ex[ng : 2 * ng], ex[2 * ng]
    enter(plan)
    x_low[...] = x[...].astype(BF16)
    turned[...] = x[...].T.astype(BF16)
    gain[...] = w_head[:, C : C + LANE].astype(F32).T[0:8, :]
    for g, (start, width) in enumerate(halves):
        cols = slice(start, start + width)

        def convolve(m, carry, cols=cols, width=width):
            rows = pl.ds(pl.multiple_of(m * MBLK * n, MBLK * n), MBLK * n)
            value = dot(x_low[rows, :], w_head[cols, 0:C], ((1,), (1,)))
            hidden[pl.ds(m * MBLK, MBLK), :, cols] = value.reshape(MBLK, n, width)
            return (
                carry[0] + jnp.sum(value.reshape(-1, 8, width), axis=0),
                carry[1] + jnp.sum((value * value).reshape(-1, 8, width), axis=0),
            )

        zero = jnp.zeros((8, width), F32)
        s, q = lax.fori_loop(0, PIX // MBLK, convolve, (zero, zero))
        if g == 0:
            entered(plan)
        share(plan, *ex_stat[g], row_sum(s), row_sum(q))
    for g, (start, width) in enumerate(halves):
        cols = slice(start, start + width)
        mean, rstd = moments(plan, collect(plan, *ex_stat[g]))
        scale = rstd * gain[0:1, cols]
        stat[0:1, cols] = rstd
        stat[1:2, cols] = -mean * rstd
        stat[2:3, cols] = 0.5 * scale
        stat[3:4, cols] = 0.5 * (gain[1:2, cols] - mean * scale)

        def chunk(j):
            return stat[2:3, lanes(j)], stat[3:4, lanes(j)]

        def activate(j, b, hoisted, totals):
            scale, shift = hoisted
            total = None
            for p in range(PIX):
                half = hidden[p, images_at(b), lanes(j)] * scale + shift
                t = half_tanh(half)
                made = half * t + half
                slope[p, images_at(b), lanes(j)] = (1.0 + t) + half * (1.0 - t * t)
                total = made if total is None else total + made
            pool[images_at(b), lanes(j)] = total * (1.0 / PIX)
            return totals

        over_tiles(plan, start // LANE, width // LANE, chunk, activate, 0, lambda j, s: None)
    pool_low = pool[...].astype(BF16)
    classes = lax.broadcasted_iota(jnp.int32, (n, KP), 1)
    valid = classes < K
    logits = dot(pool_low, w_head[:, C + LANE :]) + bias[...]
    logits = jnp.where(valid, logits, -1e30)
    top = jnp.max(logits, axis=1, keepdims=True)
    lifted = logits - top
    powers = jnp.where(valid, jnp.exp(lifted), 0.0)
    norm = jnp.sum(powers, axis=1, keepdims=True)
    log_probs = lifted - jnp.log(norm)
    picked = lax.broadcasted_iota(jnp.int32, (n, n), 1) == partner[...]
    label_two = jnp.sum(jnp.where(picked, label_row[...], 0), axis=1, keepdims=True)
    w = weight[...]
    targets = w * jnp.where(classes == label[...], 1.0 - SMOOTHING, 0.0) + (1.0 - w) * jnp.where(
        classes == label_two, 1.0 - SMOOTHING, 0.0
    )
    targets = jnp.where(valid, targets + SMOOTHING / K, 0.0)
    loss = -jnp.sum(jnp.where(valid, targets * log_probs, 0.0))
    grad_logits = (powers / norm - targets) * (float(PIX) / plan.count)
    share(plan, *ex_bias, row_sum(grad_logits), jnp.full((1, KP), loss, F32))
    grad_low = grad_logits.astype(BF16)
    pool_grad = dot(grad_low, w_head[:, C + LANE :], ((1,), (1,)))
    pool[...] = pool_grad * (0.5 / PIX)

    def put_sums(j, totals):
        for i, t in enumerate(totals):
            sums[i : i + 1, lanes(j)] = row_sum(t)

    for g, (start, width) in enumerate(halves):
        cols = slice(start, start + width)

        def chunk_back(j):
            return stat[0:1, lanes(j)], stat[1:2, lanes(j)]

        def back(j, b, hoisted, totals):
            rstd, shift = hoisted
            s, q = totals
            flow = pool[images_at(b), lanes(j)]
            for p in range(PIX):
                made = slope[p, images_at(b), lanes(j)] * flow
                slope[p, images_at(b), lanes(j)] = made
                normed = hidden[p, images_at(b), lanes(j)] * rstd + shift
                s = s + made
                q = q + made * normed
            return s, q

        over_tiles(plan, start // LANE, width // LANE, chunk_back, back, 2, put_sums)
        share(plan, *ex_grad[g], sums[0:1, cols], sums[1:2, cols])
    grad_head[0:hd, C + LANE :] = dot(pool_low.T, grad_low).astype(BF16)
    norm_grads = jnp.concatenate(
        [sums[1:2, :], sums[0:1, :], jnp.zeros((LANE - 2, hd), F32)], axis=0
    )
    grad_head[0:hd, C : C + LANE] = norm_grads.T.astype(BF16)
    for g, (start, width) in enumerate(halves):
        cols = slice(start, start + width)
        shift_total, gain_total = collect(plan, *ex_grad[g])
        scale = stat[0:1, cols] * gain[0:1, cols]
        mean_one = shift_total / plan.count
        mean_two = gain_total / plan.count
        stat[4:5, cols] = scale
        stat[5:6, cols] = -scale * stat[0:1, cols] * mean_two
        stat[6:7, cols] = -scale * (mean_one + stat[1:2, cols] * mean_two)
    def into(m, carry):
        rows = pl.ds(pl.multiple_of(m * MBLK * n, MBLK * n), MBLK * n)
        spot = pl.ds(m * MBLK, MBLK)
        value = (
            slope[spot, :, :] * stat[4:5, :] + hidden[spot, :, :] * stat[5:6, :] + stat[6:7, :]
        )
        low = value.reshape(MBLK * n, hd).astype(BF16)
        low_grad[rows, :] = low
        grad_x[rows, :] = dot(low, w_head[:, 0:C])
        return carry

    lax.fori_loop(0, PIX // MBLK, into, 0)
    for at in range(0, hd, LANE):
        part = dot(turned[...], low_grad[:, at : at + LANE])
        grad_head[at : at + LANE, 0:C] = part.T.astype(BF16)
    bias_total, loss_total = collect(plan, *ex_bias)
    totals_out[0:1, :] = bias_total
    totals_out[1:2, :] = loss_total
    for e in ex:
        finish(plan, *e)


def head(plan, x, w_head, bias, labels, partner, mix_weight):
    n, hd = plan.images, plan.hd
    big = (PIX, n, hd)
    widths = [w for _, w in plan.head_groups]
    return pl.pallas_call(
        functools.partial(head_kernel, plan),
        out_shape=(
            jax.ShapeDtypeStruct((plan.rows, C), F32),
            jax.ShapeDtypeStruct((plan.head_flat, HEAD_W), BF16),
            jax.ShapeDtypeStruct((2, KP), F32),
        ),
        in_specs=[VM] * 7,
        out_specs=(VM,) * 3,
        scratch_shapes=[
            pltpu.VMEM((plan.rows, C), BF16),
            pltpu.VMEM((C, plan.rows), BF16),
            pltpu.VMEM(big, F32),
            pltpu.VMEM(big, F32),
            pltpu.VMEM((plan.rows, hd), BF16),
            pltpu.VMEM((n, hd), F32),
            pltpu.VMEM((8, hd), F32),
            pltpu.VMEM((8, hd), F32),
            pltpu.VMEM((8, hd), F32),
        ]
        + exchange_scratch(plan, widths + widths + [KP]),
        compiler_params=pltpu.CompilerParams(
            collective_id=2, has_side_effects=True, vmem_limit_bytes=VMEM_LIMIT
        ),
        name="head",
    )(
        x,
        w_head,
        bias,
        labels.reshape(n, 1),
        labels.reshape(1, n),
        partner.reshape(n, 1),
        mix_weight.reshape(n, 1),
    )


def backward_kernel(plan, x, grad, expanded, depth, projected, stat_e, stat_c, pooled, presq, gate, we, wp, wr, wx, small, tail, later, *refs, unit):
    grad_x, packed, summed = refs[:3]
    turned, act, flow, low_proj, gated, sums, coef, squeeze_grad, flat, pair_buf = refs[3:13]
    ex = exchange_refs(refs[13:], 2 * GROUPS + 1)
    work = Reduction(unit, later, summed, refs[13 + 3 * (2 * GROUPS + 1) :])
    ex_two, ex_one, ex_three = ex[:GROUPS], ex[GROUPS : 2 * GROUPS], ex[2 * GROUPS]
    n = plan.images
    lane = lax.broadcasted_iota(jnp.int32, (1, LANE), 1)
    is_low = lane < SQ
    enter(plan)
    mean_c, rstd_c = stat_c[0:1, :], stat_c[1:2, :]
    s = row_sum(jnp.sum(grad[...].reshape(-1, 8, C), axis=0))
    q = row_sum(
        jnp.sum((grad[...] * ((projected[...] - mean_c) * rstd_c)).reshape(-1, 8, C), axis=0)
    )
    entered(plan)
    share(plan, *ex_three, s, q)
    work.start_core()
    bias_three, gain_three = s, q

    def chunk_two(j):
        return stat_e[6:7, lanes(j)], stat_e[7:8, lanes(j)]

    def activate(j, b, hoisted, totals):
        scale, shift = hoisted
        for p in range(PIX):
            half = depth[p, images_at(b), lanes(j)] * scale + shift
            act[p, images_at(b), lanes(j)] = half * half_tanh(half) + half
        return totals

    over_tiles(plan, 0, NJ, chunk_two, activate, 0, lambda j, s: None)

    def regate(m, carry):
        rows = pl.ds(pl.multiple_of(m * MBLK * n, MBLK * n), MBLK * n)
        value = (act[pl.ds(m * MBLK, MBLK), :, :] * gate[...][None]).astype(BF16)
        gated[rows, :] = value.reshape(MBLK * n, E)
        return carry

    lax.fori_loop(0, PIX // MBLK, regate, 0)
    turned[...] = x[...].T.astype(BF16)

    bias_total, gain_total = collect(plan, *ex_three)
    scale = rstd_c * tail[1:2, :]
    mean_one, mean_two = bias_total / plan.count, gain_total / plan.count
    low_proj[...] = (
        scale
        * (grad[...] - mean_one - (projected[...] - mean_c) * (rstd_c * mean_two))
    ).astype(BF16)

    def into_gated(m, carry):
        rows = pl.ds(pl.multiple_of(m * MBLK * n, MBLK * n), MBLK * n)
        value = dot(low_proj[rows, :], wp[...], ((1,), (1,)))
        flow[pl.ds(m * MBLK, MBLK), :, :] = value.reshape(MBLK, n, E)
        return carry

    lax.fori_loop(0, PIX // MBLK, into_gated, 0)
    work.start_dp()

    def gate_back(j, b, hoisted, totals):
        total = None
        for p in range(PIX):
            term = flow[p, images_at(b), lanes(j)] * act[p, images_at(b), lanes(j)]
            total = term if total is None else total + term
        opened = gate[images_at(b), lanes(j)]
        squeeze_grad[images_at(b), lanes(j)] = total * opened * (1.0 - opened)
        return totals

    over_tiles(plan, 0, NJ, lambda j: None, gate_back, 0, lambda j, s: None)
    excite_grad = squeeze_grad[...]
    sums[13:14, :] = row_sum(excite_grad)
    squeezed = silu(presq[...])
    presq_grad = dot(excite_grad, wx[...], ((1,), (1,)), HIGH) * silu_slope(presq[...])
    grad_wx = dot(squeezed.T, excite_grad, precision=HIGH)
    for j in range(NJ):
        flat[pl.ds(ROW_X + j, SQ, stride=NJ), :] = grad_wx[0:SQ, j * LANE : (j + 1) * LANE]
    grad_reduce_b = row_sum(presq_grad)
    grad_wr = dot(pooled[...].T, presq_grad, precision=HIGH)
    squeeze_grad[...] = dot(presq_grad, wr[...], ((1,), (1,)), HIGH) * (1.0 / PIX)

    def put_sums(first_row):
        def put(j, totals):
            for i, t in enumerate(totals):
                sums[first_row + i : first_row + i + 1, lanes(j)] = row_sum(t)

        return put

    def chunk_norm(j):
        return (
            stat_e[6:7, lanes(j)],
            stat_e[7:8, lanes(j)],
            stat_e[2:3, lanes(j)],
            stat_e[3:4, lanes(j)],
        )

    def back_two(j, b, hoisted, totals):
        scale, shift, mean, rstd = hoisted
        gain_sum, bias_sum = totals
        opened = gate[images_at(b), lanes(j)] * 0.5
        pool_flow = squeeze_grad[images_at(b), lanes(j)] * 0.5
        for p in range(PIX):
            value = depth[p, images_at(b), lanes(j)]
            half = value * scale + shift
            t = half_tanh(half)
            made = (flow[p, images_at(b), lanes(j)] * opened + pool_flow) * (
                (1.0 + t) + half * (1.0 - t * t)
            )
            flow[p, images_at(b), lanes(j)] = made
            bias_sum = bias_sum + made
            gain_sum = gain_sum + made * ((value - mean) * rstd)
        return gain_sum, bias_sum

    for g in range(GROUPS):
        cols = slice(g * GW, (g + 1) * GW)
        over_tiles(plan, g * (GW // LANE), GW // LANE, chunk_norm, back_two, 2, put_sums(11))
        share(plan, *ex_two[g], sums[12:13, cols], sums[11:12, cols])

    work.start_rest()
    proj_turned = low_proj[...].astype(F32).T.astype(BF16)
    for j in range(NJ):
        part = dot(proj_turned, gated[:, j * LANE : (j + 1) * LANE])
        for h in range(C // LANE):
            flat[pl.ds(ROW_P + 2 * j * LANE + h, LANE, stride=2), :] = part[
                h * LANE : (h + 1) * LANE, :
            ].T

    def norm_coefs(g, pair, row, stat_row, gain_row):
        cols = slice(g * GW, (g + 1) * GW)
        mean, rstd = stat_e[stat_row : stat_row + 1, cols], stat_e[stat_row + 1 : stat_row + 2, cols]
        scale = rstd * small[gain_row : gain_row + 1, cols]
        mean_one, mean_two = pair[0] / plan.count, pair[1] / plan.count
        coef[row : row + 1, cols] = scale
        coef[row + 1 : row + 2, cols] = -scale * rstd * mean_two
        coef[row + 2 : row + 3, cols] = -scale * (mean_one - mean * rstd * mean_two)

    def chunk_one(j):
        return (
            [coef[i : i + 1, lanes(j)] for i in range(3)],
            [small[t : t + 1, lanes(j)] for t in range(9)],
            [stat_e[i : i + 1, lanes(j)] for i in (4, 5, 0, 1)],
        )

    def back_one(j, b, hoisted, totals):
        (c_flow, c_value, c_const), w, (scale, shift, mean, rstd) = hoisted
        w_sums, gain_sum, bias_sum = list(totals[:9]), totals[9], totals[10]
        spread_grad = []
        for p in range(PIX):
            spread_grad.append(
                flow[p, images_at(b), lanes(j)] * c_flow
                + (depth[p, images_at(b), lanes(j)] * c_value + c_const)
            )
        act_one = []
        for p in range(PIX):
            half = expanded[p, images_at(b), lanes(j)] * scale + shift
            t = half_tanh(half)
            act_one.append(half * t + half)
        made = [None] * PIX
        for o, t, i in TAPS:
            w_sums[t] = w_sums[t] + spread_grad[o] * act_one[i]
            term = spread_grad[o] * w[t]
            made[i] = term if made[i] is None else made[i] + term
        for p in range(PIX):
            value = expanded[p, images_at(b), lanes(j)]
            half = value * scale + shift
            t = half_tanh(half)
            result = made[p] * (0.5 * ((1.0 + t) + half * (1.0 - t * t)))
            flow[p, images_at(b), lanes(j)] = result
            bias_sum = bias_sum + result
            gain_sum = gain_sum + result * ((value - mean) * rstd)
        return tuple(w_sums) + (gain_sum, bias_sum)

    for g in range(GROUPS):
        cols = slice(g * GW, (g + 1) * GW)
        norm_coefs(g, collect(plan, *ex_two[g]), 0, 2, 11)
        over_tiles(plan, g * (GW // LANE), GW // LANE, chunk_one, back_one, 11, put_sums(0))
        share(plan, *ex_one[g], sums[10:11, cols], sums[9:10, cols])

    work.start_copies()
    for j in range(NJ):
        flat[pl.ds(ROW_D + j, 14, stride=NJ), :] = sums[0:14, j * LANE : (j + 1) * LANE]
    pair_buf[...] = grad_wr
    evens = pair_buf[pl.ds(0, E // 2, stride=2), :]
    odds = pair_buf[pl.ds(1, E // 2, stride=2), :]
    flat[ROW_R:ROW_X, :] = jnp.where(is_low, evens, pltpu.roll(odds, SQ, 1))

    def turn(row):
        return pltpu.roll(jnp.broadcast_to(row, (8, LANE)), SQ, 1)[0:1, :]

    pieces = [turn(v[:, h * LANE : (h + 1) * LANE]) for v in (gain_three, bias_three) for h in (0, 1)]
    flat[ROW_S : ROW_S + 1, :] = jnp.where(is_low, grad_reduce_b, pieces[0])
    for i in range(3):
        flat[ROW_S + 1 + i : ROW_S + 2 + i, :] = jnp.where(is_low, pieces[i], pieces[i + 1])
    flat[ROW_S + 4 : ROW_S + 5, :] = pieces[3]

    grad_x[...] = grad[...]
    for g in range(GROUPS):
        cols = slice(g * GW, (g + 1) * GW)
        norm_coefs(g, collect(plan, *ex_one[g]), 0, 0, 9)

        def into(m, carry, cols=cols):
            rows = pl.ds(pl.multiple_of(m * MBLK * n, MBLK * n), MBLK * n)
            spot = pl.ds(m * MBLK, MBLK)
            value = (
                flow[spot, :, cols] * coef[0:1, cols]
                + expanded[spot, :, cols] * coef[1:2, cols]
                + coef[2:3, cols]
            )
            low = value.reshape(MBLK * n, GW).astype(BF16)
            gated[rows, cols] = low
            grad_x[rows, :] += dot(low, we[:, cols], ((1,), (1,)))
            return carry

        lax.fori_loop(0, PIX // MBLK, into, 0)
        for j in range(g * (GW // LANE), (g + 1) * (GW // LANE)):
            flat[pl.ds(j, C, stride=NJ), :] = dot(
                turned[...], gated[:, j * LANE : (j + 1) * LANE]
            )
    packed[...] = flat[...].astype(BF16)
    work.complete()
    for e in ex:
        finish(plan, *e)


def backward(plan, x, grad, kept, weights, later, unit, collective_id):
    n = plan.images
    big = (PIX, n, E)
    return pl.pallas_call(
        functools.partial(backward_kernel, plan, unit=unit),
        out_shape=(
            jax.ShapeDtypeStruct((plan.rows, C), F32),
            jax.ShapeDtypeStruct((plan.flat, LANE), BF16),
            jax.ShapeDtypeStruct((unit.owned, unit.width), BF16),
        ),
        in_specs=[VM] * 17,
        out_specs=(VM,) * 3,
        scratch_shapes=[
            pltpu.VMEM((C, plan.rows), BF16),
            pltpu.VMEM(big, F32),
            pltpu.VMEM(big, F32),
            pltpu.VMEM((plan.rows, C), BF16),
            pltpu.VMEM((plan.rows, E), BF16),
            pltpu.VMEM((16, E), F32),
            pltpu.VMEM((8, E), F32),
            pltpu.VMEM((n, E), F32),
            pltpu.VMEM((plan.flat, LANE), F32),
            pltpu.VMEM((E, LANE), F32),
        ]
        + exchange_scratch(plan, [GW] * (2 * GROUPS) + [C])
        + Reduction.scratch(unit),
        compiler_params=pltpu.CompilerParams(
            collective_id=collective_id, has_side_effects=True, vmem_limit_bytes=VMEM_LIMIT
        ),
        name="layer_backward",
    )(x, grad, *kept, *weights, later)


def adam_update(master, first, second, average, grad):
    first_new = BETA_ONE * first + (1.0 - BETA_ONE) * grad
    second_new = BETA_TWO * second + (1.0 - BETA_TWO) * grad * grad
    fix_one = 1.0 - BETA_ONE**STEP
    fix_two = 1.0 - BETA_TWO**STEP
    master_new = master * (1.0 - RATE * DECAY_WEIGHT) - RATE * (first_new / fix_one) / (
        jnp.sqrt(second_new / fix_two) + EPS_ADAM
    )
    average_new = EMA_RATE * average + (1.0 - EMA_RATE) * master_new
    return (master_new, first_new, second_new, average_new)


def on_device(mesh, images, partner, mix_weight, labels, *states):
    block, head_state, bias_state = states[0:4], states[4:8], states[8:12]
    row = C + 2 + K
    plan = Plan(mesh, images.shape[0], head_state[0].shape[0] // row)
    half = (plan.hd // LANE + 1) // 2 * LANE
    plan.head_groups = [(0, half), (half, plan.hd - half)]
    start = lax.axis_index("fsdp") * plan.shard
    offset = start - start // (16 * LANE) * (16 * LANE)
    weights = []
    for layer in range(LAYERS):
        flat = lax.dynamic_update_slice(
            jnp.zeros((plan.chunk * LANE,), BF16), block[0][layer].astype(BF16), (offset,)
        )
        gathered = lax.all_gather(flat.reshape(plan.chunk, LANE), "fsdp", axis=0, tiled=True)
        weights.append(unpack(plan, gathered))
    grid = head_state[0].astype(BF16).reshape(plan.head_rows, row)
    grid = jnp.concatenate(
        [
            grid[:, : C + 2],
            jnp.zeros((plan.head_rows, LANE - 2), BF16),
            grid[:, C + 2 :],
            jnp.zeros((plan.head_rows, KP - K), BF16),
        ],
        axis=1,
    )
    grid = jnp.pad(grid, ((0, plan.head_pad - plan.head_rows), (0, 0)))
    w_head = lax.all_gather(grid, "fsdp", axis=0, tiled=True)
    bias = jnp.pad(bias_state[0], (0, KP - K)).reshape(1, KP)

    stream = mix(plan, images, partner, mix_weight)
    inputs, kept = [], []
    for layer in range(LAYERS):
        inputs.append(stream)
        made = forward(plan, stream, weights[layer])
        stream = made[0]
        kept.append(made[1:])
    grad, head_grad, totals = head(plan, stream, w_head, bias, labels, partner, mix_weight)
    loss_sum = totals[1, 0]
    grad_bias = totals[0, :K]
    later, unit, sums = head_grad, plan.head_unit(), []
    for layer in reversed(range(LAYERS)):
        grad, later_next, summed = backward(
            plan, inputs[layer], grad, kept[layer], weights[layer], later, unit, 3 + len(sums[:1])
        )
        sums.append(summed)
        later, unit = later_next, plan.layer_unit()
    sums.append(reduce_last(plan, later))
    head_grad, block_grad = sums[0], jnp.stack(sums[:0:-1])
    block_grad = lax.dynamic_slice(
        block_grad.reshape(LAYERS, plan.chunk * LANE), (0, offset), (LAYERS, plan.shard)
    ).astype(F32)
    head_grad = head_grad[: plan.head_rows].astype(F32)
    head_grad = jnp.concatenate(
        [head_grad[:, : C + 2], head_grad[:, C + LANE : C + LANE + K]], axis=1
    ).reshape(-1)
    return (
        (loss_sum,)
        + adam_update(*block, block_grad)
        + adam_update(*head_state, head_grad)
        + adam_update(*bias_state, grad_bias)
    )


def solution(mesh):
    data = P(("dp", "fsdp"))
    states = (P(None, "fsdp"),) * 4 + (P("fsdp"),) * 4 + (P(),) * 4
    return jax.shard_map(
        functools.partial(on_device, mesh),
        mesh=mesh,
        in_specs=(P(("dp", "fsdp"), None, None), data, data, data) + states,
        out_specs=(P(),) + states,
        check_vma=False,
    )
```

```python
import functools
import types

import jax
import jax.numpy as jnp
from jax import lax
from jax.experimental import pallas as pl
from jax.experimental.pallas import tpu as pltpu
from jax.sharding import PartitionSpec as P

C = 256
E = 1536
SQ = 64
K = 1000
SIDE = 4
PIX = 16
LAYERS = 3
STEP = 5
EPS_NORM = 0.001
RATE = 0.05
DECAY_WEIGHT = 0.05
BETA_ONE = 0.5
BETA_TWO = 0.5
EPS_ADAM = 1e-08
EMA_RATE = 0.5
SMOOTHING = 0.1

LANE = 128
KP = 1024
HEAD_W = C + LANE + KP
PB = 2 * C * E + 2 * E * SQ + 14 * E + SQ + 2 * C
ROW_P = C * E // LANE
ROW_R = ROW_P + E * C // LANE
ROW_X = ROW_R + E * SQ // LANE
ROW_D = ROW_X + SQ * E // LANE
ROW_S = ROW_D + 14 * E // LANE
NJ = E // LANE
GROUPS = 2
GW = E // GROUPS
MBLK = 4
UN_SPREAD, UN_ACT, UN_HBACK, UN_GATE, UN_TWO, UN_ONE = 2, 4, 4, 4, 2, 1

MESH = pl.DeviceIdType.MESH
F32 = jnp.float32
BF16 = jnp.bfloat16
VMEM_LIMIT = 127 * 512 * 1024
VM = pl.BlockSpec(memory_space=pltpu.VMEM)


def ceil_to(value, unit):
    return -(-value // unit) * unit


class Plan:
    def __init__(self, mesh, images, head_rows):
        self.nd = mesh.shape["dp"]
        self.nf = mesh.shape["fsdp"]
        self.devices = self.nd * self.nf
        self.images = images
        self.rows = images * PIX
        self.count = float(self.rows * self.devices)
        self.shard = PB // self.nf
        self.base = [(self.shard * f // LANE) // 16 * 16 for f in range(self.nf)]
        self.chunk = ceil_to(-(-self.shard // LANE) + 17, 16 * self.nd)
        self.flat = self.base[-1] + self.chunk
        self.head_pad = ceil_to(head_rows, 16)
        self.hd = self.head_pad * self.nf
        self.head_rows = head_rows
        self.head_part = ceil_to(-(-head_rows // self.nd), 16)
        self.head_flat = self.head_pad * (self.nf - 1) + self.head_part * self.nd
        self.depth = self.nf // 2

    def layer_unit(self):
        return Unit(self, LANE, self.chunk // self.nd, self.flat, lambda f: self.shard * f // (16 * LANE) * 16)

    def head_unit(self):
        return Unit(self, HEAD_W, self.head_part, self.head_flat, lambda f: self.head_pad * f)


class Unit:
    def __init__(self, plan, width, part, rows, base):
        self.plan, self.width, self.part, self.rows, self.base = plan, width, part, rows, base
        self.owned = part * plan.nd


def dot(a, b, dims=((1,), (0,))):
    return lax.dot_general(a, b, (dims, ((), ())), preferred_element_type=F32)


def halves_of(value):
    high = value.astype(BF16)
    return high, (value - high.astype(F32)).astype(BF16)


def dot_rows(value, low, dims=((1,), (0,))):
    n = value.shape[0]
    both = dot(jnp.concatenate(halves_of(value), axis=0), low, dims)
    return both[0:n, :] + both[n:, :]


def dot_outer(a, b):
    a_high, a_low = halves_of(a)
    b_high, b_low = halves_of(b)
    left = jnp.concatenate([a_high, a_low, a_high], axis=0)
    right = jnp.concatenate([b_high, b_high, b_low], axis=0)
    return dot(left, right, ((0,), (0,)))


def row_sum(value):
    return jnp.sum(value, axis=0, keepdims=True)


def over_peers(plan, body):
    dp, fs = lax.axis_index("dp"), lax.axis_index("fsdp")
    deep, low = fs // 2, dp * 2 + lax.rem(fs, 2)
    near = 2 * plan.nd
    top = jnp.where(2 * deep >= plan.depth, 1, 0)

    def at(k, i, carry):
        z = top * k + (1 - top) * (plan.depth - 1 - k)
        j = lax.rem(low + i, near)

        @pl.when((z != deep) | (j != low))
        def _():
            body((j // 2, 2 * z + lax.rem(j, 2)))

        return carry

    for k in range(plan.depth):
        lax.fori_loop(0, near, functools.partial(at, k), 0)


def my_slot(plan):
    return lax.axis_index("dp") * plan.nf + lax.axis_index("fsdp")


def enter(plan):
    barrier = pltpu.get_barrier_semaphore()
    over_peers(
        plan,
        lambda device: pl.semaphore_signal(
            barrier, inc=1, device_id=device, device_id_type=MESH
        ),
    )


def entered(plan):
    pl.semaphore_wait(pltpu.get_barrier_semaphore(), plan.devices - 1)


class Exchange:
    def __init__(self, plan, buf, send, recv):
        self.plan, self.buf, self.send, self.recv, self.used = plan, buf, send, recv, False

    def share(self, first, second):
        plan, buf, send, recv = self.plan, self.buf, self.send, self.recv
        if self.used:
            self.finish()
        self.used = True
        half = first.shape[1] // LANE
        self.rows = 2 * half
        mine = my_slot(plan)
        for r in range(half):
            cols = slice(r * LANE, (r + 1) * LANE)
            buf[mine, r : r + 1, :] = first[:, cols]
            buf[mine, half + r : half + r + 1, :] = second[:, cols]
        over_peers(
            plan,
            lambda device: pltpu.make_async_remote_copy(
                src_ref=buf.at[mine, pl.ds(0, 2 * half)],
                dst_ref=buf.at[mine, pl.ds(0, 2 * half)],
                send_sem=send,
                recv_sem=recv,
                device_id=device,
                device_id_type=MESH,
            ).start(),
        )

    def others(self):
        return self.buf.at[pl.ds(1, self.plan.devices - 1), pl.ds(0, self.rows)]

    def collect(self):
        pltpu.make_async_copy(self.others(), self.others(), self.recv).wait()
        total = jnp.sum(self.buf[:, 0 : self.rows, :], axis=0)
        rows = [total[r : r + 1, :] for r in range(self.rows)]
        half = self.rows // 2
        return jnp.concatenate(rows[:half], axis=1), jnp.concatenate(rows[half:], axis=1)

    def finish(self):
        pltpu.make_async_copy(self.others(), self.others(), self.send).wait()


def moments(plan, pair):
    mean = pair[0] / plan.count
    return mean, lax.rsqrt(pair[1] / plan.count - mean * mean + EPS_NORM)


class Reduction:
    def __init__(self, unit, source, result, refs):
        self.unit, self.source, self.result = unit, source, result
        self.got_core, self.got_dp, self.sum_dp, self.got_rest = refs[:4]
        self.send, self.recv = refs[4:8], refs[8:12]
        plan = unit.plan
        self.dp, self.fs = lax.axis_index("dp"), lax.axis_index("fsdp")
        self.core, self.deep = lax.rem(self.fs, 2), self.fs // 2
        self.nd, self.nz = plan.nd, plan.depth

    @staticmethod
    def scratch(unit):
        plan = unit.plan
        nd, nz, w, part = plan.nd, plan.depth, unit.width, unit.part
        return [
            pltpu.VMEM((nz, nd, part, w), BF16),
            pltpu.VMEM((nd - 1, nz, part, w), BF16),
            pltpu.VMEM((nz, part, w), BF16),
            pltpu.VMEM((nz - 1, part, w), BF16),
        ] + [pltpu.SemaphoreType.DMA(())] * 8

    def push(self, stage, source, target, device):
        pltpu.make_async_remote_copy(
            src_ref=source,
            dst_ref=target,
            send_sem=self.send[stage],
            recv_sem=self.recv[stage],
            device_id=device,
            device_id_type=MESH,
        ).start()

    def rows_of(self, f, d=0):
        return pl.multiple_of(self.unit.base(f) + d * self.unit.part, 16)

    def start_core(self):
        def go(z, carry):
            for d in range(self.nd):
                self.push(
                    0,
                    self.source.at[pl.ds(self.rows_of(2 * z + 1 - self.core, d), self.unit.part)],
                    self.got_core.at[z, d],
                    (self.dp, 2 * self.deep + 1 - self.core),
                )
            return carry

        lax.fori_loop(0, self.nz, go, 0)

    def wait(self, sem, ref):
        pltpu.make_async_copy(ref, ref, sem).wait()

    def start_dp(self):
        self.wait(self.recv[0], self.got_core)

        def add(z, carry):
            for d in range(self.nd):
                own = self.source[pl.ds(self.rows_of(2 * z + self.core, d), self.unit.part), :]
                self.got_core[z, d] = (own.astype(F32) + self.got_core[z, d].astype(F32)).astype(BF16)
            return carry

        lax.fori_loop(0, self.nz, add, 0)

        def go(z, carry):
            for i in range(1, self.nd):
                other = lax.rem(self.dp + i, self.nd)
                self.push(1, self.got_core.at[z, other], self.got_dp.at[i - 1, z], (other, self.fs))
            return carry

        lax.fori_loop(0, self.nz, go, 0)

    def start_rest(self):
        self.wait(self.recv[1], self.got_dp)
        self.wait(self.send[1], self.got_dp)

        def add(z, carry):
            total = self.got_core[z, self.dp].astype(F32)
            for i in range(self.nd - 1):
                total = total + self.got_dp[i, z].astype(F32)
            self.sum_dp[z] = total.astype(BF16)
            return carry

        lax.fori_loop(0, self.nz, add, 0)
        for i in range(1, self.nz):
            other = lax.rem(self.deep + i, self.nz)
            self.push(2, self.sum_dp.at[other], self.got_rest.at[i - 1], (self.dp, 2 * other + self.core))

    def start_copies(self):
        self.wait(self.recv[2], self.got_rest)
        total = self.sum_dp[self.deep].astype(F32)
        for i in range(self.nz - 1):
            total = total + self.got_rest[i].astype(F32)
        rows = pl.ds(pl.multiple_of(self.dp * self.unit.part, 16), self.unit.part)
        self.result[rows, :] = total.astype(BF16)
        for i in range(1, self.nd):
            other = lax.rem(self.dp + i, self.nd)
            self.push(3, self.result.at[rows], self.result.at[rows], (other, self.fs))

    def complete(self):
        others = self.result.at[pl.ds(0, (self.nd - 1) * self.unit.part)]
        self.wait(self.recv[3], others)
        self.wait(self.send[0], self.got_core)
        self.wait(self.send[2], self.got_rest)
        self.wait(self.send[3], others)


def taps():
    found = []
    for y in range(SIDE):
        for x in range(SIDE):
            for a in range(3):
                for b in range(3):
                    iy, ix = y + a - 1, x + b - 1
                    if 0 <= iy < SIDE and 0 <= ix < SIDE:
                        found.append((y * SIDE + x, 3 * a + b, iy * SIDE + ix))
    return found


TAPS = taps()


def half_tanh(half):
    return jnp.tanh(half)


def silu(z):
    half = 0.5 * z
    return half * half_tanh(half) + half


def sigmoid(z):
    return 0.5 * half_tanh(0.5 * z) + 0.5


def silu_slope(z):
    half = 0.5 * z
    t = half_tanh(half)
    return 0.5 * (1.0 + t + half * (1.0 - t * t))


def lanes(j):
    return pl.ds(pl.multiple_of(j * LANE, LANE), LANE)


def images_at(b):
    return pl.ds(pl.multiple_of(b * 8, 8), 8)


def over_tiles(plan, first_chunk, chunks, per_chunk, body, n_sums, store_sums, unroll=1):
    blocks = plan.images // 8

    def chunk_step(jj, carry):
        j = first_chunk + jj
        hoisted = per_chunk(j)

        def step(b, sums):
            for u in range(unroll):
                sums = body(j, b * unroll + u, hoisted, sums)
            return sums

        zero = tuple(jnp.zeros((8, LANE), F32) for _ in range(n_sums))
        store_sums(j, lax.fori_loop(0, blocks // unroll, step, zero))
        return carry

    lax.fori_loop(0, chunks, chunk_step, 0)


class Gather:
    def __init__(self, plan, target, stride, rows, sems, whole=False):
        self.plan, self.target, self.stride, self.whole = plan, target, stride, whole
        self.rows = rows
        self.part = rows if whole else rows // plan.nd
        self.send, self.recv = sems[0:3], sems[3:6]
        self.dp, self.fs = lax.axis_index("dp"), lax.axis_index("fsdp")
        self.core, self.deep = lax.rem(self.fs, 2), self.fs // 2

    def at(self, deep, part=None):
        start = (2 * deep + self.core) * self.stride
        if part is None:
            return self.target.at[pl.ds(pl.multiple_of(start, 16), self.rows)]
        return self.target.at[pl.ds(pl.multiple_of(start + part * self.part, 16), self.part)]

    def push(self, stage, ref, device):
        pltpu.make_async_remote_copy(
            src_ref=ref,
            dst_ref=ref,
            send_sem=self.send[stage],
            recv_sem=self.recv[stage],
            device_id=device,
            device_id_type=MESH,
        ).start()

    def start_rest(self):
        part = None if self.whole else self.dp

        def go(i, carry):
            other = lax.rem(self.deep + i, self.plan.depth)
            self.push(0, self.at(self.deep, part), (self.dp, 2 * other + self.core))
            return carry

        lax.fori_loop(1, self.plan.depth, go, 0)

    def span(self, rows):
        return self.target.at[pl.ds(0, rows)]

    def wait(self, sem, rows):
        pltpu.make_async_copy(self.span(rows), self.span(rows), sem).wait()

    def start_dp(self):
        plan = self.plan
        self.wait(self.recv[0], (plan.depth - 1) * self.part)

        def go(i, carry):
            other = lax.rem(self.deep + i, plan.depth)
            for k in range(1, plan.nd):
                self.push(1, self.at(other, self.dp), (lax.rem(self.dp + k, plan.nd), self.fs))
            return carry

        lax.fori_loop(1, plan.depth, go, 0)

    def start_core(self):
        plan = self.plan
        if self.whole:
            self.wait(self.recv[0], (plan.depth - 1) * self.part)
        else:
            self.wait(self.recv[1], (plan.depth - 1) * (plan.nd - 1) * self.part)

        def go(z, carry):
            self.push(2, self.at(z), (self.dp, 2 * self.deep + 1 - self.core))
            return carry

        lax.fori_loop(0, plan.depth, go, 0)

    def complete(self):
        plan = self.plan
        self.wait(self.recv[2], plan.depth * self.rows)
        self.wait(self.send[0], (plan.depth - 1) * self.part)
        if not self.whole:
            self.wait(self.send[1], (plan.depth - 1) * (plan.nd - 1) * self.part)
        self.wait(self.send[2], plan.depth * self.rows)


def spread_shards(plan, block, flat, mine):
    start = lax.axis_index("fsdp") * plan.shard
    offset = start - start // (16 * LANE) * (16 * LANE)
    down, turn = offset // LANE, lax.rem(offset, LANE)
    full = plan.shard // LANE
    rest = plan.shard - full * LANE
    size = plan.chunk + 32
    lane = lax.broadcasted_iota(jnp.int32, (16, LANE), 1)
    for layer in range(LAYERS):
        flat[layer * size : layer * size + 24, :] = jnp.zeros((24, LANE), F32)

    def take(i, count):
        piece = block[:, pl.ds(pl.multiple_of(i * 8 * LANE, LANE), count * LANE)]
        for layer in range(LAYERS):
            rows = [piece[layer : layer + 1, k * LANE : (k + 1) * LANE] for k in range(count)]
            at = pl.ds(pl.multiple_of(layer * size + 24 + i * 8, 8), count)
            flat[at, :] = jnp.concatenate(rows, axis=0) if count > 1 else rows[0]

    def step(i, carry):
        take(i, 8)
        return carry

    lax.fori_loop(0, full // 8, step, 0)
    if full % 8:
        take(full // 8, full % 8)
    for layer in range(LAYERS):
        at = layer * size + 24 + full
        if rest:
            last = block[layer : layer + 1, full * LANE : full * LANE + rest]
            flat[at : at + 1, :] = jnp.concatenate([last, jnp.zeros((1, LANE - rest), F32)], axis=1)
            at += 1
        end = (layer + 1) * size
        flat[at:end, :] = jnp.zeros((end - at, LANE), F32)

    def shift(layer):
        def go(i, carry):
            begin = layer * size + 24 + i * 16 - down
            here = pltpu.roll(flat[pl.ds(begin, 16), :], turn, 1)
            before = pltpu.roll(flat[pl.ds(begin - 1, 16), :], turn, 1)
            value = jnp.where(lane >= turn, here, before)
            mine[layer][pl.ds(pl.multiple_of(i * 16, 16), 16), :] = value.astype(BF16)
            return carry

        lax.fori_loop(0, plan.chunk // 16, go, 0)

    return shift


def unpack_weights(plan, got, we, wp, wr, wx, small, tail, flat):
    lane = lax.broadcasted_iota(jnp.int32, (1, LANE), 1)
    low = lane < SQ
    for f in range(plan.nf):
        base, at = plan.base[f], f * plan.chunk
        head = got[at : at + 16, :].astype(F32)
        if f:
            head = head + flat[base : base + 16, :]
        flat[base : base + 16, :] = head
        flat[base + 16 : base + plan.chunk, :] = got[at + 16 : at + plan.chunk, :].astype(F32)
    for j in range(NJ):
        cols = slice(j * LANE, (j + 1) * LANE)
        we[:, cols] = flat[pl.ds(j, C, stride=NJ), :].astype(BF16)
        wx[0:SQ, cols] = flat[pl.ds(ROW_X + j, SQ, stride=NJ), :].astype(BF16)
        wx[SQ:LANE, cols] = jnp.zeros((LANE - SQ, LANE), BF16)
        small[0:14, cols] = flat[pl.ds(ROW_D + j, 14, stride=NJ), :]
        small[14:16, cols] = jnp.zeros((2, LANE), F32)
    for h in range(C // LANE):
        wp[:, h * LANE : (h + 1) * LANE] = flat[pl.ds(ROW_P + h, E, stride=2), :].astype(BF16)
    pairs = flat[ROW_R:ROW_X, :]
    evens, odds = jnp.where(low, pairs, 0.0), jnp.where(low, pltpu.roll(pairs, SQ, 1), 0.0)
    flat[pl.ds(0, E // 2, stride=2), :] = evens
    flat[pl.ds(1, E // 2, stride=2), :] = odds
    wr[...] = flat[0:E, :].astype(BF16)
    rows = [flat[ROW_S + i : ROW_S + i + 1, :] for i in range(5)]
    turned = [pltpu.roll(jnp.broadcast_to(r, (8, LANE)), SQ, 1)[0:1, :] for r in rows]
    tail[...] = jnp.zeros((8, C), F32)
    tail[0:1, 0:LANE] = jnp.where(low, rows[0], 0.0)
    for i, at in ((1, 0), (2, 2)):
        tail[i : i + 1, 0:LANE] = jnp.where(low, turned[at], turned[at + 1])
        tail[i : i + 1, LANE:C] = jnp.where(low, turned[at + 1], turned[at + 2])


def mix_images(plan, images, partner, share_one, stream, first, last):
    n, rows = plan.images, plan.rows
    place = lax.broadcasted_iota(jnp.int32, (n, rows), 1)
    own = lax.broadcasted_iota(jnp.int32, (n, rows), 0) * PIX
    chosen = partner * PIX

    def go(p, carry):
        mine = dot(jnp.where(place == own + p, 1.0, 0.0).astype(BF16), images[...])
        theirs = dot(jnp.where(place == chosen + p, 1.0, 0.0).astype(BF16), images[...])
        at = pl.ds(pl.multiple_of(p * n, n), n)
        stream[at, :] = share_one * mine + (1.0 - share_one) * theirs
        return carry

    lax.fori_loop(first, last, go, 0)


def forward_layer(plan, r, layer, hooks):
    x, expanded, depth, act, sums, x_low = r.stream, r.expanded, r.depth, r.flow, r.sums, r.x_low
    normed_three, stat_e, stat_c = r.normed_three.at[layer], r.stat_e.at[layer], r.stat_c.at[layer]
    pooled, presq, gate, turned = r.pooled.at[layer], r.presq.at[layer], r.gate.at[layer], r.turned.at[layer]
    we, wp, wr, wx = r.we.at[layer], r.wp.at[layer], r.wr.at[layer], r.wx.at[layer]
    small, tail = r.small.at[layer], r.tail.at[layer]
    ex_one, ex_two, ex_three = r.ex_wide[0:GROUPS], r.ex_wide[GROUPS : 2 * GROUPS], r.ex_thin
    n = plan.images
    x_low[...] = x[...].astype(BF16)
    for g in range(GROUPS):
        cols = slice(g * GW, (g + 1) * GW)

        def expand(m, carry, cols=cols):
            rows = pl.ds(pl.multiple_of(m * MBLK * n, MBLK * n), MBLK * n)
            value = dot(x_low[rows, :], we[:, cols])
            expanded[pl.ds(m * MBLK, MBLK), :, cols] = value.reshape(MBLK, n, GW)
            return (
                carry[0] + jnp.sum(value.reshape(-1, 8, GW), axis=0),
                carry[1] + jnp.sum((value * value).reshape(-1, 8, GW), axis=0),
            )

        zero = jnp.zeros((8, GW), F32)
        s, q = lax.fori_loop(0, PIX // MBLK, expand, (zero, zero))
        ex_one[g].share(row_sum(s), row_sum(q))

    def put_sums(j, totals):
        for i, t in enumerate(totals):
            sums[i : i + 1, lanes(j)] = row_sum(t)

    for g in range(GROUPS):
        cols = slice(g * GW, (g + 1) * GW)
        mean, rstd = moments(plan, ex_one[g].collect())
        if g == 0:
            r.spill_e.start(layer)
            if layer:
                r.spill_d.wait()
            hooks[0]()
        stat_e[0:1, cols] = mean
        stat_e[1:2, cols] = rstd
        scale = rstd * small[9:10, cols]
        stat_e[4:5, cols] = 0.5 * scale
        stat_e[5:6, cols] = 0.5 * (small[10:11, cols] - mean * scale)

        def chunk(j):
            return (
                stat_e[4:5, lanes(j)],
                stat_e[5:6, lanes(j)],
                [small[t : t + 1, lanes(j)] for t in range(9)],
            )

        def spread(j, b, hoisted, totals):
            scale, shift, w = hoisted
            act_one = []
            for p in range(PIX):
                half = expanded[p, images_at(b), lanes(j)] * scale + shift
                act_one.append(half * half_tanh(half) + half)
            made = [None] * PIX
            for o, t, i in TAPS:
                term = act_one[i] * w[t]
                made[o] = term if made[o] is None else made[o] + term
            s, q = totals
            for p in range(PIX):
                depth[p, images_at(b), lanes(j)] = made[p]
                s = s + made[p]
                q = q + made[p] * made[p]
            return s, q

        over_tiles(plan, g * (GW // LANE), GW // LANE, chunk, spread, 2, put_sums, UN_SPREAD)
        ex_two[g].share(sums[0:1, cols], sums[1:2, cols])

    for g in range(GROUPS):
        cols = slice(g * GW, (g + 1) * GW)
        mean, rstd = moments(plan, ex_two[g].collect())
        if g == 0:
            if layer < LAYERS - 1:
                r.spill_d.start(layer)
            hooks[1]()
        stat_e[2:3, cols] = mean
        stat_e[3:4, cols] = rstd
        scale = rstd * small[11:12, cols]
        stat_e[6:7, cols] = 0.5 * scale
        stat_e[7:8, cols] = 0.5 * (small[12:13, cols] - mean * scale)

        def chunk_two(j):
            return stat_e[6:7, lanes(j)], stat_e[7:8, lanes(j)]

        def activate(j, b, hoisted, totals):
            scale, shift = hoisted
            total = None
            for p in range(PIX):
                half = depth[p, images_at(b), lanes(j)] * scale + shift
                made = half * half_tanh(half) + half
                act[p, images_at(b), lanes(j)] = made
                total = made if total is None else total + made
            pooled[images_at(b), lanes(j)] = total * (1.0 / PIX)
            return totals

        over_tiles(
            plan, g * (GW // LANE), GW // LANE, chunk_two, activate, 0, lambda j, s: None, UN_ACT
        )
    reduced = dot_rows(pooled[...], wr[...]) + tail[0:1, 0:LANE]
    presq[...] = reduced
    gate[...] = sigmoid(dot_rows(silu(reduced), wx[...]) + small[13:14, :])

    hooks[2]()
    r.spill_e.wait()

    def project(m, carry):
        gated = (act[pl.ds(m * MBLK, MBLK), :, :] * gate[...][None]).astype(BF16)
        value = dot(gated.reshape(MBLK * n, E), wp[...])
        expanded[pl.ds(m * MBLK, MBLK), :, 0:C] = value.reshape(MBLK, n, C)
        return (
            carry[0] + jnp.sum(value.reshape(-1, 8, C), axis=0),
            carry[1] + jnp.sum((value * value).reshape(-1, 8, C), axis=0),
        )

    zero = jnp.zeros((8, C), F32)
    s, q = lax.fori_loop(0, PIX // MBLK, project, (zero, zero))
    ex_three.share(row_sum(s), row_sum(q))
    turned[...] = x[...].T.astype(BF16)
    mean, rstd = moments(plan, ex_three.collect())
    stat_c[...] = jnp.zeros((8, C), F32)
    stat_c[0:1, :] = mean
    stat_c[1:2, :] = rstd
    normed = (expanded[:, :, 0:C].reshape(n * PIX, C) - mean) * rstd
    normed_three[...] = normed.astype(BF16)
    x[...] = x[...] + normed * tail[1:2, :] + tail[2:3, :]


def head_layers(plan, r, label, label_row, partner, weight):
    x, x_low, turned, bias, totals_out = r.stream, r.x_low, r.turned.at[LAYERS], r.bias, r.totals
    w_head = grad_head = r.w_head
    hidden, slope, low_grad, pool, stat = r.expanded, r.flow, r.gated, r.squeeze_grad, r.coef
    sums, gain, grad_x = r.sums, r.sums.at[pl.ds(8, 8)], r.stream
    hd, n = plan.hd, plan.images
    halves = plan.head_groups
    ng = len(halves)
    ex_stat, ex_grad, ex_bias = r.ex_wide[0:ng], r.ex_wide[GROUPS : GROUPS + ng], r.ex_bias
    x_low[...] = x[...].astype(BF16)
    gain[:, 0:hd] = w_head[0:hd, C : C + LANE].astype(F32).T[0:8, :]
    for g, (start, width) in enumerate(halves):
        cols = slice(start, start + width)

        def convolve(m, carry, cols=cols, width=width):
            rows = pl.ds(pl.multiple_of(m * MBLK * n, MBLK * n), MBLK * n)
            value = dot(x_low[rows, :], w_head[cols, 0:C], ((1,), (1,)))
            hidden[pl.ds(m * MBLK, MBLK), :, cols] = value.reshape(MBLK, n, width)
            return (
                carry[0] + jnp.sum(value.reshape(-1, 8, width), axis=0),
                carry[1] + jnp.sum((value * value).reshape(-1, 8, width), axis=0),
            )

        zero = jnp.zeros((8, width), F32)
        s, q = lax.fori_loop(0, PIX // MBLK, convolve, (zero, zero))
        ex_stat[g].share(row_sum(s), row_sum(q))
    turned[...] = x[...].T.astype(BF16)
    for g, (start, width) in enumerate(halves):
        cols = slice(start, start + width)
        mean, rstd = moments(plan, ex_stat[g].collect())
        scale = rstd * gain[0:1, cols]
        stat[0:1, cols] = rstd
        stat[1:2, cols] = -mean * rstd
        stat[2:3, cols] = 0.5 * scale
        stat[3:4, cols] = 0.5 * (gain[1:2, cols] - mean * scale)

        def chunk(j):
            return stat[2:3, lanes(j)], stat[3:4, lanes(j)]

        def activate(j, b, hoisted, totals):
            scale, shift = hoisted
            total = None
            for p in range(PIX):
                half = hidden[p, images_at(b), lanes(j)] * scale + shift
                t = half_tanh(half)
                made = half * t + half
                slope[p, images_at(b), lanes(j)] = (1.0 + t) + half * (1.0 - t * t)
                total = made if total is None else total + made
            pool[images_at(b), lanes(j)] = total * (1.0 / PIX)
            return totals

        over_tiles(plan, start // LANE, width // LANE, chunk, activate, 0, lambda j, s: None, UN_ACT)
    pool_low = pool[:, 0:hd].astype(BF16)
    classes = lax.broadcasted_iota(jnp.int32, (n, KP), 1)
    valid = classes < K
    logits = dot(pool_low, w_head[0:hd, C + LANE :]) + bias[...]
    logits = jnp.where(valid, logits, -1e30)
    top = jnp.max(logits, axis=1, keepdims=True)
    lifted = logits - top
    powers = jnp.where(valid, jnp.exp(lifted), 0.0)
    norm = jnp.sum(powers, axis=1, keepdims=True)
    log_probs = lifted - jnp.log(norm)
    picked = lax.broadcasted_iota(jnp.int32, (n, n), 1) == partner
    label_two = jnp.sum(jnp.where(picked, label_row[...], 0), axis=1, keepdims=True)
    w = weight
    targets = w * jnp.where(classes == label, 1.0 - SMOOTHING, 0.0) + (1.0 - w) * jnp.where(
        classes == label_two, 1.0 - SMOOTHING, 0.0
    )
    targets = jnp.where(valid, targets + SMOOTHING / K, 0.0)
    loss = -jnp.sum(jnp.where(valid, targets * log_probs, 0.0))
    grad_logits = (powers / norm - targets) * (float(PIX) / plan.count)
    packed_bias = jnp.where(classes[0:1, :] == KP - 1, loss, row_sum(grad_logits))
    ex_bias.share(packed_bias[:, 0 : KP // 2], packed_bias[:, KP // 2 :])
    grad_low = grad_logits.astype(BF16)
    pool_grad = dot(grad_low, w_head[0:hd, C + LANE :], ((1,), (1,)))
    pool[:, 0:hd] = pool_grad * (0.5 / PIX)

    def put_sums(j, totals):
        flow_sum, value_sum = [row_sum(t) for t in totals]
        sums[0:1, lanes(j)] = flow_sum
        sums[1:2, lanes(j)] = value_sum * stat[0:1, lanes(j)] + flow_sum * stat[1:2, lanes(j)]

    for g, (start, width) in enumerate(halves):
        cols = slice(start, start + width)

        def back(j, b, hoisted, totals):
            s, q = totals
            flow = pool[images_at(b), lanes(j)]
            for p in range(PIX):
                made = slope[p, images_at(b), lanes(j)] * flow
                slope[p, images_at(b), lanes(j)] = made
                s = s + made
                q = q + made * hidden[p, images_at(b), lanes(j)]
            return s, q

        over_tiles(plan, start // LANE, width // LANE, lambda j: None, back, 2, put_sums, UN_HBACK)
        ex_grad[g].share(sums[0:1, cols], sums[1:2, cols])
    grad_head[0:hd, C + LANE :] = dot(pool_low.T, grad_low).astype(BF16)
    norm_grads = jnp.concatenate(
        [sums[1:2, 0:hd], sums[0:1, 0:hd], jnp.zeros((LANE - 2, hd), F32)], axis=0
    )
    grad_head[0:hd, C : C + LANE] = norm_grads.T.astype(BF16)
    for g, (start, width) in enumerate(halves):
        cols = slice(start, start + width)
        shift_total, gain_total = ex_grad[g].collect()
        scale = stat[0:1, cols] * gain[0:1, cols]
        mean_one = shift_total / plan.count
        mean_two = gain_total / plan.count
        stat[4:5, cols] = scale
        stat[5:6, cols] = -scale * stat[0:1, cols] * mean_two
        stat[6:7, cols] = -scale * (mean_one + stat[1:2, cols] * mean_two)
    def into(m, carry):
        rows = pl.ds(pl.multiple_of(m * MBLK * n, MBLK * n), MBLK * n)
        spot = pl.ds(m * MBLK, MBLK)
        value = (
            slope[spot, :, 0:hd] * stat[4:5, 0:hd]
            + hidden[spot, :, 0:hd] * stat[5:6, 0:hd]
            + stat[6:7, 0:hd]
        )
        low = value.reshape(MBLK * n, hd).astype(BF16)
        low_grad[rows, 0:hd] = low
        grad_x[rows, :] = dot(low, w_head[0:hd, 0:C])
        return carry

    lax.fori_loop(0, PIX // MBLK, into, 0)
    r.spill_e.fetch(LAYERS - 1)
    for at in range(0, hd, LANE):
        part = dot(turned[...], low_grad[:, at : at + LANE])
        grad_head[at : at + LANE, 0:C] = part.T.astype(BF16)
    totals_out[...] = jnp.concatenate(ex_bias.collect(), axis=1)


def backward_layer(plan, r, layer, work):
    expanded, depth, flow, gated, sums, coef = r.expanded, r.depth, r.flow, r.gated, r.sums, r.coef
    normed_three, stat_e, stat_c = r.normed_three.at[layer], r.stat_e.at[layer], r.stat_c.at[layer]
    pooled, presq, gate, turned = r.pooled.at[layer], r.presq.at[layer], r.gate.at[layer], r.turned.at[layer]
    we, wp, wr, wx = r.we.at[layer], r.wp.at[layer], r.wr.at[layer], r.wx.at[layer]
    small, tail = r.small.at[layer], r.tail.at[layer]
    grad = grad_x = r.stream
    low_proj, squeeze_grad, flat, packed = r.x_low, r.squeeze_grad, r.flat, r.stage
    ex_one, ex_two, ex_three = r.ex_wide[0:GROUPS], r.ex_wide[GROUPS : 2 * GROUPS], r.ex_thin
    n = plan.images
    lane = lax.broadcasted_iota(jnp.int32, (1, LANE), 1)
    is_low = lane < SQ
    rstd_c = stat_c[1:2, :]
    s = row_sum(jnp.sum(grad[...].reshape(-1, 8, C), axis=0))
    q = row_sum(
        jnp.sum((grad[...] * normed_three[...].astype(F32)).reshape(-1, 8, C), axis=0)
    )
    ex_three.share(s, q)
    work.start_core()
    bias_three, gain_three = s, q

    if layer < LAYERS - 1:
        r.spill_d.wait()

    def chunk_two(j):
        return stat_e[6:7, lanes(j)], stat_e[7:8, lanes(j)]

    def regate(p, carry):
        rows = pl.ds(pl.multiple_of(p * n, n), n)
        for j in range(NJ):
            cols = slice(j * LANE, (j + 1) * LANE)
            half = depth[p, :, cols] * stat_e[6:7, cols] + stat_e[7:8, cols]
            value = (half * half_tanh(half) + half) * gate[:, cols]
            gated[rows, cols] = value.astype(BF16)
        return carry

    lax.fori_loop(0, PIX, regate, 0)

    bias_total, gain_total = ex_three.collect()
    scale = rstd_c * tail[1:2, :]
    mean_one, mean_two = bias_total / plan.count, gain_total / plan.count
    low_proj[...] = (
        scale
        * (grad[...] - mean_one - normed_three[...].astype(F32) * mean_two)
    ).astype(BF16)

    def into_gated(m, carry):
        rows = pl.ds(pl.multiple_of(m * MBLK * n, MBLK * n), MBLK * n)
        value = dot(low_proj[rows, :], wp[...], ((1,), (1,)))
        flow[pl.ds(m * MBLK, MBLK), :, :] = value.reshape(MBLK, n, E)
        return carry

    lax.fori_loop(0, PIX // MBLK, into_gated, 0)
    work.start_dp()

    def gate_back(t, carry):
        j, b = t // (n // 16), lax.rem(t, n // 16)
        block = pl.ds(pl.multiple_of(b * 16, 16), 16)
        total = None
        for p in range(PIX):
            low = gated[pl.ds(pl.multiple_of(p * n + b * 16, 16), 16), lanes(j)].astype(F32)
            term = flow[p, block, lanes(j)] * low
            total = term if total is None else total + term
        squeeze_grad[block, lanes(j)] = total * (1.0 - gate[block, lanes(j)])
        return carry

    lax.fori_loop(0, NJ * (n // 16), gate_back, 0)
    excite_grad = squeeze_grad[...]
    sums[13:14, :] = row_sum(excite_grad)
    squeezed = silu(presq[...])
    presq_grad = dot_rows(excite_grad, wx[...], ((1,), (1,))) * silu_slope(presq[...])
    grad_wx = dot_outer(squeezed, excite_grad)
    flat[ROW_R : ROW_R + E, :] = dot_outer(pooled[...], presq_grad)
    evens = flat[pl.ds(ROW_R, E // 2, stride=2), :]
    odds = flat[pl.ds(ROW_R + 1, E // 2, stride=2), :]
    flat[ROW_R:ROW_X, :] = jnp.where(is_low, evens, pltpu.roll(odds, SQ, 1))
    for j in range(NJ):
        flat[pl.ds(ROW_X + j, SQ, stride=NJ), :] = grad_wx[0:SQ, j * LANE : (j + 1) * LANE]
    grad_reduce_b = row_sum(presq_grad)
    squeeze_grad[...] = dot_rows(presq_grad, wr[...], ((1,), (1,))) * (1.0 / PIX)

    def put_sums(first_row, stat_row):
        def put(j, totals):
            rows = [row_sum(t) for t in totals]
            mean = stat_e[stat_row : stat_row + 1, lanes(j)]
            rstd = stat_e[stat_row + 1 : stat_row + 2, lanes(j)]
            rows[-2] = (rows[-2] - mean * rows[-1]) * rstd
            for i, t in enumerate(rows):
                sums[first_row + i : first_row + i + 1, lanes(j)] = t

        return put

    def back_two(j, b, hoisted, totals):
        scale, shift = hoisted
        gain_sum, bias_sum = totals
        opened = gate[images_at(b), lanes(j)] * 0.5
        pool_flow = squeeze_grad[images_at(b), lanes(j)] * 0.5
        for p in range(PIX):
            value = depth[p, images_at(b), lanes(j)]
            half = value * scale + shift
            t = half_tanh(half)
            made = (flow[p, images_at(b), lanes(j)] * opened + pool_flow) * (
                (1.0 + t) + half * (1.0 - t * t)
            )
            flow[p, images_at(b), lanes(j)] = made
            bias_sum = bias_sum + made
            gain_sum = gain_sum + made * value
        return gain_sum, bias_sum

    for g in range(GROUPS):
        cols = slice(g * GW, (g + 1) * GW)
        over_tiles(plan, g * (GW // LANE), GW // LANE, chunk_two, back_two, 2, put_sums(11, 2), UN_TWO)
        ex_two[g].share(sums[12:13, cols], sums[11:12, cols])

    work.start_rest()
    proj_turned = low_proj[...].astype(F32).T.astype(BF16)
    for j in range(NJ):
        part = dot(proj_turned, gated[:, j * LANE : (j + 1) * LANE])
        for h in range(C // LANE):
            flat[pl.ds(ROW_P + 2 * j * LANE + h, LANE, stride=2), :] = part[
                h * LANE : (h + 1) * LANE, :
            ].T

    def norm_coefs(g, pair, row, stat_row, gain_row):
        cols = slice(g * GW, (g + 1) * GW)
        mean, rstd = stat_e[stat_row : stat_row + 1, cols], stat_e[stat_row + 1 : stat_row + 2, cols]
        scale = rstd * small[gain_row : gain_row + 1, cols]
        mean_one, mean_two = pair[0] / plan.count, pair[1] / plan.count
        coef[row : row + 1, cols] = scale
        coef[row + 1 : row + 2, cols] = -scale * rstd * mean_two
        coef[row + 2 : row + 3, cols] = -scale * (mean_one - mean * rstd * mean_two)

    def chunk_one(j):
        return (
            [coef[i : i + 1, lanes(j)] for i in range(3)],
            [small[t : t + 1, lanes(j)] for t in range(9)],
            [stat_e[i : i + 1, lanes(j)] for i in (4, 5)],
        )

    def back_one(j, b, hoisted, totals):
        (c_flow, c_value, c_const), w, (scale, shift) = hoisted
        w_sums, gain_sum, bias_sum = list(totals[:9]), totals[9], totals[10]
        spread_grad = []
        for p in range(PIX):
            spread_grad.append(
                flow[p, images_at(b), lanes(j)] * c_flow
                + (depth[p, images_at(b), lanes(j)] * c_value + c_const)
            )
        act_one, slopes = [], []
        for p in range(PIX):
            half = expanded[p, images_at(b), lanes(j)] * scale + shift
            t = half_tanh(half)
            act_one.append(half * t + half)
            slopes.append(0.5 * ((1.0 + t) + half * (1.0 - t * t)))
        made = [None] * PIX
        for o, t, i in TAPS:
            w_sums[t] = w_sums[t] + spread_grad[o] * act_one[i]
            term = spread_grad[o] * w[t]
            made[i] = term if made[i] is None else made[i] + term
        for p in range(PIX):
            value = expanded[p, images_at(b), lanes(j)]
            result = made[p] * slopes[p]
            flow[p, images_at(b), lanes(j)] = result
            bias_sum = bias_sum + result
            gain_sum = gain_sum + result * value
        return tuple(w_sums) + (gain_sum, bias_sum)

    for g in range(GROUPS):
        cols = slice(g * GW, (g + 1) * GW)
        norm_coefs(g, ex_two[g].collect(), 0, 2, 11)
        if g == 0:
            r.spill_e.wait()
        over_tiles(plan, g * (GW // LANE), GW // LANE, chunk_one, back_one, 11, put_sums(0, 0), UN_ONE)
        ex_one[g].share(sums[10:11, cols], sums[9:10, cols])

    if layer:
        r.spill_d.fetch(layer - 1)
    work.start_copies()
    for j in range(NJ):
        flat[pl.ds(ROW_D + j, 14, stride=NJ), :] = sums[0:14, j * LANE : (j + 1) * LANE]

    def turn(row):
        return pltpu.roll(jnp.broadcast_to(row, (8, LANE)), SQ, 1)[0:1, :]

    pieces = [turn(v[:, h * LANE : (h + 1) * LANE]) for v in (gain_three, bias_three) for h in (0, 1)]
    flat[ROW_S : ROW_S + 1, :] = jnp.where(is_low, grad_reduce_b, pieces[0])
    for i in range(3):
        flat[ROW_S + 1 + i : ROW_S + 2 + i, :] = jnp.where(is_low, pieces[i], pieces[i + 1])
    flat[ROW_S + 4 : ROW_S + 5, :] = pieces[3]

    for g in range(GROUPS):
        cols = slice(g * GW, (g + 1) * GW)
        norm_coefs(g, ex_one[g].collect(), 0, 0, 9)

        def into(m, carry, cols=cols):
            rows = pl.ds(pl.multiple_of(m * MBLK * n, MBLK * n), MBLK * n)
            spot = pl.ds(m * MBLK, MBLK)
            value = (
                flow[spot, :, cols] * coef[0:1, cols]
                + expanded[spot, :, cols] * coef[1:2, cols]
                + coef[2:3, cols]
            )
            low = value.reshape(MBLK * n, GW).astype(BF16)
            gated[rows, cols] = low
            grad_x[rows, :] += dot(low, we[:, cols], ((1,), (1,)))
            return carry

        lax.fori_loop(0, PIX // MBLK, into, 0)
        for j in range(g * (GW // LANE), (g + 1) * (GW // LANE)):
            flat[pl.ds(j, C, stride=NJ), :] = dot(
                turned[...], gated[:, j * LANE : (j + 1) * LANE]
            )
    if layer:
        r.spill_e.fetch(layer - 1)
    work.complete()
    packed[0 : plan.flat, :] = flat[0 : plan.flat, :].astype(BF16)


class Spill:
    def __init__(self, held, kept, sem):
        self.held, self.kept, self.sem = held, kept, sem

    def start(self, layer):
        self.copy = pltpu.make_async_copy(self.held, self.kept.at[layer], self.sem)
        self.copy.start()

    def fetch(self, layer):
        self.copy = pltpu.make_async_copy(self.kept.at[layer], self.held, self.sem)
        self.copy.start()

    def wait(self):
        self.copy.wait()


INPUTS = ("block", "w_own", "images", "per_image", "bias")
OUTPUTS = ("block_sums", "head_sums", "totals", "kept_e", "kept_d")


def scratch_of(plan):
    n, rows, hd = plan.images, plan.rows, plan.hd
    wide = (plan.devices, 2 * GW // LANE, LANE)
    vm = lambda shape, dtype=F32: pltpu.VMEM(shape, dtype)
    held = {
        "expanded": vm((PIX, n, E)),
        "depth": vm((PIX, n, E)),
        "flow": vm((PIX, n, E)),
        "gated": vm((rows, E), BF16),
        "stream": vm((rows, C)),
        "x_low": vm((rows, C), BF16),
        "turned": vm((LAYERS + 1, C, rows), BF16),
        "normed_three": vm((LAYERS, rows, C), BF16),
        "stat_e": vm((LAYERS, 8, E)),
        "stat_c": vm((LAYERS, 8, C)),
        "pooled": vm((LAYERS, n, E)),
        "presq": vm((LAYERS, n, LANE)),
        "gate": vm((LAYERS, n, E)),
        "we": vm((LAYERS, C, E), BF16),
        "wp": vm((LAYERS, E, C), BF16),
        "wr": vm((LAYERS, E, LANE), BF16),
        "wx": vm((LAYERS, LANE, E), BF16),
        "small": vm((LAYERS, 16, E)),
        "tail": vm((LAYERS, 8, C)),
        "w_head": vm((plan.head_flat, HEAD_W), BF16),
        "squeeze_grad": vm((n, E)),
        "sums": vm((16, E)),
        "coef": vm((8, E)),
        "flat": vm((max(plan.flat, LAYERS * (plan.chunk + 32)), LANE)),
        "stage": vm((max(plan.nf * plan.chunk, plan.flat), LANE), BF16),
        "spill_sems": pltpu.SemaphoreType.DMA((2,)),
    }
    for i in range(2 * GROUPS):
        held[f"wide{i}"] = vm(wide)
    held["thin"] = vm((plan.devices, 2 * C // LANE, LANE))
    held["thick"] = vm((plan.devices, KP // LANE, LANE))
    for name in [f"wide{i}" for i in range(2 * GROUPS)] + ["thin", "thick"]:
        held[name + "_send"] = pltpu.SemaphoreType.DMA(())
        held[name + "_recv"] = pltpu.SemaphoreType.DMA(())
    for name in ("block", "head"):
        for i in range(6):
            held[f"gather_{name}{i}"] = pltpu.SemaphoreType.DMA(())
    for name, unit in (("block", plan.layer_unit()), ("head", plan.head_unit())):
        for i, shape in enumerate(Reduction.scratch(unit)):
            held[f"reduce_{name}{i}"] = shape
    for i, shape in enumerate(Reduction.scratch(plan.layer_unit())[3:]):
        held[f"reduce_last{i}"] = shape
    return held


def step_kernel(plan, names, *refs):
    r = types.SimpleNamespace(**dict(zip(names, refs, strict=True)))
    held = vars(r)
    exchange = lambda name: Exchange(plan, held[name], held[name + "_send"], held[name + "_recv"])
    r.ex_wide = [exchange(f"wide{i}") for i in range(2 * GROUPS)]
    r.ex_thin, r.ex_bias = exchange("thin"), exchange("thick")
    r.spill_e = Spill(r.expanded, r.kept_e, r.spill_sems.at[0])
    r.spill_d = Spill(r.depth, r.kept_d, r.spill_sems.at[1])
    reduce_refs = {
        name: [held[f"reduce_{name}{i}"] for i in range(12)] for name in ("block", "head")
    }
    reduce_refs["last"] = reduce_refs["block"][:3] + [held[f"reduce_last{i}"] for i in range(9)]
    fs = lax.axis_index("fsdp")
    n = plan.images

    enter(plan)
    mine = [r.gated.at[pl.ds(0, plan.chunk), pl.ds(C + i * LANE, LANE)] for i in range(LAYERS)]
    images = r.gated.at[pl.ds(0, plan.rows), pl.ds(0, C)]
    take_images = pltpu.make_async_copy(r.images, images, r.spill_sems.at[0])
    take_images.start()
    take_head = pltpu.make_async_copy(
        r.w_own,
        r.w_head.at[pl.ds(pl.multiple_of(fs * plan.head_pad, 16), plan.head_pad)],
        r.spill_sems.at[1],
    )
    take_head.start()
    shift = spread_shards(plan, r.block, r.flat, mine)
    own_rows = pl.ds(pl.multiple_of(fs * plan.chunk, 16), plan.chunk)

    def gather_of(layer):
        r.stage[own_rows, :] = mine[layer][...]
        return Gather(
            plan, r.stage, plan.chunk, plan.chunk, [held[f"gather_block{i}"] for i in range(6)]
        )

    def unpack(layer):
        unpack_weights(
            plan,
            r.stage,
            r.we.at[layer],
            r.wp.at[layer],
            r.wr.at[layer],
            r.wx.at[layer],
            r.small.at[layer],
            r.tail.at[layer],
            r.flat,
        )

    shift(0)
    gather = gather_of(0)
    entered(plan)
    gather.start_rest()
    for layer in range(1, LAYERS):
        shift(layer)
    take_images.wait()
    take_head.wait()
    columns = jnp.concatenate([r.per_image[...], jnp.zeros((8, LANE - n), F32)], axis=1).T
    weight, label, partner = (columns[0:n, i : i + 1] for i in range(3))
    label, partner = label.astype(jnp.int32), partner.astype(jnp.int32)
    label_row = r.per_image[1:2, :].astype(jnp.int32)
    gather.start_dp()
    mix_images(plan, images, partner, weight, r.stream, 0, PIX // 2)
    gather.start_core()
    mix_images(plan, images, partner, weight, r.stream, PIX // 2, PIX)
    gather.complete()
    unpack(0)

    head_gather = Gather(
        plan,
        r.w_head,
        plan.head_pad,
        plan.head_pad,
        [held[f"gather_head{i}"] for i in range(6)],
        whole=True,
    )
    for layer in range(LAYERS):
        if layer < LAYERS - 1:
            box = []

            def begin(layer=layer, box=box):
                box.append(gather_of(layer + 1))
                box[0].start_rest()

            hooks = (begin, lambda box=box: box[0].start_dp(), lambda box=box: box[0].start_core())
        else:
            hooks = (head_gather.start_rest, lambda: None, head_gather.start_core)
        forward_layer(plan, r, layer, hooks)
        if layer < LAYERS - 1:
            box[0].complete()
            unpack(layer + 1)
    head_gather.complete()
    head_layers(plan, r, label, label_row, partner, weight)
    work = Reduction(plan.head_unit(), r.w_head, r.head_sums, reduce_refs["head"])
    for layer in reversed(range(LAYERS)):
        backward_layer(plan, r, layer, work)
        name = "block" if layer else "last"
        work = Reduction(plan.layer_unit(), r.stage, r.block_sums.at[layer], reduce_refs[name])
    work.start_core()
    work.start_dp()
    work.start_rest()
    work.start_copies()
    work.complete()
    for e in r.ex_wide + [r.ex_thin, r.ex_bias]:
        e.finish()


def train_step(plan, block, w_own, images, per_image, bias):
    held = scratch_of(plan)
    block_unit, head_unit = plan.layer_unit(), plan.head_unit()
    big = (PIX, plan.images, E)
    anywhere = pl.BlockSpec(memory_space=pl.ANY)
    return pl.pallas_call(
        functools.partial(step_kernel, plan, INPUTS + OUTPUTS + tuple(held)),
        out_shape=(
            jax.ShapeDtypeStruct((LAYERS, block_unit.owned, LANE), BF16),
            jax.ShapeDtypeStruct((head_unit.owned, HEAD_W), BF16),
            jax.ShapeDtypeStruct((1, KP), F32),
            jax.ShapeDtypeStruct((LAYERS,) + big, F32),
            jax.ShapeDtypeStruct((LAYERS - 1,) + big, F32),
        ),
        in_specs=[VM, anywhere, anywhere, VM, VM],
        out_specs=(VM, VM, VM, anywhere, anywhere),
        scratch_shapes=list(held.values()),
        compiler_params=pltpu.CompilerParams(
            collective_id=1, has_side_effects=True, vmem_limit_bytes=VMEM_LIMIT
        ),
        name="train_step",
    )(block, w_own, images, per_image, bias)


def adam_update(master, first, second, average, grad):
    first_new = BETA_ONE * first + (1.0 - BETA_ONE) * grad
    second_new = BETA_TWO * second + (1.0 - BETA_TWO) * grad * grad
    fix_one = 1.0 - BETA_ONE**STEP
    fix_two = 1.0 - BETA_TWO**STEP
    master_new = master * (1.0 - RATE * DECAY_WEIGHT) - RATE * (first_new / fix_one) / (
        jnp.sqrt(second_new / fix_two) + EPS_ADAM
    )
    average_new = EMA_RATE * average + (1.0 - EMA_RATE) * master_new
    return (master_new, first_new, second_new, average_new)


def on_device(mesh, images, partner, mix_weight, labels, *states):
    block, head_state, bias_state = states[0:4], states[4:8], states[8:12]
    row = C + 2 + K
    plan = Plan(mesh, images.shape[0], head_state[0].shape[0] // row)
    half = (plan.hd // LANE + 1) // 2 * LANE
    plan.head_groups = [(0, half), (half, plan.hd - half)]
    start = lax.axis_index("fsdp") * plan.shard
    offset = start - start // (16 * LANE) * (16 * LANE)
    grid = head_state[0].astype(BF16).reshape(plan.head_rows, row)
    grid = jnp.concatenate(
        [
            grid[:, : C + 2],
            jnp.zeros((plan.head_rows, LANE - 2), BF16),
            grid[:, C + 2 :],
            jnp.zeros((plan.head_rows, KP - K), BF16),
        ],
        axis=1,
    )
    grid = jnp.pad(grid, ((0, plan.head_pad - plan.head_rows), (0, 0)))
    bias = jnp.pad(bias_state[0], (0, KP - K)).reshape(1, KP)
    per_image = jnp.stack(
        [mix_weight, labels.astype(F32), partner.astype(F32)] + [jnp.zeros_like(mix_weight)] * 5
    )
    block_grad, head_grad, totals = train_step(
        plan, block[0], grid, images.reshape(plan.rows, C), per_image, bias
    )[:3]
    loss_sum = totals[0, KP - 1]
    grad_bias = totals[0, :K]
    block_grad = lax.dynamic_slice(
        block_grad.reshape(LAYERS, plan.chunk * LANE), (0, offset), (LAYERS, plan.shard)
    ).astype(F32)
    head_grad = head_grad[: plan.head_rows].astype(F32)
    head_grad = jnp.concatenate(
        [head_grad[:, : C + 2], head_grad[:, C + LANE : C + LANE + K]], axis=1
    ).reshape(-1)
    return (
        (loss_sum,)
        + adam_update(*block, block_grad)
        + adam_update(*head_state, head_grad)
        + adam_update(*bias_state, grad_bias)
    )


def solution(mesh):
    data = P(("dp", "fsdp"))
    states = (P(None, "fsdp"),) * 4 + (P("fsdp"),) * 4 + (P(),) * 4
    return jax.shard_map(
        functools.partial(on_device, mesh),
        mesh=mesh,
        in_specs=(P(("dp", "fsdp"), None, None), data, data, data) + states,
        out_specs=(P(),) + states,
        check_vma=False,
    )
```

```python
import functools
import types

import jax
import jax.numpy as jnp
from jax import lax
from jax.experimental import pallas as pl
from jax.experimental.pallas import tpu as pltpu
from jax.sharding import PartitionSpec as P

C = 256
E = 1536
SQ = 64
K = 1000
SIDE = 4
PIX = 16
LAYERS = 3
STEP = 5
EPS_NORM = 0.001
RATE = 0.05
DECAY_WEIGHT = 0.05
BETA_ONE = 0.5
BETA_TWO = 0.5
EPS_ADAM = 1e-08
EMA_RATE = 0.5
SMOOTHING = 0.1

LANE = 128
KP = 1024
HEAD_W = C + LANE + KP
PB = 2 * C * E + 2 * E * SQ + 14 * E + SQ + 2 * C
ROW_P = C * E // LANE
ROW_R = ROW_P + E * C // LANE
ROW_X = ROW_R + E * SQ // LANE
ROW_D = ROW_X + SQ * E // LANE
ROW_S = ROW_D + 14 * E // LANE
NJ = E // LANE
GROUPS = 2
GW = E // GROUPS
MBLK = 4
UN_SPREAD, UN_ACT, UN_HBACK, UN_GATE, UN_TWO, UN_ONE = 2, 4, 4, 4, 2, 1

MESH = pl.DeviceIdType.MESH
F32 = jnp.float32
BF16 = jnp.bfloat16
VMEM_LIMIT = 127 * 512 * 1024
VM = pl.BlockSpec(memory_space=pltpu.VMEM)


def ceil_to(value, unit):
    return -(-value // unit) * unit


class Plan:
    def __init__(self, mesh, images, head_rows):
        self.nd = mesh.shape["dp"]
        self.nf = mesh.shape["fsdp"]
        self.devices = self.nd * self.nf
        self.images = images
        self.rows = images * PIX
        self.count = float(self.rows * self.devices)
        self.shard = PB // self.nf
        self.base = [(self.shard * f // LANE) // 16 * 16 for f in range(self.nf)]
        self.chunk = ceil_to(-(-self.shard // LANE) + 17, 16 * self.nd)
        self.flat = self.base[-1] + self.chunk
        self.head_pad = ceil_to(head_rows, 16)
        self.hd = self.head_pad * self.nf
        self.head_rows = head_rows
        self.head_part = ceil_to(-(-head_rows // self.nd), 16)
        self.head_flat = self.head_pad * (self.nf - 1) + self.head_part * self.nd
        self.depth = self.nf // 2

    def layer_unit(self):
        return Unit(self, LANE, self.chunk // self.nd, self.flat, lambda f: self.shard * f // (16 * LANE) * 16)

    def head_unit(self):
        return Unit(self, HEAD_W, self.head_part, self.head_flat, lambda f: self.head_pad * f)


class Unit:
    def __init__(self, plan, width, part, rows, base):
        self.plan, self.width, self.part, self.rows, self.base = plan, width, part, rows, base
        self.owned = part * plan.nd


def dot(a, b, dims=((1,), (0,))):
    return lax.dot_general(a, b, (dims, ((), ())), preferred_element_type=F32)


def halves_of(value):
    high = value.astype(BF16)
    return high, (value - high.astype(F32)).astype(BF16)


def dot_rows(value, low, dims=((1,), (0,))):
    n = value.shape[0]
    both = dot(jnp.concatenate(halves_of(value), axis=0), low, dims)
    return both[0:n, :] + both[n:, :]


def dot_outer(a, b):
    a_high, a_low = halves_of(a)
    b_high, b_low = halves_of(b)
    left = jnp.concatenate([a_high, a_low, a_high], axis=0)
    right = jnp.concatenate([b_high, b_high, b_low], axis=0)
    return dot(left, right, ((0,), (0,)))


def row_sum(value):
    return jnp.sum(value, axis=0, keepdims=True)


def over_peers(plan, body):
    dp, fs = lax.axis_index("dp"), lax.axis_index("fsdp")
    deep, low = fs // 2, dp * 2 + lax.rem(fs, 2)
    near = 2 * plan.nd
    top = jnp.where(2 * deep >= plan.depth, 1, 0)

    def at(k, i, carry):
        z = top * k + (1 - top) * (plan.depth - 1 - k)
        j = lax.rem(low + i, near)

        @pl.when((z != deep) | (j != low))
        def _():
            body((j // 2, 2 * z + lax.rem(j, 2)))

        return carry

    for k in range(plan.depth):
        lax.fori_loop(0, near, functools.partial(at, k), 0)


def my_slot(plan):
    return lax.axis_index("dp") * plan.nf + lax.axis_index("fsdp")


def enter(plan):
    barrier = pltpu.get_barrier_semaphore()
    over_peers(
        plan,
        lambda device: pl.semaphore_signal(
            barrier, inc=1, device_id=device, device_id_type=MESH
        ),
    )


def entered(plan):
    pl.semaphore_wait(pltpu.get_barrier_semaphore(), plan.devices - 1)


class Exchange:
    def __init__(self, plan, buf, send, recv):
        self.plan, self.buf, self.send, self.recv, self.used = plan, buf, send, recv, False

    def share(self, first, second):
        plan, buf, send, recv = self.plan, self.buf, self.send, self.recv
        if self.used:
            self.finish()
        self.used = True
        half = first.shape[1] // LANE
        self.rows = 2 * half
        mine = my_slot(plan)
        for r in range(half):
            cols = slice(r * LANE, (r + 1) * LANE)
            buf[mine, r : r + 1, :] = first[:, cols]
            buf[mine, half + r : half + r + 1, :] = second[:, cols]
        over_peers(
            plan,
            lambda device: pltpu.make_async_remote_copy(
                src_ref=buf.at[mine, pl.ds(0, 2 * half)],
                dst_ref=buf.at[mine, pl.ds(0, 2 * half)],
                send_sem=send,
                recv_sem=recv,
                device_id=device,
                device_id_type=MESH,
            ).start(),
        )

    def others(self):
        return self.buf.at[pl.ds(1, self.plan.devices - 1), pl.ds(0, self.rows)]

    def collect(self):
        pltpu.make_async_copy(self.others(), self.others(), self.recv).wait()
        total = jnp.sum(self.buf[:, 0 : self.rows, :], axis=0)
        rows = [total[r : r + 1, :] for r in range(self.rows)]
        half = self.rows // 2
        return jnp.concatenate(rows[:half], axis=1), jnp.concatenate(rows[half:], axis=1)

    def finish(self):
        pltpu.make_async_copy(self.others(), self.others(), self.send).wait()


class PairedExchange:
    def __init__(self, plan, pair, buf, sems):
        self.plan, self.pair, self.buf, self.sems, self.used = plan, pair, buf, sems, False
        self.dp, self.fs = lax.axis_index("dp"), lax.axis_index("fsdp")
        self.core, self.deep = lax.rem(self.fs, 2), self.fs // 2
        self.mine = self.dp * plan.depth + self.deep

    def share(self, first, second):
        if self.used:
            self.finish()
        self.used = True
        half = first.shape[1] // LANE
        self.rows = 2 * half
        for i in range(half):
            cols = slice(i * LANE, (i + 1) * LANE)
            self.pair[0, i : i + 1, :] = first[:, cols]
            self.pair[0, half + i : half + i + 1, :] = second[:, cols]
        rows = pl.ds(0, self.rows)
        pltpu.make_async_remote_copy(
            src_ref=self.pair.at[0, rows],
            dst_ref=self.pair.at[1, rows],
            send_sem=self.sems[0],
            recv_sem=self.sems[1],
            device_id=(self.dp, 2 * self.deep + 1 - self.core),
            device_id_type=MESH,
        ).start()

    def relay(self):
        plan, rows = self.plan, pl.ds(0, self.rows)
        got = self.pair.at[1, rows]
        pltpu.make_async_copy(got, got, self.sems[1]).wait()
        self.buf[self.mine, rows, :] = self.pair[0, rows, :] + self.pair[1, rows, :]
        top = jnp.where(2 * self.deep >= plan.depth, 1, 0)
        for k in range(plan.depth):
            z = top * k + (1 - top) * (plan.depth - 1 - k)

            def go(i, carry, z=z):
                d = lax.rem(self.dp + i, plan.nd)

                @pl.when((z != self.deep) | (d != self.dp))
                def _():
                    pltpu.make_async_remote_copy(
                        src_ref=self.buf.at[self.mine, rows],
                        dst_ref=self.buf.at[self.mine, rows],
                        send_sem=self.sems[2],
                        recv_sem=self.sems[3],
                        device_id=(d, 2 * z + self.core),
                        device_id_type=MESH,
                    ).start()

                return carry

            lax.fori_loop(0, plan.nd, go, 0)

    def others(self):
        return self.buf.at[pl.ds(1, self.plan.devices // 2 - 1), pl.ds(0, self.rows)]

    def collect(self):
        pltpu.make_async_copy(self.others(), self.others(), self.sems[3]).wait()
        total = jnp.sum(self.buf[:, 0 : self.rows, :], axis=0)
        rows = [total[i : i + 1, :] for i in range(self.rows)]
        half = self.rows // 2
        return jnp.concatenate(rows[:half], axis=1), jnp.concatenate(rows[half:], axis=1)

    def finish(self):
        sent = self.pair.at[0, pl.ds(0, self.rows)]
        pltpu.make_async_copy(sent, sent, self.sems[0]).wait()
        pltpu.make_async_copy(self.others(), self.others(), self.sems[2]).wait()


def moments(plan, pair):
    mean = pair[0] / plan.count
    return mean, lax.rsqrt(pair[1] / plan.count - mean * mean + EPS_NORM)


class Reduction:
    def __init__(self, unit, source, result, refs):
        self.unit, self.source, self.result = unit, source, result
        self.got_core, self.got_dp, self.sum_dp, self.got_rest = refs[:4]
        self.send, self.recv = refs[4:8], refs[8:12]
        plan = unit.plan
        self.dp, self.fs = lax.axis_index("dp"), lax.axis_index("fsdp")
        self.core, self.deep = lax.rem(self.fs, 2), self.fs // 2
        self.nd, self.nz = plan.nd, plan.depth

    @staticmethod
    def scratch(unit):
        plan = unit.plan
        nd, nz, w, part = plan.nd, plan.depth, unit.width, unit.part
        return [
            pltpu.VMEM((nz, nd, part, w), BF16),
            pltpu.VMEM((nd - 1, nz, part, w), BF16),
            pltpu.VMEM((nz, part, w), BF16),
            pltpu.VMEM((nz - 1, part, w), BF16),
        ] + [pltpu.SemaphoreType.DMA(())] * 8

    def push(self, stage, source, target, device):
        pltpu.make_async_remote_copy(
            src_ref=source,
            dst_ref=target,
            send_sem=self.send[stage],
            recv_sem=self.recv[stage],
            device_id=device,
            device_id_type=MESH,
        ).start()

    def rows_of(self, f, d=0):
        return pl.multiple_of(self.unit.base(f) + d * self.unit.part, 16)

    def start_core(self):
        def go(z, carry):
            for d in range(self.nd):
                self.push(
                    0,
                    self.source.at[pl.ds(self.rows_of(2 * z + 1 - self.core, d), self.unit.part)],
                    self.got_core.at[z, d],
                    (self.dp, 2 * self.deep + 1 - self.core),
                )
            return carry

        lax.fori_loop(0, self.nz, go, 0)

    def wait(self, sem, ref):
        pltpu.make_async_copy(ref, ref, sem).wait()

    def start_dp(self):
        self.wait(self.recv[0], self.got_core)

        def add(z, carry):
            for d in range(self.nd):
                own = self.source[pl.ds(self.rows_of(2 * z + self.core, d), self.unit.part), :]
                self.got_core[z, d] = (own.astype(F32) + self.got_core[z, d].astype(F32)).astype(BF16)
            return carry

        lax.fori_loop(0, self.nz, add, 0)

        def go(z, carry):
            for i in range(1, self.nd):
                other = lax.rem(self.dp + i, self.nd)
                self.push(1, self.got_core.at[z, other], self.got_dp.at[i - 1, z], (other, self.fs))
            return carry

        lax.fori_loop(0, self.nz, go, 0)

    def start_rest(self):
        self.wait(self.recv[1], self.got_dp)
        self.wait(self.send[1], self.got_dp)

        def add(z, carry):
            total = self.got_core[z, self.dp].astype(F32)
            for i in range(self.nd - 1):
                total = total + self.got_dp[i, z].astype(F32)
            self.sum_dp[z] = total.astype(BF16)
            return carry

        lax.fori_loop(0, self.nz, add, 0)
        for i in range(1, self.nz):
            other = lax.rem(self.deep + i, self.nz)
            self.push(2, self.sum_dp.at[other], self.got_rest.at[i - 1], (self.dp, 2 * other + self.core))

    def start_copies(self):
        self.wait(self.recv[2], self.got_rest)
        total = self.sum_dp[self.deep].astype(F32)
        for i in range(self.nz - 1):
            total = total + self.got_rest[i].astype(F32)
        rows = pl.ds(pl.multiple_of(self.dp * self.unit.part, 16), self.unit.part)
        self.result[rows, :] = total.astype(BF16)
        for i in range(1, self.nd):
            other = lax.rem(self.dp + i, self.nd)
            self.push(3, self.result.at[rows], self.result.at[rows], (other, self.fs))

    def complete(self):
        others = self.result.at[pl.ds(0, (self.nd - 1) * self.unit.part)]
        self.wait(self.recv[3], others)
        self.wait(self.send[0], self.got_core)
        self.wait(self.send[2], self.got_rest)
        self.wait(self.send[3], others)


def taps():
    found = []
    for y in range(SIDE):
        for x in range(SIDE):
            for a in range(3):
                for b in range(3):
                    iy, ix = y + a - 1, x + b - 1
                    if 0 <= iy < SIDE and 0 <= ix < SIDE:
                        found.append((y * SIDE + x, 3 * a + b, iy * SIDE + ix))
    return found


TAPS = taps()


def half_tanh(half):
    return jnp.tanh(half)


def silu(z):
    half = 0.5 * z
    return half * half_tanh(half) + half


def sigmoid(z):
    return 0.5 * half_tanh(0.5 * z) + 0.5


def silu_slope(z):
    half = 0.5 * z
    t = half_tanh(half)
    return 0.5 * (1.0 + t + half * (1.0 - t * t))


def lanes(j):
    return pl.ds(pl.multiple_of(j * LANE, LANE), LANE)


def images_at(b):
    return pl.ds(pl.multiple_of(b * 8, 8), 8)


def over_tiles(plan, first_chunk, chunks, per_chunk, body, n_sums, store_sums, unroll=1):
    blocks = plan.images // 8

    def chunk_step(jj, carry):
        j = first_chunk + jj
        hoisted = per_chunk(j)

        def step(b, sums):
            for u in range(unroll):
                sums = body(j, b * unroll + u, hoisted, sums)
            return sums

        zero = tuple(jnp.zeros((8, LANE), F32) for _ in range(n_sums))
        store_sums(j, lax.fori_loop(0, blocks // unroll, step, zero))
        return carry

    lax.fori_loop(0, chunks, chunk_step, 0)


def over_tiles_and(plan, first_chunk, chunks, between, *rest):
    if between is None:
        over_tiles(plan, first_chunk, chunks, *rest)
    else:
        over_tiles(plan, first_chunk, 2, *rest)
        between()
        over_tiles(plan, first_chunk + 2, chunks - 2, *rest)


class Gather:
    def __init__(self, plan, target, rows, sems):
        self.plan, self.target, self.rows = plan, target, rows
        tiles = rows // 16
        counts = [tiles // plan.nd + (1 if d < tiles % plan.nd else 0) for d in range(plan.nd)]
        self.parts = [(16 * sum(counts[:d]), 16 * counts[d]) for d in range(plan.nd)]
        self.send, self.recv = sems[0:3], sems[3:6]
        self.dp, self.fs = lax.axis_index("dp"), lax.axis_index("fsdp")
        self.core, self.deep = lax.rem(self.fs, 2), self.fs // 2

    def by_part(self, body):
        if len({size for _, size in self.parts}) == 1:
            size = self.parts[0][1]
            body(self.dp * size, size)
            return
        for d, (start, size) in enumerate(self.parts):
            pl.when(self.dp == d)(functools.partial(body, start, size))

    def at(self, deep, start, size):
        begin = (2 * deep + self.core) * self.rows + start
        return self.target.at[pl.ds(pl.multiple_of(begin, 16), size)]

    def push(self, stage, ref, device):
        pltpu.make_async_remote_copy(
            src_ref=ref,
            dst_ref=ref,
            send_sem=self.send[stage],
            recv_sem=self.recv[stage],
            device_id=device,
            device_id_type=MESH,
        ).start()

    def wait(self, sem, rows):
        if rows:
            span = self.target.at[pl.ds(0, rows)]
            pltpu.make_async_copy(span, span, sem).wait()

    def start_rest(self):
        def body(start, size):
            def go(i, carry):
                other = lax.rem(self.deep + i, self.plan.depth)
                self.push(0, self.at(self.deep, start, size), (self.dp, 2 * other + self.core))
                return carry

            if size:
                lax.fori_loop(1, self.plan.depth, go, 0)

        self.by_part(body)

    def start_dp(self):
        plan = self.plan

        def body(start, size):
            self.wait(self.recv[0], (plan.depth - 1) * size)

            def go(i, carry):
                other = lax.rem(self.deep + i, plan.depth)
                for k in range(1, plan.nd):
                    self.push(
                        1, self.at(other, start, size), (lax.rem(self.dp + k, plan.nd), self.fs)
                    )
                return carry

            if size:
                lax.fori_loop(1, plan.depth, go, 0)

        self.by_part(body)

    def start_core(self):
        plan = self.plan
        self.by_part(
            lambda start, size: self.wait(self.recv[1], (plan.depth - 1) * (self.rows - size))
        )

        def go(z, carry):
            self.push(2, self.at(z, 0, self.rows), (self.dp, 2 * self.deep + 1 - self.core))
            return carry

        lax.fori_loop(0, plan.depth, go, 0)

    def complete(self):
        plan = self.plan
        self.wait(self.recv[2], plan.depth * self.rows)

        def body(start, size):
            self.wait(self.send[0], (plan.depth - 1) * size)
            self.wait(self.send[1], (plan.depth - 1) * (plan.nd - 1) * size)

        self.by_part(body)
        self.wait(self.send[2], plan.depth * self.rows)


def spread_shards(plan, block, flat, mine):
    start = lax.axis_index("fsdp") * plan.shard
    offset = start - start // (16 * LANE) * (16 * LANE)
    down, turn = offset // LANE, lax.rem(offset, LANE)
    full = plan.shard // LANE
    rest = plan.shard - full * LANE
    size = plan.chunk + 32
    lane = lax.broadcasted_iota(jnp.int32, (16, LANE), 1)
    for layer in range(LAYERS):
        flat[layer * size : layer * size + 24, :] = jnp.zeros((24, LANE), F32)

    def take(i, count):
        piece = block[:, pl.ds(pl.multiple_of(i * 8 * LANE, LANE), count * LANE)]
        for layer in range(LAYERS):
            rows = [piece[layer : layer + 1, k * LANE : (k + 1) * LANE] for k in range(count)]
            at = pl.ds(pl.multiple_of(layer * size + 24 + i * 8, 8), count)
            flat[at, :] = jnp.concatenate(rows, axis=0) if count > 1 else rows[0]

    def step(i, carry):
        take(i, 8)
        return carry

    lax.fori_loop(0, full // 8, step, 0)
    if full % 8:
        take(full // 8, full % 8)
    for layer in range(LAYERS):
        at = layer * size + 24 + full
        if rest:
            last = block[layer : layer + 1, full * LANE : full * LANE + rest]
            flat[at : at + 1, :] = jnp.concatenate([last, jnp.zeros((1, LANE - rest), F32)], axis=1)
            at += 1
        end = (layer + 1) * size
        flat[at:end, :] = jnp.zeros((end - at, LANE), F32)

    def shift(layer):
        def go(i, carry):
            begin = layer * size + 24 + i * 16 - down
            here = pltpu.roll(flat[pl.ds(begin, 16), :], turn, 1)
            before = pltpu.roll(flat[pl.ds(begin - 1, 16), :], turn, 1)
            value = jnp.where(lane >= turn, here, before)
            mine[layer][pl.ds(pl.multiple_of(i * 16, 16), 16), :] = value.astype(BF16)
            return carry

        lax.fori_loop(0, plan.chunk // 16, go, 0)

    return shift


def unpack_weights(plan, got, we, wp, wr, wx, small, tail, flat):
    lane = lax.broadcasted_iota(jnp.int32, (1, LANE), 1)
    low = lane < SQ
    for f in range(plan.nf):
        base, at = plan.base[f], f * plan.chunk
        head = got[at : at + 16, :].astype(F32)
        if f:
            head = head + flat[base : base + 16, :]
        flat[base : base + 16, :] = head
        flat[base + 16 : base + plan.chunk, :] = got[at + 16 : at + plan.chunk, :].astype(F32)
    for j in range(NJ):
        cols = slice(j * LANE, (j + 1) * LANE)
        we[:, cols] = flat[pl.ds(j, C, stride=NJ), :].astype(BF16)
        wx[0:SQ, cols] = flat[pl.ds(ROW_X + j, SQ, stride=NJ), :].astype(BF16)
        wx[SQ:LANE, cols] = jnp.zeros((LANE - SQ, LANE), BF16)
        small[0:14, cols] = flat[pl.ds(ROW_D + j, 14, stride=NJ), :]
        small[14:16, cols] = jnp.zeros((2, LANE), F32)
    for h in range(C // LANE):
        wp[:, h * LANE : (h + 1) * LANE] = flat[pl.ds(ROW_P + h, E, stride=2), :].astype(BF16)
    pairs = flat[ROW_R:ROW_X, :]
    evens, odds = jnp.where(low, pairs, 0.0), jnp.where(low, pltpu.roll(pairs, SQ, 1), 0.0)
    flat[pl.ds(0, E // 2, stride=2), :] = evens
    flat[pl.ds(1, E // 2, stride=2), :] = odds
    wr[...] = flat[0:E, :].astype(BF16)
    rows = [flat[ROW_S + i : ROW_S + i + 1, :] for i in range(5)]
    turned = [pltpu.roll(jnp.broadcast_to(r, (8, LANE)), SQ, 1)[0:1, :] for r in rows]
    tail[...] = jnp.zeros((8, C), F32)
    tail[0:1, 0:LANE] = jnp.where(low, rows[0], 0.0)
    for i, at in ((1, 0), (2, 2)):
        tail[i : i + 1, 0:LANE] = jnp.where(low, turned[at], turned[at + 1])
        tail[i : i + 1, LANE:C] = jnp.where(low, turned[at + 1], turned[at + 2])


def mix_images(plan, images, partner, share_one, stream, first, last):
    n, rows = plan.images, plan.rows
    place = lax.broadcasted_iota(jnp.int32, (n, rows), 1)
    own = lax.broadcasted_iota(jnp.int32, (n, rows), 0) * PIX
    chosen = partner * PIX

    def go(p, carry):
        mine = dot(jnp.where(place == own + p, 1.0, 0.0).astype(BF16), images[...])
        theirs = dot(jnp.where(place == chosen + p, 1.0, 0.0).astype(BF16), images[...])
        at = pl.ds(pl.multiple_of(p * n, n), n)
        stream[at, :] = share_one * mine + (1.0 - share_one) * theirs
        return carry

    lax.fori_loop(first, last, go, 0)


def forward_layer(plan, r, layer, hooks):
    x, expanded, depth, act, sums, x_low = r.stream, r.expanded, r.depth, r.flow, r.sums, r.x_low
    normed_three, stat_e, stat_c = r.normed_three.at[layer], r.stat_e.at[layer], r.stat_c.at[layer]
    pooled, presq, gate, turned = r.pooled.at[layer], r.presq.at[layer], r.gate.at[layer], r.turned.at[layer]
    we, wp, wr, wx = r.we.at[layer], r.wp.at[layer], r.wr.at[layer], r.wx.at[layer]
    small, tail = r.small.at[layer], r.tail.at[layer]
    ex_one, ex_two, ex_three = r.ex_wide[0:GROUPS], r.ex_wide[GROUPS : 2 * GROUPS], r.ex_thin
    n = plan.images
    x_low[...] = x[...].astype(BF16)
    for g in range(GROUPS):
        cols = slice(g * GW, (g + 1) * GW)

        def expand(m, carry, cols=cols):
            rows = pl.ds(pl.multiple_of(m * MBLK * n, MBLK * n), MBLK * n)
            value = dot(x_low[rows, :], we[:, cols])
            expanded[pl.ds(m * MBLK, MBLK), :, cols] = value.reshape(MBLK, n, GW)
            return (
                carry[0] + jnp.sum(value.reshape(-1, 8, GW), axis=0),
                carry[1] + jnp.sum((value * value).reshape(-1, 8, GW), axis=0),
            )

        zero = jnp.zeros((8, GW), F32)
        s, q = lax.fori_loop(0, PIX // MBLK, expand, (zero, zero))
        if g:
            ex_one[g - 1].relay()
        ex_one[g].share(row_sum(s), row_sum(q))
    turned[...] = x[...].T.astype(BF16)
    ex_one[GROUPS - 1].relay()

    def put_sums(j, totals):
        for i, t in enumerate(totals):
            sums[i : i + 1, lanes(j)] = row_sum(t)

    for g in range(GROUPS):
        cols = slice(g * GW, (g + 1) * GW)
        mean, rstd = moments(plan, ex_one[g].collect())
        if g == 0:
            r.spill_e.start(layer)
            if layer:
                r.spill_d.wait()
        stat_e[0:1, cols] = mean
        stat_e[1:2, cols] = rstd
        scale = rstd * small[9:10, cols]
        stat_e[4:5, cols] = 0.5 * scale
        stat_e[5:6, cols] = 0.5 * (small[10:11, cols] - mean * scale)

        def chunk(j):
            return (
                stat_e[4:5, lanes(j)],
                stat_e[5:6, lanes(j)],
                [small[t : t + 1, lanes(j)] for t in range(9)],
            )

        def spread(j, b, hoisted, totals):
            scale, shift, w = hoisted
            act_one = []
            for p in range(PIX):
                half = expanded[p, images_at(b), lanes(j)] * scale + shift
                act_one.append(half * half_tanh(half) + half)
            made = [None] * PIX
            for o, t, i in TAPS:
                term = act_one[i] * w[t]
                made[o] = term if made[o] is None else made[o] + term
            s, q = totals
            for p in range(PIX):
                depth[p, images_at(b), lanes(j)] = made[p]
                s = s + made[p]
                q = q + made[p] * made[p]
            return s, q

        between = ex_two[g - 1].relay if g else None
        over_tiles_and(
            plan, g * (GW // LANE), GW // LANE, between, chunk, spread, 2, put_sums, UN_SPREAD
        )
        ex_two[g].share(sums[0:1, cols], sums[1:2, cols])
        if g == 0:
            hooks[0]()
    ex_two[GROUPS - 1].relay()
    hooks[1]()

    for g in range(GROUPS):
        cols = slice(g * GW, (g + 1) * GW)
        mean, rstd = moments(plan, ex_two[g].collect())
        if g == 0:
            if layer < LAYERS - 1:
                r.spill_d.start(layer)
        stat_e[2:3, cols] = mean
        stat_e[3:4, cols] = rstd
        scale = rstd * small[11:12, cols]
        stat_e[6:7, cols] = 0.5 * scale
        stat_e[7:8, cols] = 0.5 * (small[12:13, cols] - mean * scale)

        def chunk_two(j):
            return stat_e[6:7, lanes(j)], stat_e[7:8, lanes(j)]

        def activate(j, b, hoisted, totals):
            scale, shift = hoisted
            total = None
            for p in range(PIX):
                half = depth[p, images_at(b), lanes(j)] * scale + shift
                made = half * half_tanh(half) + half
                act[p, images_at(b), lanes(j)] = made
                total = made if total is None else total + made
            pooled[images_at(b), lanes(j)] = total * (1.0 / PIX)
            return totals

        over_tiles(
            plan, g * (GW // LANE), GW // LANE, chunk_two, activate, 0, lambda j, s: None, UN_ACT
        )
    reduced = dot_rows(pooled[...], wr[...]) + tail[0:1, 0:LANE]
    presq[...] = reduced
    gate[...] = sigmoid(dot_rows(silu(reduced), wx[...]) + small[13:14, :])

    hooks[2]()
    r.spill_e.wait()

    def project(m, carry):
        gated = (act[pl.ds(m * MBLK, MBLK), :, :] * gate[...][None]).astype(BF16)
        value = dot(gated.reshape(MBLK * n, E), wp[...])
        expanded[pl.ds(m * MBLK, MBLK), :, 0:C] = value.reshape(MBLK, n, C)
        return (
            carry[0] + jnp.sum(value.reshape(-1, 8, C), axis=0),
            carry[1] + jnp.sum((value * value).reshape(-1, 8, C), axis=0),
        )

    zero = jnp.zeros((8, C), F32)
    s, q = lax.fori_loop(0, PIX // MBLK, project, (zero, zero))
    ex_three.share(row_sum(s), row_sum(q))
    hooks[3]()
    mean, rstd = moments(plan, ex_three.collect())
    stat_c[...] = jnp.zeros((8, C), F32)
    stat_c[0:1, :] = mean
    stat_c[1:2, :] = rstd
    normed = (expanded[:, :, 0:C].reshape(n * PIX, C) - mean) * rstd
    normed_three[...] = normed.astype(BF16)
    x[...] = x[...] + normed * tail[1:2, :] + tail[2:3, :]


def head_layers(plan, r, label, label_row, partner, weight):
    x, x_low, turned, bias, totals_out = r.stream, r.x_low, r.turned.at[LAYERS], r.bias, r.totals
    w_head = grad_head = r.w_head
    hidden, slope, low_grad, pool, stat = r.expanded, r.flow, r.gated, r.squeeze_grad, r.coef
    sums, gain, grad_x = r.sums, r.sums.at[pl.ds(8, 8)], r.stream
    hd, n = plan.hd, plan.images
    halves = plan.head_groups
    ng = len(halves)
    ex_stat, ex_grad, ex_bias = r.ex_wide[0:ng], r.ex_wide[GROUPS : GROUPS + ng], r.ex_bias
    x_low[...] = x[...].astype(BF16)
    gain[:, 0:hd] = w_head[0:hd, C : C + LANE].astype(F32).T[0:8, :]
    for g, (start, width) in enumerate(halves):
        cols = slice(start, start + width)

        def convolve(m, carry, cols=cols, width=width):
            rows = pl.ds(pl.multiple_of(m * MBLK * n, MBLK * n), MBLK * n)
            value = dot(x_low[rows, :], w_head[cols, 0:C], ((1,), (1,)))
            hidden[pl.ds(m * MBLK, MBLK), :, cols] = value.reshape(MBLK, n, width)
            return (
                carry[0] + jnp.sum(value.reshape(-1, 8, width), axis=0),
                carry[1] + jnp.sum((value * value).reshape(-1, 8, width), axis=0),
            )

        zero = jnp.zeros((8, width), F32)
        s, q = lax.fori_loop(0, PIX // MBLK, convolve, (zero, zero))
        if g:
            ex_stat[g - 1].relay()
        ex_stat[g].share(row_sum(s), row_sum(q))
    turned[...] = x[...].T.astype(BF16)
    ex_stat[ng - 1].relay()
    for g, (start, width) in enumerate(halves):
        cols = slice(start, start + width)
        mean, rstd = moments(plan, ex_stat[g].collect())
        scale = rstd * gain[0:1, cols]
        stat[0:1, cols] = rstd
        stat[1:2, cols] = -mean * rstd
        stat[2:3, cols] = 0.5 * scale
        stat[3:4, cols] = 0.5 * (gain[1:2, cols] - mean * scale)

        def chunk(j):
            return stat[2:3, lanes(j)], stat[3:4, lanes(j)]

        def activate(j, b, hoisted, totals):
            scale, shift = hoisted
            total = None
            for p in range(PIX):
                half = hidden[p, images_at(b), lanes(j)] * scale + shift
                t = half_tanh(half)
                made = half * t + half
                slope[p, images_at(b), lanes(j)] = (1.0 + t) + half * (1.0 - t * t)
                total = made if total is None else total + made
            pool[images_at(b), lanes(j)] = total * (1.0 / PIX)
            return totals

        over_tiles(plan, start // LANE, width // LANE, chunk, activate, 0, lambda j, s: None, UN_ACT)
    pool_low = pool[:, 0:hd].astype(BF16)
    classes = lax.broadcasted_iota(jnp.int32, (n, KP), 1)
    valid = classes < K
    logits = dot(pool_low, w_head[0:hd, C + LANE :]) + bias[...]
    logits = jnp.where(valid, logits, -1e30)
    top = jnp.max(logits, axis=1, keepdims=True)
    lifted = logits - top
    powers = jnp.where(valid, jnp.exp(lifted), 0.0)
    norm = jnp.sum(powers, axis=1, keepdims=True)
    log_probs = lifted - jnp.log(norm)
    picked = lax.broadcasted_iota(jnp.int32, (n, n), 1) == partner
    label_two = jnp.sum(jnp.where(picked, label_row[...], 0), axis=1, keepdims=True)
    w = weight
    targets = w * jnp.where(classes == label, 1.0 - SMOOTHING, 0.0) + (1.0 - w) * jnp.where(
        classes == label_two, 1.0 - SMOOTHING, 0.0
    )
    targets = jnp.where(valid, targets + SMOOTHING / K, 0.0)
    loss = -jnp.sum(jnp.where(valid, targets * log_probs, 0.0))
    grad_logits = (powers / norm - targets) * (float(PIX) / plan.count)
    packed_bias = jnp.where(classes[0:1, :] == KP - 1, loss, row_sum(grad_logits))
    ex_bias.share(packed_bias[:, 0 : KP // 2], packed_bias[:, KP // 2 :])
    grad_low = grad_logits.astype(BF16)
    pool_grad = dot(grad_low, w_head[0:hd, C + LANE :], ((1,), (1,)))
    pool[:, 0:hd] = pool_grad * (0.5 / PIX)

    def put_sums(j, totals):
        flow_sum, value_sum = [row_sum(t) for t in totals]
        sums[0:1, lanes(j)] = flow_sum
        sums[1:2, lanes(j)] = value_sum * stat[0:1, lanes(j)] + flow_sum * stat[1:2, lanes(j)]

    for g, (start, width) in enumerate(halves):
        cols = slice(start, start + width)

        def back(j, b, hoisted, totals):
            s, q = totals
            flow = pool[images_at(b), lanes(j)]
            for p in range(PIX):
                made = slope[p, images_at(b), lanes(j)] * flow
                slope[p, images_at(b), lanes(j)] = made
                s = s + made
                q = q + made * hidden[p, images_at(b), lanes(j)]
            return s, q

        between = ex_grad[g - 1].relay if g else None
        over_tiles_and(
            plan, start // LANE, width // LANE, between, lambda j: None, back, 2, put_sums, UN_HBACK
        )
        ex_grad[g].share(sums[0:1, cols], sums[1:2, cols])
    grad_head[0:hd, C + LANE :] = dot(pool_low.T, grad_low).astype(BF16)
    ex_grad[ng - 1].relay()
    norm_grads = jnp.concatenate(
        [sums[1:2, 0:hd], sums[0:1, 0:hd], jnp.zeros((LANE - 2, hd), F32)], axis=0
    )
    grad_head[0:hd, C : C + LANE] = norm_grads.T.astype(BF16)
    for g, (start, width) in enumerate(halves):
        cols = slice(start, start + width)
        shift_total, gain_total = ex_grad[g].collect()
        scale = stat[0:1, cols] * gain[0:1, cols]
        mean_one = shift_total / plan.count
        mean_two = gain_total / plan.count
        stat[4:5, cols] = scale
        stat[5:6, cols] = -scale * stat[0:1, cols] * mean_two
        stat[6:7, cols] = -scale * (mean_one + stat[1:2, cols] * mean_two)
    def into(m, carry):
        rows = pl.ds(pl.multiple_of(m * MBLK * n, MBLK * n), MBLK * n)
        spot = pl.ds(m * MBLK, MBLK)
        value = (
            slope[spot, :, 0:hd] * stat[4:5, 0:hd]
            + hidden[spot, :, 0:hd] * stat[5:6, 0:hd]
            + stat[6:7, 0:hd]
        )
        low = value.reshape(MBLK * n, hd).astype(BF16)
        low_grad[rows, 0:hd] = low
        grad_x[rows, :] = dot(low, w_head[0:hd, 0:C])
        return carry

    lax.fori_loop(0, PIX // MBLK, into, 0)
    r.spill_e.fetch(LAYERS - 1)
    for at in range(0, hd, LANE):
        part = dot(turned[...], low_grad[:, at : at + LANE])
        grad_head[at : at + LANE, 0:C] = part.T.astype(BF16)
    totals_out[...] = jnp.concatenate(ex_bias.collect(), axis=1)


def backward_layer(plan, r, layer, hooks):
    expanded, depth, flow, gated, sums, coef = r.expanded, r.depth, r.flow, r.gated, r.sums, r.coef
    normed_three, stat_e, stat_c = r.normed_three.at[layer], r.stat_e.at[layer], r.stat_c.at[layer]
    pooled, presq, gate, turned = r.pooled.at[layer], r.presq.at[layer], r.gate.at[layer], r.turned.at[layer]
    we, wp, wr, wx = r.we.at[layer], r.wp.at[layer], r.wr.at[layer], r.wx.at[layer]
    small, tail = r.small.at[layer], r.tail.at[layer]
    grad = grad_x = r.stream
    low_proj, squeeze_grad, flat, packed = r.x_low, r.squeeze_grad, r.flat, r.stage
    ex_one, ex_two, ex_three = r.ex_wide[0:GROUPS], r.ex_wide[GROUPS : 2 * GROUPS], r.ex_thin
    n = plan.images
    lane = lax.broadcasted_iota(jnp.int32, (1, LANE), 1)
    is_low = lane < SQ
    rstd_c = stat_c[1:2, :]
    s = row_sum(jnp.sum(grad[...].reshape(-1, 8, C), axis=0))
    q = row_sum(
        jnp.sum((grad[...] * normed_three[...].astype(F32)).reshape(-1, 8, C), axis=0)
    )
    ex_three.share(s, q)
    hooks[0]()
    bias_three, gain_three = s, q

    if layer < LAYERS - 1:
        r.spill_d.wait()

    def chunk_two(j):
        return stat_e[6:7, lanes(j)], stat_e[7:8, lanes(j)]

    def regate(p, carry):
        rows = pl.ds(pl.multiple_of(p * n, n), n)
        for j in range(NJ):
            cols = slice(j * LANE, (j + 1) * LANE)
            half = depth[p, :, cols] * stat_e[6:7, cols] + stat_e[7:8, cols]
            value = (half * half_tanh(half) + half) * gate[:, cols]
            gated[rows, cols] = value.astype(BF16)
        return carry

    lax.fori_loop(0, PIX, regate, 0)

    bias_total, gain_total = ex_three.collect()
    scale = rstd_c * tail[1:2, :]
    mean_one, mean_two = bias_total / plan.count, gain_total / plan.count
    low_proj[...] = (
        scale
        * (grad[...] - mean_one - normed_three[...].astype(F32) * mean_two)
    ).astype(BF16)

    def into_gated(m, carry):
        rows = pl.ds(pl.multiple_of(m * MBLK * n, MBLK * n), MBLK * n)
        value = dot(low_proj[rows, :], wp[...], ((1,), (1,)))
        flow[pl.ds(m * MBLK, MBLK), :, :] = value.reshape(MBLK, n, E)
        return carry

    lax.fori_loop(0, PIX // MBLK, into_gated, 0)
    hooks[1]()

    def gate_back(t, carry):
        j, b = t // (n // 16), lax.rem(t, n // 16)
        block = pl.ds(pl.multiple_of(b * 16, 16), 16)
        total = None
        for p in range(PIX):
            low = gated[pl.ds(pl.multiple_of(p * n + b * 16, 16), 16), lanes(j)].astype(F32)
            term = flow[p, block, lanes(j)] * low
            total = term if total is None else total + term
        squeeze_grad[block, lanes(j)] = total * (1.0 - gate[block, lanes(j)])
        return carry

    lax.fori_loop(0, NJ * (n // 16), gate_back, 0)
    excite_grad = squeeze_grad[...]
    sums[13:14, :] = row_sum(excite_grad)
    squeezed = silu(presq[...])
    presq_grad = dot_rows(excite_grad, wx[...], ((1,), (1,))) * silu_slope(presq[...])
    grad_wx = dot_outer(squeezed, excite_grad)
    flat[ROW_R : ROW_R + E, :] = dot_outer(pooled[...], presq_grad)
    evens = flat[pl.ds(ROW_R, E // 2, stride=2), :]
    odds = flat[pl.ds(ROW_R + 1, E // 2, stride=2), :]
    flat[ROW_R:ROW_X, :] = jnp.where(is_low, evens, pltpu.roll(odds, SQ, 1))
    for j in range(NJ):
        flat[pl.ds(ROW_X + j, SQ, stride=NJ), :] = grad_wx[0:SQ, j * LANE : (j + 1) * LANE]
    grad_reduce_b = row_sum(presq_grad)
    squeeze_grad[...] = dot_rows(presq_grad, wr[...], ((1,), (1,))) * (1.0 / PIX)

    def put_sums(first_row, stat_row):
        def put(j, totals):
            rows = [row_sum(t) for t in totals]
            mean = stat_e[stat_row : stat_row + 1, lanes(j)]
            rstd = stat_e[stat_row + 1 : stat_row + 2, lanes(j)]
            rows[-2] = (rows[-2] - mean * rows[-1]) * rstd
            for i, t in enumerate(rows):
                sums[first_row + i : first_row + i + 1, lanes(j)] = t

        return put

    def back_two(j, b, hoisted, totals):
        scale, shift = hoisted
        gain_sum, bias_sum = totals
        opened = gate[images_at(b), lanes(j)] * 0.5
        pool_flow = squeeze_grad[images_at(b), lanes(j)] * 0.5
        for p in range(PIX):
            value = depth[p, images_at(b), lanes(j)]
            half = value * scale + shift
            t = half_tanh(half)
            made = (flow[p, images_at(b), lanes(j)] * opened + pool_flow) * (
                (1.0 + t) + half * (1.0 - t * t)
            )
            flow[p, images_at(b), lanes(j)] = made
            bias_sum = bias_sum + made
            gain_sum = gain_sum + made * value
        return gain_sum, bias_sum

    for g in range(GROUPS):
        cols = slice(g * GW, (g + 1) * GW)
        between = ex_two[g - 1].relay if g else None
        over_tiles_and(
            plan, g * (GW // LANE), GW // LANE, between, chunk_two, back_two, 2, put_sums(11, 2), UN_TWO
        )
        ex_two[g].share(sums[12:13, cols], sums[11:12, cols])

    proj_turned = low_proj[...].astype(F32).T.astype(BF16)
    ex_two[GROUPS - 1].relay()
    hooks[2]()
    for j in range(NJ):
        part = dot(proj_turned, gated[:, j * LANE : (j + 1) * LANE])
        for h in range(C // LANE):
            flat[pl.ds(ROW_P + 2 * j * LANE + h, LANE, stride=2), :] = part[
                h * LANE : (h + 1) * LANE, :
            ].T

    def norm_coefs(g, pair, row, stat_row, gain_row):
        cols = slice(g * GW, (g + 1) * GW)
        mean, rstd = stat_e[stat_row : stat_row + 1, cols], stat_e[stat_row + 1 : stat_row + 2, cols]
        scale = rstd * small[gain_row : gain_row + 1, cols]
        mean_one, mean_two = pair[0] / plan.count, pair[1] / plan.count
        coef[row : row + 1, cols] = scale
        coef[row + 1 : row + 2, cols] = -scale * rstd * mean_two
        coef[row + 2 : row + 3, cols] = -scale * (mean_one - mean * rstd * mean_two)

    def chunk_one(j):
        return (
            [coef[i : i + 1, lanes(j)] for i in range(3)],
            [small[t : t + 1, lanes(j)] for t in range(9)],
            [stat_e[i : i + 1, lanes(j)] for i in (4, 5)],
        )

    def back_one(j, b, hoisted, totals):
        (c_flow, c_value, c_const), w, (scale, shift) = hoisted
        w_sums, gain_sum, bias_sum = list(totals[:9]), totals[9], totals[10]
        spread_grad = []
        for p in range(PIX):
            spread_grad.append(
                flow[p, images_at(b), lanes(j)] * c_flow
                + (depth[p, images_at(b), lanes(j)] * c_value + c_const)
            )
        act_one, slopes = [], []
        for p in range(PIX):
            half = expanded[p, images_at(b), lanes(j)] * scale + shift
            t = half_tanh(half)
            act_one.append(half * t + half)
            slopes.append(0.5 * ((1.0 + t) + half * (1.0 - t * t)))
        made = [None] * PIX
        for o, t, i in TAPS:
            w_sums[t] = w_sums[t] + spread_grad[o] * act_one[i]
            term = spread_grad[o] * w[t]
            made[i] = term if made[i] is None else made[i] + term
        for p in range(PIX):
            value = expanded[p, images_at(b), lanes(j)]
            result = made[p] * slopes[p]
            flow[p, images_at(b), lanes(j)] = result
            bias_sum = bias_sum + result
            gain_sum = gain_sum + result * value
        return tuple(w_sums) + (gain_sum, bias_sum)

    for g in range(GROUPS):
        cols = slice(g * GW, (g + 1) * GW)
        norm_coefs(g, ex_two[g].collect(), 0, 2, 11)
        if g == 0:
            r.spill_e.wait()
        between = ex_one[g - 1].relay if g else None
        over_tiles_and(
            plan, g * (GW // LANE), GW // LANE, between, chunk_one, back_one, 11, put_sums(0, 0), UN_ONE
        )
        ex_one[g].share(sums[10:11, cols], sums[9:10, cols])

    if layer:
        r.spill_d.fetch(layer - 1)
    for j in range(NJ):
        flat[pl.ds(ROW_D + j, 14, stride=NJ), :] = sums[0:14, j * LANE : (j + 1) * LANE]

    def turn(row):
        return pltpu.roll(jnp.broadcast_to(row, (8, LANE)), SQ, 1)[0:1, :]

    pieces = [turn(v[:, h * LANE : (h + 1) * LANE]) for v in (gain_three, bias_three) for h in (0, 1)]
    flat[ROW_S : ROW_S + 1, :] = jnp.where(is_low, grad_reduce_b, pieces[0])
    for i in range(3):
        flat[ROW_S + 1 + i : ROW_S + 2 + i, :] = jnp.where(is_low, pieces[i], pieces[i + 1])
    flat[ROW_S + 4 : ROW_S + 5, :] = pieces[3]
    ex_one[GROUPS - 1].relay()
    hooks[3]()

    for g in range(GROUPS):
        cols = slice(g * GW, (g + 1) * GW)
        norm_coefs(g, ex_one[g].collect(), 0, 0, 9)

        def into(m, carry, cols=cols):
            rows = pl.ds(pl.multiple_of(m * MBLK * n, MBLK * n), MBLK * n)
            spot = pl.ds(m * MBLK, MBLK)
            value = (
                flow[spot, :, cols] * coef[0:1, cols]
                + expanded[spot, :, cols] * coef[1:2, cols]
                + coef[2:3, cols]
            )
            low = value.reshape(MBLK * n, GW).astype(BF16)
            gated[rows, cols] = low
            grad_x[rows, :] += dot(low, we[:, cols], ((1,), (1,)))
            return carry

        lax.fori_loop(0, PIX // MBLK, into, 0)
        for j in range(g * (GW // LANE), (g + 1) * (GW // LANE)):
            flat[pl.ds(j, C, stride=NJ), :] = dot(
                turned[...], gated[:, j * LANE : (j + 1) * LANE]
            )
    if layer:
        r.spill_e.fetch(layer - 1)
    hooks[4]()
    packed[0 : plan.flat, :] = flat[0 : plan.flat, :].astype(BF16)


class Spill:
    def __init__(self, held, kept, sem):
        self.held, self.kept, self.sem = held, kept, sem

    def start(self, layer):
        self.copy = pltpu.make_async_copy(self.held, self.kept.at[layer], self.sem)
        self.copy.start()

    def fetch(self, layer):
        self.copy = pltpu.make_async_copy(self.kept.at[layer], self.held, self.sem)
        self.copy.start()

    def wait(self):
        self.copy.wait()


INPUTS = ("block", "w_own", "images", "per_image", "bias")
OUTPUTS = ("block_sums", "head_sums", "totals", "kept_e", "kept_d")


def scratch_of(plan):
    n, rows, hd = plan.images, plan.rows, plan.hd
    wide = 2 * GW // LANE
    vm = lambda shape, dtype=F32: pltpu.VMEM(shape, dtype)
    held = {
        "expanded": vm((PIX, n, E)),
        "depth": vm((PIX, n, E)),
        "flow": vm((PIX, n, E)),
        "gated": vm((rows, E), BF16),
        "stream": vm((rows, C)),
        "x_low": vm((rows, C), BF16),
        "turned": vm((LAYERS + 1, C, rows), BF16),
        "normed_three": vm((LAYERS, rows, C), BF16),
        "stat_e": vm((LAYERS, 8, E)),
        "stat_c": vm((LAYERS, 8, C)),
        "pooled": vm((LAYERS, n, E)),
        "presq": vm((LAYERS, n, LANE)),
        "gate": vm((LAYERS, n, E)),
        "we": vm((LAYERS, C, E), BF16),
        "wp": vm((LAYERS, E, C), BF16),
        "wr": vm((LAYERS, E, LANE), BF16),
        "wx": vm((LAYERS, LANE, E), BF16),
        "small": vm((LAYERS, 16, E)),
        "tail": vm((LAYERS, 8, C)),
        "w_head": vm((plan.head_flat, HEAD_W), BF16),
        "squeeze_grad": vm((n, E)),
        "sums": vm((16, E)),
        "coef": vm((8, E)),
        "flat": vm((max(plan.flat, LAYERS * (plan.chunk + 32)), LANE)),
        "stage": vm((max(plan.nf * plan.chunk, plan.flat), LANE), BF16),
        "spill_sems": pltpu.SemaphoreType.DMA((2,)),
    }
    for i in range(2 * GROUPS):
        held[f"pair{i}"] = vm((2, wide, LANE))
        held[f"wide{i}"] = vm((plan.devices // 2, wide, LANE))
        for k in range(4):
            held[f"wide{i}_{k}"] = pltpu.SemaphoreType.DMA(())
    held["thin"] = vm((plan.devices, 2 * C // LANE, LANE))
    held["thick"] = vm((plan.devices, KP // LANE, LANE))
    for name in ("thin", "thick"):
        held[name + "_send"] = pltpu.SemaphoreType.DMA(())
        held[name + "_recv"] = pltpu.SemaphoreType.DMA(())
    for name in ("block", "head"):
        for i in range(6):
            held[f"gather_{name}{i}"] = pltpu.SemaphoreType.DMA(())
    for name, unit in (("block", plan.layer_unit()), ("head", plan.head_unit())):
        for i, shape in enumerate(Reduction.scratch(unit)):
            held[f"reduce_{name}{i}"] = shape
    for i, shape in enumerate(Reduction.scratch(plan.layer_unit())[3:]):
        held[f"reduce_last{i}"] = shape
    return held


def step_kernel(plan, names, *refs):
    r = types.SimpleNamespace(**dict(zip(names, refs, strict=True)))
    held = vars(r)
    exchange = lambda name: Exchange(plan, held[name], held[name + "_send"], held[name + "_recv"])
    r.ex_wide = [
        PairedExchange(
            plan, held[f"pair{i}"], held[f"wide{i}"], [held[f"wide{i}_{k}"] for k in range(4)]
        )
        for i in range(2 * GROUPS)
    ]
    r.ex_thin, r.ex_bias = exchange("thin"), exchange("thick")
    r.spill_e = Spill(r.expanded, r.kept_e, r.spill_sems.at[0])
    r.spill_d = Spill(r.depth, r.kept_d, r.spill_sems.at[1])
    reduce_refs = {
        name: [held[f"reduce_{name}{i}"] for i in range(12)] for name in ("block", "head")
    }
    reduce_refs["last"] = reduce_refs["block"][:3] + [held[f"reduce_last{i}"] for i in range(9)]
    fs = lax.axis_index("fsdp")
    n = plan.images

    enter(plan)
    mine = [r.gated.at[pl.ds(0, plan.chunk), pl.ds(C + i * LANE, LANE)] for i in range(LAYERS)]
    images = r.gated.at[pl.ds(0, plan.rows), pl.ds(0, C)]
    take_images = pltpu.make_async_copy(r.images, images, r.spill_sems.at[0])
    take_images.start()
    take_head = pltpu.make_async_copy(
        r.w_own,
        r.w_head.at[pl.ds(pl.multiple_of(fs * plan.head_pad, 16), plan.head_pad)],
        r.spill_sems.at[1],
    )
    take_head.start()
    shift = spread_shards(plan, r.block, r.flat, mine)
    own_rows = pl.ds(pl.multiple_of(fs * plan.chunk, 16), plan.chunk)

    def gather_of(layer):
        r.stage[own_rows, :] = mine[layer][...]
        return Gather(
            plan, r.stage, plan.chunk, [held[f"gather_block{i}"] for i in range(6)]
        )

    def unpack(layer):
        unpack_weights(
            plan,
            r.stage,
            r.we.at[layer],
            r.wp.at[layer],
            r.wr.at[layer],
            r.wx.at[layer],
            r.small.at[layer],
            r.tail.at[layer],
            r.flat,
        )

    shift(0)
    gather = gather_of(0)
    entered(plan)
    gather.start_rest()
    for layer in range(1, LAYERS):
        shift(layer)
    take_images.wait()
    take_head.wait()
    columns = jnp.concatenate([r.per_image[...], jnp.zeros((8, LANE - n), F32)], axis=1).T
    weight, label, partner = (columns[0:n, i : i + 1] for i in range(3))
    label, partner = label.astype(jnp.int32), partner.astype(jnp.int32)
    label_row = r.per_image[1:2, :].astype(jnp.int32)
    gather.start_dp()
    mix_images(plan, images, partner, weight, r.stream, 0, PIX // 2)
    gather.start_core()
    mix_images(plan, images, partner, weight, r.stream, PIX // 2, PIX)
    gather.complete()
    unpack(0)

    head_gather = Gather(
        plan, r.w_head, plan.head_pad, [held[f"gather_head{i}"] for i in range(6)]
    )
    for layer in range(LAYERS):
        if layer < LAYERS - 1:
            box = []

            def begin(layer=layer, box=box):
                box.append(gather_of(layer + 1))
                box[0].start_rest()

            def arrive(layer=layer, box=box):
                box[0].complete()
                unpack(layer + 1)

            hooks = (
                begin,
                lambda box=box: box[0].start_dp(),
                lambda box=box: box[0].start_core(),
                arrive,
            )
        else:
            hooks = (
                head_gather.start_rest,
                head_gather.start_dp,
                head_gather.start_core,
                lambda: None,
            )
        forward_layer(plan, r, layer, hooks)
    head_gather.complete()
    head_layers(plan, r, label, label_row, partner, weight)

    head_work = Reduction(plan.head_unit(), r.w_head, r.head_sums, reduce_refs["head"])
    works = [
        Reduction(
            plan.layer_unit(),
            r.stage,
            r.block_sums.at[layer],
            reduce_refs["block" if layer else "last"],
        )
        for layer in range(LAYERS)
    ]

    def both(*steps):
        return lambda: [step() for step in steps]

    last = LAYERS - 1
    for layer in reversed(range(LAYERS)):
        if layer == last:
            hooks = (
                head_work.start_core,
                head_work.start_dp,
                lambda: None,
                head_work.start_rest,
                lambda: None,
            )
        else:
            work = works[layer + 1]
            hooks = (
                work.start_core,
                work.start_dp,
                work.start_rest,
                work.start_copies,
                work.complete,
            )
            if layer == last - 1:
                hooks = (
                    hooks[0],
                    both(hooks[1], head_work.start_copies),
                    hooks[2],
                    hooks[3],
                    both(hooks[4], head_work.complete),
                )
        backward_layer(plan, r, layer, hooks)
    works[0].start_core()
    works[0].start_dp()
    works[0].start_rest()
    works[0].start_copies()
    works[0].complete()
    for e in r.ex_wide + [r.ex_thin, r.ex_bias]:
        e.finish()


def train_step(plan, block, w_own, images, per_image, bias):
    held = scratch_of(plan)
    block_unit, head_unit = plan.layer_unit(), plan.head_unit()
    big = (PIX, plan.images, E)
    anywhere = pl.BlockSpec(memory_space=pl.ANY)
    return pl.pallas_call(
        functools.partial(step_kernel, plan, INPUTS + OUTPUTS + tuple(held)),
        out_shape=(
            jax.ShapeDtypeStruct((LAYERS, block_unit.owned, LANE), BF16),
            jax.ShapeDtypeStruct((head_unit.owned, HEAD_W), BF16),
            jax.ShapeDtypeStruct((1, KP), F32),
            jax.ShapeDtypeStruct((LAYERS,) + big, F32),
            jax.ShapeDtypeStruct((LAYERS - 1,) + big, F32),
        ),
        in_specs=[VM, anywhere, anywhere, VM, VM],
        out_specs=(VM, VM, VM, anywhere, anywhere),
        scratch_shapes=list(held.values()),
        compiler_params=pltpu.CompilerParams(
            collective_id=1, has_side_effects=True, vmem_limit_bytes=VMEM_LIMIT
        ),
        name="train_step",
    )(block, w_own, images, per_image, bias)


def adam_update(master, first, second, average, grad):
    first_new = BETA_ONE * first + (1.0 - BETA_ONE) * grad
    second_new = BETA_TWO * second + (1.0 - BETA_TWO) * grad * grad
    fix_one = 1.0 - BETA_ONE**STEP
    fix_two = 1.0 - BETA_TWO**STEP
    master_new = master * (1.0 - RATE * DECAY_WEIGHT) - RATE * (first_new / fix_one) / (
        jnp.sqrt(second_new / fix_two) + EPS_ADAM
    )
    average_new = EMA_RATE * average + (1.0 - EMA_RATE) * master_new
    return (master_new, first_new, second_new, average_new)


def on_device(mesh, images, partner, mix_weight, labels, *states):
    block, head_state, bias_state = states[0:4], states[4:8], states[8:12]
    row = C + 2 + K
    plan = Plan(mesh, images.shape[0], head_state[0].shape[0] // row)
    half = (plan.hd // LANE + 1) // 2 * LANE
    plan.head_groups = [(0, half), (half, plan.hd - half)]
    start = lax.axis_index("fsdp") * plan.shard
    offset = start - start // (16 * LANE) * (16 * LANE)
    grid = head_state[0].astype(BF16).reshape(plan.head_rows, row)
    grid = jnp.concatenate(
        [
            grid[:, : C + 2],
            jnp.zeros((plan.head_rows, LANE - 2), BF16),
            grid[:, C + 2 :],
            jnp.zeros((plan.head_rows, KP - K), BF16),
        ],
        axis=1,
    )
    grid = jnp.pad(grid, ((0, plan.head_pad - plan.head_rows), (0, 0)))
    bias = jnp.pad(bias_state[0], (0, KP - K)).reshape(1, KP)
    per_image = jnp.stack(
        [mix_weight, labels.astype(F32), partner.astype(F32)] + [jnp.zeros_like(mix_weight)] * 5
    )
    block_grad, head_grad, totals = train_step(
        plan, block[0], grid, images.reshape(plan.rows, C), per_image, bias
    )[:3]
    loss_sum = totals[0, KP - 1]
    grad_bias = totals[0, :K]
    block_grad = lax.dynamic_slice(
        block_grad.reshape(LAYERS, plan.chunk * LANE), (0, offset), (LAYERS, plan.shard)
    ).astype(F32)
    head_grad = head_grad[: plan.head_rows].astype(F32)
    head_grad = jnp.concatenate(
        [head_grad[:, : C + 2], head_grad[:, C + LANE : C + LANE + K]], axis=1
    ).reshape(-1)
    return (
        (loss_sum,)
        + adam_update(*block, block_grad)
        + adam_update(*head_state, head_grad)
        + adam_update(*bias_state, grad_bias)
    )


def solution(mesh):
    data = P(("dp", "fsdp"))
    states = (P(None, "fsdp"),) * 4 + (P("fsdp"),) * 4 + (P(),) * 4
    return jax.shard_map(
        functools.partial(on_device, mesh),
        mesh=mesh,
        in_specs=(P(("dp", "fsdp"), None, None), data, data, data) + states,
        out_specs=(P(),) + states,
        check_vma=False,
    )
```

```python
import functools
import types

import jax
import jax.numpy as jnp
from jax import lax
from jax.experimental import pallas as pl
from jax.experimental.pallas import tpu as pltpu
from jax.sharding import PartitionSpec as P

C = 256
E = 1536
SQ = 64
K = 1000
SIDE = 4
PIX = 16
LAYERS = 3
STEP = 5
EPS_NORM = 0.001
RATE = 0.05
DECAY_WEIGHT = 0.05
BETA_ONE = 0.5
BETA_TWO = 0.5
EPS_ADAM = 1e-08
EMA_RATE = 0.5
SMOOTHING = 0.1

LANE = 128
KP = 1024
HEAD_W = C + LANE + KP
PB = 2 * C * E + 2 * E * SQ + 14 * E + SQ + 2 * C
ROW_P = C * E // LANE
ROW_R = ROW_P + E * C // LANE
ROW_X = ROW_R + E * SQ // LANE
ROW_D = ROW_X + SQ * E // LANE
ROW_S = ROW_D + 14 * E // LANE
NJ = E // LANE
GROUPS = 2
GW = E // GROUPS
MBLK = 4
UN_SPREAD, UN_ACT, UN_HBACK, UN_GATE, UN_TWO, UN_ONE = 2, 4, 4, 4, 2, 1

MESH = pl.DeviceIdType.MESH
F32 = jnp.float32
BF16 = jnp.bfloat16
VMEM_LIMIT = 127 * 512 * 1024
VM = pl.BlockSpec(memory_space=pltpu.VMEM)


def ceil_to(value, unit):
    return -(-value // unit) * unit


class Plan:
    def __init__(self, mesh, images, head_rows):
        self.nd = mesh.shape["dp"]
        self.nf = mesh.shape["fsdp"]
        self.devices = self.nd * self.nf
        self.images = images
        self.rows = images * PIX
        self.count = float(self.rows * self.devices)
        self.shard = PB // self.nf
        self.base = [(self.shard * f // LANE) // 16 * 16 for f in range(self.nf)]
        self.chunk = ceil_to(-(-self.shard // LANE) + 17, 16 * self.nd)
        self.flat = self.base[-1] + self.chunk
        self.head_pad = ceil_to(head_rows, 16)
        self.hd = self.head_pad * self.nf
        self.head_rows = head_rows
        self.head_part = ceil_to(-(-head_rows // self.nd), 16)
        self.head_flat = self.head_pad * (self.nf - 1) + self.head_part * self.nd
        self.depth = self.nf // 2

    def layer_unit(self):
        return Unit(self, LANE, self.chunk // self.nd, self.flat, lambda f: self.shard * f // (16 * LANE) * 16)

    def head_unit(self):
        return Unit(self, HEAD_W, self.head_part, self.head_flat, lambda f: self.head_pad * f)


class Unit:
    def __init__(self, plan, width, part, rows, base):
        self.plan, self.width, self.part, self.rows, self.base = plan, width, part, rows, base
        self.owned = part * plan.nd


def dot(a, b, dims=((1,), (0,))):
    return lax.dot_general(a, b, (dims, ((), ())), preferred_element_type=F32)


def halves_of(value):
    high = value.astype(BF16)
    return high, (value - high.astype(F32)).astype(BF16)


def dot_rows(value, low, dims=((1,), (0,))):
    n = value.shape[0]
    both = dot(jnp.concatenate(halves_of(value), axis=0), low, dims)
    return both[0:n, :] + both[n:, :]


def dot_outer(a, b):
    a_high, a_low = halves_of(a)
    b_high, b_low = halves_of(b)
    left = jnp.concatenate([a_high, a_low, a_high], axis=0)
    right = jnp.concatenate([b_high, b_high, b_low], axis=0)
    return dot(left, right, ((0,), (0,)))


def row_sum(value):
    return jnp.sum(value, axis=0, keepdims=True)


def over_peers(plan, body):
    dp, fs = lax.axis_index("dp"), lax.axis_index("fsdp")
    deep, low = fs // 2, dp * 2 + lax.rem(fs, 2)
    near = 2 * plan.nd
    top = jnp.where(2 * deep >= plan.depth, 1, 0)

    def at(k, i, carry):
        z = top * k + (1 - top) * (plan.depth - 1 - k)
        j = lax.rem(low + i, near)

        @pl.when((z != deep) | (j != low))
        def _():
            body((j // 2, 2 * z + lax.rem(j, 2)))

        return carry

    for k in range(plan.depth):
        lax.fori_loop(0, near, functools.partial(at, k), 0)


def my_slot(plan):
    return lax.axis_index("dp") * plan.nf + lax.axis_index("fsdp")


def enter(plan):
    barrier = pltpu.get_barrier_semaphore()
    over_peers(
        plan,
        lambda device: pl.semaphore_signal(
            barrier, inc=1, device_id=device, device_id_type=MESH
        ),
    )


def entered(plan):
    pl.semaphore_wait(pltpu.get_barrier_semaphore(), plan.devices - 1)


class Exchange:
    def __init__(self, plan, buf, send, recv):
        self.plan, self.buf, self.send, self.recv, self.used = plan, buf, send, recv, False

    def share(self, first, second):
        plan, buf, send, recv = self.plan, self.buf, self.send, self.recv
        if self.used:
            self.finish()
        self.used = True
        half = first.shape[1] // LANE
        self.rows = 2 * half
        mine = my_slot(plan)
        for r in range(half):
            cols = slice(r * LANE, (r + 1) * LANE)
            buf[mine, r : r + 1, :] = first[:, cols]
            buf[mine, half + r : half + r + 1, :] = second[:, cols]
        over_peers(
            plan,
            lambda device: pltpu.make_async_remote_copy(
                src_ref=buf.at[mine, pl.ds(0, 2 * half)],
                dst_ref=buf.at[mine, pl.ds(0, 2 * half)],
                send_sem=send,
                recv_sem=recv,
                device_id=device,
                device_id_type=MESH,
            ).start(),
        )

    def others(self):
        return self.buf.at[pl.ds(1, self.plan.devices - 1), pl.ds(0, self.rows)]

    def collect(self):
        pltpu.make_async_copy(self.others(), self.others(), self.recv).wait()
        total = jnp.sum(self.buf[:, 0 : self.rows, :], axis=0)
        rows = [total[r : r + 1, :] for r in range(self.rows)]
        half = self.rows // 2
        return jnp.concatenate(rows[:half], axis=1), jnp.concatenate(rows[half:], axis=1)

    def finish(self):
        pltpu.make_async_copy(self.others(), self.others(), self.send).wait()


class PairedExchange:
    def __init__(self, plan, pair, buf, sems):
        self.plan, self.pair, self.buf, self.sems, self.used = plan, pair, buf, sems, False
        self.dp, self.fs = lax.axis_index("dp"), lax.axis_index("fsdp")
        self.core, self.deep = lax.rem(self.fs, 2), self.fs // 2
        self.mine = self.dp * plan.depth + self.deep

    def share(self, first, second):
        if self.used:
            self.finish()
        self.used = True
        half = first.shape[1] // LANE
        self.rows = 2 * half
        for i in range(half):
            cols = slice(i * LANE, (i + 1) * LANE)
            self.pair[0, i : i + 1, :] = first[:, cols]
            self.pair[0, half + i : half + i + 1, :] = second[:, cols]
        rows = pl.ds(0, self.rows)
        pltpu.make_async_remote_copy(
            src_ref=self.pair.at[0, rows],
            dst_ref=self.pair.at[1, rows],
            send_sem=self.sems[0],
            recv_sem=self.sems[1],
            device_id=(self.dp, 2 * self.deep + 1 - self.core),
            device_id_type=MESH,
        ).start()

    def relay(self):
        plan, rows = self.plan, pl.ds(0, self.rows)
        got = self.pair.at[1, rows]
        pltpu.make_async_copy(got, got, self.sems[1]).wait()
        self.buf[self.mine, rows, :] = self.pair[0, rows, :] + self.pair[1, rows, :]
        top = jnp.where(2 * self.deep >= plan.depth, 1, 0)
        for k in range(plan.depth):
            z = top * k + (1 - top) * (plan.depth - 1 - k)

            def go(i, carry, z=z):
                d = lax.rem(self.dp + i, plan.nd)

                @pl.when((z != self.deep) | (d != self.dp))
                def _():
                    pltpu.make_async_remote_copy(
                        src_ref=self.buf.at[self.mine, rows],
                        dst_ref=self.buf.at[self.mine, rows],
                        send_sem=self.sems[2],
                        recv_sem=self.sems[3],
                        device_id=(d, 2 * z + self.core),
                        device_id_type=MESH,
                    ).start()

                return carry

            lax.fori_loop(0, plan.nd, go, 0)

    def others(self):
        return self.buf.at[pl.ds(1, self.plan.devices // 2 - 1), pl.ds(0, self.rows)]

    def collect(self):
        pltpu.make_async_copy(self.others(), self.others(), self.sems[3]).wait()
        total = jnp.sum(self.buf[:, 0 : self.rows, :], axis=0)
        rows = [total[i : i + 1, :] for i in range(self.rows)]
        half = self.rows // 2
        return jnp.concatenate(rows[:half], axis=1), jnp.concatenate(rows[half:], axis=1)

    def finish(self):
        sent = self.pair.at[0, pl.ds(0, self.rows)]
        pltpu.make_async_copy(sent, sent, self.sems[0]).wait()
        pltpu.make_async_copy(self.others(), self.others(), self.sems[2]).wait()


def moments(plan, pair):
    mean = pair[0] / plan.count
    return mean, lax.rsqrt(pair[1] / plan.count - mean * mean + EPS_NORM)


class Reduction:
    def __init__(self, unit, source, result, refs, skip=0, size=None):
        self.unit, self.source, self.result = unit, source, result
        self.skip, self.size = skip, size or unit.part
        rows = pl.ds(skip, self.size)
        self.got_core, self.got_dp = (ref.at[:, :, rows] for ref in refs[:2])
        self.sum_dp, self.got_rest = (ref.at[:, rows] for ref in refs[2:4])
        self.send, self.recv = refs[4:8], refs[8:12]
        plan = unit.plan
        self.dp, self.fs = lax.axis_index("dp"), lax.axis_index("fsdp")
        self.core, self.deep = lax.rem(self.fs, 2), self.fs // 2
        self.nd, self.nz = plan.nd, plan.depth

    @staticmethod
    def scratch(unit):
        plan = unit.plan
        nd, nz, w, part = plan.nd, plan.depth, unit.width, unit.part
        return [
            pltpu.VMEM((nz, nd, part, w), BF16),
            pltpu.VMEM((nd - 1, nz, part, w), BF16),
            pltpu.VMEM((nz, part, w), BF16),
            pltpu.VMEM((nz - 1, part, w), BF16),
        ] + [pltpu.SemaphoreType.DMA(())] * 8

    def push(self, stage, source, target, device):
        pltpu.make_async_remote_copy(
            src_ref=source,
            dst_ref=target,
            send_sem=self.send[stage],
            recv_sem=self.recv[stage],
            device_id=device,
            device_id_type=MESH,
        ).start()

    def rows_of(self, f, d=0):
        return pl.multiple_of(self.unit.base(f) + d * self.unit.part + self.skip, 16)

    def start_core(self):
        def go(z, carry):
            for d in range(self.nd):
                self.push(
                    0,
                    self.source.at[pl.ds(self.rows_of(2 * z + 1 - self.core, d), self.size)],
                    self.got_core.at[z, d],
                    (self.dp, 2 * self.deep + 1 - self.core),
                )
            return carry

        lax.fori_loop(0, self.nz, go, 0)

    def wait(self, sem, ref):
        pltpu.make_async_copy(ref, ref, sem).wait()

    def start_dp(self):
        self.wait(self.recv[0], self.got_core)

        def add(z, carry):
            for d in range(self.nd):
                own = self.source[pl.ds(self.rows_of(2 * z + self.core, d), self.size), :]
                self.got_core[z, d] = (own.astype(F32) + self.got_core[z, d].astype(F32)).astype(BF16)
            return carry

        lax.fori_loop(0, self.nz, add, 0)

        def go(z, carry):
            for i in range(1, self.nd):
                other = lax.rem(self.dp + i, self.nd)
                self.push(1, self.got_core.at[z, other], self.got_dp.at[i - 1, z], (other, self.fs))
            return carry

        lax.fori_loop(0, self.nz, go, 0)

    def start_rest(self):
        self.wait(self.recv[1], self.got_dp)
        self.wait(self.send[1], self.got_dp)

        def add(z, carry):
            total = self.got_core[z, self.dp].astype(F32)
            for i in range(self.nd - 1):
                total = total + self.got_dp[i, z].astype(F32)
            self.sum_dp[z] = total.astype(BF16)
            return carry

        lax.fori_loop(0, self.nz, add, 0)
        for i in range(1, self.nz):
            other = lax.rem(self.deep + i, self.nz)
            self.push(2, self.sum_dp.at[other], self.got_rest.at[i - 1], (self.dp, 2 * other + self.core))

    def start_copies(self):
        self.wait(self.recv[2], self.got_rest)
        total = self.sum_dp[self.deep].astype(F32)
        for i in range(self.nz - 1):
            total = total + self.got_rest[i].astype(F32)
        rows = pl.ds(pl.multiple_of(self.dp * self.unit.part + self.skip, 16), self.size)
        self.result[rows, :] = total.astype(BF16)
        for i in range(1, self.nd):
            other = lax.rem(self.dp + i, self.nd)
            self.push(3, self.result.at[rows], self.result.at[rows], (other, self.fs))

    def complete(self):
        others = self.result.at[pl.ds(0, (self.nd - 1) * self.size)]
        self.wait(self.recv[3], others)
        self.wait(self.send[0], self.got_core)
        self.wait(self.send[2], self.got_rest)
        self.wait(self.send[3], others)


def taps():
    found = []
    for y in range(SIDE):
        for x in range(SIDE):
            for a in range(3):
                for b in range(3):
                    iy, ix = y + a - 1, x + b - 1
                    if 0 <= iy < SIDE and 0 <= ix < SIDE:
                        found.append((y * SIDE + x, 3 * a + b, iy * SIDE + ix))
    return found


TAPS = taps()


def half_tanh(half):
    return jnp.tanh(half)


def silu(z):
    half = 0.5 * z
    return half * half_tanh(half) + half


def sigmoid(z):
    return 0.5 * half_tanh(0.5 * z) + 0.5


def silu_slope(z):
    half = 0.5 * z
    t = half_tanh(half)
    return 0.5 * (1.0 + t + half * (1.0 - t * t))


def lanes(j):
    return pl.ds(pl.multiple_of(j * LANE, LANE), LANE)


def images_at(b):
    return pl.ds(pl.multiple_of(b * 8, 8), 8)


def over_tiles(plan, first_chunk, chunks, per_chunk, body, n_sums, store_sums, unroll=1):
    blocks = plan.images // 8

    def chunk_step(jj, carry):
        j = first_chunk + jj
        hoisted = per_chunk(j)

        def step(b, sums):
            for u in range(unroll):
                sums = body(j, b * unroll + u, hoisted, sums)
            return sums

        zero = tuple(jnp.zeros((8, LANE), F32) for _ in range(n_sums))
        store_sums(j, lax.fori_loop(0, blocks // unroll, step, zero))
        return carry

    lax.fori_loop(0, chunks, chunk_step, 0)


def over_tiles_and(plan, first_chunk, chunks, between, *rest):
    if between is None:
        over_tiles(plan, first_chunk, chunks, *rest)
    else:
        over_tiles(plan, first_chunk, 2, *rest)
        between()
        over_tiles(plan, first_chunk + 2, chunks - 2, *rest)


class Gather:
    def __init__(self, plan, target, rows, sems, half=None):
        self.plan, self.target, self.rows = plan, target, rows
        tiles = rows // 16
        counts = [tiles // plan.nd + (1 if d < tiles % plan.nd else 0) for d in range(plan.nd)]
        self.parts = [(16 * sum(counts[:d]), 16 * counts[d]) for d in range(plan.nd)]
        if half is not None:
            first = ceil_to(self.parts[0][1] // 2, 16)
            ends = ((0, first), (first, self.parts[0][1]))[half]
            self.parts = [(start + ends[0], ends[1] - ends[0]) for start, _ in self.parts]
        self.whole = half is None
        self.covered = sum(size for _, size in self.parts)
        self.send, self.recv = sems[0:3], sems[3:6]
        self.dp, self.fs = lax.axis_index("dp"), lax.axis_index("fsdp")
        self.core, self.deep = lax.rem(self.fs, 2), self.fs // 2

    def by_part(self, body):
        if len({size for _, size in self.parts}) == 1:
            body(self.parts[0][0] + self.dp * (self.rows // self.plan.nd), self.parts[0][1])
            return
        for d, (start, size) in enumerate(self.parts):
            pl.when(self.dp == d)(functools.partial(body, start, size))

    def at(self, deep, start, size):
        begin = (2 * deep + self.core) * self.rows + start
        return self.target.at[pl.ds(pl.multiple_of(begin, 16), size)]

    def push(self, stage, ref, device):
        pltpu.make_async_remote_copy(
            src_ref=ref,
            dst_ref=ref,
            send_sem=self.send[stage],
            recv_sem=self.recv[stage],
            device_id=device,
            device_id_type=MESH,
        ).start()

    def wait(self, sem, rows):
        if rows:
            span = self.target.at[pl.ds(0, rows)]
            pltpu.make_async_copy(span, span, sem).wait()

    def start_rest(self):
        def body(start, size):
            def go(i, carry):
                other = lax.rem(self.deep + i, self.plan.depth)
                self.push(0, self.at(self.deep, start, size), (self.dp, 2 * other + self.core))
                return carry

            if size:
                lax.fori_loop(1, self.plan.depth, go, 0)

        self.by_part(body)

    def start_dp(self):
        plan = self.plan

        def body(start, size):
            self.wait(self.recv[0], (plan.depth - 1) * size)

            def go(i, carry):
                other = lax.rem(self.deep + i, plan.depth)
                for k in range(1, plan.nd):
                    self.push(
                        1, self.at(other, start, size), (lax.rem(self.dp + k, plan.nd), self.fs)
                    )
                return carry

            if size:
                lax.fori_loop(1, plan.depth, go, 0)

        self.by_part(body)

    def start_core(self):
        plan = self.plan
        self.by_part(
            lambda start, size: self.wait(self.recv[1], (plan.depth - 1) * (self.covered - size))
        )

        def go(z, carry):
            for start, size in [(0, self.rows)] if self.whole else self.parts:
                self.push(2, self.at(z, start, size), (self.dp, 2 * self.deep + 1 - self.core))
            return carry

        lax.fori_loop(0, plan.depth, go, 0)

    def complete(self):
        plan = self.plan
        self.wait(self.recv[2], plan.depth * self.covered)

        def body(start, size):
            self.wait(self.send[0], (plan.depth - 1) * size)
            self.wait(self.send[1], (plan.depth - 1) * (plan.nd - 1) * size)

        self.by_part(body)
        self.wait(self.send[2], plan.depth * self.covered)


def spread_shards(plan, block, flat, mine):
    start = lax.axis_index("fsdp") * plan.shard
    offset = start - start // (16 * LANE) * (16 * LANE)
    down, turn = offset // LANE, lax.rem(offset, LANE)
    full = plan.shard // LANE
    rest = plan.shard - full * LANE
    size = plan.chunk + 32
    lane = lax.broadcasted_iota(jnp.int32, (16, LANE), 1)
    for layer in range(LAYERS):
        flat[layer * size : layer * size + 24, :] = jnp.zeros((24, LANE), F32)

    def take(layer, i, count):
        piece = block[:, pl.ds(pl.multiple_of(i * 8 * LANE, LANE), count * LANE)]
        rows = [piece[layer : layer + 1, k * LANE : (k + 1) * LANE] for k in range(count)]
        at = pl.ds(pl.multiple_of(layer * size + 24 + i * 8, 8), count)
        flat[at, :] = jnp.concatenate(rows, axis=0) if count > 1 else rows[0]

    def fill(layer):
        def step(i, carry):
            take(layer, i, 8)
            return carry

        lax.fori_loop(0, full // 8, step, 0)
        if full % 8:
            take(layer, full // 8, full % 8)
        at = layer * size + 24 + full
        if rest:
            last = block[layer : layer + 1, full * LANE : full * LANE + rest]
            flat[at : at + 1, :] = jnp.concatenate([last, jnp.zeros((1, LANE - rest), F32)], axis=1)
            at += 1
        end = (layer + 1) * size
        flat[at:end, :] = jnp.zeros((end - at, LANE), F32)

    def shift(layer):
        fill(layer)

        def go(i, carry):
            begin = layer * size + 24 + i * 16 - down
            here = pltpu.roll(flat[pl.ds(begin, 16), :], turn, 1)
            before = pltpu.roll(flat[pl.ds(begin - 1, 16), :], turn, 1)
            value = jnp.where(lane >= turn, here, before)
            mine[layer][pl.ds(pl.multiple_of(i * 16, 16), 16), :] = value.astype(BF16)
            return carry

        lax.fori_loop(0, plan.chunk // 16, go, 0)

    return shift


def unpack_weights(plan, got, we, wp, wr, wx, small, tail, flat):
    lane = lax.broadcasted_iota(jnp.int32, (1, LANE), 1)
    low = lane < SQ
    for f in range(plan.nf):
        base, at = plan.base[f], f * plan.chunk
        head = got[at : at + 16, :].astype(F32)
        if f:
            head = head + flat[base : base + 16, :]
        flat[base : base + 16, :] = head
        flat[base + 16 : base + plan.chunk, :] = got[at + 16 : at + plan.chunk, :].astype(F32)
    for j in range(NJ):
        cols = slice(j * LANE, (j + 1) * LANE)
        we[:, cols] = flat[pl.ds(j, C, stride=NJ), :].astype(BF16)
        wx[0:SQ, cols] = flat[pl.ds(ROW_X + j, SQ, stride=NJ), :].astype(BF16)
        wx[SQ:LANE, cols] = jnp.zeros((LANE - SQ, LANE), BF16)
        small[0:14, cols] = flat[pl.ds(ROW_D + j, 14, stride=NJ), :]
        small[14:16, cols] = jnp.zeros((2, LANE), F32)
    for h in range(C // LANE):
        wp[:, h * LANE : (h + 1) * LANE] = flat[pl.ds(ROW_P + h, E, stride=2), :].astype(BF16)
    pairs = flat[ROW_R:ROW_X, :]
    evens, odds = jnp.where(low, pairs, 0.0), jnp.where(low, pltpu.roll(pairs, SQ, 1), 0.0)
    flat[pl.ds(0, E // 2, stride=2), :] = evens
    flat[pl.ds(1, E // 2, stride=2), :] = odds
    wr[...] = flat[0:E, :].astype(BF16)
    rows = [flat[ROW_S + i : ROW_S + i + 1, :] for i in range(5)]
    turned = [pltpu.roll(jnp.broadcast_to(r, (8, LANE)), SQ, 1)[0:1, :] for r in rows]
    tail[...] = jnp.zeros((8, C), F32)
    tail[0:1, 0:LANE] = jnp.where(low, rows[0], 0.0)
    for i, at in ((1, 0), (2, 2)):
        tail[i : i + 1, 0:LANE] = jnp.where(low, turned[at], turned[at + 1])
        tail[i : i + 1, LANE:C] = jnp.where(low, turned[at + 1], turned[at + 2])


def mix_images(plan, images, partner, share_one, stream, first, last):
    n, rows = plan.images, plan.rows
    place = lax.broadcasted_iota(jnp.int32, (n, rows), 1)
    own = lax.broadcasted_iota(jnp.int32, (n, rows), 0) * PIX
    chosen = partner * PIX

    def go(p, carry):
        mine = dot(jnp.where(place == own + p, 1.0, 0.0).astype(BF16), images[...])
        theirs = dot(jnp.where(place == chosen + p, 1.0, 0.0).astype(BF16), images[...])
        at = pl.ds(pl.multiple_of(p * n, n), n)
        stream[at, :] = share_one * mine + (1.0 - share_one) * theirs
        return carry

    lax.fori_loop(first, last, go, 0)


def forward_layer(plan, r, layer, hooks):
    x, expanded, depth, act, sums, x_low = r.stream, r.expanded, r.depth, r.flow, r.sums, r.x_low
    normed_three, stat_e, stat_c = r.normed_three.at[layer], r.stat_e.at[layer], r.stat_c.at[layer]
    pooled, presq, gate, turned = r.pooled.at[layer], r.presq.at[layer], r.gate.at[layer], r.turned.at[layer]
    we, wp, wr, wx = r.we.at[layer], r.wp.at[layer], r.wr.at[layer], r.wx.at[layer]
    small, tail = r.small.at[layer], r.tail.at[layer]
    ex_one, ex_two, ex_three = r.ex_wide[0:GROUPS], r.ex_wide[GROUPS : 2 * GROUPS], r.ex_thin
    n = plan.images
    x_low[...] = x[...].astype(BF16)
    for g in range(GROUPS):
        cols = slice(g * GW, (g + 1) * GW)

        def expand(m, carry, cols=cols):
            rows = pl.ds(pl.multiple_of(m * MBLK * n, MBLK * n), MBLK * n)
            value = dot(x_low[rows, :], we[:, cols])
            expanded[pl.ds(m * MBLK, MBLK), :, cols] = value.reshape(MBLK, n, GW)
            return (
                carry[0] + jnp.sum(value.reshape(-1, 8, GW), axis=0),
                carry[1] + jnp.sum((value * value).reshape(-1, 8, GW), axis=0),
            )

        zero = jnp.zeros((8, GW), F32)
        s, q = lax.fori_loop(0, PIX // MBLK, expand, (zero, zero))
        if g:
            ex_one[g - 1].relay()
        ex_one[g].share(row_sum(s), row_sum(q))
    turned[...] = x[...].T.astype(BF16)
    ex_one[GROUPS - 1].relay()

    def put_sums(j, totals):
        for i, t in enumerate(totals):
            sums[i : i + 1, lanes(j)] = row_sum(t)

    for g in range(GROUPS):
        cols = slice(g * GW, (g + 1) * GW)
        mean, rstd = moments(plan, ex_one[g].collect())
        if g == 0:
            r.spill_e.start(layer)
            if layer:
                r.spill_d.wait()
        stat_e[0:1, cols] = mean
        stat_e[1:2, cols] = rstd
        scale = rstd * small[9:10, cols]
        stat_e[4:5, cols] = 0.5 * scale
        stat_e[5:6, cols] = 0.5 * (small[10:11, cols] - mean * scale)

        def chunk(j):
            return (
                stat_e[4:5, lanes(j)],
                stat_e[5:6, lanes(j)],
                [small[t : t + 1, lanes(j)] for t in range(9)],
            )

        def spread(j, b, hoisted, totals):
            scale, shift, w = hoisted
            act_one = []
            for p in range(PIX):
                half = expanded[p, images_at(b), lanes(j)] * scale + shift
                act_one.append(half * half_tanh(half) + half)
            made = [None] * PIX
            for o, t, i in TAPS:
                term = act_one[i] * w[t]
                made[o] = term if made[o] is None else made[o] + term
            s, q = totals
            for p in range(PIX):
                depth[p, images_at(b), lanes(j)] = made[p]
                s = s + made[p]
                q = q + made[p] * made[p]
            return s, q

        between = ex_two[g - 1].relay if g else None
        over_tiles_and(
            plan, g * (GW // LANE), GW // LANE, between, chunk, spread, 2, put_sums, UN_SPREAD
        )
        ex_two[g].share(sums[0:1, cols], sums[1:2, cols])
        if g == 0:
            hooks[0]()
    ex_two[GROUPS - 1].relay()
    hooks[1]()

    for g in range(GROUPS):
        cols = slice(g * GW, (g + 1) * GW)
        mean, rstd = moments(plan, ex_two[g].collect())
        if g == 0:
            if layer < LAYERS - 1:
                r.spill_d.start(layer)
        stat_e[2:3, cols] = mean
        stat_e[3:4, cols] = rstd
        scale = rstd * small[11:12, cols]
        stat_e[6:7, cols] = 0.5 * scale
        stat_e[7:8, cols] = 0.5 * (small[12:13, cols] - mean * scale)

        def chunk_two(j):
            return stat_e[6:7, lanes(j)], stat_e[7:8, lanes(j)]

        def activate(j, b, hoisted, totals):
            scale, shift = hoisted
            total = None
            for p in range(PIX):
                half = depth[p, images_at(b), lanes(j)] * scale + shift
                made = half * half_tanh(half) + half
                act[p, images_at(b), lanes(j)] = made
                total = made if total is None else total + made
            pooled[images_at(b), lanes(j)] = total * (1.0 / PIX)
            return totals

        over_tiles(
            plan, g * (GW // LANE), GW // LANE, chunk_two, activate, 0, lambda j, s: None, UN_ACT
        )
    reduced = dot_rows(pooled[...], wr[...]) + tail[0:1, 0:LANE]
    presq[...] = reduced
    gate[...] = sigmoid(dot_rows(silu(reduced), wx[...]) + small[13:14, :])

    hooks[2]()
    r.spill_e.wait()

    def project(m, carry):
        gated = (act[pl.ds(m * MBLK, MBLK), :, :] * gate[...][None]).astype(BF16)
        value = dot(gated.reshape(MBLK * n, E), wp[...])
        expanded[pl.ds(m * MBLK, MBLK), :, 0:C] = value.reshape(MBLK, n, C)
        return (
            carry[0] + jnp.sum(value.reshape(-1, 8, C), axis=0),
            carry[1] + jnp.sum((value * value).reshape(-1, 8, C), axis=0),
        )

    zero = jnp.zeros((8, C), F32)
    s, q = lax.fori_loop(0, PIX // MBLK, project, (zero, zero))
    ex_three.share(row_sum(s), row_sum(q))
    hooks[3]()
    mean, rstd = moments(plan, ex_three.collect())
    stat_c[...] = jnp.zeros((8, C), F32)
    stat_c[0:1, :] = mean
    stat_c[1:2, :] = rstd
    normed = (expanded[:, :, 0:C].reshape(n * PIX, C) - mean) * rstd
    normed_three[...] = normed.astype(BF16)
    x[...] = x[...] + normed * tail[1:2, :] + tail[2:3, :]


def head_layers(plan, r, label, label_row, partner, weight):
    x, x_low, turned, bias, totals_out = r.stream, r.x_low, r.turned.at[LAYERS], r.bias, r.totals
    w_head = grad_head = r.w_head
    hidden, slope, low_grad, pool, stat = r.expanded, r.flow, r.gated, r.squeeze_grad, r.coef
    sums, gain, grad_x = r.sums, r.sums.at[pl.ds(8, 8)], r.stream
    hd, n = plan.hd, plan.images
    halves = plan.head_groups
    ng = len(halves)
    ex_stat, ex_grad, ex_bias = r.ex_wide[0:ng], r.ex_wide[GROUPS : GROUPS + ng], r.ex_bias
    x_low[...] = x[...].astype(BF16)
    gain[:, 0:hd] = w_head[0:hd, C : C + LANE].astype(F32).T[0:8, :]
    for g, (start, width) in enumerate(halves):
        cols = slice(start, start + width)

        def convolve(m, carry, cols=cols, width=width):
            rows = pl.ds(pl.multiple_of(m * MBLK * n, MBLK * n), MBLK * n)
            value = dot(x_low[rows, :], w_head[cols, 0:C], ((1,), (1,)))
            hidden[pl.ds(m * MBLK, MBLK), :, cols] = value.reshape(MBLK, n, width)
            return (
                carry[0] + jnp.sum(value.reshape(-1, 8, width), axis=0),
                carry[1] + jnp.sum((value * value).reshape(-1, 8, width), axis=0),
            )

        zero = jnp.zeros((8, width), F32)
        s, q = lax.fori_loop(0, PIX // MBLK, convolve, (zero, zero))
        if g:
            ex_stat[g - 1].relay()
        ex_stat[g].share(row_sum(s), row_sum(q))
    turned[...] = x[...].T.astype(BF16)
    ex_stat[ng - 1].relay()
    for g, (start, width) in enumerate(halves):
        cols = slice(start, start + width)
        mean, rstd = moments(plan, ex_stat[g].collect())
        scale = rstd * gain[0:1, cols]
        stat[0:1, cols] = rstd
        stat[1:2, cols] = -mean * rstd
        stat[2:3, cols] = 0.5 * scale
        stat[3:4, cols] = 0.5 * (gain[1:2, cols] - mean * scale)

        def chunk(j):
            return stat[2:3, lanes(j)], stat[3:4, lanes(j)]

        def activate(j, b, hoisted, totals):
            scale, shift = hoisted
            total = None
            for p in range(PIX):
                half = hidden[p, images_at(b), lanes(j)] * scale + shift
                t = half_tanh(half)
                made = half * t + half
                slope[p, images_at(b), lanes(j)] = (1.0 + t) + half * (1.0 - t * t)
                total = made if total is None else total + made
            pool[images_at(b), lanes(j)] = total * (1.0 / PIX)
            return totals

        over_tiles(plan, start // LANE, width // LANE, chunk, activate, 0, lambda j, s: None, UN_ACT)
    pool_low = pool[:, 0:hd].astype(BF16)
    classes = lax.broadcasted_iota(jnp.int32, (n, KP), 1)
    valid = classes < K
    logits = dot(pool_low, w_head[0:hd, C + LANE :]) + bias[...]
    logits = jnp.where(valid, logits, -1e30)
    top = jnp.max(logits, axis=1, keepdims=True)
    lifted = logits - top
    powers = jnp.where(valid, jnp.exp(lifted), 0.0)
    norm = jnp.sum(powers, axis=1, keepdims=True)
    log_probs = lifted - jnp.log(norm)
    picked = lax.broadcasted_iota(jnp.int32, (n, n), 1) == partner
    label_two = jnp.sum(jnp.where(picked, label_row[...], 0), axis=1, keepdims=True)
    w = weight
    targets = w * jnp.where(classes == label, 1.0 - SMOOTHING, 0.0) + (1.0 - w) * jnp.where(
        classes == label_two, 1.0 - SMOOTHING, 0.0
    )
    targets = jnp.where(valid, targets + SMOOTHING / K, 0.0)
    loss = -jnp.sum(jnp.where(valid, targets * log_probs, 0.0))
    grad_logits = (powers / norm - targets) * (float(PIX) / plan.count)
    packed_bias = jnp.where(classes[0:1, :] == KP - 1, loss, row_sum(grad_logits))
    ex_bias.share(packed_bias[:, 0 : KP // 2], packed_bias[:, KP // 2 :])
    grad_low = grad_logits.astype(BF16)
    pool_grad = dot(grad_low, w_head[0:hd, C + LANE :], ((1,), (1,)))
    pool[:, 0:hd] = pool_grad * (0.5 / PIX)

    def put_sums(j, totals):
        flow_sum, value_sum = [row_sum(t) for t in totals]
        sums[0:1, lanes(j)] = flow_sum
        sums[1:2, lanes(j)] = value_sum * stat[0:1, lanes(j)] + flow_sum * stat[1:2, lanes(j)]

    for g, (start, width) in enumerate(halves):
        cols = slice(start, start + width)

        def back(j, b, hoisted, totals):
            s, q = totals
            flow = pool[images_at(b), lanes(j)]
            for p in range(PIX):
                made = slope[p, images_at(b), lanes(j)] * flow
                slope[p, images_at(b), lanes(j)] = made
                s = s + made
                q = q + made * hidden[p, images_at(b), lanes(j)]
            return s, q

        between = ex_grad[g - 1].relay if g else None
        over_tiles_and(
            plan, start // LANE, width // LANE, between, lambda j: None, back, 2, put_sums, UN_HBACK
        )
        ex_grad[g].share(sums[0:1, cols], sums[1:2, cols])
    grad_head[0:hd, C + LANE :] = dot(pool_low.T, grad_low).astype(BF16)
    ex_grad[ng - 1].relay()
    norm_grads = jnp.concatenate(
        [sums[1:2, 0:hd], sums[0:1, 0:hd], jnp.zeros((LANE - 2, hd), F32)], axis=0
    )
    grad_head[0:hd, C : C + LANE] = norm_grads.T.astype(BF16)
    for g, (start, width) in enumerate(halves):
        cols = slice(start, start + width)
        shift_total, gain_total = ex_grad[g].collect()
        scale = stat[0:1, cols] * gain[0:1, cols]
        mean_one = shift_total / plan.count
        mean_two = gain_total / plan.count
        stat[4:5, cols] = scale
        stat[5:6, cols] = -scale * stat[0:1, cols] * mean_two
        stat[6:7, cols] = -scale * (mean_one + stat[1:2, cols] * mean_two)
    def into(m, carry):
        rows = pl.ds(pl.multiple_of(m * MBLK * n, MBLK * n), MBLK * n)
        spot = pl.ds(m * MBLK, MBLK)
        value = (
            slope[spot, :, 0:hd] * stat[4:5, 0:hd]
            + hidden[spot, :, 0:hd] * stat[5:6, 0:hd]
            + stat[6:7, 0:hd]
        )
        low = value.reshape(MBLK * n, hd).astype(BF16)
        low_grad[rows, 0:hd] = low
        grad_x[rows, :] = dot(low, w_head[0:hd, 0:C])
        return carry

    lax.fori_loop(0, PIX // MBLK, into, 0)
    r.spill_e.fetch(LAYERS - 1)
    for at in range(0, hd, LANE):
        part = dot(turned[...], low_grad[:, at : at + LANE])
        grad_head[at : at + LANE, 0:C] = part.T.astype(BF16)
    totals_out[...] = jnp.concatenate(ex_bias.collect(), axis=1)


def backward_layer(plan, r, layer, hooks):
    expanded, depth, flow, gated, sums, coef = r.expanded, r.depth, r.flow, r.gated, r.sums, r.coef
    normed_three, stat_e, stat_c = r.normed_three.at[layer], r.stat_e.at[layer], r.stat_c.at[layer]
    pooled, presq, gate, turned = r.pooled.at[layer], r.presq.at[layer], r.gate.at[layer], r.turned.at[layer]
    we, wp, wr, wx = r.we.at[layer], r.wp.at[layer], r.wr.at[layer], r.wx.at[layer]
    small, tail = r.small.at[layer], r.tail.at[layer]
    grad = grad_x = r.stream
    low_proj, squeeze_grad, flat, packed = r.x_low, r.squeeze_grad, r.flat, r.stage
    ex_one, ex_two, ex_three = r.ex_wide[0:GROUPS], r.ex_wide[GROUPS : 2 * GROUPS], r.ex_thin
    n = plan.images
    lane = lax.broadcasted_iota(jnp.int32, (1, LANE), 1)
    is_low = lane < SQ
    rstd_c = stat_c[1:2, :]
    s = row_sum(jnp.sum(grad[...].reshape(-1, 8, C), axis=0))
    q = row_sum(
        jnp.sum((grad[...] * normed_three[...].astype(F32)).reshape(-1, 8, C), axis=0)
    )
    ex_three.share(s, q)
    hooks[0]()
    bias_three, gain_three = s, q

    if layer < LAYERS - 1:
        r.spill_d.wait()

    def chunk_two(j):
        return stat_e[6:7, lanes(j)], stat_e[7:8, lanes(j)]

    def regate(p, carry):
        rows = pl.ds(pl.multiple_of(p * n, n), n)
        for j in range(NJ):
            cols = slice(j * LANE, (j + 1) * LANE)
            half = depth[p, :, cols] * stat_e[6:7, cols] + stat_e[7:8, cols]
            value = (half * half_tanh(half) + half) * gate[:, cols]
            gated[rows, cols] = value.astype(BF16)
        return carry

    lax.fori_loop(0, PIX, regate, 0)

    bias_total, gain_total = ex_three.collect()
    scale = rstd_c * tail[1:2, :]
    mean_one, mean_two = bias_total / plan.count, gain_total / plan.count
    low_proj[...] = (
        scale
        * (grad[...] - mean_one - normed_three[...].astype(F32) * mean_two)
    ).astype(BF16)

    def into_gated(m, carry):
        rows = pl.ds(pl.multiple_of(m * MBLK * n, MBLK * n), MBLK * n)
        value = dot(low_proj[rows, :], wp[...], ((1,), (1,)))
        flow[pl.ds(m * MBLK, MBLK), :, :] = value.reshape(MBLK, n, E)
        return carry

    lax.fori_loop(0, PIX // MBLK, into_gated, 0)
    hooks[1]()

    def gate_back(t, carry):
        j, b = t // (n // 16), lax.rem(t, n // 16)
        block = pl.ds(pl.multiple_of(b * 16, 16), 16)
        total = None
        for p in range(PIX):
            low = gated[pl.ds(pl.multiple_of(p * n + b * 16, 16), 16), lanes(j)].astype(F32)
            term = flow[p, block, lanes(j)] * low
            total = term if total is None else total + term
        squeeze_grad[block, lanes(j)] = total * (1.0 - gate[block, lanes(j)])
        return carry

    lax.fori_loop(0, NJ * (n // 16), gate_back, 0)
    excite_grad = squeeze_grad[...]
    sums[13:14, :] = row_sum(excite_grad)
    squeezed = silu(presq[...])
    presq_grad = dot_rows(excite_grad, wx[...], ((1,), (1,))) * silu_slope(presq[...])
    grad_wx = dot_outer(squeezed, excite_grad)
    flat[ROW_R : ROW_R + E, :] = dot_outer(pooled[...], presq_grad)
    evens = flat[pl.ds(ROW_R, E // 2, stride=2), :]
    odds = flat[pl.ds(ROW_R + 1, E // 2, stride=2), :]
    flat[ROW_R:ROW_X, :] = jnp.where(is_low, evens, pltpu.roll(odds, SQ, 1))
    for j in range(NJ):
        flat[pl.ds(ROW_X + j, SQ, stride=NJ), :] = grad_wx[0:SQ, j * LANE : (j + 1) * LANE]
    grad_reduce_b = row_sum(presq_grad)
    squeeze_grad[...] = dot_rows(presq_grad, wr[...], ((1,), (1,))) * (1.0 / PIX)

    def put_sums(first_row, stat_row):
        def put(j, totals):
            rows = [row_sum(t) for t in totals]
            mean = stat_e[stat_row : stat_row + 1, lanes(j)]
            rstd = stat_e[stat_row + 1 : stat_row + 2, lanes(j)]
            rows[-2] = (rows[-2] - mean * rows[-1]) * rstd
            for i, t in enumerate(rows):
                sums[first_row + i : first_row + i + 1, lanes(j)] = t

        return put

    def back_two(j, b, hoisted, totals):
        scale, shift = hoisted
        gain_sum, bias_sum = totals
        opened = gate[images_at(b), lanes(j)] * 0.5
        pool_flow = squeeze_grad[images_at(b), lanes(j)] * 0.5
        for p in range(PIX):
            value = depth[p, images_at(b), lanes(j)]
            half = value * scale + shift
            t = half_tanh(half)
            made = (flow[p, images_at(b), lanes(j)] * opened + pool_flow) * (
                (1.0 + t) + half * (1.0 - t * t)
            )
            flow[p, images_at(b), lanes(j)] = made
            bias_sum = bias_sum + made
            gain_sum = gain_sum + made * value
        return gain_sum, bias_sum

    for g in range(GROUPS):
        cols = slice(g * GW, (g + 1) * GW)
        between = ex_two[g - 1].relay if g else None
        over_tiles_and(
            plan, g * (GW // LANE), GW // LANE, between, chunk_two, back_two, 2, put_sums(11, 2), UN_TWO
        )
        ex_two[g].share(sums[12:13, cols], sums[11:12, cols])

    proj_turned = low_proj[...].astype(F32).T.astype(BF16)
    ex_two[GROUPS - 1].relay()
    hooks[2]()
    for j in range(NJ):
        part = dot(proj_turned, gated[:, j * LANE : (j + 1) * LANE])
        for h in range(C // LANE):
            flat[pl.ds(ROW_P + 2 * j * LANE + h, LANE, stride=2), :] = part[
                h * LANE : (h + 1) * LANE, :
            ].T

    def norm_coefs(g, pair, row, stat_row, gain_row):
        cols = slice(g * GW, (g + 1) * GW)
        mean, rstd = stat_e[stat_row : stat_row + 1, cols], stat_e[stat_row + 1 : stat_row + 2, cols]
        scale = rstd * small[gain_row : gain_row + 1, cols]
        mean_one, mean_two = pair[0] / plan.count, pair[1] / plan.count
        coef[row : row + 1, cols] = scale
        coef[row + 1 : row + 2, cols] = -scale * rstd * mean_two
        coef[row + 2 : row + 3, cols] = -scale * (mean_one - mean * rstd * mean_two)

    def chunk_one(j):
        return (
            [coef[i : i + 1, lanes(j)] for i in range(3)],
            [small[t : t + 1, lanes(j)] for t in range(9)],
            [stat_e[i : i + 1, lanes(j)] for i in (4, 5)],
        )

    def back_one(j, b, hoisted, totals):
        (c_flow, c_value, c_const), w, (scale, shift) = hoisted
        w_sums, gain_sum, bias_sum = list(totals[:9]), totals[9], totals[10]
        spread_grad = []
        for p in range(PIX):
            spread_grad.append(
                flow[p, images_at(b), lanes(j)] * c_flow
                + (depth[p, images_at(b), lanes(j)] * c_value + c_const)
            )
        act_one, slopes = [], []
        for p in range(PIX):
            half = expanded[p, images_at(b), lanes(j)] * scale + shift
            t = half_tanh(half)
            act_one.append(half * t + half)
            slopes.append(0.5 * ((1.0 + t) + half * (1.0 - t * t)))
        made = [None] * PIX
        for o, t, i in TAPS:
            w_sums[t] = w_sums[t] + spread_grad[o] * act_one[i]
            term = spread_grad[o] * w[t]
            made[i] = term if made[i] is None else made[i] + term
        for p in range(PIX):
            value = expanded[p, images_at(b), lanes(j)]
            result = made[p] * slopes[p]
            flow[p, images_at(b), lanes(j)] = result
            bias_sum = bias_sum + result
            gain_sum = gain_sum + result * value
        return tuple(w_sums) + (gain_sum, bias_sum)

    for g in range(GROUPS):
        cols = slice(g * GW, (g + 1) * GW)
        norm_coefs(g, ex_two[g].collect(), 0, 2, 11)
        if g == 0:
            r.spill_e.wait()
        between = ex_one[g - 1].relay if g else None
        over_tiles_and(
            plan, g * (GW // LANE), GW // LANE, between, chunk_one, back_one, 11, put_sums(0, 0), UN_ONE
        )
        ex_one[g].share(sums[10:11, cols], sums[9:10, cols])

    if layer:
        r.spill_d.fetch(layer - 1)
    for j in range(NJ):
        flat[pl.ds(ROW_D + j, 14, stride=NJ), :] = sums[0:14, j * LANE : (j + 1) * LANE]

    def turn(row):
        return pltpu.roll(jnp.broadcast_to(row, (8, LANE)), SQ, 1)[0:1, :]

    pieces = [turn(v[:, h * LANE : (h + 1) * LANE]) for v in (gain_three, bias_three) for h in (0, 1)]
    flat[ROW_S : ROW_S + 1, :] = jnp.where(is_low, grad_reduce_b, pieces[0])
    for i in range(3):
        flat[ROW_S + 1 + i : ROW_S + 2 + i, :] = jnp.where(is_low, pieces[i], pieces[i + 1])
    flat[ROW_S + 4 : ROW_S + 5, :] = pieces[3]
    ex_one[GROUPS - 1].relay()
    hooks[3]()

    for g in range(GROUPS):
        cols = slice(g * GW, (g + 1) * GW)
        norm_coefs(g, ex_one[g].collect(), 0, 0, 9)

        def into(m, carry, cols=cols):
            rows = pl.ds(pl.multiple_of(m * MBLK * n, MBLK * n), MBLK * n)
            spot = pl.ds(m * MBLK, MBLK)
            value = (
                flow[spot, :, cols] * coef[0:1, cols]
                + expanded[spot, :, cols] * coef[1:2, cols]
                + coef[2:3, cols]
            )
            low = value.reshape(MBLK * n, GW).astype(BF16)
            gated[rows, cols] = low
            grad_x[rows, :] += dot(low, we[:, cols], ((1,), (1,)))
            return carry

        lax.fori_loop(0, PIX // MBLK, into, 0)
        for j in range(g * (GW // LANE), (g + 1) * (GW // LANE)):
            flat[pl.ds(j, C, stride=NJ), :] = dot(
                turned[...], gated[:, j * LANE : (j + 1) * LANE]
            )
    if layer:
        r.spill_e.fetch(layer - 1)
    hooks[4]()
    packed[0 : plan.flat, :] = flat[0 : plan.flat, :].astype(BF16)


class Spill:
    def __init__(self, held, kept, sem):
        self.held, self.kept, self.sem = held, kept, sem

    def start(self, layer):
        self.copy = pltpu.make_async_copy(self.held, self.kept.at[layer], self.sem)
        self.copy.start()

    def fetch(self, layer):
        self.copy = pltpu.make_async_copy(self.kept.at[layer], self.held, self.sem)
        self.copy.start()

    def wait(self):
        self.copy.wait()


INPUTS = ("block", "w_own", "images", "per_image", "bias")
OUTPUTS = ("block_sums", "head_sums", "totals", "kept_e", "kept_d")


def scratch_of(plan):
    n, rows, hd = plan.images, plan.rows, plan.hd
    wide = 2 * GW // LANE
    vm = lambda shape, dtype=F32: pltpu.VMEM(shape, dtype)
    held = {
        "expanded": vm((PIX, n, E)),
        "depth": vm((PIX, n, E)),
        "flow": vm((PIX, n, E)),
        "gated": vm((rows, E), BF16),
        "stream": vm((rows, C)),
        "x_low": vm((rows, C), BF16),
        "turned": vm((LAYERS + 1, C, rows), BF16),
        "normed_three": vm((LAYERS, rows, C), BF16),
        "stat_e": vm((LAYERS, 8, E)),
        "stat_c": vm((LAYERS, 8, C)),
        "pooled": vm((LAYERS, n, E)),
        "presq": vm((LAYERS, n, LANE)),
        "gate": vm((LAYERS, n, E)),
        "we": vm((LAYERS, C, E), BF16),
        "wp": vm((LAYERS, E, C), BF16),
        "wr": vm((LAYERS, E, LANE), BF16),
        "wx": vm((LAYERS, LANE, E), BF16),
        "small": vm((LAYERS, 16, E)),
        "tail": vm((LAYERS, 8, C)),
        "w_head": vm((plan.head_flat, HEAD_W), BF16),
        "squeeze_grad": vm((n, E)),
        "sums": vm((16, E)),
        "coef": vm((8, E)),
        "flat": vm((max(plan.flat, LAYERS * (plan.chunk + 32)), LANE)),
        "stage": vm((max(plan.nf * plan.chunk, plan.flat), LANE), BF16),
        "spill_sems": pltpu.SemaphoreType.DMA((2,)),
    }
    for i in range(2 * GROUPS):
        held[f"pair{i}"] = vm((2, wide, LANE))
        held[f"wide{i}"] = vm((plan.devices // 2, wide, LANE))
        for k in range(4):
            held[f"wide{i}_{k}"] = pltpu.SemaphoreType.DMA(())
    held["thin"] = vm((plan.devices, 2 * C // LANE, LANE))
    held["thick"] = vm((plan.devices, KP // LANE, LANE))
    for name in ("thin", "thick"):
        held[name + "_send"] = pltpu.SemaphoreType.DMA(())
        held[name + "_recv"] = pltpu.SemaphoreType.DMA(())
    for name in ("block", "head", "half"):
        for i in range(6):
            held[f"gather_{name}{i}"] = pltpu.SemaphoreType.DMA(())
    for name, unit in (("block", plan.layer_unit()), ("head", plan.head_unit())):
        for i, shape in enumerate(Reduction.scratch(unit)):
            held[f"reduce_{name}{i}"] = shape
    for i, shape in enumerate(Reduction.scratch(plan.layer_unit())[3:]):
        held[f"reduce_last{i}"] = shape
    for i in range(8):
        held[f"reduce_half{i}"] = pltpu.SemaphoreType.DMA(())
    return held


def step_kernel(plan, names, *refs):
    r = types.SimpleNamespace(**dict(zip(names, refs, strict=True)))
    held = vars(r)
    exchange = lambda name: Exchange(plan, held[name], held[name + "_send"], held[name + "_recv"])
    r.ex_wide = [
        PairedExchange(
            plan, held[f"pair{i}"], held[f"wide{i}"], [held[f"wide{i}_{k}"] for k in range(4)]
        )
        for i in range(2 * GROUPS)
    ]
    r.ex_thin, r.ex_bias = exchange("thin"), exchange("thick")
    r.spill_e = Spill(r.expanded, r.kept_e, r.spill_sems.at[0])
    r.spill_d = Spill(r.depth, r.kept_d, r.spill_sems.at[1])
    reduce_refs = {
        name: [held[f"reduce_{name}{i}"] for i in range(12)] for name in ("block", "head")
    }
    reduce_refs["last"] = reduce_refs["block"][:3] + [held[f"reduce_last{i}"] for i in range(9)]
    reduce_refs["half"] = reduce_refs["last"][:4] + [held[f"reduce_half{i}"] for i in range(8)]
    fs = lax.axis_index("fsdp")
    n = plan.images

    enter(plan)
    mine = [r.gated.at[pl.ds(0, plan.chunk), pl.ds(C + i * LANE, LANE)] for i in range(LAYERS)]
    images = r.gated.at[pl.ds(0, plan.rows), pl.ds(0, C)]
    take_images = pltpu.make_async_copy(r.images, images, r.spill_sems.at[0])
    take_images.start()
    take_head = pltpu.make_async_copy(
        r.w_own,
        r.w_head.at[pl.ds(pl.multiple_of(fs * plan.head_pad, 16), plan.head_pad)],
        r.spill_sems.at[1],
    )
    take_head.start()
    shift = spread_shards(plan, r.block, r.flat, mine)
    own_rows = pl.ds(pl.multiple_of(fs * plan.chunk, 16), plan.chunk)

    def gather_of(layer, name="block", half=None):
        if not half:
            r.stage[own_rows, :] = mine[layer][...]
        sems = [held[f"gather_{name}{i}"] for i in range(6)]
        return Gather(plan, r.stage, plan.chunk, sems, half)

    def unpack(layer):
        unpack_weights(
            plan,
            r.stage,
            r.we.at[layer],
            r.wp.at[layer],
            r.wr.at[layer],
            r.wx.at[layer],
            r.small.at[layer],
            r.tail.at[layer],
            r.flat,
        )

    shift(0)
    gathers = [gather_of(0, "block", 0), gather_of(0, "half", 1)]
    head_gather = Gather(
        plan, r.w_head, plan.head_pad, [held[f"gather_head{i}"] for i in range(6)]
    )
    entered(plan)
    for gather in gathers:
        gather.start_rest()
    columns = jnp.concatenate([r.per_image[...], jnp.zeros((8, LANE - n), F32)], axis=1).T
    weight, label, partner = (columns[0:n, i : i + 1] for i in range(3))
    label, partner = label.astype(jnp.int32), partner.astype(jnp.int32)
    label_row = r.per_image[1:2, :].astype(jnp.int32)
    take_images.wait()
    take_head.wait()
    mix_images(plan, images, partner, weight, r.stream, 0, PIX // 2)
    for gather in gathers:
        gather.start_dp()
    head_gather.start_rest()
    mix_images(plan, images, partner, weight, r.stream, PIX // 2, PIX)
    gathers[0].start_core()
    shift(1)
    gathers[1].start_core()
    head_gather.start_dp()
    shift(2)
    for gather in gathers:
        gather.complete()
    unpack(0)

    for layer in range(LAYERS):
        if layer < LAYERS - 1:
            box = []

            def begin(layer=layer, box=box):
                box.append(gather_of(layer + 1))
                box[0].start_rest()

            def arrive(layer=layer, box=box):
                box[0].complete()
                unpack(layer + 1)

            hooks = (
                begin,
                lambda box=box: box[0].start_dp(),
                lambda box=box: box[0].start_core(),
                arrive,
            )
            if layer == 0:
                hooks = (begin, hooks[1], hooks[2], lambda arrive=arrive: [arrive(), head_gather.start_core()])
        else:
            hooks = (lambda: None,) * 4
        forward_layer(plan, r, layer, hooks)
    head_gather.complete()
    head_layers(plan, r, label, label_row, partner, weight)

    head_work = Reduction(plan.head_unit(), r.w_head, r.head_sums, reduce_refs["head"])
    unit = plan.layer_unit()
    works = [None] + [
        Reduction(unit, r.stage, r.block_sums.at[layer], reduce_refs["block"])
        for layer in range(1, LAYERS)
    ]

    def both(*steps):
        return lambda: [step() for step in steps]

    nothing = lambda: None
    last = LAYERS - 1
    for layer in reversed(range(LAYERS)):
        if layer == last:
            hooks = (head_work.start_core, head_work.start_dp, nothing, nothing, nothing)
        else:
            work = works[layer + 1]
            hooks = (
                work.start_core,
                work.start_dp,
                work.start_rest,
                work.start_copies,
                work.complete,
            )
            if layer == last - 1:
                hooks = (
                    both(hooks[0], head_work.start_rest),
                    hooks[1],
                    hooks[2],
                    both(hooks[3], head_work.start_copies),
                    both(hooks[4], head_work.complete),
                )
        backward_layer(plan, r, layer, hooks)
    first = ceil_to(-(-unit.part // 2), 16)
    halves = [
        Reduction(unit, r.stage, r.block_sums.at[0], reduce_refs["last"], 0, first),
        Reduction(unit, r.stage, r.block_sums.at[0], reduce_refs["half"], first, unit.part - first),
    ]
    for step in ("start_core", "start_dp", "start_rest", "start_copies", "complete"):
        for half in halves:
            getattr(half, step)()
    for e in r.ex_wide + [r.ex_thin, r.ex_bias]:
        e.finish()


def train_step(plan, block, w_own, images, per_image, bias):
    held = scratch_of(plan)
    block_unit, head_unit = plan.layer_unit(), plan.head_unit()
    big = (PIX, plan.images, E)
    anywhere = pl.BlockSpec(memory_space=pl.ANY)
    return pl.pallas_call(
        functools.partial(step_kernel, plan, INPUTS + OUTPUTS + tuple(held)),
        out_shape=(
            jax.ShapeDtypeStruct((LAYERS, block_unit.owned, LANE), BF16),
            jax.ShapeDtypeStruct((head_unit.owned, HEAD_W), BF16),
            jax.ShapeDtypeStruct((1, KP), F32),
            jax.ShapeDtypeStruct((LAYERS,) + big, F32),
            jax.ShapeDtypeStruct((LAYERS - 1,) + big, F32),
        ),
        in_specs=[VM, anywhere, anywhere, VM, VM],
        out_specs=(VM, VM, VM, anywhere, anywhere),
        scratch_shapes=list(held.values()),
        compiler_params=pltpu.CompilerParams(
            collective_id=1, has_side_effects=True, vmem_limit_bytes=VMEM_LIMIT
        ),
        name="train_step",
    )(block, w_own, images, per_image, bias)


def adam_update(master, first, second, average, grad):
    first_new = BETA_ONE * first + (1.0 - BETA_ONE) * grad
    second_new = BETA_TWO * second + (1.0 - BETA_TWO) * grad * grad
    fix_one = 1.0 - BETA_ONE**STEP
    fix_two = 1.0 - BETA_TWO**STEP
    master_new = master * (1.0 - RATE * DECAY_WEIGHT) - RATE * (first_new / fix_one) / (
        jnp.sqrt(second_new / fix_two) + EPS_ADAM
    )
    average_new = EMA_RATE * average + (1.0 - EMA_RATE) * master_new
    return (master_new, first_new, second_new, average_new)


def on_device(mesh, images, partner, mix_weight, labels, *states):
    block, head_state, bias_state = states[0:4], states[4:8], states[8:12]
    row = C + 2 + K
    plan = Plan(mesh, images.shape[0], head_state[0].shape[0] // row)
    half = (plan.hd // LANE + 1) // 2 * LANE
    plan.head_groups = [(0, half), (half, plan.hd - half)]
    start = lax.axis_index("fsdp") * plan.shard
    offset = start - start // (16 * LANE) * (16 * LANE)
    grid = head_state[0].astype(BF16).reshape(plan.head_rows, row)
    grid = jnp.concatenate(
        [
            grid[:, : C + 2],
            jnp.zeros((plan.head_rows, LANE - 2), BF16),
            grid[:, C + 2 :],
            jnp.zeros((plan.head_rows, KP - K), BF16),
        ],
        axis=1,
    )
    grid = jnp.pad(grid, ((0, plan.head_pad - plan.head_rows), (0, 0)))
    bias = jnp.pad(bias_state[0], (0, KP - K)).reshape(1, KP)
    per_image = jnp.stack(
        [mix_weight, labels.astype(F32), partner.astype(F32)] + [jnp.zeros_like(mix_weight)] * 5
    )
    block_grad, head_grad, totals = train_step(
        plan, block[0], grid, images.reshape(plan.rows, C), per_image, bias
    )[:3]
    loss_sum = totals[0, KP - 1]
    grad_bias = totals[0, :K]
    block_grad = lax.dynamic_slice(
        block_grad.reshape(LAYERS, plan.chunk * LANE), (0, offset), (LAYERS, plan.shard)
    ).astype(F32)
    head_grad = head_grad[: plan.head_rows].astype(F32)
    head_grad = jnp.concatenate(
        [head_grad[:, : C + 2], head_grad[:, C + LANE : C + LANE + K]], axis=1
    ).reshape(-1)
    return (
        (loss_sum,)
        + adam_update(*block, block_grad)
        + adam_update(*head_state, head_grad)
        + adam_update(*bias_state, grad_bias)
    )


def solution(mesh):
    data = P(("dp", "fsdp"))
    states = (P(None, "fsdp"),) * 4 + (P("fsdp"),) * 4 + (P(),) * 4
    return jax.shard_map(
        functools.partial(on_device, mesh),
        mesh=mesh,
        in_specs=(P(("dp", "fsdp"), None, None), data, data, data) + states,
        out_specs=(P(),) + states,
        check_vma=False,
    )
```

```python
import functools
import types

import jax
import jax.numpy as jnp
from jax import lax
from jax.experimental import pallas as pl
from jax.experimental.pallas import tpu as pltpu
from jax.sharding import PartitionSpec as P

C = 256
E = 1536
SQ = 64
K = 1000
SIDE = 4
PIX = 16
LAYERS = 3
STEP = 5
EPS_NORM = 0.001
RATE = 0.05
DECAY_WEIGHT = 0.05
BETA_ONE = 0.5
BETA_TWO = 0.5
EPS_ADAM = 1e-08
EMA_RATE = 0.5
SMOOTHING = 0.1

LANE = 128
KP = 1024
HEAD_W = C + LANE + KP
PB = 2 * C * E + 2 * E * SQ + 14 * E + SQ + 2 * C
ROW_P = C * E // LANE
ROW_R = ROW_P + E * C // LANE
ROW_X = ROW_R + E * SQ // LANE
ROW_D = ROW_X + SQ * E // LANE
ROW_S = ROW_D + 14 * E // LANE
NJ = E // LANE
GROUPS = 2
GW = E // GROUPS
MBLK = 4
UN_SPREAD, UN_ACT, UN_HBACK, UN_GATE, UN_TWO, UN_ONE = 2, 4, 4, 4, 2, 1

MESH = pl.DeviceIdType.MESH
F32 = jnp.float32
BF16 = jnp.bfloat16
VMEM_LIMIT = 127 * 512 * 1024
VM = pl.BlockSpec(memory_space=pltpu.VMEM)


def ceil_to(value, unit):
    return -(-value // unit) * unit


class Plan:
    def __init__(self, mesh, images, head_rows):
        self.nd = mesh.shape["dp"]
        self.nf = mesh.shape["fsdp"]
        self.devices = self.nd * self.nf
        self.images = images
        self.rows = images * PIX
        self.count = float(self.rows * self.devices)
        self.shard = PB // self.nf
        self.base = [(self.shard * f // LANE) // 16 * 16 for f in range(self.nf)]
        self.chunk = ceil_to(-(-self.shard // LANE) + 17, 16 * self.nd)
        self.flat = self.base[-1] + self.chunk
        self.head_pad = ceil_to(head_rows, 16)
        self.hd = self.head_pad * self.nf
        self.head_rows = head_rows
        self.head_part = ceil_to(-(-head_rows // self.nd), 16)
        self.head_flat = self.head_pad * (self.nf - 1) + self.head_part * self.nd
        self.depth = self.nf // 2
        third = ceil_to(-(-self.head_part // 3), 16)
        ends = list(range(0, self.head_part, third)) + [self.head_part]
        self.head_thirds = [(a, b - a) for a, b in zip(ends[:-1], ends[1:])]

    def layer_unit(self):
        return Unit(self, LANE, self.chunk // self.nd, self.flat, lambda f: self.shard * f // (16 * LANE) * 16)

    def head_unit(self):
        return Unit(self, HEAD_W, self.head_part, self.head_flat, lambda f: self.head_pad * f)


class Unit:
    def __init__(self, plan, width, part, rows, base):
        self.plan, self.width, self.part, self.rows, self.base = plan, width, part, rows, base
        self.owned = part * plan.nd


def dot(a, b, dims=((1,), (0,))):
    return lax.dot_general(a, b, (dims, ((), ())), preferred_element_type=F32)


def halves_of(value):
    high = value.astype(BF16)
    return high, (value - high.astype(F32)).astype(BF16)


def dot_rows(value, low, dims=((1,), (0,))):
    n = value.shape[0]
    both = dot(jnp.concatenate(halves_of(value), axis=0), low, dims)
    return both[0:n, :] + both[n:, :]


def dot_outer(a, b):
    a_high, a_low = halves_of(a)
    b_high, b_low = halves_of(b)
    left = jnp.concatenate([a_high, a_low, a_high], axis=0)
    right = jnp.concatenate([b_high, b_high, b_low], axis=0)
    return dot(left, right, ((0,), (0,)))


def row_sum(value):
    return jnp.sum(value, axis=0, keepdims=True)


def over_peers(plan, body):
    dp, fs = lax.axis_index("dp"), lax.axis_index("fsdp")
    deep, low = fs // 2, dp * 2 + lax.rem(fs, 2)
    near = 2 * plan.nd
    top = jnp.where(2 * deep >= plan.depth, 1, 0)

    def at(k, i, carry):
        z = top * k + (1 - top) * (plan.depth - 1 - k)
        j = lax.rem(low + i, near)

        @pl.when((z != deep) | (j != low))
        def _():
            body((j // 2, 2 * z + lax.rem(j, 2)))

        return carry

    for k in range(plan.depth):
        lax.fori_loop(0, near, functools.partial(at, k), 0)


def my_slot(plan):
    return lax.axis_index("dp") * plan.nf + lax.axis_index("fsdp")


def enter(plan):
    barrier = pltpu.get_barrier_semaphore()
    over_peers(
        plan,
        lambda device: pl.semaphore_signal(
            barrier, inc=1, device_id=device, device_id_type=MESH
        ),
    )


def entered(plan):
    pl.semaphore_wait(pltpu.get_barrier_semaphore(), plan.devices - 1)


class Exchange:
    def __init__(self, plan, buf, send, recv):
        self.plan, self.buf, self.send, self.recv, self.used = plan, buf, send, recv, False

    def share(self, first, second):
        plan, buf, send, recv = self.plan, self.buf, self.send, self.recv
        if self.used:
            self.finish()
        self.used = True
        half = first.shape[1] // LANE
        self.rows = 2 * half
        mine = my_slot(plan)
        for r in range(half):
            cols = slice(r * LANE, (r + 1) * LANE)
            buf[mine, r : r + 1, :] = first[:, cols]
            buf[mine, half + r : half + r + 1, :] = second[:, cols]
        over_peers(
            plan,
            lambda device: pltpu.make_async_remote_copy(
                src_ref=buf.at[mine, pl.ds(0, 2 * half)],
                dst_ref=buf.at[mine, pl.ds(0, 2 * half)],
                send_sem=send,
                recv_sem=recv,
                device_id=device,
                device_id_type=MESH,
            ).start(),
        )

    def others(self):
        return self.buf.at[pl.ds(1, self.plan.devices - 1), pl.ds(0, self.rows)]

    def collect(self):
        pltpu.make_async_copy(self.others(), self.others(), self.recv).wait()
        total = jnp.sum(self.buf[:, 0 : self.rows, :], axis=0)
        rows = [total[r : r + 1, :] for r in range(self.rows)]
        half = self.rows // 2
        return jnp.concatenate(rows[:half], axis=1), jnp.concatenate(rows[half:], axis=1)

    def finish(self):
        pltpu.make_async_copy(self.others(), self.others(), self.send).wait()


class PairedExchange:
    def __init__(self, plan, pair, buf, sems):
        self.plan, self.pair, self.buf, self.sems, self.used = plan, pair, buf, sems, False
        self.dp, self.fs = lax.axis_index("dp"), lax.axis_index("fsdp")
        self.core, self.deep = lax.rem(self.fs, 2), self.fs // 2
        self.mine = self.dp * plan.depth + self.deep

    def share(self, first, second):
        if self.used:
            self.finish()
        self.used = True
        half = first.shape[1] // LANE
        self.rows = 2 * half
        for i in range(half):
            cols = slice(i * LANE, (i + 1) * LANE)
            self.pair[0, i : i + 1, :] = first[:, cols]
            self.pair[0, half + i : half + i + 1, :] = second[:, cols]
        rows = pl.ds(0, self.rows)
        pltpu.make_async_remote_copy(
            src_ref=self.pair.at[0, rows],
            dst_ref=self.pair.at[1, rows],
            send_sem=self.sems[0],
            recv_sem=self.sems[1],
            device_id=(self.dp, 2 * self.deep + 1 - self.core),
            device_id_type=MESH,
        ).start()

    def relay(self):
        plan, rows = self.plan, pl.ds(0, self.rows)
        got = self.pair.at[1, rows]
        pltpu.make_async_copy(got, got, self.sems[1]).wait()
        self.buf[self.mine, rows, :] = self.pair[0, rows, :] + self.pair[1, rows, :]
        top = jnp.where(2 * self.deep >= plan.depth, 1, 0)
        for k in range(plan.depth):
            z = top * k + (1 - top) * (plan.depth - 1 - k)

            def go(i, carry, z=z):
                d = lax.rem(self.dp + i, plan.nd)

                @pl.when((z != self.deep) | (d != self.dp))
                def _():
                    pltpu.make_async_remote_copy(
                        src_ref=self.buf.at[self.mine, rows],
                        dst_ref=self.buf.at[self.mine, rows],
                        send_sem=self.sems[2],
                        recv_sem=self.sems[3],
                        device_id=(d, 2 * z + self.core),
                        device_id_type=MESH,
                    ).start()

                return carry

            lax.fori_loop(0, plan.nd, go, 0)

    def others(self):
        return self.buf.at[pl.ds(1, self.plan.devices // 2 - 1), pl.ds(0, self.rows)]

    def collect(self):
        pltpu.make_async_copy(self.others(), self.others(), self.sems[3]).wait()
        total = jnp.sum(self.buf[:, 0 : self.rows, :], axis=0)
        rows = [total[i : i + 1, :] for i in range(self.rows)]
        half = self.rows // 2
        return jnp.concatenate(rows[:half], axis=1), jnp.concatenate(rows[half:], axis=1)

    def finish(self):
        sent = self.pair.at[0, pl.ds(0, self.rows)]
        pltpu.make_async_copy(sent, sent, self.sems[0]).wait()
        pltpu.make_async_copy(self.others(), self.others(), self.sems[2]).wait()


def moments(plan, pair):
    mean = pair[0] / plan.count
    return mean, lax.rsqrt(pair[1] / plan.count - mean * mean + EPS_NORM)


class Reduction:
    def __init__(self, unit, source, result, refs, skip=0, size=None):
        self.unit, self.source, self.result = unit, source, result
        self.skip, self.size = skip, size or unit.part
        rows = pl.ds(skip, self.size)
        self.got_core, self.got_dp = (ref.at[:, :, rows] for ref in refs[:2])
        self.sum_dp, self.got_rest = (ref.at[:, rows] for ref in refs[2:4])
        self.send, self.recv = refs[4:8], refs[8:12]
        plan = unit.plan
        self.dp, self.fs = lax.axis_index("dp"), lax.axis_index("fsdp")
        self.core, self.deep = lax.rem(self.fs, 2), self.fs // 2
        self.nd, self.nz = plan.nd, plan.depth

    @staticmethod
    def scratch(unit):
        plan = unit.plan
        nd, nz, w, part = plan.nd, plan.depth, unit.width, unit.part
        return [
            pltpu.VMEM((nz, nd, part, w), BF16),
            pltpu.VMEM((nd - 1, nz, part, w), BF16),
            pltpu.VMEM((nz, part, w), BF16),
            pltpu.VMEM((nz - 1, part, w), BF16),
        ] + [pltpu.SemaphoreType.DMA(())] * 8

    def push(self, stage, source, target, device):
        pltpu.make_async_remote_copy(
            src_ref=source,
            dst_ref=target,
            send_sem=self.send[stage],
            recv_sem=self.recv[stage],
            device_id=device,
            device_id_type=MESH,
        ).start()

    def rows_of(self, f, d=0):
        return pl.multiple_of(self.unit.base(f) + d * self.unit.part + self.skip, 16)

    def start_core(self):
        def go(z, carry):
            for d in range(self.nd):
                self.push(
                    0,
                    self.source.at[pl.ds(self.rows_of(2 * z + 1 - self.core, d), self.size)],
                    self.got_core.at[z, d],
                    (self.dp, 2 * self.deep + 1 - self.core),
                )
            return carry

        lax.fori_loop(0, self.nz, go, 0)

    def wait(self, sem, ref):
        pltpu.make_async_copy(ref, ref, sem).wait()

    def start_dp(self):
        self.wait(self.recv[0], self.got_core)

        def add(z, carry):
            for d in range(self.nd):
                own = self.source[pl.ds(self.rows_of(2 * z + self.core, d), self.size), :]
                self.got_core[z, d] = (own.astype(F32) + self.got_core[z, d].astype(F32)).astype(BF16)
            return carry

        lax.fori_loop(0, self.nz, add, 0)

        def go(z, carry):
            for i in range(1, self.nd):
                other = lax.rem(self.dp + i, self.nd)
                self.push(1, self.got_core.at[z, other], self.got_dp.at[i - 1, z], (other, self.fs))
            return carry

        lax.fori_loop(0, self.nz, go, 0)

    def sum_dp_parts(self):
        self.wait(self.recv[1], self.got_dp)
        self.wait(self.send[0], self.got_core)
        self.wait(self.send[1], self.got_dp)

        def add(z, carry):
            total = self.got_core[z, self.dp].astype(F32)
            for i in range(self.nd - 1):
                total = total + self.got_dp[i, z].astype(F32)
            self.sum_dp[z] = total.astype(BF16)
            return carry

        lax.fori_loop(0, self.nz, add, 0)

    def start_rest(self):
        for i in range(1, self.nz):
            other = lax.rem(self.deep + i, self.nz)
            self.push(2, self.sum_dp.at[other], self.got_rest.at[i - 1], (self.dp, 2 * other + self.core))

    def start_copies(self):
        self.wait(self.recv[2], self.got_rest)
        total = self.sum_dp[self.deep].astype(F32)
        for i in range(self.nz - 1):
            total = total + self.got_rest[i].astype(F32)
        rows = pl.ds(pl.multiple_of(self.dp * self.unit.part + self.skip, 16), self.size)
        self.result[rows, :] = total.astype(BF16)
        for i in range(1, self.nd):
            other = lax.rem(self.dp + i, self.nd)
            self.push(3, self.result.at[rows], self.result.at[rows], (other, self.fs))

    def complete(self):
        others = self.result.at[pl.ds(0, (self.nd - 1) * self.size)]
        self.wait(self.recv[3], others)
        self.wait(self.send[2], self.got_rest)
        self.wait(self.send[3], others)


def taps():
    found = []
    for y in range(SIDE):
        for x in range(SIDE):
            for a in range(3):
                for b in range(3):
                    iy, ix = y + a - 1, x + b - 1
                    if 0 <= iy < SIDE and 0 <= ix < SIDE:
                        found.append((y * SIDE + x, 3 * a + b, iy * SIDE + ix))
    return found


TAPS = taps()


def half_tanh(half):
    return jnp.tanh(half)


def silu(z):
    half = 0.5 * z
    return half * half_tanh(half) + half


def sigmoid(z):
    return 0.5 * half_tanh(0.5 * z) + 0.5


def silu_slope(z):
    half = 0.5 * z
    t = half_tanh(half)
    return 0.5 * (1.0 + t + half * (1.0 - t * t))


def lanes(j):
    return pl.ds(pl.multiple_of(j * LANE, LANE), LANE)


def images_at(b):
    return pl.ds(pl.multiple_of(b * 8, 8), 8)


def over_tiles(plan, first_chunk, chunks, per_chunk, body, n_sums, store_sums, unroll=1):
    blocks = plan.images // 8

    def chunk_step(jj, carry):
        j = first_chunk + jj
        hoisted = per_chunk(j)

        def step(b, sums):
            for u in range(unroll):
                sums = body(j, b * unroll + u, hoisted, sums)
            return sums

        zero = tuple(jnp.zeros((8, LANE), F32) for _ in range(n_sums))
        store_sums(j, lax.fori_loop(0, blocks // unroll, step, zero))
        return carry

    lax.fori_loop(0, chunks, chunk_step, 0)


def over_tiles_and(plan, first_chunk, chunks, between, *rest):
    if between is None:
        over_tiles(plan, first_chunk, chunks, *rest)
    else:
        over_tiles(plan, first_chunk, 2, *rest)
        between()
        over_tiles(plan, first_chunk + 2, chunks - 2, *rest)


class Gather:
    def __init__(self, plan, target, rows, sems, half=None):
        self.plan, self.target, self.rows = plan, target, rows
        tiles = rows // 16
        counts = [tiles // plan.nd + (1 if d < tiles % plan.nd else 0) for d in range(plan.nd)]
        self.parts = [(16 * sum(counts[:d]), 16 * counts[d]) for d in range(plan.nd)]
        if half is not None:
            first = ceil_to(self.parts[0][1] // 2, 16)
            ends = ((0, first), (first, self.parts[0][1]))[half]
            self.parts = [(start + ends[0], ends[1] - ends[0]) for start, _ in self.parts]
        self.whole = half is None
        self.covered = sum(size for _, size in self.parts)
        self.send, self.recv = sems[0:3], sems[3:6]
        self.dp, self.fs = lax.axis_index("dp"), lax.axis_index("fsdp")
        self.core, self.deep = lax.rem(self.fs, 2), self.fs // 2

    def by_part(self, body):
        if len({size for _, size in self.parts}) == 1:
            body(self.parts[0][0] + self.dp * (self.rows // self.plan.nd), self.parts[0][1])
            return
        for d, (start, size) in enumerate(self.parts):
            pl.when(self.dp == d)(functools.partial(body, start, size))

    def at(self, deep, start, size):
        begin = (2 * deep + self.core) * self.rows + start
        return self.target.at[pl.ds(pl.multiple_of(begin, 16), size)]

    def push(self, stage, ref, device):
        pltpu.make_async_remote_copy(
            src_ref=ref,
            dst_ref=ref,
            send_sem=self.send[stage],
            recv_sem=self.recv[stage],
            device_id=device,
            device_id_type=MESH,
        ).start()

    def wait(self, sem, rows):
        if rows:
            span = self.target.at[pl.ds(0, rows)]
            pltpu.make_async_copy(span, span, sem).wait()

    def start_rest(self):
        def body(start, size):
            def go(i, carry):
                other = lax.rem(self.deep + i, self.plan.depth)
                self.push(0, self.at(self.deep, start, size), (self.dp, 2 * other + self.core))
                return carry

            if size:
                lax.fori_loop(1, self.plan.depth, go, 0)

        self.by_part(body)

    def start_dp(self):
        plan = self.plan

        def body(start, size):
            self.wait(self.recv[0], (plan.depth - 1) * size)

            def go(i, carry):
                other = lax.rem(self.deep + i, plan.depth)
                for k in range(1, plan.nd):
                    self.push(
                        1, self.at(other, start, size), (lax.rem(self.dp + k, plan.nd), self.fs)
                    )
                return carry

            if size:
                lax.fori_loop(1, plan.depth, go, 0)

        self.by_part(body)

    def start_core(self):
        plan = self.plan
        self.by_part(
            lambda start, size: self.wait(self.recv[1], (plan.depth - 1) * (self.covered - size))
        )

        def go(z, carry):
            for start, size in [(0, self.rows)] if self.whole else self.parts:
                self.push(2, self.at(z, start, size), (self.dp, 2 * self.deep + 1 - self.core))
            return carry

        lax.fori_loop(0, plan.depth, go, 0)

    def complete(self):
        plan = self.plan
        self.wait(self.recv[2], plan.depth * self.covered)

        def body(start, size):
            self.wait(self.send[0], (plan.depth - 1) * size)
            self.wait(self.send[1], (plan.depth - 1) * (plan.nd - 1) * size)

        self.by_part(body)
        self.wait(self.send[2], plan.depth * self.covered)


def spread_shards(plan, block, flat, mine):
    start = lax.axis_index("fsdp") * plan.shard
    offset = start - start // (16 * LANE) * (16 * LANE)
    down, turn = offset // LANE, lax.rem(offset, LANE)
    full = plan.shard // LANE
    rest = plan.shard - full * LANE
    size = plan.chunk + 32
    lane = lax.broadcasted_iota(jnp.int32, (16, LANE), 1)
    for layer in range(LAYERS):
        flat[layer * size : layer * size + 24, :] = jnp.zeros((24, LANE), F32)

    def take(layer, i, count):
        piece = block[:, pl.ds(pl.multiple_of(i * 8 * LANE, LANE), count * LANE)]
        rows = [piece[layer : layer + 1, k * LANE : (k + 1) * LANE] for k in range(count)]
        at = pl.ds(pl.multiple_of(layer * size + 24 + i * 8, 8), count)
        flat[at, :] = jnp.concatenate(rows, axis=0) if count > 1 else rows[0]

    def fill(layer):
        def step(i, carry):
            take(layer, i, 8)
            return carry

        lax.fori_loop(0, full // 8, step, 0)
        if full % 8:
            take(layer, full // 8, full % 8)
        at = layer * size + 24 + full
        if rest:
            last = block[layer : layer + 1, full * LANE : full * LANE + rest]
            flat[at : at + 1, :] = jnp.concatenate([last, jnp.zeros((1, LANE - rest), F32)], axis=1)
            at += 1
        end = (layer + 1) * size
        flat[at:end, :] = jnp.zeros((end - at, LANE), F32)

    def shift(layer):
        fill(layer)

        def go(i, carry):
            begin = layer * size + 24 + i * 16 - down
            here = pltpu.roll(flat[pl.ds(begin, 16), :], turn, 1)
            before = pltpu.roll(flat[pl.ds(begin - 1, 16), :], turn, 1)
            value = jnp.where(lane >= turn, here, before)
            mine[layer][pl.ds(pl.multiple_of(i * 16, 16), 16), :] = value.astype(BF16)
            return carry

        lax.fori_loop(0, plan.chunk // 16, go, 0)

    return shift


def unpack_weights(plan, got, we, wp, wr, wx, small, tail, flat):
    lane = lax.broadcasted_iota(jnp.int32, (1, LANE), 1)
    low = lane < SQ
    for f in range(plan.nf):
        base, at = plan.base[f], f * plan.chunk
        head = got[at : at + 16, :].astype(F32)
        if f:
            head = head + flat[base : base + 16, :]
        flat[base : base + 16, :] = head
        flat[base + 16 : base + plan.chunk, :] = got[at + 16 : at + plan.chunk, :].astype(F32)
    for j in range(NJ):
        cols = slice(j * LANE, (j + 1) * LANE)
        we[:, cols] = flat[pl.ds(j, C, stride=NJ), :].astype(BF16)
        wx[0:SQ, cols] = flat[pl.ds(ROW_X + j, SQ, stride=NJ), :].astype(BF16)
        wx[SQ:LANE, cols] = jnp.zeros((LANE - SQ, LANE), BF16)
        small[0:14, cols] = flat[pl.ds(ROW_D + j, 14, stride=NJ), :]
        small[14:16, cols] = jnp.zeros((2, LANE), F32)
    for h in range(C // LANE):
        wp[:, h * LANE : (h + 1) * LANE] = flat[pl.ds(ROW_P + h, E, stride=2), :].astype(BF16)
    pairs = flat[ROW_R:ROW_X, :]
    evens, odds = jnp.where(low, pairs, 0.0), jnp.where(low, pltpu.roll(pairs, SQ, 1), 0.0)
    flat[pl.ds(0, E // 2, stride=2), :] = evens
    flat[pl.ds(1, E // 2, stride=2), :] = odds
    wr[...] = flat[0:E, :].astype(BF16)
    rows = [flat[ROW_S + i : ROW_S + i + 1, :] for i in range(5)]
    turned = [pltpu.roll(jnp.broadcast_to(r, (8, LANE)), SQ, 1)[0:1, :] for r in rows]
    tail[...] = jnp.zeros((8, C), F32)
    tail[0:1, 0:LANE] = jnp.where(low, rows[0], 0.0)
    for i, at in ((1, 0), (2, 2)):
        tail[i : i + 1, 0:LANE] = jnp.where(low, turned[at], turned[at + 1])
        tail[i : i + 1, LANE:C] = jnp.where(low, turned[at + 1], turned[at + 2])


def mix_images(plan, images, partner, share_one, stream, first, last):
    n, rows = plan.images, plan.rows
    place = lax.broadcasted_iota(jnp.int32, (n, rows), 1)
    own = lax.broadcasted_iota(jnp.int32, (n, rows), 0) * PIX
    chosen = partner * PIX

    def go(p, carry):
        mine = dot(jnp.where(place == own + p, 1.0, 0.0).astype(BF16), images[...])
        theirs = dot(jnp.where(place == chosen + p, 1.0, 0.0).astype(BF16), images[...])
        at = pl.ds(pl.multiple_of(p * n, n), n)
        stream[at, :] = share_one * mine + (1.0 - share_one) * theirs
        return carry

    lax.fori_loop(first, last, go, 0)


def forward_layer(plan, r, layer, hooks):
    x, expanded, depth, act, sums, x_low = r.stream, r.expanded, r.depth, r.flow, r.sums, r.x_low
    normed_three, stat_e, stat_c = r.normed_three.at[layer], r.stat_e.at[layer], r.stat_c.at[layer]
    pooled, presq, gate, turned = r.pooled.at[layer], r.presq.at[layer], r.gate.at[layer], r.turned.at[layer]
    we, wp, wr, wx = r.we.at[layer], r.wp.at[layer], r.wr.at[layer], r.wx.at[layer]
    small, tail = r.small.at[layer], r.tail.at[layer]
    ex_one, ex_two, ex_three = r.ex_wide[0:GROUPS], r.ex_wide[GROUPS : 2 * GROUPS], r.ex_thin
    n = plan.images
    x_low[...] = x[...].astype(BF16)
    for g in range(GROUPS):
        cols = slice(g * GW, (g + 1) * GW)

        def expand(m, carry, cols=cols):
            rows = pl.ds(pl.multiple_of(m * MBLK * n, MBLK * n), MBLK * n)
            value = dot(x_low[rows, :], we[:, cols])
            expanded[pl.ds(m * MBLK, MBLK), :, cols] = value.reshape(MBLK, n, GW)
            return (
                carry[0] + jnp.sum(value.reshape(-1, 8, GW), axis=0),
                carry[1] + jnp.sum((value * value).reshape(-1, 8, GW), axis=0),
            )

        zero = jnp.zeros((8, GW), F32)
        s, q = lax.fori_loop(0, PIX // MBLK, expand, (zero, zero))
        if g:
            ex_one[g - 1].relay()
        ex_one[g].share(row_sum(s), row_sum(q))
    turned[...] = x[...].T.astype(BF16)
    ex_one[GROUPS - 1].relay()

    def put_sums(j, totals):
        for i, t in enumerate(totals):
            sums[i : i + 1, lanes(j)] = row_sum(t)

    for g in range(GROUPS):
        cols = slice(g * GW, (g + 1) * GW)
        mean, rstd = moments(plan, ex_one[g].collect())
        if g == 0:
            r.spill_e.start(layer)
            if layer:
                r.spill_d.wait()
        stat_e[0:1, cols] = mean
        stat_e[1:2, cols] = rstd
        scale = rstd * small[9:10, cols]
        stat_e[4:5, cols] = 0.5 * scale
        stat_e[5:6, cols] = 0.5 * (small[10:11, cols] - mean * scale)

        def chunk(j):
            return (
                stat_e[4:5, lanes(j)],
                stat_e[5:6, lanes(j)],
                [small[t : t + 1, lanes(j)] for t in range(9)],
            )

        def spread(j, b, hoisted, totals):
            scale, shift, w = hoisted
            act_one = []
            for p in range(PIX):
                half = expanded[p, images_at(b), lanes(j)] * scale + shift
                act_one.append(half * half_tanh(half) + half)
            made = [None] * PIX
            for o, t, i in TAPS:
                term = act_one[i] * w[t]
                made[o] = term if made[o] is None else made[o] + term
            s, q = totals
            for p in range(PIX):
                depth[p, images_at(b), lanes(j)] = made[p]
                s = s + made[p]
                q = q + made[p] * made[p]
            return s, q

        between = ex_two[g - 1].relay if g else None
        over_tiles_and(
            plan, g * (GW // LANE), GW // LANE, between, chunk, spread, 2, put_sums, UN_SPREAD
        )
        ex_two[g].share(sums[0:1, cols], sums[1:2, cols])
        if g == 0:
            hooks[0]()
    ex_two[GROUPS - 1].relay()
    hooks[1]()

    for g in range(GROUPS):
        cols = slice(g * GW, (g + 1) * GW)
        mean, rstd = moments(plan, ex_two[g].collect())
        if g == 0:
            if layer < LAYERS - 1:
                r.spill_d.start(layer)
        stat_e[2:3, cols] = mean
        stat_e[3:4, cols] = rstd
        scale = rstd * small[11:12, cols]
        stat_e[6:7, cols] = 0.5 * scale
        stat_e[7:8, cols] = 0.5 * (small[12:13, cols] - mean * scale)

        def chunk_two(j):
            return stat_e[6:7, lanes(j)], stat_e[7:8, lanes(j)]

        def activate(j, b, hoisted, totals):
            scale, shift = hoisted
            total = None
            for p in range(PIX):
                half = depth[p, images_at(b), lanes(j)] * scale + shift
                made = half * half_tanh(half) + half
                act[p, images_at(b), lanes(j)] = made
                total = made if total is None else total + made
            pooled[images_at(b), lanes(j)] = total * (1.0 / PIX)
            return totals

        over_tiles(
            plan, g * (GW // LANE), GW // LANE, chunk_two, activate, 0, lambda j, s: None, UN_ACT
        )
    reduced = dot_rows(pooled[...], wr[...]) + tail[0:1, 0:LANE]
    presq[...] = reduced
    gate[...] = sigmoid(dot_rows(silu(reduced), wx[...]) + small[13:14, :])

    hooks[2]()
    r.spill_e.wait()

    def project(m, carry):
        gated = (act[pl.ds(m * MBLK, MBLK), :, :] * gate[...][None]).astype(BF16)
        value = dot(gated.reshape(MBLK * n, E), wp[...])
        expanded[pl.ds(m * MBLK, MBLK), :, 0:C] = value.reshape(MBLK, n, C)
        return (
            carry[0] + jnp.sum(value.reshape(-1, 8, C), axis=0),
            carry[1] + jnp.sum((value * value).reshape(-1, 8, C), axis=0),
        )

    zero = jnp.zeros((8, C), F32)
    s, q = lax.fori_loop(0, PIX // MBLK, project, (zero, zero))
    ex_three.share(row_sum(s), row_sum(q))
    hooks[3]()
    mean, rstd = moments(plan, ex_three.collect())
    stat_c[...] = jnp.zeros((8, C), F32)
    stat_c[0:1, :] = mean
    stat_c[1:2, :] = rstd
    normed = (expanded[:, :, 0:C].reshape(n * PIX, C) - mean) * rstd
    normed_three[...] = normed.astype(BF16)
    x[...] = x[...] + normed * tail[1:2, :] + tail[2:3, :]


def head_layers(plan, r, label, label_row, partner, weight):
    x, x_low, turned, bias, totals_out = r.stream, r.x_low, r.turned.at[LAYERS], r.bias, r.totals
    w_head = grad_head = r.w_head
    hidden, slope, low_grad, pool, stat = r.expanded, r.flow, r.gated, r.squeeze_grad, r.coef
    sums, gain, grad_x = r.sums, r.sums.at[pl.ds(8, 8)], r.stream
    hd, n = plan.hd, plan.images
    halves = plan.head_groups
    ng = len(halves)
    ex_stat, ex_grad, ex_bias = r.ex_wide[0:ng], r.ex_wide[GROUPS : GROUPS + ng], r.ex_bias
    x_low[...] = x[...].astype(BF16)
    gain[:, 0:hd] = w_head[0:hd, C : C + LANE].astype(F32).T[0:8, :]
    for g, (start, width) in enumerate(halves):
        cols = slice(start, start + width)

        def convolve(m, carry, cols=cols, width=width):
            rows = pl.ds(pl.multiple_of(m * MBLK * n, MBLK * n), MBLK * n)
            value = dot(x_low[rows, :], w_head[cols, 0:C], ((1,), (1,)))
            hidden[pl.ds(m * MBLK, MBLK), :, cols] = value.reshape(MBLK, n, width)
            return (
                carry[0] + jnp.sum(value.reshape(-1, 8, width), axis=0),
                carry[1] + jnp.sum((value * value).reshape(-1, 8, width), axis=0),
            )

        zero = jnp.zeros((8, width), F32)
        s, q = lax.fori_loop(0, PIX // MBLK, convolve, (zero, zero))
        if g:
            ex_stat[g - 1].relay()
        ex_stat[g].share(row_sum(s), row_sum(q))
    turned[...] = x[...].T.astype(BF16)
    ex_stat[ng - 1].relay()
    for g, (start, width) in enumerate(halves):
        cols = slice(start, start + width)
        mean, rstd = moments(plan, ex_stat[g].collect())
        scale = rstd * gain[0:1, cols]
        stat[0:1, cols] = rstd
        stat[1:2, cols] = -mean * rstd
        stat[2:3, cols] = 0.5 * scale
        stat[3:4, cols] = 0.5 * (gain[1:2, cols] - mean * scale)

        def chunk(j):
            return stat[2:3, lanes(j)], stat[3:4, lanes(j)]

        def activate(j, b, hoisted, totals):
            scale, shift = hoisted
            total = None
            for p in range(PIX):
                half = hidden[p, images_at(b), lanes(j)] * scale + shift
                t = half_tanh(half)
                made = half * t + half
                slope[p, images_at(b), lanes(j)] = (1.0 + t) + half * (1.0 - t * t)
                total = made if total is None else total + made
            pool[images_at(b), lanes(j)] = total * (1.0 / PIX)
            return totals

        over_tiles(plan, start // LANE, width // LANE, chunk, activate, 0, lambda j, s: None, UN_ACT)
    pool_low = pool[:, 0:hd].astype(BF16)
    classes = lax.broadcasted_iota(jnp.int32, (n, KP), 1)
    valid = classes < K
    logits = dot(pool_low, w_head[0:hd, C + LANE :]) + bias[...]
    logits = jnp.where(valid, logits, -1e30)
    top = jnp.max(logits, axis=1, keepdims=True)
    lifted = logits - top
    powers = jnp.where(valid, jnp.exp(lifted), 0.0)
    norm = jnp.sum(powers, axis=1, keepdims=True)
    log_probs = lifted - jnp.log(norm)
    picked = lax.broadcasted_iota(jnp.int32, (n, n), 1) == partner
    label_two = jnp.sum(jnp.where(picked, label_row[...], 0), axis=1, keepdims=True)
    w = weight
    targets = w * jnp.where(classes == label, 1.0 - SMOOTHING, 0.0) + (1.0 - w) * jnp.where(
        classes == label_two, 1.0 - SMOOTHING, 0.0
    )
    targets = jnp.where(valid, targets + SMOOTHING / K, 0.0)
    loss = -jnp.sum(jnp.where(valid, targets * log_probs, 0.0))
    grad_logits = (powers / norm - targets) * (float(PIX) / plan.count)
    packed_bias = jnp.where(classes[0:1, :] == KP - 1, loss, row_sum(grad_logits))
    ex_bias.share(packed_bias[:, 0 : KP // 2], packed_bias[:, KP // 2 :])
    grad_low = grad_logits.astype(BF16)
    pool_grad = dot(grad_low, w_head[0:hd, C + LANE :], ((1,), (1,)))
    pool[:, 0:hd] = pool_grad * (0.5 / PIX)

    def put_sums(j, totals):
        flow_sum, value_sum = [row_sum(t) for t in totals]
        sums[0:1, lanes(j)] = flow_sum
        sums[1:2, lanes(j)] = value_sum * stat[0:1, lanes(j)] + flow_sum * stat[1:2, lanes(j)]

    for g, (start, width) in enumerate(halves):
        cols = slice(start, start + width)

        def back(j, b, hoisted, totals):
            s, q = totals
            flow = pool[images_at(b), lanes(j)]
            for p in range(PIX):
                made = slope[p, images_at(b), lanes(j)] * flow
                slope[p, images_at(b), lanes(j)] = made
                s = s + made
                q = q + made * hidden[p, images_at(b), lanes(j)]
            return s, q

        between = ex_grad[g - 1].relay if g else None
        over_tiles_and(
            plan, start // LANE, width // LANE, between, lambda j: None, back, 2, put_sums, UN_HBACK
        )
        ex_grad[g].share(sums[0:1, cols], sums[1:2, cols])
    grad_head[0:hd, C + LANE :] = dot(pool_low.T, grad_low).astype(BF16)
    ex_grad[ng - 1].relay()
    norm_grads = jnp.concatenate(
        [sums[1:2, 0:hd], sums[0:1, 0:hd], jnp.zeros((LANE - 2, hd), F32)], axis=0
    )
    grad_head[0:hd, C : C + LANE] = norm_grads.T.astype(BF16)
    for g, (start, width) in enumerate(halves):
        cols = slice(start, start + width)
        shift_total, gain_total = ex_grad[g].collect()
        scale = stat[0:1, cols] * gain[0:1, cols]
        mean_one = shift_total / plan.count
        mean_two = gain_total / plan.count
        stat[4:5, cols] = scale
        stat[5:6, cols] = -scale * stat[0:1, cols] * mean_two
        stat[6:7, cols] = -scale * (mean_one + stat[1:2, cols] * mean_two)
    def into(m, carry):
        rows = pl.ds(pl.multiple_of(m * MBLK * n, MBLK * n), MBLK * n)
        spot = pl.ds(m * MBLK, MBLK)
        value = (
            slope[spot, :, 0:hd] * stat[4:5, 0:hd]
            + hidden[spot, :, 0:hd] * stat[5:6, 0:hd]
            + stat[6:7, 0:hd]
        )
        low = value.reshape(MBLK * n, hd).astype(BF16)
        low_grad[rows, 0:hd] = low
        grad_x[rows, :] = dot(low, w_head[0:hd, 0:C])
        return carry

    lax.fori_loop(0, PIX // MBLK, into, 0)
    r.spill_e.fetch(LAYERS - 1)
    for at in range(0, hd, LANE):
        part = dot(turned[...], low_grad[:, at : at + LANE])
        grad_head[at : at + LANE, 0:C] = part.T.astype(BF16)
    totals_out[...] = jnp.concatenate(ex_bias.collect(), axis=1)


def backward_layer(plan, r, layer, hooks):
    expanded, depth, flow, gated, sums, coef = r.expanded, r.depth, r.flow, r.gated, r.sums, r.coef
    normed_three, stat_e, stat_c = r.normed_three.at[layer], r.stat_e.at[layer], r.stat_c.at[layer]
    pooled, presq, gate, turned = r.pooled.at[layer], r.presq.at[layer], r.gate.at[layer], r.turned.at[layer]
    we, wp, wr, wx = r.we.at[layer], r.wp.at[layer], r.wr.at[layer], r.wx.at[layer]
    small, tail = r.small.at[layer], r.tail.at[layer]
    grad = grad_x = r.stream
    low_proj, squeeze_grad, flat, packed = r.x_low, r.squeeze_grad, r.flat, r.stage
    ex_one, ex_two, ex_three = r.ex_wide[0:GROUPS], r.ex_wide[GROUPS : 2 * GROUPS], r.ex_thin
    n = plan.images
    lane = lax.broadcasted_iota(jnp.int32, (1, LANE), 1)
    is_low = lane < SQ
    rstd_c = stat_c[1:2, :]
    s = row_sum(jnp.sum(grad[...].reshape(-1, 8, C), axis=0))
    q = row_sum(
        jnp.sum((grad[...] * normed_three[...].astype(F32)).reshape(-1, 8, C), axis=0)
    )
    ex_three.share(s, q)
    hooks[0]()
    bias_three, gain_three = s, q

    if layer < LAYERS - 1:
        r.spill_d.wait()

    def chunk_two(j):
        return stat_e[6:7, lanes(j)], stat_e[7:8, lanes(j)]

    def regate(p, carry):
        rows = pl.ds(pl.multiple_of(p * n, n), n)
        for j in range(NJ):
            cols = slice(j * LANE, (j + 1) * LANE)
            half = depth[p, :, cols] * stat_e[6:7, cols] + stat_e[7:8, cols]
            value = (half * half_tanh(half) + half) * gate[:, cols]
            gated[rows, cols] = value.astype(BF16)
        return carry

    lax.fori_loop(0, PIX, regate, 0)

    bias_total, gain_total = ex_three.collect()
    scale = rstd_c * tail[1:2, :]
    mean_one, mean_two = bias_total / plan.count, gain_total / plan.count
    low_proj[...] = (
        scale
        * (grad[...] - mean_one - normed_three[...].astype(F32) * mean_two)
    ).astype(BF16)

    def into_gated(m, carry):
        rows = pl.ds(pl.multiple_of(m * MBLK * n, MBLK * n), MBLK * n)
        value = dot(low_proj[rows, :], wp[...], ((1,), (1,)))
        flow[pl.ds(m * MBLK, MBLK), :, :] = value.reshape(MBLK, n, E)
        return carry

    lax.fori_loop(0, PIX // MBLK, into_gated, 0)
    hooks[1]()

    def gate_back(t, carry):
        j, b = t // (n // 16), lax.rem(t, n // 16)
        block = pl.ds(pl.multiple_of(b * 16, 16), 16)
        total = None
        for p in range(PIX):
            low = gated[pl.ds(pl.multiple_of(p * n + b * 16, 16), 16), lanes(j)].astype(F32)
            term = flow[p, block, lanes(j)] * low
            total = term if total is None else total + term
        squeeze_grad[block, lanes(j)] = total * (1.0 - gate[block, lanes(j)])
        return carry

    lax.fori_loop(0, NJ * (n // 16), gate_back, 0)
    excite_grad = squeeze_grad[...]
    sums[13:14, :] = row_sum(excite_grad)
    squeezed = silu(presq[...])
    presq_grad = dot_rows(excite_grad, wx[...], ((1,), (1,))) * silu_slope(presq[...])
    grad_wx = dot_outer(squeezed, excite_grad)
    flat[ROW_R : ROW_R + E, :] = dot_outer(pooled[...], presq_grad)
    evens = flat[pl.ds(ROW_R, E // 2, stride=2), :]
    odds = flat[pl.ds(ROW_R + 1, E // 2, stride=2), :]
    flat[ROW_R:ROW_X, :] = jnp.where(is_low, evens, pltpu.roll(odds, SQ, 1))
    for j in range(NJ):
        flat[pl.ds(ROW_X + j, SQ, stride=NJ), :] = grad_wx[0:SQ, j * LANE : (j + 1) * LANE]
    grad_reduce_b = row_sum(presq_grad)
    squeeze_grad[...] = dot_rows(presq_grad, wr[...], ((1,), (1,))) * (1.0 / PIX)

    def put_sums(first_row, stat_row):
        def put(j, totals):
            rows = [row_sum(t) for t in totals]
            mean = stat_e[stat_row : stat_row + 1, lanes(j)]
            rstd = stat_e[stat_row + 1 : stat_row + 2, lanes(j)]
            rows[-2] = (rows[-2] - mean * rows[-1]) * rstd
            for i, t in enumerate(rows):
                sums[first_row + i : first_row + i + 1, lanes(j)] = t

        return put

    def back_two(j, b, hoisted, totals):
        scale, shift = hoisted
        gain_sum, bias_sum = totals
        opened = gate[images_at(b), lanes(j)] * 0.5
        pool_flow = squeeze_grad[images_at(b), lanes(j)] * 0.5
        for p in range(PIX):
            value = depth[p, images_at(b), lanes(j)]
            half = value * scale + shift
            t = half_tanh(half)
            made = (flow[p, images_at(b), lanes(j)] * opened + pool_flow) * (
                (1.0 + t) + half * (1.0 - t * t)
            )
            flow[p, images_at(b), lanes(j)] = made
            bias_sum = bias_sum + made
            gain_sum = gain_sum + made * value
        return gain_sum, bias_sum

    for g in range(GROUPS):
        cols = slice(g * GW, (g + 1) * GW)
        between = ex_two[g - 1].relay if g else None
        over_tiles_and(
            plan, g * (GW // LANE), GW // LANE, between, chunk_two, back_two, 2, put_sums(11, 2), UN_TWO
        )
        ex_two[g].share(sums[12:13, cols], sums[11:12, cols])

    proj_turned = low_proj[...].astype(F32).T.astype(BF16)
    ex_two[GROUPS - 1].relay()
    hooks[2]()
    for j in range(NJ):
        part = dot(proj_turned, gated[:, j * LANE : (j + 1) * LANE])
        for h in range(C // LANE):
            flat[pl.ds(ROW_P + 2 * j * LANE + h, LANE, stride=2), :] = part[
                h * LANE : (h + 1) * LANE, :
            ].T

    def norm_coefs(g, pair, row, stat_row, gain_row):
        cols = slice(g * GW, (g + 1) * GW)
        mean, rstd = stat_e[stat_row : stat_row + 1, cols], stat_e[stat_row + 1 : stat_row + 2, cols]
        scale = rstd * small[gain_row : gain_row + 1, cols]
        mean_one, mean_two = pair[0] / plan.count, pair[1] / plan.count
        coef[row : row + 1, cols] = scale
        coef[row + 1 : row + 2, cols] = -scale * rstd * mean_two
        coef[row + 2 : row + 3, cols] = -scale * (mean_one - mean * rstd * mean_two)

    def chunk_one(j):
        return (
            [coef[i : i + 1, lanes(j)] for i in range(3)],
            [small[t : t + 1, lanes(j)] for t in range(9)],
            [stat_e[i : i + 1, lanes(j)] for i in (4, 5)],
        )

    def back_one(j, b, hoisted, totals):
        (c_flow, c_value, c_const), w, (scale, shift) = hoisted
        w_sums, gain_sum, bias_sum = list(totals[:9]), totals[9], totals[10]
        spread_grad = []
        for p in range(PIX):
            spread_grad.append(
                flow[p, images_at(b), lanes(j)] * c_flow
                + (depth[p, images_at(b), lanes(j)] * c_value + c_const)
            )
        act_one, slopes = [], []
        for p in range(PIX):
            half = expanded[p, images_at(b), lanes(j)] * scale + shift
            t = half_tanh(half)
            act_one.append(half * t + half)
            slopes.append(0.5 * ((1.0 + t) + half * (1.0 - t * t)))
        made = [None] * PIX
        for o, t, i in TAPS:
            w_sums[t] = w_sums[t] + spread_grad[o] * act_one[i]
            term = spread_grad[o] * w[t]
            made[i] = term if made[i] is None else made[i] + term
        for p in range(PIX):
            value = expanded[p, images_at(b), lanes(j)]
            result = made[p] * slopes[p]
            flow[p, images_at(b), lanes(j)] = result
            bias_sum = bias_sum + result
            gain_sum = gain_sum + result * value
        return tuple(w_sums) + (gain_sum, bias_sum)

    for g in range(GROUPS):
        cols = slice(g * GW, (g + 1) * GW)
        norm_coefs(g, ex_two[g].collect(), 0, 2, 11)
        if g == 0:
            r.spill_e.wait()
        between = ex_one[g - 1].relay if g else None
        over_tiles_and(
            plan, g * (GW // LANE), GW // LANE, between, chunk_one, back_one, 11, put_sums(0, 0), UN_ONE
        )
        ex_one[g].share(sums[10:11, cols], sums[9:10, cols])

    if layer:
        r.spill_d.fetch(layer - 1)
    for j in range(NJ):
        flat[pl.ds(ROW_D + j, 14, stride=NJ), :] = sums[0:14, j * LANE : (j + 1) * LANE]

    def turn(row):
        return pltpu.roll(jnp.broadcast_to(row, (8, LANE)), SQ, 1)[0:1, :]

    pieces = [turn(v[:, h * LANE : (h + 1) * LANE]) for v in (gain_three, bias_three) for h in (0, 1)]
    flat[ROW_S : ROW_S + 1, :] = jnp.where(is_low, grad_reduce_b, pieces[0])
    for i in range(3):
        flat[ROW_S + 1 + i : ROW_S + 2 + i, :] = jnp.where(is_low, pieces[i], pieces[i + 1])
    flat[ROW_S + 4 : ROW_S + 5, :] = pieces[3]
    hooks[3]()
    ex_one[GROUPS - 1].relay()
    hooks[4]()

    for g in range(GROUPS):
        cols = slice(g * GW, (g + 1) * GW)
        norm_coefs(g, ex_one[g].collect(), 0, 0, 9)

        def into(m, carry, cols=cols):
            rows = pl.ds(pl.multiple_of(m * MBLK * n, MBLK * n), MBLK * n)
            spot = pl.ds(m * MBLK, MBLK)
            value = (
                flow[spot, :, cols] * coef[0:1, cols]
                + expanded[spot, :, cols] * coef[1:2, cols]
                + coef[2:3, cols]
            )
            low = value.reshape(MBLK * n, GW).astype(BF16)
            gated[rows, cols] = low
            grad_x[rows, :] += dot(low, we[:, cols], ((1,), (1,)))
            return carry

        lax.fori_loop(0, PIX // MBLK, into, 0)
        for j in range(g * (GW // LANE), (g + 1) * (GW // LANE)):
            flat[pl.ds(j, C, stride=NJ), :] = dot(
                turned[...], gated[:, j * LANE : (j + 1) * LANE]
            )
    if layer:
        r.spill_e.fetch(layer - 1)
    packed[0 : plan.flat, :] = flat[0 : plan.flat, :].astype(BF16)
    hooks[5]()


class Spill:
    def __init__(self, held, kept, sem):
        self.held, self.kept, self.sem = held, kept, sem

    def start(self, layer):
        self.copy = pltpu.make_async_copy(self.held, self.kept.at[layer], self.sem)
        self.copy.start()

    def fetch(self, layer):
        self.copy = pltpu.make_async_copy(self.kept.at[layer], self.held, self.sem)
        self.copy.start()

    def wait(self):
        self.copy.wait()


INPUTS = ("block", "w_own", "images", "per_image", "bias")
OUTPUTS = ("block_sums", "head_sums", "totals", "kept_e", "kept_d")


def scratch_of(plan):
    n, rows, hd = plan.images, plan.rows, plan.hd
    wide = 2 * GW // LANE
    vm = lambda shape, dtype=F32: pltpu.VMEM(shape, dtype)
    held = {
        "expanded": vm((PIX, n, E)),
        "depth": vm((PIX, n, E)),
        "flow": vm((PIX, n, E)),
        "gated": vm((rows, E), BF16),
        "stream": vm((rows, C)),
        "x_low": vm((rows, C), BF16),
        "turned": vm((LAYERS + 1, C, rows), BF16),
        "normed_three": vm((LAYERS, rows, C), BF16),
        "stat_e": vm((LAYERS, 8, E)),
        "stat_c": vm((LAYERS, 8, C)),
        "pooled": vm((LAYERS, n, E)),
        "presq": vm((LAYERS, n, LANE)),
        "gate": vm((LAYERS, n, E)),
        "we": vm((LAYERS, C, E), BF16),
        "wp": vm((LAYERS, E, C), BF16),
        "wr": vm((LAYERS, E, LANE), BF16),
        "wx": vm((LAYERS, LANE, E), BF16),
        "small": vm((LAYERS, 16, E)),
        "tail": vm((LAYERS, 8, C)),
        "w_head": vm((plan.head_flat, HEAD_W), BF16),
        "squeeze_grad": vm((n, E)),
        "sums": vm((16, E)),
        "coef": vm((8, E)),
        "flat": vm((max(plan.flat, LAYERS * (plan.chunk + 32)), LANE)),
        "stage": vm((max(plan.nf * plan.chunk, plan.flat), LANE), BF16),
        "spill_sems": pltpu.SemaphoreType.DMA((2,)),
    }
    for i in range(2 * GROUPS):
        held[f"pair{i}"] = vm((2, wide, LANE))
        held[f"wide{i}"] = vm((plan.devices // 2, wide, LANE))
        for k in range(4):
            held[f"wide{i}_{k}"] = pltpu.SemaphoreType.DMA(())
    held["thin"] = vm((plan.devices, 2 * C // LANE, LANE))
    held["thick"] = vm((plan.devices, KP // LANE, LANE))
    for name in ("thin", "thick"):
        held[name + "_send"] = pltpu.SemaphoreType.DMA(())
        held[name + "_recv"] = pltpu.SemaphoreType.DMA(())
    for name in ("block", "head", "half"):
        for i in range(6):
            held[f"gather_{name}{i}"] = pltpu.SemaphoreType.DMA(())
    for name, unit in (("block", plan.layer_unit()), ("head", plan.head_unit())):
        for i, shape in enumerate(Reduction.scratch(unit)):
            if name == "block" or i < 4:
                held[f"reduce_{name}{i}"] = shape
    for i, shape in enumerate(Reduction.scratch(plan.layer_unit())[3:]):
        held[f"reduce_last{i}"] = shape
    for i in range(8):
        held[f"reduce_half{i}"] = pltpu.SemaphoreType.DMA(())
    for i in range(8 * len(plan.head_thirds)):
        held[f"reduce_third{i}"] = pltpu.SemaphoreType.DMA(())
    return held


def step_kernel(plan, names, *refs):
    r = types.SimpleNamespace(**dict(zip(names, refs, strict=True)))
    held = vars(r)
    exchange = lambda name: Exchange(plan, held[name], held[name + "_send"], held[name + "_recv"])
    r.ex_wide = [
        PairedExchange(
            plan, held[f"pair{i}"], held[f"wide{i}"], [held[f"wide{i}_{k}"] for k in range(4)]
        )
        for i in range(2 * GROUPS)
    ]
    r.ex_thin, r.ex_bias = exchange("thin"), exchange("thick")
    r.spill_e = Spill(r.expanded, r.kept_e, r.spill_sems.at[0])
    r.spill_d = Spill(r.depth, r.kept_d, r.spill_sems.at[1])
    reduce_refs = {
        name: [held[f"reduce_{name}{i}"] for i in range(count)]
        for name, count in (("block", 12), ("head", 4))
    }
    reduce_refs["last"] = reduce_refs["block"][:3] + [held[f"reduce_last{i}"] for i in range(9)]
    reduce_refs["half"] = reduce_refs["last"][:4] + [held[f"reduce_half{i}"] for i in range(8)]
    fs = lax.axis_index("fsdp")
    n = plan.images

    enter(plan)
    mine = [r.gated.at[pl.ds(0, plan.chunk), pl.ds(C + i * LANE, LANE)] for i in range(LAYERS)]
    images = r.gated.at[pl.ds(0, plan.rows), pl.ds(0, C)]
    take_images = pltpu.make_async_copy(r.images, images, r.spill_sems.at[0])
    take_images.start()
    take_head = pltpu.make_async_copy(
        r.w_own,
        r.w_head.at[pl.ds(pl.multiple_of(fs * plan.head_pad, 16), plan.head_pad)],
        r.spill_sems.at[1],
    )
    take_head.start()
    shift = spread_shards(plan, r.block, r.flat, mine)
    own_rows = pl.ds(pl.multiple_of(fs * plan.chunk, 16), plan.chunk)

    def gather_of(layer, name="block", half=None):
        if not half:
            r.stage[own_rows, :] = mine[layer][...]
        sems = [held[f"gather_{name}{i}"] for i in range(6)]
        return Gather(plan, r.stage, plan.chunk, sems, half)

    def unpack(layer):
        unpack_weights(
            plan,
            r.stage,
            r.we.at[layer],
            r.wp.at[layer],
            r.wr.at[layer],
            r.wx.at[layer],
            r.small.at[layer],
            r.tail.at[layer],
            r.flat,
        )

    shift(0)
    gathers = [gather_of(0, "block", 0), gather_of(0, "half", 1)]
    head_gather = Gather(
        plan, r.w_head, plan.head_pad, [held[f"gather_head{i}"] for i in range(6)]
    )
    entered(plan)
    for gather in gathers:
        gather.start_rest()
    columns = jnp.concatenate([r.per_image[...], jnp.zeros((8, LANE - n), F32)], axis=1).T
    weight, label, partner = (columns[0:n, i : i + 1] for i in range(3))
    label, partner = label.astype(jnp.int32), partner.astype(jnp.int32)
    label_row = r.per_image[1:2, :].astype(jnp.int32)
    take_images.wait()
    take_head.wait()
    mix_images(plan, images, partner, weight, r.stream, 0, PIX // 2)
    for gather in gathers:
        gather.start_dp()
    head_gather.start_rest()
    mix_images(plan, images, partner, weight, r.stream, PIX // 2, PIX)
    gathers[0].start_core()
    shift(1)
    gathers[1].start_core()
    head_gather.start_dp()
    shift(2)
    for gather in gathers:
        gather.complete()
    unpack(0)

    for layer in range(LAYERS):
        if layer < LAYERS - 1:
            box = []

            def begin(layer=layer, box=box):
                box.append(gather_of(layer + 1))
                box[0].start_rest()

            def arrive(layer=layer, box=box):
                box[0].complete()
                unpack(layer + 1)

            hooks = (
                begin,
                lambda box=box: box[0].start_dp(),
                lambda box=box: box[0].start_core(),
                arrive,
            )
            if layer == 0:
                hooks = (begin, hooks[1], hooks[2], lambda arrive=arrive: [arrive(), head_gather.start_core()])
        else:
            hooks = (lambda: None,) * 4
        forward_layer(plan, r, layer, hooks)
    head_gather.complete()
    head_layers(plan, r, label, label_row, partner, weight)

    head_unit = plan.head_unit()
    head_works = []
    for i, (skip, size) in enumerate(plan.head_thirds):
        sems = [held[f"reduce_third{8 * i + k}"] for k in range(8)]
        refs = reduce_refs["head"][:4] + sems
        head_works.append(Reduction(head_unit, r.w_head, r.head_sums, refs, skip, size))
    unit = plan.layer_unit()
    works = [None] + [
        Reduction(unit, r.stage, r.block_sums.at[layer], reduce_refs["block"])
        for layer in range(1, LAYERS)
    ]

    def both(*steps):
        return lambda: [step() for step in steps]

    last = LAYERS - 1
    for layer in reversed(range(LAYERS)):
        hooks = [[] for _ in range(6)]
        if layer == last:
            hooks[0] += [w.start_core for w in head_works] + [head_works[0].start_dp]
            for w, at in zip(head_works[1:], (2, 4)):
                hooks[at].append(w.start_dp)
        else:
            work = works[layer + 1]
            hooks[0].append(work.start_dp)
            hooks[2] += [work.sum_dp_parts, work.start_rest]
            hooks[4].append(work.start_copies)
        if layer == last - 1:
            for w in head_works:
                hooks[0] += [w.sum_dp_parts, w.start_rest]
                hooks[2].append(w.start_copies)
                hooks[4].append(w.complete)
        if layer + 2 <= last:
            hooks[1].append(works[layer + 2].complete)
        if layer:
            hooks[5].append(works[layer].start_core)
        backward_layer(plan, r, layer, [both(*steps) for steps in hooks])
    first = ceil_to(-(-unit.part // 2), 16)
    halves = [
        Reduction(unit, r.stage, r.block_sums.at[0], reduce_refs["last"], 0, first),
        Reduction(unit, r.stage, r.block_sums.at[0], reduce_refs["half"], first, unit.part - first),
    ]
    for half in halves:
        half.start_core()
    for half in halves:
        half.start_dp()
    works[1].complete()
    for half in halves:
        half.sum_dp_parts()
        half.start_rest()
    for half in halves:
        half.start_copies()
    for half in halves:
        half.complete()
    for e in r.ex_wide + [r.ex_thin, r.ex_bias]:
        e.finish()


def train_step(plan, block, w_own, images, per_image, bias):
    held = scratch_of(plan)
    block_unit, head_unit = plan.layer_unit(), plan.head_unit()
    big = (PIX, plan.images, E)
    anywhere = pl.BlockSpec(memory_space=pl.ANY)
    return pl.pallas_call(
        functools.partial(step_kernel, plan, INPUTS + OUTPUTS + tuple(held)),
        out_shape=(
            jax.ShapeDtypeStruct((LAYERS, block_unit.owned, LANE), BF16),
            jax.ShapeDtypeStruct((head_unit.owned, HEAD_W), BF16),
            jax.ShapeDtypeStruct((1, KP), F32),
            jax.ShapeDtypeStruct((LAYERS,) + big, F32),
            jax.ShapeDtypeStruct((LAYERS - 1,) + big, F32),
        ),
        in_specs=[VM, anywhere, anywhere, VM, VM],
        out_specs=(VM, VM, VM, anywhere, anywhere),
        scratch_shapes=list(held.values()),
        compiler_params=pltpu.CompilerParams(
            collective_id=1, has_side_effects=True, vmem_limit_bytes=VMEM_LIMIT
        ),
        name="train_step",
    )(block, w_own, images, per_image, bias)


def adam_update(master, first, second, average, grad):
    first_new = BETA_ONE * first + (1.0 - BETA_ONE) * grad
    second_new = BETA_TWO * second + (1.0 - BETA_TWO) * grad * grad
    fix_one = 1.0 - BETA_ONE**STEP
    fix_two = 1.0 - BETA_TWO**STEP
    master_new = master * (1.0 - RATE * DECAY_WEIGHT) - RATE * (first_new / fix_one) / (
        jnp.sqrt(second_new / fix_two) + EPS_ADAM
    )
    average_new = EMA_RATE * average + (1.0 - EMA_RATE) * master_new
    return (master_new, first_new, second_new, average_new)


def on_device(mesh, images, partner, mix_weight, labels, *states):
    block, head_state, bias_state = states[0:4], states[4:8], states[8:12]
    row = C + 2 + K
    plan = Plan(mesh, images.shape[0], head_state[0].shape[0] // row)
    half = (plan.hd // LANE + 1) // 2 * LANE
    plan.head_groups = [(0, half), (half, plan.hd - half)]
    start = lax.axis_index("fsdp") * plan.shard
    offset = start - start // (16 * LANE) * (16 * LANE)
    grid = head_state[0].astype(BF16).reshape(plan.head_rows, row)
    grid = jnp.concatenate(
        [
            grid[:, : C + 2],
            jnp.zeros((plan.head_rows, LANE - 2), BF16),
            grid[:, C + 2 :],
            jnp.zeros((plan.head_rows, KP - K), BF16),
        ],
        axis=1,
    )
    grid = jnp.pad(grid, ((0, plan.head_pad - plan.head_rows), (0, 0)))
    bias = jnp.pad(bias_state[0], (0, KP - K)).reshape(1, KP)
    per_image = jnp.stack(
        [mix_weight, labels.astype(F32), partner.astype(F32)] + [jnp.zeros_like(mix_weight)] * 5
    )
    block_grad, head_grad, totals = train_step(
        plan, block[0], grid, images.reshape(plan.rows, C), per_image, bias
    )[:3]
    loss_sum = totals[0, KP - 1]
    grad_bias = totals[0, :K]
    block_grad = lax.dynamic_slice(
        block_grad.reshape(LAYERS, plan.chunk * LANE), (0, offset), (LAYERS, plan.shard)
    ).astype(F32)
    head_grad = head_grad[: plan.head_rows].astype(F32)
    head_grad = jnp.concatenate(
        [head_grad[:, : C + 2], head_grad[:, C + LANE : C + LANE + K]], axis=1
    ).reshape(-1)
    return (
        (loss_sum,)
        + adam_update(*block, block_grad)
        + adam_update(*head_state, head_grad)
        + adam_update(*bias_state, grad_bias)
    )


def solution(mesh):
    data = P(("dp", "fsdp"))
    states = (P(None, "fsdp"),) * 4 + (P("fsdp"),) * 4 + (P(),) * 4
    return jax.shard_map(
        functools.partial(on_device, mesh),
        mesh=mesh,
        in_specs=(P(("dp", "fsdp"), None, None), data, data, data) + states,
        out_specs=(P(),) + states,
        check_vma=False,
    )
```

```python
import functools
import types

import jax
import jax.numpy as jnp
from jax import lax
from jax.experimental import pallas as pl
from jax.experimental.pallas import tpu as pltpu
from jax.sharding import PartitionSpec as P

C = 256
E = 1536
SQ = 64
K = 1000
SIDE = 4
PIX = 16
LAYERS = 3
STEP = 5
EPS_NORM = 0.001
RATE = 0.05
DECAY_WEIGHT = 0.05
BETA_ONE = 0.5
BETA_TWO = 0.5
EPS_ADAM = 1e-08
EMA_RATE = 0.5
SMOOTHING = 0.1

LANE = 128
KP = 1024
HEAD_W = C + LANE + KP
PB = 2 * C * E + 2 * E * SQ + 14 * E + SQ + 2 * C
ROW_P = C * E // LANE
ROW_R = ROW_P + E * C // LANE
ROW_X = ROW_R + E * SQ // LANE
ROW_D = ROW_X + SQ * E // LANE
ROW_S = ROW_D + 14 * E // LANE
NJ = E // LANE
GROUPS = 2
GW = E // GROUPS
MBLK = 4
UN_SPREAD, UN_ACT, UN_HBACK, UN_GATE, UN_TWO, UN_ONE = 4, 8, 8, 4, 4, 1

MESH = pl.DeviceIdType.MESH
F32 = jnp.float32
BF16 = jnp.bfloat16
VMEM_LIMIT = 127 * 512 * 1024
VM = pl.BlockSpec(memory_space=pltpu.VMEM)


def ceil_to(value, unit):
    return -(-value // unit) * unit


class Plan:
    def __init__(self, mesh, images, head_rows):
        self.nd = mesh.shape["dp"]
        self.nf = mesh.shape["fsdp"]
        self.devices = self.nd * self.nf
        self.images = images
        self.rows = images * PIX
        self.count = float(self.rows * self.devices)
        self.shard = PB // self.nf
        self.base = [(self.shard * f // LANE) // 16 * 16 for f in range(self.nf)]
        self.chunk = ceil_to(-(-self.shard // LANE) + 17, 16 * self.nd)
        self.flat = self.base[-1] + self.chunk
        self.head_pad = ceil_to(head_rows, 16)
        self.hd = self.head_pad * self.nf
        self.head_rows = head_rows
        self.head_part = ceil_to(-(-head_rows // self.nd), 16)
        self.head_flat = self.head_pad * (self.nf - 1) + self.head_part * self.nd
        self.depth = self.nf // 2
        third = ceil_to(-(-self.head_part // 3), 16)
        ends = list(range(0, self.head_part, third)) + [self.head_part]
        self.head_thirds = [(a, b - a) for a, b in zip(ends[:-1], ends[1:])]

    def layer_unit(self):
        return Unit(self, LANE, self.chunk // self.nd, self.flat, lambda f: self.shard * f // (16 * LANE) * 16)

    def head_unit(self):
        return Unit(self, HEAD_W, self.head_part, self.head_flat, lambda f: self.head_pad * f)


class Unit:
    def __init__(self, plan, width, part, rows, base):
        self.plan, self.width, self.part, self.rows, self.base = plan, width, part, rows, base
        self.owned = part * plan.nd


def dot(a, b, dims=((1,), (0,))):
    return lax.dot_general(a, b, (dims, ((), ())), preferred_element_type=F32)


def halves_of(value):
    high = value.astype(BF16)
    return high, (value - high.astype(F32)).astype(BF16)


def dot_rows(value, low, dims=((1,), (0,))):
    n = value.shape[0]
    both = dot(jnp.concatenate(halves_of(value), axis=0), low, dims)
    return both[0:n, :] + both[n:, :]


def dot_outer(a, b):
    a_high, a_low = halves_of(a)
    b_high, b_low = halves_of(b)
    left = jnp.concatenate([a_high, a_low, a_high], axis=0)
    right = jnp.concatenate([b_high, b_high, b_low], axis=0)
    return dot(left, right, ((0,), (0,)))


def row_sum(value):
    return jnp.sum(value, axis=0, keepdims=True)


def over_peers(plan, body):
    dp, fs = lax.axis_index("dp"), lax.axis_index("fsdp")
    deep, low = fs // 2, dp * 2 + lax.rem(fs, 2)
    near = 2 * plan.nd
    top = jnp.where(2 * deep >= plan.depth, 1, 0)

    def at(k, i, carry):
        z = top * k + (1 - top) * (plan.depth - 1 - k)
        j = lax.rem(low + i, near)

        @pl.when((z != deep) | (j != low))
        def _():
            body((j // 2, 2 * z + lax.rem(j, 2)))

        return carry

    for k in range(plan.depth):
        lax.fori_loop(0, near, functools.partial(at, k), 0)


def my_slot(plan):
    return lax.axis_index("dp") * plan.nf + lax.axis_index("fsdp")


def enter(plan):
    barrier = pltpu.get_barrier_semaphore()
    over_peers(
        plan,
        lambda device: pl.semaphore_signal(
            barrier, inc=1, device_id=device, device_id_type=MESH
        ),
    )


def entered(plan):
    pl.semaphore_wait(pltpu.get_barrier_semaphore(), plan.devices - 1)


class Exchange:
    def __init__(self, plan, buf, send, recv):
        self.plan, self.buf, self.send, self.recv, self.used = plan, buf, send, recv, False

    def share(self, first, second):
        plan, buf, send, recv = self.plan, self.buf, self.send, self.recv
        if self.used:
            self.finish()
        self.used = True
        half = first.shape[1] // LANE
        self.rows = 2 * half
        mine = my_slot(plan)
        for r in range(half):
            cols = slice(r * LANE, (r + 1) * LANE)
            buf[mine, r : r + 1, :] = first[:, cols]
            buf[mine, half + r : half + r + 1, :] = second[:, cols]
        over_peers(
            plan,
            lambda device: pltpu.make_async_remote_copy(
                src_ref=buf.at[mine, pl.ds(0, 2 * half)],
                dst_ref=buf.at[mine, pl.ds(0, 2 * half)],
                send_sem=send,
                recv_sem=recv,
                device_id=device,
                device_id_type=MESH,
            ).start(),
        )

    def others(self):
        return self.buf.at[pl.ds(1, self.plan.devices - 1), pl.ds(0, self.rows)]

    def collect(self):
        pltpu.make_async_copy(self.others(), self.others(), self.recv).wait()
        total = jnp.sum(self.buf[:, 0 : self.rows, :], axis=0)
        rows = [total[r : r + 1, :] for r in range(self.rows)]
        half = self.rows // 2
        return jnp.concatenate(rows[:half], axis=1), jnp.concatenate(rows[half:], axis=1)

    def finish(self):
        pltpu.make_async_copy(self.others(), self.others(), self.send).wait()


class PairedExchange:
    def __init__(self, plan, pair, buf, sems):
        self.plan, self.pair, self.buf, self.sems, self.used = plan, pair, buf, sems, False
        self.dp, self.fs = lax.axis_index("dp"), lax.axis_index("fsdp")
        self.core, self.deep = lax.rem(self.fs, 2), self.fs // 2
        self.mine = self.dp * plan.depth + self.deep

    def share(self, first, second):
        if self.used:
            self.finish()
        self.used = True
        half = first.shape[1] // LANE
        self.rows = 2 * half
        for i in range(half):
            cols = slice(i * LANE, (i + 1) * LANE)
            self.pair[0, i : i + 1, :] = first[:, cols]
            self.pair[0, half + i : half + i + 1, :] = second[:, cols]
        rows = pl.ds(0, self.rows)
        pltpu.make_async_remote_copy(
            src_ref=self.pair.at[0, rows],
            dst_ref=self.pair.at[1, rows],
            send_sem=self.sems[0],
            recv_sem=self.sems[1],
            device_id=(self.dp, 2 * self.deep + 1 - self.core),
            device_id_type=MESH,
        ).start()

    def relay(self):
        plan, rows = self.plan, pl.ds(0, self.rows)
        got = self.pair.at[1, rows]
        pltpu.make_async_copy(got, got, self.sems[1]).wait()
        self.buf[self.mine, rows, :] = self.pair[0, rows, :] + self.pair[1, rows, :]
        top = jnp.where(2 * self.deep >= plan.depth, 1, 0)
        for k in range(plan.depth):
            z = top * k + (1 - top) * (plan.depth - 1 - k)

            def go(i, carry, z=z):
                d = lax.rem(self.dp + i, plan.nd)

                @pl.when((z != self.deep) | (d != self.dp))
                def _():
                    pltpu.make_async_remote_copy(
                        src_ref=self.buf.at[self.mine, rows],
                        dst_ref=self.buf.at[self.mine, rows],
                        send_sem=self.sems[2],
                        recv_sem=self.sems[3],
                        device_id=(d, 2 * z + self.core),
                        device_id_type=MESH,
                    ).start()

                return carry

            lax.fori_loop(0, plan.nd, go, 0)

    def others(self):
        return self.buf.at[pl.ds(1, self.plan.devices // 2 - 1), pl.ds(0, self.rows)]

    def collect(self):
        pltpu.make_async_copy(self.others(), self.others(), self.sems[3]).wait()
        total = jnp.sum(self.buf[:, 0 : self.rows, :], axis=0)
        rows = [total[i : i + 1, :] for i in range(self.rows)]
        half = self.rows // 2
        return jnp.concatenate(rows[:half], axis=1), jnp.concatenate(rows[half:], axis=1)

    def finish(self):
        sent = self.pair.at[0, pl.ds(0, self.rows)]
        pltpu.make_async_copy(sent, sent, self.sems[0]).wait()
        pltpu.make_async_copy(self.others(), self.others(), self.sems[2]).wait()


def moments(plan, pair):
    mean = pair[0] / plan.count
    return mean, lax.rsqrt(pair[1] / plan.count - mean * mean + EPS_NORM)


class Reduction:
    def __init__(self, unit, source, result, refs, skip=0, size=None):
        self.unit, self.source, self.result = unit, source, result
        self.skip, self.size = skip, size or unit.part
        rows = pl.ds(skip, self.size)
        self.got_core, self.got_dp = (ref.at[:, :, rows] for ref in refs[:2])
        self.sum_dp, self.got_rest = (ref.at[:, rows] for ref in refs[2:4])
        self.send, self.recv = refs[4:8], refs[8:12]
        plan = unit.plan
        self.dp, self.fs = lax.axis_index("dp"), lax.axis_index("fsdp")
        self.core, self.deep = lax.rem(self.fs, 2), self.fs // 2
        self.nd, self.nz = plan.nd, plan.depth

    @staticmethod
    def scratch(unit):
        plan = unit.plan
        nd, nz, w, part = plan.nd, plan.depth, unit.width, unit.part
        return [
            pltpu.VMEM((nz, nd, part, w), BF16),
            pltpu.VMEM((nd - 1, nz, part, w), BF16),
            pltpu.VMEM((nz, part, w), BF16),
            pltpu.VMEM((nz - 1, part, w), BF16),
        ] + [pltpu.SemaphoreType.DMA(())] * 8

    def push(self, stage, source, target, device):
        pltpu.make_async_remote_copy(
            src_ref=source,
            dst_ref=target,
            send_sem=self.send[stage],
            recv_sem=self.recv[stage],
            device_id=device,
            device_id_type=MESH,
        ).start()

    def rows_of(self, f, d=0):
        return pl.multiple_of(self.unit.base(f) + d * self.unit.part + self.skip, 16)

    def start_core(self):
        def go(z, carry):
            for d in range(self.nd):
                self.push(
                    0,
                    self.source.at[pl.ds(self.rows_of(2 * z + 1 - self.core, d), self.size)],
                    self.got_core.at[z, d],
                    (self.dp, 2 * self.deep + 1 - self.core),
                )
            return carry

        lax.fori_loop(0, self.nz, go, 0)

    def wait(self, sem, ref):
        pltpu.make_async_copy(ref, ref, sem).wait()

    def start_dp(self):
        self.wait(self.recv[0], self.got_core)

        def add(z, carry):
            for d in range(self.nd):
                own = self.source[pl.ds(self.rows_of(2 * z + self.core, d), self.size), :]
                self.got_core[z, d] = (own.astype(F32) + self.got_core[z, d].astype(F32)).astype(BF16)
            return carry

        lax.fori_loop(0, self.nz, add, 0)

        def go(z, carry):
            for i in range(1, self.nd):
                other = lax.rem(self.dp + i, self.nd)
                self.push(1, self.got_core.at[z, other], self.got_dp.at[i - 1, z], (other, self.fs))
            return carry

        lax.fori_loop(0, self.nz, go, 0)

    def sum_dp_parts(self):
        self.wait(self.recv[1], self.got_dp)
        self.wait(self.send[0], self.got_core)
        self.wait(self.send[1], self.got_dp)

        def add(z, carry):
            total = self.got_core[z, self.dp].astype(F32)
            for i in range(self.nd - 1):
                total = total + self.got_dp[i, z].astype(F32)
            self.sum_dp[z] = total.astype(BF16)
            return carry

        lax.fori_loop(0, self.nz, add, 0)

    def start_rest(self):
        for i in range(1, self.nz):
            other = lax.rem(self.deep + i, self.nz)
            self.push(2, self.sum_dp.at[other], self.got_rest.at[i - 1], (self.dp, 2 * other + self.core))

    def start_copies(self):
        self.wait(self.recv[2], self.got_rest)
        total = self.sum_dp[self.deep].astype(F32)
        for i in range(self.nz - 1):
            total = total + self.got_rest[i].astype(F32)
        rows = pl.ds(pl.multiple_of(self.dp * self.unit.part + self.skip, 16), self.size)
        self.result[rows, :] = total.astype(BF16)
        for i in range(1, self.nd):
            other = lax.rem(self.dp + i, self.nd)
            self.push(3, self.result.at[rows], self.result.at[rows], (other, self.fs))

    def complete(self):
        others = self.result.at[pl.ds(0, (self.nd - 1) * self.size)]
        self.wait(self.recv[3], others)
        self.wait(self.send[2], self.got_rest)
        self.wait(self.send[3], others)


def taps():
    found = []
    for y in range(SIDE):
        for x in range(SIDE):
            for a in range(3):
                for b in range(3):
                    iy, ix = y + a - 1, x + b - 1
                    if 0 <= iy < SIDE and 0 <= ix < SIDE:
                        found.append((y * SIDE + x, 3 * a + b, iy * SIDE + ix))
    return found


TAPS = taps()


def half_tanh(half):
    return jnp.tanh(half)


def silu(z):
    half = 0.5 * z
    return half * half_tanh(half) + half


def sigmoid(z):
    return 0.5 * half_tanh(0.5 * z) + 0.5


def silu_slope(z):
    half = 0.5 * z
    t = half_tanh(half)
    return 0.5 * (1.0 + t + half * (1.0 - t * t))


def lanes(j):
    return pl.ds(pl.multiple_of(j * LANE, LANE), LANE)


def images_at(b):
    return pl.ds(pl.multiple_of(b * 8, 8), 8)


def over_tiles(plan, first_chunk, chunks, per_chunk, body, n_sums, store_sums, unroll=1):
    blocks = plan.images // 8

    def chunk_step(jj, carry):
        j = first_chunk + jj
        hoisted = per_chunk(j)

        def step(b, sums):
            for u in range(unroll):
                sums = body(j, b * unroll + u, hoisted, sums)
            return sums

        zero = tuple(jnp.zeros((8, LANE), F32) for _ in range(n_sums))
        store_sums(j, lax.fori_loop(0, blocks // unroll, step, zero))
        return carry

    lax.fori_loop(0, chunks, chunk_step, 0)


def over_tiles_and(plan, first_chunk, chunks, between, *rest):
    if between is None:
        over_tiles(plan, first_chunk, chunks, *rest)
    else:
        over_tiles(plan, first_chunk, 2, *rest)
        between()
        over_tiles(plan, first_chunk + 2, chunks - 2, *rest)


class Gather:
    def __init__(self, plan, target, rows, sems, half=None):
        self.plan, self.target, self.rows = plan, target, rows
        tiles = rows // 16
        counts = [tiles // plan.nd + (1 if d < tiles % plan.nd else 0) for d in range(plan.nd)]
        self.parts = [(16 * sum(counts[:d]), 16 * counts[d]) for d in range(plan.nd)]
        if half is not None:
            first = ceil_to(self.parts[0][1] // 2, 16)
            ends = ((0, first), (first, self.parts[0][1]))[half]
            self.parts = [(start + ends[0], ends[1] - ends[0]) for start, _ in self.parts]
        self.whole = half is None
        self.covered = sum(size for _, size in self.parts)
        self.send, self.recv = sems[0:3], sems[3:6]
        self.dp, self.fs = lax.axis_index("dp"), lax.axis_index("fsdp")
        self.core, self.deep = lax.rem(self.fs, 2), self.fs // 2

    def by_part(self, body):
        if len({size for _, size in self.parts}) == 1:
            body(self.parts[0][0] + self.dp * (self.rows // self.plan.nd), self.parts[0][1])
            return
        for d, (start, size) in enumerate(self.parts):
            pl.when(self.dp == d)(functools.partial(body, start, size))

    def at(self, deep, start, size):
        begin = (2 * deep + self.core) * self.rows + start
        return self.target.at[pl.ds(pl.multiple_of(begin, 16), size)]

    def push(self, stage, ref, device):
        pltpu.make_async_remote_copy(
            src_ref=ref,
            dst_ref=ref,
            send_sem=self.send[stage],
            recv_sem=self.recv[stage],
            device_id=device,
            device_id_type=MESH,
        ).start()

    def wait(self, sem, rows):
        if rows:
            span = self.target.at[pl.ds(0, rows)]
            pltpu.make_async_copy(span, span, sem).wait()

    def start_rest(self):
        def body(start, size):
            def go(i, carry):
                other = lax.rem(self.deep + i, self.plan.depth)
                self.push(0, self.at(self.deep, start, size), (self.dp, 2 * other + self.core))
                return carry

            if size:
                lax.fori_loop(1, self.plan.depth, go, 0)

        self.by_part(body)

    def start_dp(self):
        plan = self.plan

        def body(start, size):
            self.wait(self.recv[0], (plan.depth - 1) * size)

            def go(i, carry):
                other = lax.rem(self.deep + i, plan.depth)
                for k in range(1, plan.nd):
                    self.push(
                        1, self.at(other, start, size), (lax.rem(self.dp + k, plan.nd), self.fs)
                    )
                return carry

            if size:
                lax.fori_loop(1, plan.depth, go, 0)

        self.by_part(body)

    def start_core(self):
        plan = self.plan
        self.by_part(
            lambda start, size: self.wait(self.recv[1], (plan.depth - 1) * (self.covered - size))
        )

        def go(z, carry):
            for start, size in [(0, self.rows)] if self.whole else self.parts:
                self.push(2, self.at(z, start, size), (self.dp, 2 * self.deep + 1 - self.core))
            return carry

        lax.fori_loop(0, plan.depth, go, 0)

    def complete(self):
        plan = self.plan
        self.wait(self.recv[2], plan.depth * self.covered)

        def body(start, size):
            self.wait(self.send[0], (plan.depth - 1) * size)
            self.wait(self.send[1], (plan.depth - 1) * (plan.nd - 1) * size)

        self.by_part(body)
        self.wait(self.send[2], plan.depth * self.covered)


def spread_shards(plan, block, flat, mine):
    start = lax.axis_index("fsdp") * plan.shard
    offset = start - start // (16 * LANE) * (16 * LANE)
    down, turn = offset // LANE, lax.rem(offset, LANE)
    full = plan.shard // LANE
    rest = plan.shard - full * LANE
    size = plan.chunk + 32
    lane = lax.broadcasted_iota(jnp.int32, (16, LANE), 1)
    for layer in range(LAYERS):
        flat[layer * size : layer * size + 24, :] = jnp.zeros((24, LANE), F32)

    def take(layer, i, count):
        piece = block[:, pl.ds(pl.multiple_of(i * 8 * LANE, LANE), count * LANE)]
        rows = [piece[layer : layer + 1, k * LANE : (k + 1) * LANE] for k in range(count)]
        at = pl.ds(pl.multiple_of(layer * size + 24 + i * 8, 8), count)
        flat[at, :] = jnp.concatenate(rows, axis=0) if count > 1 else rows[0]

    def fill(layer):
        def step(i, carry):
            take(layer, i, 8)
            return carry

        lax.fori_loop(0, full // 8, step, 0)
        if full % 8:
            take(layer, full // 8, full % 8)
        at = layer * size + 24 + full
        if rest:
            last = block[layer : layer + 1, full * LANE : full * LANE + rest]
            flat[at : at + 1, :] = jnp.concatenate([last, jnp.zeros((1, LANE - rest), F32)], axis=1)
            at += 1
        end = (layer + 1) * size
        flat[at:end, :] = jnp.zeros((end - at, LANE), F32)

    def shift(layer):
        fill(layer)

        def go(i, carry):
            begin = layer * size + 24 + i * 16 - down
            here = pltpu.roll(flat[pl.ds(begin, 16), :], turn, 1)
            before = pltpu.roll(flat[pl.ds(begin - 1, 16), :], turn, 1)
            value = jnp.where(lane >= turn, here, before)
            mine[layer][pl.ds(pl.multiple_of(i * 16, 16), 16), :] = value.astype(BF16)
            return carry

        lax.fori_loop(0, plan.chunk // 16, go, 0)

    return shift


def unpack_weights(plan, got, we, wp, wr, wx, small, tail, flat):
    lane = lax.broadcasted_iota(jnp.int32, (1, LANE), 1)
    low = lane < SQ
    for f in range(plan.nf):
        base, at = plan.base[f], f * plan.chunk
        head = got[at : at + 16, :].astype(F32)
        if f:
            head = head + flat[base : base + 16, :]
        flat[base : base + 16, :] = head
        flat[base + 16 : base + plan.chunk, :] = got[at + 16 : at + plan.chunk, :].astype(F32)
    for j in range(NJ):
        cols = slice(j * LANE, (j + 1) * LANE)
        we[:, cols] = flat[pl.ds(j, C, stride=NJ), :].astype(BF16)
        wx[0:SQ, cols] = flat[pl.ds(ROW_X + j, SQ, stride=NJ), :].astype(BF16)
        wx[SQ:LANE, cols] = jnp.zeros((LANE - SQ, LANE), BF16)
        small[0:14, cols] = flat[pl.ds(ROW_D + j, 14, stride=NJ), :]
        small[14:16, cols] = jnp.zeros((2, LANE), F32)
    for h in range(C // LANE):
        wp[:, h * LANE : (h + 1) * LANE] = flat[pl.ds(ROW_P + h, E, stride=2), :].astype(BF16)
    pairs = flat[ROW_R:ROW_X, :]
    evens, odds = jnp.where(low, pairs, 0.0), jnp.where(low, pltpu.roll(pairs, SQ, 1), 0.0)
    flat[pl.ds(0, E // 2, stride=2), :] = evens
    flat[pl.ds(1, E // 2, stride=2), :] = odds
    wr[...] = flat[0:E, :].astype(BF16)
    rows = [flat[ROW_S + i : ROW_S + i + 1, :] for i in range(5)]
    turned = [pltpu.roll(jnp.broadcast_to(r, (8, LANE)), SQ, 1)[0:1, :] for r in rows]
    tail[...] = jnp.zeros((8, C), F32)
    tail[0:1, 0:LANE] = jnp.where(low, rows[0], 0.0)
    for i, at in ((1, 0), (2, 2)):
        tail[i : i + 1, 0:LANE] = jnp.where(low, turned[at], turned[at + 1])
        tail[i : i + 1, LANE:C] = jnp.where(low, turned[at + 1], turned[at + 2])


def mix_images(plan, images, partner, share_one, stream, first, last):
    n, rows = plan.images, plan.rows
    place = lax.broadcasted_iota(jnp.int32, (n, rows), 1)
    own = lax.broadcasted_iota(jnp.int32, (n, rows), 0) * PIX
    chosen = partner * PIX

    def go(p, carry):
        mine = dot(jnp.where(place == own + p, 1.0, 0.0).astype(BF16), images[...])
        theirs = dot(jnp.where(place == chosen + p, 1.0, 0.0).astype(BF16), images[...])
        at = pl.ds(pl.multiple_of(p * n, n), n)
        stream[at, :] = share_one * mine + (1.0 - share_one) * theirs
        return carry

    lax.fori_loop(first, last, go, 0)


def forward_layer(plan, r, layer, hooks):
    x, expanded, depth, act, sums, x_low = r.stream, r.expanded, r.depth, r.flow, r.sums, r.x_low
    normed_three, stat_e, stat_c = r.normed_three.at[layer], r.stat_e.at[layer], r.stat_c.at[layer]
    pooled, presq, gate, turned = r.pooled.at[layer], r.presq.at[layer], r.gate.at[layer], r.turned.at[layer]
    we, wp, wr, wx = r.we.at[layer], r.wp.at[layer], r.wr.at[layer], r.wx.at[layer]
    small, tail = r.small.at[layer], r.tail.at[layer]
    ex_one, ex_two, ex_three = r.ex_wide[0:GROUPS], r.ex_wide[GROUPS : 2 * GROUPS], r.ex_thin
    n = plan.images
    x_low[...] = x[...].astype(BF16)
    for g in range(GROUPS):
        cols = slice(g * GW, (g + 1) * GW)

        def expand(m, carry, cols=cols):
            rows = pl.ds(pl.multiple_of(m * MBLK * n, MBLK * n), MBLK * n)
            value = dot(x_low[rows, :], we[:, cols])
            expanded[pl.ds(m * MBLK, MBLK), :, cols] = value.reshape(MBLK, n, GW)
            return (
                carry[0] + jnp.sum(value.reshape(-1, 8, GW), axis=0),
                carry[1] + jnp.sum((value * value).reshape(-1, 8, GW), axis=0),
            )

        zero = jnp.zeros((8, GW), F32)
        s, q = lax.fori_loop(0, PIX // MBLK, expand, (zero, zero))
        if g:
            ex_one[g - 1].relay()
        ex_one[g].share(row_sum(s), row_sum(q))
    turned[...] = x[...].T.astype(BF16)
    ex_one[GROUPS - 1].relay()

    def put_sums(j, totals):
        for i, t in enumerate(totals):
            sums[i : i + 1, lanes(j)] = row_sum(t)

    for g in range(GROUPS):
        cols = slice(g * GW, (g + 1) * GW)
        mean, rstd = moments(plan, ex_one[g].collect())
        if g == 0:
            r.spill_e.start(layer)
            if layer:
                r.spill_d.wait()
            hooks[0]()
        stat_e[0:1, cols] = mean
        stat_e[1:2, cols] = rstd
        scale = rstd * small[9:10, cols]
        stat_e[4:5, cols] = 0.5 * scale
        stat_e[5:6, cols] = 0.5 * (small[10:11, cols] - mean * scale)

        def chunk(j):
            return (
                stat_e[4:5, lanes(j)],
                stat_e[5:6, lanes(j)],
                [small[t : t + 1, lanes(j)] for t in range(9)],
            )

        def spread(j, b, hoisted, totals):
            scale, shift, w = hoisted
            act_one = []
            for p in range(PIX):
                half = expanded[p, images_at(b), lanes(j)] * scale + shift
                act_one.append(half * half_tanh(half) + half)
            made = [None] * PIX
            for o, t, i in TAPS:
                term = act_one[i] * w[t]
                made[o] = term if made[o] is None else made[o] + term
            s, q = totals
            for p in range(PIX):
                depth[p, images_at(b), lanes(j)] = made[p]
                s = s + made[p]
                q = q + made[p] * made[p]
            return s, q

        between = ex_two[g - 1].relay if g else None
        over_tiles_and(
            plan, g * (GW // LANE), GW // LANE, between, chunk, spread, 2, put_sums, UN_SPREAD
        )
        ex_two[g].share(sums[0:1, cols], sums[1:2, cols])
    ex_two[GROUPS - 1].relay()
    hooks[1]()

    for g in range(GROUPS):
        cols = slice(g * GW, (g + 1) * GW)
        mean, rstd = moments(plan, ex_two[g].collect())
        if g == 0:
            if layer < LAYERS - 1:
                r.spill_d.start(layer)
        stat_e[2:3, cols] = mean
        stat_e[3:4, cols] = rstd
        scale = rstd * small[11:12, cols]
        stat_e[6:7, cols] = 0.5 * scale
        stat_e[7:8, cols] = 0.5 * (small[12:13, cols] - mean * scale)

        def chunk_two(j):
            return stat_e[6:7, lanes(j)], stat_e[7:8, lanes(j)]

        def activate(j, b, hoisted, totals):
            scale, shift = hoisted
            total = None
            for p in range(PIX):
                half = depth[p, images_at(b), lanes(j)] * scale + shift
                made = half * half_tanh(half) + half
                act[p, images_at(b), lanes(j)] = made
                total = made if total is None else total + made
            pooled[images_at(b), lanes(j)] = total * (1.0 / PIX)
            return totals

        over_tiles(
            plan, g * (GW // LANE), GW // LANE, chunk_two, activate, 0, lambda j, s: None, UN_ACT
        )
    reduced = dot_rows(pooled[...], wr[...]) + tail[0:1, 0:LANE]
    presq[...] = reduced
    gate[...] = sigmoid(dot_rows(silu(reduced), wx[...]) + small[13:14, :])

    hooks[2]()
    r.spill_e.wait()

    def project(m, carry):
        gated = (act[pl.ds(m * MBLK, MBLK), :, :] * gate[...][None]).astype(BF16)
        value = dot(gated.reshape(MBLK * n, E), wp[...])
        expanded[pl.ds(m * MBLK, MBLK), :, 0:C] = value.reshape(MBLK, n, C)
        return (
            carry[0] + jnp.sum(value.reshape(-1, 8, C), axis=0),
            carry[1] + jnp.sum((value * value).reshape(-1, 8, C), axis=0),
        )

    zero = jnp.zeros((8, C), F32)
    s, q = lax.fori_loop(0, PIX // MBLK, project, (zero, zero))
    ex_three.share(row_sum(s), row_sum(q))
    hooks[3]()
    mean, rstd = moments(plan, ex_three.collect())
    stat_c[...] = jnp.zeros((8, C), F32)
    stat_c[0:1, :] = mean
    stat_c[1:2, :] = rstd
    normed = (expanded[:, :, 0:C].reshape(n * PIX, C) - mean) * rstd
    normed_three[...] = normed.astype(BF16)
    x[...] = x[...] + normed * tail[1:2, :] + tail[2:3, :]


def head_layers(plan, r, label, label_row, partner, weight):
    x, x_low, turned, bias, totals_out = r.stream, r.x_low, r.turned.at[LAYERS], r.bias, r.totals
    w_head = grad_head = r.w_head
    hidden, slope, low_grad, pool, stat = r.expanded, r.flow, r.gated, r.squeeze_grad, r.coef
    sums, gain, grad_x = r.sums, r.sums.at[pl.ds(8, 8)], r.stream
    hd, n = plan.hd, plan.images
    halves = plan.head_groups
    ng = len(halves)
    ex_stat, ex_grad, ex_bias = r.ex_wide[0:ng], r.ex_wide[GROUPS : GROUPS + ng], r.ex_bias
    x_low[...] = x[...].astype(BF16)
    gain[:, 0:hd] = w_head[0:hd, C : C + LANE].astype(F32).T[0:8, :]
    for g, (start, width) in enumerate(halves):
        cols = slice(start, start + width)

        def convolve(m, carry, cols=cols, width=width):
            rows = pl.ds(pl.multiple_of(m * MBLK * n, MBLK * n), MBLK * n)
            value = dot(x_low[rows, :], w_head[cols, 0:C], ((1,), (1,)))
            hidden[pl.ds(m * MBLK, MBLK), :, cols] = value.reshape(MBLK, n, width)
            return (
                carry[0] + jnp.sum(value.reshape(-1, 8, width), axis=0),
                carry[1] + jnp.sum((value * value).reshape(-1, 8, width), axis=0),
            )

        zero = jnp.zeros((8, width), F32)
        s, q = lax.fori_loop(0, PIX // MBLK, convolve, (zero, zero))
        if g:
            ex_stat[g - 1].relay()
        ex_stat[g].share(row_sum(s), row_sum(q))
    turned[...] = x[...].T.astype(BF16)
    ex_stat[ng - 1].relay()
    for g, (start, width) in enumerate(halves):
        cols = slice(start, start + width)
        mean, rstd = moments(plan, ex_stat[g].collect())
        scale = rstd * gain[0:1, cols]
        stat[0:1, cols] = rstd
        stat[1:2, cols] = -mean * rstd
        stat[2:3, cols] = 0.5 * scale
        stat[3:4, cols] = 0.5 * (gain[1:2, cols] - mean * scale)

        def chunk(j):
            return stat[2:3, lanes(j)], stat[3:4, lanes(j)]

        def activate(j, b, hoisted, totals):
            scale, shift = hoisted
            total = None
            for p in range(PIX):
                half = hidden[p, images_at(b), lanes(j)] * scale + shift
                t = half_tanh(half)
                made = half * t + half
                slope[p, images_at(b), lanes(j)] = (1.0 + t) + half * (1.0 - t * t)
                total = made if total is None else total + made
            pool[images_at(b), lanes(j)] = total * (1.0 / PIX)
            return totals

        over_tiles(plan, start // LANE, width // LANE, chunk, activate, 0, lambda j, s: None, UN_ACT)
    pool_low = pool[:, 0:hd].astype(BF16)
    classes = lax.broadcasted_iota(jnp.int32, (n, KP), 1)
    valid = classes < K
    logits = dot(pool_low, w_head[0:hd, C + LANE :]) + bias[...]
    logits = jnp.where(valid, logits, -1e30)
    top = jnp.max(logits, axis=1, keepdims=True)
    lifted = logits - top
    powers = jnp.where(valid, jnp.exp(lifted), 0.0)
    norm = jnp.sum(powers, axis=1, keepdims=True)
    log_probs = lifted - jnp.log(norm)
    picked = lax.broadcasted_iota(jnp.int32, (n, n), 1) == partner
    label_two = jnp.sum(jnp.where(picked, label_row[...], 0), axis=1, keepdims=True)
    w = weight
    targets = w * jnp.where(classes == label, 1.0 - SMOOTHING, 0.0) + (1.0 - w) * jnp.where(
        classes == label_two, 1.0 - SMOOTHING, 0.0
    )
    targets = jnp.where(valid, targets + SMOOTHING / K, 0.0)
    loss = -jnp.sum(jnp.where(valid, targets * log_probs, 0.0))
    grad_logits = (powers / norm - targets) * (float(PIX) / plan.count)
    packed_bias = jnp.where(classes[0:1, :] == KP - 1, loss, row_sum(grad_logits))
    ex_bias.share(packed_bias[:, 0 : KP // 2], packed_bias[:, KP // 2 :])
    grad_low = grad_logits.astype(BF16)
    pool_grad = dot(grad_low, w_head[0:hd, C + LANE :], ((1,), (1,)))
    pool[:, 0:hd] = pool_grad * (0.5 / PIX)

    def put_sums(j, totals):
        flow_sum, value_sum = [row_sum(t) for t in totals]
        sums[0:1, lanes(j)] = flow_sum
        sums[1:2, lanes(j)] = value_sum * stat[0:1, lanes(j)] + flow_sum * stat[1:2, lanes(j)]

    for g, (start, width) in enumerate(halves):
        cols = slice(start, start + width)

        def back(j, b, hoisted, totals):
            s, q = totals
            flow = pool[images_at(b), lanes(j)]
            for p in range(PIX):
                made = slope[p, images_at(b), lanes(j)] * flow
                slope[p, images_at(b), lanes(j)] = made
                s = s + made
                q = q + made * hidden[p, images_at(b), lanes(j)]
            return s, q

        between = ex_grad[g - 1].relay if g else None
        over_tiles_and(
            plan, start // LANE, width // LANE, between, lambda j: None, back, 2, put_sums, UN_HBACK
        )
        ex_grad[g].share(sums[0:1, cols], sums[1:2, cols])
    grad_head[0:hd, C + LANE :] = dot(pool_low.T, grad_low).astype(BF16)
    ex_grad[ng - 1].relay()
    norm_grads = jnp.concatenate(
        [sums[1:2, 0:hd], sums[0:1, 0:hd], jnp.zeros((LANE - 2, hd), F32)], axis=0
    )
    grad_head[0:hd, C : C + LANE] = norm_grads.T.astype(BF16)
    for g, (start, width) in enumerate(halves):
        cols = slice(start, start + width)
        shift_total, gain_total = ex_grad[g].collect()
        scale = stat[0:1, cols] * gain[0:1, cols]
        mean_one = shift_total / plan.count
        mean_two = gain_total / plan.count
        stat[4:5, cols] = scale
        stat[5:6, cols] = -scale * stat[0:1, cols] * mean_two
        stat[6:7, cols] = -scale * (mean_one + stat[1:2, cols] * mean_two)
    def into(m, carry):
        rows = pl.ds(pl.multiple_of(m * MBLK * n, MBLK * n), MBLK * n)
        spot = pl.ds(m * MBLK, MBLK)
        value = (
            slope[spot, :, 0:hd] * stat[4:5, 0:hd]
            + hidden[spot, :, 0:hd] * stat[5:6, 0:hd]
            + stat[6:7, 0:hd]
        )
        low = value.reshape(MBLK * n, hd).astype(BF16)
        low_grad[rows, 0:hd] = low
        grad_x[rows, :] = dot(low, w_head[0:hd, 0:C])
        return carry

    lax.fori_loop(0, PIX // MBLK, into, 0)
    r.spill_e.fetch(LAYERS - 1)
    for at in range(0, hd, LANE):
        part = dot(turned[...], low_grad[:, at : at + LANE])
        grad_head[at : at + LANE, 0:C] = part.T.astype(BF16)
    totals_out[...] = jnp.concatenate(ex_bias.collect(), axis=1)


def backward_layer(plan, r, layer, hooks):
    expanded, depth, flow, gated, sums, coef = r.expanded, r.depth, r.flow, r.gated, r.sums, r.coef
    normed_three, stat_e, stat_c = r.normed_three.at[layer], r.stat_e.at[layer], r.stat_c.at[layer]
    pooled, presq, gate, turned = r.pooled.at[layer], r.presq.at[layer], r.gate.at[layer], r.turned.at[layer]
    we, wp, wr, wx = r.we.at[layer], r.wp.at[layer], r.wr.at[layer], r.wx.at[layer]
    small, tail = r.small.at[layer], r.tail.at[layer]
    grad = grad_x = r.stream
    low_proj, squeeze_grad, flat, packed = r.x_low, r.squeeze_grad, r.flat, r.stage
    ex_one, ex_two, ex_three = r.ex_wide[0:GROUPS], r.ex_wide[GROUPS : 2 * GROUPS], r.ex_thin
    n = plan.images
    lane = lax.broadcasted_iota(jnp.int32, (1, LANE), 1)
    is_low = lane < SQ
    rstd_c = stat_c[1:2, :]
    s = row_sum(jnp.sum(grad[...].reshape(-1, 8, C), axis=0))
    q = row_sum(
        jnp.sum((grad[...] * normed_three[...].astype(F32)).reshape(-1, 8, C), axis=0)
    )
    ex_three.share(s, q)
    hooks[0]()
    bias_three, gain_three = s, q

    if layer < LAYERS - 1:
        r.spill_d.wait()

    def chunk_two(j):
        return stat_e[6:7, lanes(j)], stat_e[7:8, lanes(j)]

    def regate(p, carry):
        rows = pl.ds(pl.multiple_of(p * n, n), n)
        for j in range(NJ):
            cols = slice(j * LANE, (j + 1) * LANE)
            half = depth[p, :, cols] * stat_e[6:7, cols] + stat_e[7:8, cols]
            value = (half * half_tanh(half) + half) * gate[:, cols]
            gated[rows, cols] = value.astype(BF16)
        return carry

    lax.fori_loop(0, PIX, regate, 0)

    bias_total, gain_total = ex_three.collect()
    scale = rstd_c * tail[1:2, :]
    mean_one, mean_two = bias_total / plan.count, gain_total / plan.count
    low_proj[...] = (
        scale
        * (grad[...] - mean_one - normed_three[...].astype(F32) * mean_two)
    ).astype(BF16)

    def into_gated(m, carry):
        rows = pl.ds(pl.multiple_of(m * MBLK * n, MBLK * n), MBLK * n)
        value = dot(low_proj[rows, :], wp[...], ((1,), (1,)))
        flow[pl.ds(m * MBLK, MBLK), :, :] = value.reshape(MBLK, n, E)
        return carry

    lax.fori_loop(0, PIX // MBLK, into_gated, 0)
    hooks[1]()

    def gate_back(t, carry):
        j, b = t // (n // 16), lax.rem(t, n // 16)
        block = pl.ds(pl.multiple_of(b * 16, 16), 16)
        total = None
        for p in range(PIX):
            low = gated[pl.ds(pl.multiple_of(p * n + b * 16, 16), 16), lanes(j)].astype(F32)
            term = flow[p, block, lanes(j)] * low
            total = term if total is None else total + term
        squeeze_grad[block, lanes(j)] = total * (1.0 - gate[block, lanes(j)])
        return carry

    lax.fori_loop(0, NJ * (n // 16), gate_back, 0)
    excite_grad = squeeze_grad[...]
    sums[13:14, :] = row_sum(excite_grad)
    squeezed = silu(presq[...])
    presq_grad = dot_rows(excite_grad, wx[...], ((1,), (1,))) * silu_slope(presq[...])
    grad_wx = dot_outer(squeezed, excite_grad)
    flat[ROW_R : ROW_R + E, :] = dot_outer(pooled[...], presq_grad)
    evens = flat[pl.ds(ROW_R, E // 2, stride=2), :]
    odds = flat[pl.ds(ROW_R + 1, E // 2, stride=2), :]
    flat[ROW_R:ROW_X, :] = jnp.where(is_low, evens, pltpu.roll(odds, SQ, 1))
    for j in range(NJ):
        flat[pl.ds(ROW_X + j, SQ, stride=NJ), :] = grad_wx[0:SQ, j * LANE : (j + 1) * LANE]
    grad_reduce_b = row_sum(presq_grad)
    squeeze_grad[...] = dot_rows(presq_grad, wr[...], ((1,), (1,))) * (1.0 / PIX)

    def put_sums(first_row, stat_row):
        def put(j, totals):
            rows = [row_sum(t) for t in totals]
            mean = stat_e[stat_row : stat_row + 1, lanes(j)]
            rstd = stat_e[stat_row + 1 : stat_row + 2, lanes(j)]
            rows[-2] = (rows[-2] - mean * rows[-1]) * rstd
            for i, t in enumerate(rows):
                sums[first_row + i : first_row + i + 1, lanes(j)] = t

        return put

    def back_two(j, b, hoisted, totals):
        scale, shift = hoisted
        gain_sum, bias_sum = totals
        opened = gate[images_at(b), lanes(j)] * 0.5
        pool_flow = squeeze_grad[images_at(b), lanes(j)] * 0.5
        for p in range(PIX):
            value = depth[p, images_at(b), lanes(j)]
            half = value * scale + shift
            t = half_tanh(half)
            made = (flow[p, images_at(b), lanes(j)] * opened + pool_flow) * (
                (1.0 + t) + half * (1.0 - t * t)
            )
            flow[p, images_at(b), lanes(j)] = made
            bias_sum = bias_sum + made
            gain_sum = gain_sum + made * value
        return gain_sum, bias_sum

    for g in range(GROUPS):
        cols = slice(g * GW, (g + 1) * GW)
        between = ex_two[g - 1].relay if g else None
        over_tiles_and(
            plan, g * (GW // LANE), GW // LANE, between, chunk_two, back_two, 2, put_sums(11, 2), UN_TWO
        )
        ex_two[g].share(sums[12:13, cols], sums[11:12, cols])

    proj_turned = low_proj[...].astype(F32).T.astype(BF16)
    ex_two[GROUPS - 1].relay()
    hooks[2]()
    for j in range(NJ):
        part = dot(proj_turned, gated[:, j * LANE : (j + 1) * LANE])
        for h in range(C // LANE):
            flat[pl.ds(ROW_P + 2 * j * LANE + h, LANE, stride=2), :] = part[
                h * LANE : (h + 1) * LANE, :
            ].T

    def norm_coefs(g, pair, row, stat_row, gain_row):
        cols = slice(g * GW, (g + 1) * GW)
        mean, rstd = stat_e[stat_row : stat_row + 1, cols], stat_e[stat_row + 1 : stat_row + 2, cols]
        scale = rstd * small[gain_row : gain_row + 1, cols]
        mean_one, mean_two = pair[0] / plan.count, pair[1] / plan.count
        coef[row : row + 1, cols] = scale
        coef[row + 1 : row + 2, cols] = -scale * rstd * mean_two
        coef[row + 2 : row + 3, cols] = -scale * (mean_one - mean * rstd * mean_two)

    def chunk_one(j):
        return (
            [coef[i : i + 1, lanes(j)] for i in range(3)],
            [small[t : t + 1, lanes(j)] for t in range(9)],
            [stat_e[i : i + 1, lanes(j)] for i in (4, 5)],
        )

    def back_one(j, b, hoisted, totals):
        (c_flow, c_value, c_const), w, (scale, shift) = hoisted
        w_sums, gain_sum, bias_sum = list(totals[:9]), totals[9], totals[10]
        spread_grad = []
        for p in range(PIX):
            spread_grad.append(
                flow[p, images_at(b), lanes(j)] * c_flow
                + (depth[p, images_at(b), lanes(j)] * c_value + c_const)
            )
        act_one, slopes = [], []
        for p in range(PIX):
            half = expanded[p, images_at(b), lanes(j)] * scale + shift
            t = half_tanh(half)
            act_one.append(half * t + half)
            slopes.append(0.5 * ((1.0 + t) + half * (1.0 - t * t)))
        made = [None] * PIX
        for o, t, i in TAPS:
            w_sums[t] = w_sums[t] + spread_grad[o] * act_one[i]
            term = spread_grad[o] * w[t]
            made[i] = term if made[i] is None else made[i] + term
        for p in range(PIX):
            value = expanded[p, images_at(b), lanes(j)]
            result = made[p] * slopes[p]
            flow[p, images_at(b), lanes(j)] = result
            bias_sum = bias_sum + result
            gain_sum = gain_sum + result * value
        return tuple(w_sums) + (gain_sum, bias_sum)

    for g in range(GROUPS):
        cols = slice(g * GW, (g + 1) * GW)
        norm_coefs(g, ex_two[g].collect(), 0, 2, 11)
        if g == 0:
            r.spill_e.wait()
        between = ex_one[g - 1].relay if g else None
        over_tiles_and(
            plan, g * (GW // LANE), GW // LANE, between, chunk_one, back_one, 11, put_sums(0, 0), UN_ONE
        )
        ex_one[g].share(sums[10:11, cols], sums[9:10, cols])

    if layer:
        r.spill_d.fetch(layer - 1)
    for j in range(NJ):
        flat[pl.ds(ROW_D + j, 14, stride=NJ), :] = sums[0:14, j * LANE : (j + 1) * LANE]

    def turn(row):
        return pltpu.roll(jnp.broadcast_to(row, (8, LANE)), SQ, 1)[0:1, :]

    pieces = [turn(v[:, h * LANE : (h + 1) * LANE]) for v in (gain_three, bias_three) for h in (0, 1)]
    flat[ROW_S : ROW_S + 1, :] = jnp.where(is_low, grad_reduce_b, pieces[0])
    for i in range(3):
        flat[ROW_S + 1 + i : ROW_S + 2 + i, :] = jnp.where(is_low, pieces[i], pieces[i + 1])
    flat[ROW_S + 4 : ROW_S + 5, :] = pieces[3]
    hooks[3]()
    ex_one[GROUPS - 1].relay()
    hooks[4]()

    for g in range(GROUPS):
        cols = slice(g * GW, (g + 1) * GW)
        norm_coefs(g, ex_one[g].collect(), 0, 0, 9)

        def into(m, carry, cols=cols):
            rows = pl.ds(pl.multiple_of(m * MBLK * n, MBLK * n), MBLK * n)
            spot = pl.ds(m * MBLK, MBLK)
            value = (
                flow[spot, :, cols] * coef[0:1, cols]
                + expanded[spot, :, cols] * coef[1:2, cols]
                + coef[2:3, cols]
            )
            low = value.reshape(MBLK * n, GW).astype(BF16)
            gated[rows, cols] = low
            grad_x[rows, :] += dot(low, we[:, cols], ((1,), (1,)))
            return carry

        lax.fori_loop(0, PIX // MBLK, into, 0)
        for j in range(g * (GW // LANE), (g + 1) * (GW // LANE)):
            flat[pl.ds(j, C, stride=NJ), :] = dot(
                turned[...], gated[:, j * LANE : (j + 1) * LANE]
            )
    if layer:
        r.spill_e.fetch(layer - 1)
    packed[0 : plan.flat, :] = flat[0 : plan.flat, :].astype(BF16)
    hooks[5]()


class Spill:
    def __init__(self, held, kept, sem):
        self.held, self.kept, self.sem = held, kept, sem

    def start(self, layer):
        self.copy = pltpu.make_async_copy(self.held, self.kept.at[layer], self.sem)
        self.copy.start()

    def fetch(self, layer):
        self.copy = pltpu.make_async_copy(self.kept.at[layer], self.held, self.sem)
        self.copy.start()

    def wait(self):
        self.copy.wait()


INPUTS = ("block", "w_own", "images", "per_image", "bias")
OUTPUTS = ("block_sums", "head_sums", "totals", "kept_e", "kept_d")


def scratch_of(plan):
    n, rows, hd = plan.images, plan.rows, plan.hd
    wide = 2 * GW // LANE
    vm = lambda shape, dtype=F32: pltpu.VMEM(shape, dtype)
    held = {
        "expanded": vm((PIX, n, E)),
        "depth": vm((PIX, n, E)),
        "flow": vm((PIX, n, E)),
        "gated": vm((rows, E), BF16),
        "stream": vm((rows, C)),
        "x_low": vm((rows, C), BF16),
        "turned": vm((LAYERS + 1, C, rows), BF16),
        "normed_three": vm((LAYERS, rows, C), BF16),
        "stat_e": vm((LAYERS, 8, E)),
        "stat_c": vm((LAYERS, 8, C)),
        "pooled": vm((LAYERS, n, E)),
        "presq": vm((LAYERS, n, LANE)),
        "gate": vm((LAYERS, n, E)),
        "we": vm((LAYERS, C, E), BF16),
        "wp": vm((LAYERS, E, C), BF16),
        "wr": vm((LAYERS, E, LANE), BF16),
        "wx": vm((LAYERS, LANE, E), BF16),
        "small": vm((LAYERS, 16, E)),
        "tail": vm((LAYERS, 8, C)),
        "w_head": vm((plan.head_flat, HEAD_W), BF16),
        "squeeze_grad": vm((n, E)),
        "sums": vm((16, E)),
        "coef": vm((8, E)),
        "flat": vm((max(plan.flat, LAYERS * (plan.chunk + 32)), LANE)),
        "stage": vm((max(plan.nf * plan.chunk, plan.flat), LANE), BF16),
        "spill_sems": pltpu.SemaphoreType.DMA((2,)),
    }
    for i in range(2 * GROUPS):
        held[f"pair{i}"] = vm((2, wide, LANE))
        held[f"wide{i}"] = vm((plan.devices // 2, wide, LANE))
        for k in range(4):
            held[f"wide{i}_{k}"] = pltpu.SemaphoreType.DMA(())
    held["thin"] = vm((plan.devices, 2 * C // LANE, LANE))
    held["thick"] = vm((plan.devices, KP // LANE, LANE))
    for name in ("thin", "thick"):
        held[name + "_send"] = pltpu.SemaphoreType.DMA(())
        held[name + "_recv"] = pltpu.SemaphoreType.DMA(())
    for name in ("block", "head", "half"):
        for i in range(6):
            held[f"gather_{name}{i}"] = pltpu.SemaphoreType.DMA(())
    for name, unit in (("block", plan.layer_unit()), ("head", plan.head_unit())):
        for i, shape in enumerate(Reduction.scratch(unit)):
            if name == "block" or i < 4:
                held[f"reduce_{name}{i}"] = shape
    for i, shape in enumerate(Reduction.scratch(plan.layer_unit())[3:]):
        held[f"reduce_last{i}"] = shape
    for i in range(8):
        held[f"reduce_half{i}"] = pltpu.SemaphoreType.DMA(())
    for i in range(8 * len(plan.head_thirds)):
        held[f"reduce_third{i}"] = pltpu.SemaphoreType.DMA(())
    return held


def step_kernel(plan, names, *refs):
    r = types.SimpleNamespace(**dict(zip(names, refs, strict=True)))
    held = vars(r)
    exchange = lambda name: Exchange(plan, held[name], held[name + "_send"], held[name + "_recv"])
    r.ex_wide = [
        PairedExchange(
            plan, held[f"pair{i}"], held[f"wide{i}"], [held[f"wide{i}_{k}"] for k in range(4)]
        )
        for i in range(2 * GROUPS)
    ]
    r.ex_thin, r.ex_bias = exchange("thin"), exchange("thick")
    r.spill_e = Spill(r.expanded, r.kept_e, r.spill_sems.at[0])
    r.spill_d = Spill(r.depth, r.kept_d, r.spill_sems.at[1])
    reduce_refs = {
        name: [held[f"reduce_{name}{i}"] for i in range(count)]
        for name, count in (("block", 12), ("head", 4))
    }
    reduce_refs["last"] = reduce_refs["block"][:3] + [held[f"reduce_last{i}"] for i in range(9)]
    reduce_refs["half"] = reduce_refs["last"][:4] + [held[f"reduce_half{i}"] for i in range(8)]
    fs = lax.axis_index("fsdp")
    n = plan.images

    enter(plan)
    mine = [r.gated.at[pl.ds(0, plan.chunk), pl.ds(C + i * LANE, LANE)] for i in range(LAYERS)]
    images = r.gated.at[pl.ds(0, plan.rows), pl.ds(0, C)]
    take_images = pltpu.make_async_copy(r.images, images, r.spill_sems.at[0])
    take_images.start()
    take_head = pltpu.make_async_copy(
        r.w_own,
        r.w_head.at[pl.ds(pl.multiple_of(fs * plan.head_pad, 16), plan.head_pad)],
        r.spill_sems.at[1],
    )
    take_head.start()
    shift = spread_shards(plan, r.block, r.flat, mine)
    own_rows = pl.ds(pl.multiple_of(fs * plan.chunk, 16), plan.chunk)

    def gather_of(layer, name="block", half=None):
        if not half:
            r.stage[own_rows, :] = mine[layer][...]
        sems = [held[f"gather_{name}{i}"] for i in range(6)]
        return Gather(plan, r.stage, plan.chunk, sems, half)

    def unpack(layer):
        unpack_weights(
            plan,
            r.stage,
            r.we.at[layer],
            r.wp.at[layer],
            r.wr.at[layer],
            r.wx.at[layer],
            r.small.at[layer],
            r.tail.at[layer],
            r.flat,
        )

    shift(0)
    gathers = [gather_of(0, "block", 0), gather_of(0, "half", 1)]
    head_gather = Gather(
        plan, r.w_head, plan.head_pad, [held[f"gather_head{i}"] for i in range(6)]
    )
    entered(plan)
    for gather in gathers:
        gather.start_rest()
    columns = jnp.concatenate([r.per_image[...], jnp.zeros((8, LANE - n), F32)], axis=1).T
    weight, label, partner = (columns[0:n, i : i + 1] for i in range(3))
    label, partner = label.astype(jnp.int32), partner.astype(jnp.int32)
    label_row = r.per_image[1:2, :].astype(jnp.int32)
    take_images.wait()
    take_head.wait()
    mix_images(plan, images, partner, weight, r.stream, 0, PIX // 2)
    for gather in gathers:
        gather.start_dp()
    head_gather.start_rest()
    mix_images(plan, images, partner, weight, r.stream, PIX // 2, PIX)
    gathers[0].start_core()
    shift(1)
    gathers[1].start_core()
    head_gather.start_dp()
    shift(2)
    for gather in gathers:
        gather.complete()
    unpack(0)

    for layer in range(LAYERS):
        if layer < LAYERS - 1:
            box = []

            def begin(layer=layer, box=box):
                box.append(gather_of(layer + 1))
                box[0].start_rest()

            def arrive(layer=layer, box=box):
                box[0].complete()
                unpack(layer + 1)

            hooks = (
                begin,
                lambda box=box: box[0].start_dp(),
                lambda box=box: box[0].start_core(),
                arrive,
            )
            if layer == 0:
                hooks = (begin, hooks[1], hooks[2], lambda arrive=arrive: [arrive(), head_gather.start_core()])
        else:
            hooks = (lambda: None,) * 4
        forward_layer(plan, r, layer, hooks)
    head_gather.complete()
    head_layers(plan, r, label, label_row, partner, weight)

    head_unit = plan.head_unit()
    head_works = []
    for i, (skip, size) in enumerate(plan.head_thirds):
        sems = [held[f"reduce_third{8 * i + k}"] for k in range(8)]
        refs = reduce_refs["head"][:4] + sems
        head_works.append(Reduction(head_unit, r.w_head, r.head_sums, refs, skip, size))
    unit = plan.layer_unit()
    works = [None] + [
        Reduction(unit, r.stage, r.block_sums.at[layer], reduce_refs["block"])
        for layer in range(1, LAYERS)
    ]

    def both(*steps):
        return lambda: [step() for step in steps]

    last = LAYERS - 1
    for layer in reversed(range(LAYERS)):
        hooks = [[] for _ in range(6)]
        if layer == last:
            hooks[0] += [w.start_core for w in head_works] + [head_works[0].start_dp]
            for w, at in zip(head_works[1:], (2, 4)):
                hooks[at].append(w.start_dp)
        else:
            work = works[layer + 1]
            hooks[0].append(work.start_dp)
            hooks[2] += [work.sum_dp_parts, work.start_rest]
            hooks[4].append(work.start_copies)
        if layer == last - 1:
            for w in head_works:
                hooks[0] += [w.sum_dp_parts, w.start_rest]
                hooks[2].append(w.start_copies)
                hooks[4].append(w.complete)
        if layer + 2 <= last:
            hooks[1].append(works[layer + 2].complete)
        if layer:
            hooks[5].append(works[layer].start_core)
        backward_layer(plan, r, layer, [both(*steps) for steps in hooks])
    first = ceil_to(-(-unit.part // 2), 16)
    halves = [
        Reduction(unit, r.stage, r.block_sums.at[0], reduce_refs["last"], 0, first),
        Reduction(unit, r.stage, r.block_sums.at[0], reduce_refs["half"], first, unit.part - first),
    ]
    for half in halves:
        half.start_core()
    for half in halves:
        half.start_dp()
    works[1].complete()
    for half in halves:
        half.sum_dp_parts()
        half.start_rest()
    for half in halves:
        half.start_copies()
    for half in halves:
        half.complete()
    for e in r.ex_wide + [r.ex_thin, r.ex_bias]:
        e.finish()


def train_step(plan, block, w_own, images, per_image, bias):
    held = scratch_of(plan)
    block_unit, head_unit = plan.layer_unit(), plan.head_unit()
    big = (PIX, plan.images, E)
    anywhere = pl.BlockSpec(memory_space=pl.ANY)
    return pl.pallas_call(
        functools.partial(step_kernel, plan, INPUTS + OUTPUTS + tuple(held)),
        out_shape=(
            jax.ShapeDtypeStruct((LAYERS, block_unit.owned, LANE), BF16),
            jax.ShapeDtypeStruct((head_unit.owned, HEAD_W), BF16),
            jax.ShapeDtypeStruct((1, KP), F32),
            jax.ShapeDtypeStruct((LAYERS,) + big, F32),
            jax.ShapeDtypeStruct((LAYERS - 1,) + big, F32),
        ),
        in_specs=[VM, anywhere, anywhere, VM, VM],
        out_specs=(VM, VM, VM, anywhere, anywhere),
        scratch_shapes=list(held.values()),
        compiler_params=pltpu.CompilerParams(
            collective_id=1, has_side_effects=True, vmem_limit_bytes=VMEM_LIMIT
        ),
        name="train_step",
    )(block, w_own, images, per_image, bias)


def adam_update(master, first, second, average, grad):
    first_new = BETA_ONE * first + (1.0 - BETA_ONE) * grad
    second_new = BETA_TWO * second + (1.0 - BETA_TWO) * grad * grad
    fix_one = 1.0 - BETA_ONE**STEP
    fix_two = 1.0 - BETA_TWO**STEP
    master_new = master * (1.0 - RATE * DECAY_WEIGHT) - RATE * (first_new / fix_one) / (
        jnp.sqrt(second_new / fix_two) + EPS_ADAM
    )
    average_new = EMA_RATE * average + (1.0 - EMA_RATE) * master_new
    return (master_new, first_new, second_new, average_new)


def on_device(mesh, images, partner, mix_weight, labels, *states):
    block, head_state, bias_state = states[0:4], states[4:8], states[8:12]
    row = C + 2 + K
    plan = Plan(mesh, images.shape[0], head_state[0].shape[0] // row)
    half = (plan.hd // LANE + 1) // 2 * LANE
    plan.head_groups = [(0, half), (half, plan.hd - half)]
    start = lax.axis_index("fsdp") * plan.shard
    offset = start - start // (16 * LANE) * (16 * LANE)
    grid = head_state[0].astype(BF16).reshape(plan.head_rows, row)
    grid = jnp.concatenate(
        [
            grid[:, : C + 2],
            jnp.zeros((plan.head_rows, LANE - 2), BF16),
            grid[:, C + 2 :],
            jnp.zeros((plan.head_rows, KP - K), BF16),
        ],
        axis=1,
    )
    grid = jnp.pad(grid, ((0, plan.head_pad - plan.head_rows), (0, 0)))
    bias = jnp.pad(bias_state[0], (0, KP - K)).reshape(1, KP)
    per_image = jnp.stack(
        [mix_weight, labels.astype(F32), partner.astype(F32)] + [jnp.zeros_like(mix_weight)] * 5
    )
    block_grad, head_grad, totals = train_step(
        plan, block[0], grid, images.reshape(plan.rows, C), per_image, bias
    )[:3]
    loss_sum = totals[0, KP - 1]
    grad_bias = totals[0, :K]
    block_grad = lax.dynamic_slice(
        block_grad.reshape(LAYERS, plan.chunk * LANE), (0, offset), (LAYERS, plan.shard)
    ).astype(F32)
    head_grad = head_grad[: plan.head_rows].astype(F32)
    head_grad = jnp.concatenate(
        [head_grad[:, : C + 2], head_grad[:, C + LANE : C + LANE + K]], axis=1
    ).reshape(-1)
    return (
        (loss_sum,)
        + adam_update(*block, block_grad)
        + adam_update(*head_state, head_grad)
        + adam_update(*bias_state, grad_bias)
    )


def solution(mesh):
    data = P(("dp", "fsdp"))
    states = (P(None, "fsdp"),) * 4 + (P("fsdp"),) * 4 + (P(),) * 4
    return jax.shard_map(
        functools.partial(on_device, mesh),
        mesh=mesh,
        in_specs=(P(("dp", "fsdp"), None, None), data, data, data) + states,
        out_specs=(P(),) + states,
        check_vma=False,
    )
```
